32 devices in a mesh: dp: 4 (over y, core), ctx: 4 (over z), fsdp: 2 (over x).
Axes of the slice: x: 2, y: 2, z: 4, core: 2. Of those that a mesh axis runs over, the one named last changes fastest.
Arguments:
- residual_in: bfloat16 [16, 1024, 1024], P(('dp', 'fsdp'), 'ctx'), may hold values from -6 to 6
- lengths: int32 [16], P(('dp', 'fsdp')), may hold values from 256 to 1024, as said below
- gain_attn: bfloat16 [1024], P('fsdp'), may hold values from 0.25 to 1.75
- shift_attn: bfloat16 [1024], P('fsdp'), may hold values from -1 to 1
- weight_qkv: bfloat16 [1024, 3072], P('fsdp'), may hold values from -0.1875 to 0.1875
- bias_qkv: bfloat16 [3072], P('fsdp'), may hold values from -1.5 to 1.5
- weight_out: bfloat16 [1024, 1024], P('fsdp'), may hold values from -1.5 to 1.5
- bias_out: bfloat16 [1024], P('fsdp'), may hold values from -1.5 to 1.5
- gain_ffn: bfloat16 [1024], P('fsdp'), may hold values from 0.25 to 1.75
- shift_ffn: bfloat16 [1024], P('fsdp'), may hold values from -1 to 1
- weight_fc: bfloat16 [1024, 4096], P('fsdp'), may hold values from -0.1875 to 0.1875
- bias_fc: bfloat16 [4096], P('fsdp'), may hold values from -2.5 to 2.5
- weight_proj: bfloat16 [4096, 1024], P('fsdp'), may hold values from -0.09375 to 0.09375
- bias_proj: bfloat16 [1024], P('fsdp'), may hold values from -1.5 to 1.5
- cotangent: bfloat16 [16, 1024, 1024], P(('dp', 'fsdp'), 'ctx'), may hold values from -6 to 6
Outputs:
- residual_out: bfloat16 [16, 1024, 1024], P(('dp', 'fsdp'), 'ctx')
- residual_grad: bfloat16 [16, 1024, 1024], P(('dp', 'fsdp'), 'ctx')
- grad_gain_attn: float32 [1024], P('fsdp')
- grad_shift_attn: float32 [1024], P('fsdp')
- grad_weight_qkv: float32 [1024, 3072], P('fsdp')
- grad_bias_qkv: float32 [3072], P('fsdp')
- grad_weight_out: float32 [1024, 1024], P('fsdp')
- grad_bias_out: float32 [1024], P('fsdp')
- grad_gain_ffn: float32 [1024], P('fsdp')
- grad_shift_ffn: float32 [1024], P('fsdp')
- grad_weight_fc: float32 [1024, 4096], P('fsdp')
- grad_bias_fc: float32 [4096], P('fsdp')
- grad_weight_proj: float32 [4096, 1024], P('fsdp')
- grad_bias_proj: float32 [1024], P('fsdp')
The draws below stay inside these ranges and needn't reach their ends.
Inputs may be any that keep to these rules, and one draw needn't show every extreme that they name: `lengths`: among the 2 sequences of each aligned run (those held by one device position along dp and fsdp), at least one has the full length 1024.
All inputs are finite; a program needn't handle non-finite values.
Results may differ from the reference program's by a relative error of at most 0.018.
Values may be sent and summed in bfloat16 or wider, within the bound.
A program may use at most 192 MiB of HBM per device.

```python
import math
import jax
import jax.numpy as jnp
from jax import lax

D = 1024
HEADS = 16
HDIM = 64
ROT = 16
FF = 4096
SEQS = 2
LEN = 1024
NSEQ = 16


def draw_lengths(key, part):
    key = jax.random.fold_in(key, 7)
    first_key, second_key = jax.random.split(key)
    base_lengths = jax.random.randint(first_key, (NSEQ,), LEN // 4, LEN + 1, dtype=jnp.int32)
    full_slot = jax.random.randint(second_key, (NSEQ // SEQS,), 0, SEQS, dtype=jnp.int32)
    slot_index = jnp.arange(NSEQ, dtype=jnp.int32) % SEQS
    full_repeated = jnp.repeat(full_slot, SEQS, total_repeat_length=NSEQ)
    return jnp.where(slot_index == full_repeated, LEN, base_lengths).astype(jnp.int32)


def block_levels(stream_key, extent, pieces, smallest, high):
    def one(dim, parts):
        heights = jax.random.uniform(jax.random.fold_in(jax.random.fold_in(stream_key, 6), dim), (parts,), jnp.float32, smallest / len(pieces), high / len(pieces))
        return jnp.repeat(jnp.exp(heights), extent[dim] // parts).reshape((-1,) + (1,) * (len(extent) - dim - 1))

    level = one(*pieces[0])
    for cut in pieces[1:]:
        level = level * one(*cut)
    return level


def scatter_about(key, dims, scale, most, shards=(), held_as=jnp.bfloat16):
    result = jax.random.normal(key, dims, jnp.float32) * scale
    if len(shards) > 0:
        result = block_levels(key, dims, shards, -0.22, 0.18) * result
    return jnp.clip(result, min=-most, max=most).astype(held_as)


def setup_inputs(seed: int = 0) -> dict:
    key_of = jax.random.split(jax.random.key(seed), 16)
    return {
        "residual_in": scatter_about(key_of[0], (NSEQ, LEN, D), 1.0, 6.0, ((0, 8), (1, 4))),
        "lengths": draw_lengths(jax.random.fold_in(key_of[15], 71), 0),
        "gain_attn": jnp.clip(1.0 + 0.15 * jax.random.normal(key_of[2], (D,), jnp.float32), 0.25, 1.75).astype(jnp.bfloat16),
        "shift_attn": scatter_about(key_of[3], (D,), 0.2, 1.0, ((0, 2),)),
        "weight_qkv": scatter_about(key_of[4], (D, 3 * D), D ** -0.5, 0.1875, ((0, 2),)),
        "bias_qkv": scatter_about(key_of[5], (3 * D,), 0.3, 1.5, ((0, 2),)),
        "weight_out": scatter_about(key_of[6], (D, D), (D // 64) ** -0.5, 1.5, ((0, 2),)),
        "bias_out": scatter_about(key_of[7], (D,), 0.3, 1.5, ((0, 2),)),
        "gain_ffn": jnp.clip(1.0 + 0.15 * jax.random.normal(key_of[8], (D,), jnp.float32), 0.25, 1.75).astype(jnp.bfloat16),
        "shift_ffn": scatter_about(key_of[9], (D,), 0.2, 1.0, ((0, 2),)),
        "weight_fc": scatter_about(key_of[10], (D, FF), D ** -0.5, 0.1875, ((0, 2),)),
        "bias_fc": scatter_about(key_of[11], (FF,), 0.5, 2.5, ((0, 2),)),
        "weight_proj": scatter_about(key_of[12], (FF, D), FF ** -0.5, 0.09375, ((0, 2),)),
        "bias_proj": scatter_about(key_of[13], (D,), 0.3, 1.5, ((0, 2),)),
        "cotangent": scatter_about(key_of[14], (NSEQ, LEN, D), 1.0, 6.0, ((0, 8), (1, 4))),
    }


epsilon = 1e-05
rope_base = 10000.0
masked_score = -1e+30
highest = lax.Precision.HIGHEST

@jax.custom_vjp
def low(v):
    return lax.optimization_barrier(v.astype(jnp.bfloat16)).astype(jnp.float32)

@jax.custom_vjp
def low_back(v):
    return v

def low_keep(v):
    return (low(v), None)

def low_pass(kept, grad):
    return (grad,)

def back_keep(v):
    return (v, None)

def back_low(kept, grad):
    return (low(grad),)
low.defvjp(low_keep, low_pass)
low_back.defvjp(back_keep, back_low)

def layer_norm(features, scale_gain, shift_bias):
    center = features - lax.optimization_barrier(jnp.mean(features, axis=-1, keepdims=True))
    spread = lax.optimization_barrier(jnp.mean(center * center, axis=-1, keepdims=True))
    return center * lax.rsqrt(spread + epsilon) * scale_gain + shift_bias

def rotate(features, positions, rot_dims):
    half_rot = rot_dims // 2
    inverse = rope_base ** (-(2.0 * jnp.arange(half_rot, dtype=jnp.float32)) / rot_dims)
    angles = positions[:, None] * inverse[None, :]
    angles = jnp.concatenate([angles, angles], axis=-1)
    cosine = jnp.cos(angles)[:, None, :]
    sine_part = jnp.sin(angles)[:, None, :]
    turned = features[..., :rot_dims]
    swapped = jnp.concatenate([-turned[..., half_rot:], turned[..., :half_rot]], axis=-1)
    return jnp.concatenate([turned * cosine + swapped * sine_part, features[..., rot_dims:]], axis=-1)

def matmul_high(left, right):
    return jnp.einsum('gtd,de->gte', left, right, precision=highest)

def attention(queries, keys, values, lengths_group):
    query_rows = math.gcd(LEN, 512)
    block_count = LEN // query_rows
    score_scale = 1.0 / math.sqrt(HDIM)
    key_pos = jnp.arange(LEN, dtype=jnp.int32)

    def one_block(block_index):
        start = block_index * query_rows
        query_block = lax.dynamic_slice_in_dim(queries, start, query_rows, 1)
        scores = low_back(jnp.einsum('gqhd,gkhd->ghqk', query_block, keys, precision=highest) * score_scale)
        query_pos = start + jnp.arange(query_rows, dtype=jnp.int32)
        allowed = (key_pos[None, None, None, :] <= query_pos[None, None, :, None]) & (key_pos[None, None, None, :] < lengths_group[:, None, None, None])
        masked = jnp.where(allowed, scores, masked_score)
        row_top = lax.optimization_barrier(jnp.max(masked, axis=-1, keepdims=True))
        expanded = jnp.where(allowed, jnp.exp(masked - row_top), 0.0)
        probs = expanded / lax.optimization_barrier(jnp.sum(expanded, axis=-1, keepdims=True))
        return jnp.einsum('ghqk,gkhd->gqhd', probs, values, precision=highest)
    blocks = lax.map(jax.checkpoint(one_block), jnp.arange(block_count, dtype=jnp.int32))
    return jnp.moveaxis(blocks, 0, 1).reshape(queries.shape)

def forward(features, params, lengths_group):
    gain_one, shift_one, w_qkv, b_qkv, w_out, b_out, gain_two, shift_two, w_fc, b_fc, w_proj, b_proj = params
    hidden_one = low(layer_norm(features, gain_one, shift_one))
    projected = low_back(matmul_high(hidden_one, w_qkv) + b_qkv)
    positions = jnp.arange(LEN, dtype=jnp.float32)
    head_shape = features.shape[:2] + (HEADS, HDIM)
    queries = low(rotate(projected[..., :D].reshape(head_shape), positions, ROT))
    keys = low(rotate(projected[..., D:2 * D].reshape(head_shape), positions, ROT))
    values = low(projected[..., 2 * D:].reshape(head_shape))
    attended = attention(queries, keys, values, lengths_group).reshape(features.shape)
    attended = low(low_back(attended))
    attn_branch = matmul_high(attended, w_out) + b_out
    hidden_two = low(layer_norm(features, gain_two, shift_two))
    up_pre = low_back(matmul_high(hidden_two, w_fc) + b_fc)
    activated = low(jax.nn.gelu(up_pre, approximate=False))
    return features + attn_branch + matmul_high(activated, w_proj) + b_proj

def reference(residual_in, lengths, gain_attn, shift_attn, weight_qkv, bias_qkv, weight_out, bias_out, gain_ffn, shift_ffn, weight_fc, bias_fc, weight_proj, bias_proj, cotangent):
    group_size = math.gcd(NSEQ, max(1, 4096 // LEN))
    group_count = NSEQ // group_size
    params = tuple((a.astype(jnp.float32) for a in (gain_attn, shift_attn, weight_qkv, bias_qkv, weight_out, bias_out, gain_ffn, shift_ffn, weight_fc, bias_fc, weight_proj, bias_proj)))
    inputs_grouped = residual_in.astype(jnp.float32).reshape(group_count, group_size, LEN, D)
    cot_grouped = cotangent.astype(jnp.float32).reshape(group_count, group_size, LEN, D)
    lengths_grouped = lengths.reshape(group_count, group_size)

    def one_group(totals, group_item):
        inputs_now, cot_now, lengths_now = group_item
        valid = (jnp.arange(LEN, dtype=jnp.int32)[None, :] < lengths_now[:, None]).astype(jnp.float32)

        def run_layer(inputs_here, *weights):
            return forward(inputs_here, weights, lengths_now)
        layer_out, pull_back = jax.vjp(run_layer, inputs_now, *params)
        all_grads = pull_back(cot_now * valid[..., None])
        new_totals = tuple((a + b for a, b in zip(totals, all_grads[1:])))
        return (new_totals, (layer_out.astype(jnp.bfloat16), all_grads[0].astype(jnp.bfloat16)))
    init = tuple((jnp.zeros_like(p) for p in params))
    totals, (layer_outs, input_grads) = lax.scan(one_group, init, (inputs_grouped, cot_grouped, lengths_grouped))
    return (layer_outs.reshape(NSEQ, LEN, D), input_grads.reshape(NSEQ, LEN, D), totals[0], totals[1], totals[2], totals[3], totals[4], totals[5], totals[6], totals[7], totals[8], totals[9], totals[10], totals[11])
```

```python
import functools
import math

import jax
import jax.numpy as jnp
from jax import lax
from jax.experimental import pallas as pl
from jax.experimental.pallas import tpu as pltpu
from jax.sharding import PartitionSpec as P

HEADS = 16
ROT = 16
LANES = 256
ROWS = 256

epsilon = 1e-05
rope_base = 10000.0
masked_score = -1e30

f32 = jnp.float32
bf16 = jnp.bfloat16


def dot_nn(a, b):
    return lax.dot_general(a, b, (((1,), (0,)), ((), ())), preferred_element_type=f32)


def dot_nt(a, b):
    return lax.dot_general(a, b, (((1,), (1,)), ((), ())), preferred_element_type=f32)


def attn_kernel(
    length_ref,
    h_ref,
    dy_ref,
    wq_ref,
    wk_ref,
    wv_ref,
    wo_ref,
    b_ref,
    rope_ref,
    out_ref,
    dh_ref,
    gqkv_ref,
    gout_ref,
    gb_ref,
    ht_s,
    q_s,
    k_s,
    v_s,
    do_s,
    kt_s,
    vt_s,
    dot_s,
    ot_s,
    dqt_s,
    dk_s,
    dv_s,
    p_s,
    kb_s,
):
    group = pl.program_id(0)
    total, width = h_ref.shape
    blocks = total // ROWS
    head_size = 64
    heads_here = LANES // head_size
    length = length_ref[0]

    @pl.when(group == 0)
    def _():
        for r in range(blocks):
            ht_s[:, r * ROWS : (r + 1) * ROWS] = h_ref[r * ROWS : (r + 1) * ROWS, :].T
        key_pos = lax.broadcasted_iota(jnp.int32, (total, 128), 0)
        kb_s[...] = jnp.where(key_pos < length, 0.0, masked_score)

    def turn(v, rows):
        left = pltpu.roll(v, LANES - ROT // 2, 1)
        right = pltpu.roll(v, ROT // 2, 1)
        return v * rope_ref[0, rows, :] + left * rope_ref[1, rows, :] + right * rope_ref[2, rows, :]

    def turn_back(v, rows):
        left = pltpu.roll(v, LANES - ROT // 2, 1)
        right = pltpu.roll(v, ROT // 2, 1)
        return v * rope_ref[0, rows, :] - left * rope_ref[1, rows, :] - right * rope_ref[2, rows, :]

    for r in range(blocks):
        rows = slice(r * ROWS, (r + 1) * ROWS)
        hr = h_ref[rows, :]
        q = turn(dot_nn(hr, wq_ref[...]) + b_ref[0, 0:1, :], rows).astype(bf16)
        q_s[rows, :] = (q.astype(f32) * 0.125).astype(bf16)
        k = turn(dot_nn(hr, wk_ref[...]) + b_ref[1, 0:1, :], rows).astype(bf16)
        k_s[rows, :] = k
        kt_s[:, rows] = k.T
        v = (dot_nn(hr, wv_ref[...]) + b_ref[2, 0:1, :]).astype(bf16)
        v_s[rows, :] = v
        vt_s[:, rows] = v.T
        do = dot_nt(dy_ref[rows, :], wo_ref[...]).astype(bf16)
        do_s[rows, :] = do
        dot_s[:, rows] = do.T

    dk_s[...] = jnp.zeros_like(dk_s)
    dv_s[...] = jnp.zeros_like(dv_s)
    lane = lax.broadcasted_iota(jnp.int32, (ROWS, LANES), 1)
    causal = lax.broadcasted_iota(jnp.int32, (ROWS, ROWS), 0) <= lax.broadcasted_iota(
        jnp.int32, (ROWS, ROWS), 1
    )

    def one_head(head, carry):
        feats = pl.ds(pl.multiple_of(head * head_size, head_size), head_size)
        mine = (lane // head_size) == head
        zero = jnp.zeros((ROWS, LANES), bf16)
        for i in range(blocks):
            rows = slice(i * ROWS, (i + 1) * ROWS)
            qm = jnp.where(mine, q_s[rows, :], zero)
            dom = jnp.where(mine, do_s[rows, :], zero)
            scores = []
            top = None
            for b in range(i + 1):
                keys = slice(b * ROWS, (b + 1) * ROWS)
                sc = dot_nt(k_s[keys, :], qm)
                kb = kb_s[keys, :]
                sc = sc + jnp.concatenate([kb, kb], axis=1)
                if b == i:
                    sc = jnp.where(causal, sc, masked_score)
                best = jnp.max(sc, axis=0, keepdims=True)
                top = best if top is None else jnp.maximum(top, best)
                scores.append(sc)
            row_sum = None
            for b in range(i + 1):
                scores[b] = jnp.exp(scores[b] - top)
                part = jnp.sum(scores[b], axis=0, keepdims=True)
                row_sum = part if row_sum is None else row_sum + part
            inverse = 1.0 / row_sum
            o_t = None
            for b in range(i + 1):
                keys = slice(b * ROWS, (b + 1) * ROWS)
                scores[b] = scores[b] * inverse
                low = scores[b].astype(bf16)
                dv_s[keys, :] += dot_nn(low, dom)
                part = dot_nn(vt_s[feats, keys], low)
                o_t = part if o_t is None else o_t + part
            ot_s[feats, rows] = o_t
            delta = jnp.sum(dot_s[feats, rows].astype(f32) * o_t, axis=0, keepdims=True)
            dq_t = None
            for b in range(i + 1):
                keys = slice(b * ROWS, (b + 1) * ROWS)
                dp = dot_nt(v_s[keys, :], dom)
                ds = (scores[b] * (dp - delta)).astype(bf16)
                dk_s[keys, :] += dot_nn(ds, qm)
                part = dot_nn(kt_s[feats, keys], ds)
                dq_t = part if dq_t is None else dq_t + part
            dqt_s[feats, rows] = dq_t * 0.125
        return carry

    lax.fori_loop(0, heads_here, one_head, 0)

    sums = [jnp.zeros((1, LANES), f32) for _ in range(3)]
    for r in range(blocks):
        rows = slice(r * ROWS, (r + 1) * ROWS)
        dq = turn_back(dqt_s[:, rows].T, rows).astype(bf16)
        dk = turn_back(dk_s[rows, :], rows).astype(bf16)
        dv = dv_s[rows, :].astype(bf16)
        for at, grad in enumerate((dq, dk, dv)):
            sums[at] = sums[at] + jnp.sum(grad.astype(f32), axis=0, keepdims=True)
            p_s[at, rows, :] = grad
        o = ot_s[:, rows].T.astype(bf16)
        out_part = dot_nn(o, wo_ref[...])
        dh_part = (
            dot_nt(dq, wq_ref[...]) + dot_nt(dk, wk_ref[...]) + dot_nt(dv, wv_ref[...])
        )

        @pl.when(group == 0)
        def _():
            out_ref[rows, :] = out_part
            dh_ref[rows, :] = dh_part

        @pl.when(group > 0)
        def _():
            out_ref[rows, :] += out_part
            dh_ref[rows, :] += dh_part

    for at in range(3):
        gb_ref[at] = jnp.broadcast_to(sums[at], (8, LANES))
        for r in range(width // ROWS):
            rows = slice(r * ROWS, (r + 1) * ROWS)
            gqkv_ref[at, rows, :] = dot_nn(ht_s[rows, :], p_s[at]).astype(bf16)
    gout_ref[...] = dot_nn(ot_s[...].astype(bf16), dy_ref[...]).astype(bf16)


def attention_branch(length, hidden, out_grad, w_qkv, w_out, b_qkv, rope):
    total, width = hidden.shape
    inner = w_out.shape[0]
    groups = inner // LANES
    whole = lambda g: (0, 0)
    flops = 2 * total * width * inner * 12 + 2 * groups * 4 * total * total * LANES * 4
    return pl.pallas_call(
        attn_kernel,
        grid=(groups,),
        in_specs=[
            pl.BlockSpec(memory_space=pltpu.SMEM),
            pl.BlockSpec((total, width), whole),
            pl.BlockSpec((total, width), whole),
            pl.BlockSpec((width, LANES), lambda g: (0, g)),
            pl.BlockSpec((width, LANES), lambda g: (0, groups + g)),
            pl.BlockSpec((width, LANES), lambda g: (0, 2 * groups + g)),
            pl.BlockSpec((LANES, width), lambda g: (g, 0)),
            pl.BlockSpec((3, 8, LANES), lambda g: (0, 0, g)),
            pl.BlockSpec((3, total, LANES), lambda g: (0, 0, 0)),
        ],
        out_specs=[
            pl.BlockSpec((total, width), whole),
            pl.BlockSpec((total, width), whole),
            pl.BlockSpec((3, width, LANES), lambda g: (0, 0, g)),
            pl.BlockSpec((LANES, width), lambda g: (g, 0)),
            pl.BlockSpec((3, 8, LANES), lambda g: (0, 0, g)),
        ],
        out_shape=[
            jax.ShapeDtypeStruct((total, width), f32),
            jax.ShapeDtypeStruct((total, width), f32),
            jax.ShapeDtypeStruct((3, width, inner), bf16),
            jax.ShapeDtypeStruct((inner, width), bf16),
            jax.ShapeDtypeStruct((3, 8, inner), f32),
        ],
        scratch_shapes=[
            pltpu.VMEM((width, total), bf16),
            pltpu.VMEM((total, LANES), bf16),
            pltpu.VMEM((total, LANES), bf16),
            pltpu.VMEM((total, LANES), bf16),
            pltpu.VMEM((total, LANES), bf16),
            pltpu.VMEM((LANES, total), bf16),
            pltpu.VMEM((LANES, total), bf16),
            pltpu.VMEM((LANES, total), bf16),
            pltpu.VMEM((LANES, total), f32),
            pltpu.VMEM((LANES, total), f32),
            pltpu.VMEM((total, LANES), f32),
            pltpu.VMEM((total, LANES), f32),
            pltpu.VMEM((3, total, LANES), bf16),
            pltpu.VMEM((total, 128), f32),
        ],
        compiler_params=pltpu.CompilerParams(vmem_limit_bytes=60 * 2**20),
        cost_estimate=pl.CostEstimate(
            flops=flops, bytes_accessed=24 * 2**20, transcendentals=8 * total * total
        ),
        name="attention",
    )(length, hidden, out_grad, w_qkv, w_qkv, w_qkv, w_out, b_qkv, rope)


def ffn_kernel(
    h_ref,
    dy_ref,
    wf_ref,
    wp_ref,
    b_ref,
    out_ref,
    dh_ref,
    gf_ref,
    gp_ref,
    gb_ref,
    ht_s,
    act_s,
    dup_s,
):
    step = pl.program_id(0)
    total, width = h_ref.shape
    blocks = total // ROWS
    chunk = wf_ref.shape[1]

    @pl.when(step == 0)
    def _():
        for r in range(blocks):
            ht_s[:, r * ROWS : (r + 1) * ROWS] = h_ref[r * ROWS : (r + 1) * ROWS, :].T

    def one(r, total_grad):
        rows = pl.ds(pl.multiple_of(r * ROWS, ROWS), ROWS)
        up = dot_nn(h_ref[rows, :], wf_ref[...]) + b_ref[0:1, :]
        half = 0.5 + 0.5 * lax.erf(up * (1.0 / math.sqrt(2.0)))
        act = (up * half).astype(bf16)
        slope = half + up * (jnp.exp(-0.5 * up * up) * (1.0 / math.sqrt(2.0 * math.pi)))
        act_grad = dot_nt(dy_ref[rows, :], wp_ref[...])
        up_grad = (slope * act_grad).astype(bf16)
        act_s[rows, :] = act
        dup_s[rows, :] = up_grad
        out_part = dot_nn(act, wp_ref[...])
        dh_part = dot_nt(up_grad, wf_ref[...])

        @pl.when(step == 0)
        def _():
            out_ref[rows, :] = out_part
            dh_ref[rows, :] = dh_part

        @pl.when(step > 0)
        def _():
            out_ref[rows, :] += out_part
            dh_ref[rows, :] += dh_part

        return total_grad + jnp.sum(up_grad.astype(f32), axis=0, keepdims=True)

    sums = lax.fori_loop(0, blocks, one, jnp.zeros((1, chunk), f32))
    gb_ref[...] = jnp.broadcast_to(sums, (8, chunk))
    for r in range(width // ROWS):
        rows = slice(r * ROWS, (r + 1) * ROWS)
        gf_ref[rows, :] = dot_nn(ht_s[rows, :], dup_s[...]).astype(bf16)
    for r in range(chunk // ROWS):
        cols = slice(r * ROWS, (r + 1) * ROWS)
        gp_ref[cols, :] = dot_nn(act_s[:, cols].T, dy_ref[...]).astype(bf16)


def ffn_branch(hidden, out_grad, w_fc, w_proj, b_fc):
    total, width = hidden.shape
    units = w_proj.shape[0]
    chunk = min(512, units)
    whole = lambda s: (0, 0)
    return pl.pallas_call(
        ffn_kernel,
        grid=(units // chunk,),
        in_specs=[
            pl.BlockSpec((total, width), whole),
            pl.BlockSpec((total, width), whole),
            pl.BlockSpec((width, chunk), lambda s: (0, s)),
            pl.BlockSpec((chunk, width), lambda s: (s, 0)),
            pl.BlockSpec((8, chunk), lambda s: (0, s)),
        ],
        out_specs=[
            pl.BlockSpec((total, width), whole),
            pl.BlockSpec((total, width), whole),
            pl.BlockSpec((width, chunk), lambda s: (0, s)),
            pl.BlockSpec((chunk, width), lambda s: (s, 0)),
            pl.BlockSpec((8, chunk), lambda s: (0, s)),
        ],
        out_shape=[
            jax.ShapeDtypeStruct((total, width), f32),
            jax.ShapeDtypeStruct((total, width), f32),
            jax.ShapeDtypeStruct((width, units), bf16),
            jax.ShapeDtypeStruct((units, width), bf16),
            jax.ShapeDtypeStruct((8, units), f32),
        ],
        scratch_shapes=[
            pltpu.VMEM((width, total), bf16),
            pltpu.VMEM((total, chunk), bf16),
            pltpu.VMEM((total, chunk), bf16),
        ],
        compiler_params=pltpu.CompilerParams(vmem_limit_bytes=60 * 2**20),
        cost_estimate=pl.CostEstimate(
            flops=2 * total * width * units * 6,
            bytes_accessed=28 * 2**20,
            transcendentals=2 * total * units,
        ),
        name="feed_forward",
    )(hidden, out_grad, w_fc, w_proj, b_fc)


def shift(block, axis, distance):
    count = lax.axis_size(axis)
    return lax.ppermute(block, axis, [(i, (i + distance) % count) for i in range(count)])


def swap_bit(block, axis, bit):
    return lax.ppermute(block, axis, [(i, i ^ bit) for i in range(lax.axis_size(axis))])


def shift_within(block, axis, size, distance):
    count = lax.axis_size(axis)
    return lax.ppermute(
        block,
        axis,
        [(i, i // size * size + (i % size + distance) % size) for i in range(count)],
    )


def pick(array, index, axis=0):
    return lax.dynamic_index_in_dim(array, index, axis, keepdims=False)


def order_two(flag, mine, other):
    first = flag == 0
    return jnp.stack([jnp.where(first, mine, other), jnp.where(first, other, mine)])


def gather_rows(local, place):
    dp, y, core, f = place["dp"], place["y"], place["core"], place["f"]
    count = lax.axis_size("fsdp")
    rows, cols = local.shape
    share = rows // lax.axis_size("dp")
    mine = lax.dynamic_slice_in_dim(local, dp * share, share, 0)
    got = jnp.stack([shift(mine, "fsdp", e) for e in range(1, count)])
    got = order_two(y, got, swap_bit(got, "dp", 2))
    got = order_two(core, got, swap_bit(got, "dp", 1))
    got = jnp.transpose(got, (2, 1, 0, 3, 4)).reshape(count - 1, rows, cols)
    if count == 2:
        return order_two(f, local, got[0])
    whole = jnp.zeros((count, rows, cols), local.dtype)
    whole = lax.dynamic_update_index_in_dim(whole, local, f, 0)
    for e in range(1, count):
        whole = lax.dynamic_update_index_in_dim(whole, got[e - 1], (f - e) % count, 0)
    return whole


def reduce_rows(partial, place, parts):
    dp, y, core, f, j = (place[k] for k in ("dp", "y", "core", "f", "j"))
    count, rows, cols = partial.shape
    share = rows // 4
    a = partial.reshape(count, 2, 2, share, cols)
    a = pick(a, core, 2) + swap_bit(pick(a, 1 - core, 2), "dp", 1)
    total = pick(a, f)
    for e in range(1, count):
        total = total + shift(pick(a, (f + e) % count), "fsdp", e)
    total = pick(total, y) + swap_bit(pick(total, 1 - y), "dp", 2)
    total = total + shift(total, "ctx", parts)
    if parts == 2:
        both = order_two(j, total, shift_within(total, "ctx", 2, 1))
    else:
        both = jnp.zeros((parts,) + total.shape, total.dtype)
        both = lax.dynamic_update_index_in_dim(both, total, j, 0)
        for e in range(1, parts):
            got = shift_within(total, "ctx", parts, e)
            both = lax.dynamic_update_index_in_dim(both, got, (j - e) % parts, 0)
    both = order_two(y, both, swap_bit(both, "dp", 2))
    both = order_two(core, both, swap_bit(both, "dp", 1))
    return jnp.transpose(both, (1, 0, 3, 2, 4)).reshape(rows, parts, cols).astype(f32)


def sum_everywhere(vector):
    for bit in (1, 2):
        vector = vector + swap_bit(vector, "dp", bit)
    for axis in ("fsdp", "ctx"):
        bit = 1
        while bit < lax.axis_size(axis):
            vector = vector + swap_bit(vector, axis, bit)
            bit *= 2
    return vector


def gather_sequence(blocks, place, parts):
    s, c = place["s"], place["c"]
    count = lax.axis_size("ctx")
    seqs, rows, width = blocks.shape
    pieces = [(c, pick(blocks, s))]
    for d in range(1, seqs):
        got = shift(pick(blocks, (s + d) % seqs), "ctx", d * parts)
        pieces.append(((c - d * parts) % count, got))
    arrived = []
    for d in range(seqs):
        arrived.append(pieces[d])
        for e in range(1, parts):
            source = s * parts + (place["j"] - e) % parts
            got = shift_within(pieces[d][1], "ctx", parts, e)
            arrived.append(((source - d * parts) % count, got))
    whole = jnp.zeros((count, rows, width), blocks.dtype)
    for at, piece in arrived:
        whole = lax.dynamic_update_index_in_dim(whole, piece, at, 0)
    return whole.reshape(count * rows, width)


def return_blocks(partial, place, parts, seqs):
    s, c, j = place["s"], place["c"], place["j"]
    count = lax.axis_size("ctx")
    rows = partial.shape[0] // count
    blocks = partial.reshape(seqs, parts, rows, -1)
    total = pick(blocks, j, 1).astype(f32)
    for e in range(1, parts):
        total = total + shift_within(pick(blocks, (j + e) % parts, 1), "ctx", parts, e).astype(f32)
    mine = [pick(total, s)]
    for d in range(1, seqs):
        mine.append(shift(pick(total, (s + d) % seqs).astype(bf16), "ctx", d * parts).astype(f32))
    if seqs == 2:
        return order_two(s, mine[0], mine[1])
    whole = jnp.zeros((seqs, rows, partial.shape[1]), f32)
    for d in range(seqs):
        whole = lax.dynamic_update_index_in_dim(whole, mine[d], (s - d) % seqs, 0)
    return whole


def normalize(features):
    center = features - jnp.mean(features, axis=-1, keepdims=True)
    spread = jnp.mean(center * center, axis=-1, keepdims=True)
    inverse = lax.rsqrt(spread + epsilon)
    return center * inverse, inverse


def rope_tables(total, head_size):
    half = ROT // 2
    inverse = rope_base ** (-(2.0 * jnp.arange(half, dtype=f32)) / ROT)
    angles = jnp.arange(total, dtype=jnp.int32).astype(f32)[:, None] * inverse[None, :]
    cosine, sine = jnp.cos(angles), jnp.sin(angles)
    rest = jnp.zeros((total, head_size - ROT), f32)
    none = jnp.zeros((total, half), f32)
    same = jnp.concatenate([cosine, cosine, rest + 1.0], axis=1)
    ahead = jnp.concatenate([-sine, none, rest], axis=1)
    behind = jnp.concatenate([none, sine, rest], axis=1)
    return jnp.tile(jnp.stack([same, ahead, behind]), (1, 1, LANES // head_size))


def per_device(
    residual_in,
    lengths,
    gain_attn,
    shift_attn,
    weight_qkv,
    bias_qkv,
    weight_out,
    bias_out,
    gain_ffn,
    shift_ffn,
    weight_fc,
    bias_fc,
    weight_proj,
    bias_proj,
    cotangent,
):
    seqs, block_rows, width = residual_in.shape
    n_ctx, n_fsdp = lax.axis_size("ctx"), lax.axis_size("fsdp")
    parts = n_ctx // seqs
    total = n_ctx * block_rows
    units = weight_fc.shape[1]
    head_size = width // HEADS
    c, f, dp = lax.axis_index("ctx"), lax.axis_index("fsdp"), lax.axis_index("dp")
    s, j = c // parts, c % parts
    place = dict(c=c, f=f, dp=dp, s=s, j=j, y=dp // 2, core=dp % 2)
    spread_heads = HEADS % (n_fsdp * parts) == 0
    n_h = n_fsdp if spread_heads else 1
    inner = width // parts

    small_local = jnp.concatenate(
        [gain_attn, shift_attn, gain_ffn, shift_ffn, bias_out, bias_proj, bias_qkv, bias_fc]
    )
    small = lax.all_gather(small_local, "fsdp", axis=0)
    part_width = width // n_fsdp
    vec = lambda at, size: small[:, at : at + size].reshape(-1).astype(f32)
    gain_one, shift_one, gain_two, shift_two, b_out, b_proj = (
        vec(i * part_width, part_width) for i in range(6)
    )
    b_qkv = vec(6 * part_width, 3 * part_width)
    b_fc = vec(9 * part_width, units // n_fsdp)

    rows_here = weight_qkv.shape[0]
    fc_local = pick(weight_fc.reshape(rows_here, n_fsdp, parts, -1), j, 2).reshape(rows_here, -1)
    proj_local = pick(weight_proj.reshape(parts, -1, width), j)
    qkv_local = pick(weight_qkv.reshape(rows_here, 3, n_h, parts, -1), j, 3).reshape(rows_here, -1)
    seq_in = gather_sequence(residual_in, place, parts)
    w_fc = gather_rows(fc_local, place).reshape(width, -1)
    w_proj = gather_rows(proj_local, place).reshape(-1, width)
    seq_grad = gather_sequence(cotangent, place, parts)
    w_qkv = gather_rows(qkv_local, place).reshape(width, -1)
    if spread_heads:
        w_out = gather_rows(pick(weight_out.reshape(parts, -1, width), j), place).reshape(-1, width)
    else:
        w_out = lax.all_gather(weight_out, "fsdp", axis=0, tiled=True)
        w_out = pick(w_out.reshape(parts, -1, width), j)
    b_qkv_j = pick(b_qkv.reshape(3, n_h, parts, -1), j, 2).reshape(3, 1, inner)
    b_qkv_j = jnp.broadcast_to(b_qkv_j, (3, 8, inner))
    b_fc_j = pick(b_fc.reshape(n_fsdp, parts, -1), j, 1).reshape(1, -1)
    b_fc_j = jnp.broadcast_to(b_fc_j, (8, b_fc_j.shape[1]))

    length = pick(lengths, s)
    positions = jnp.arange(total, dtype=jnp.int32)
    seq_grad = jnp.where((positions < length)[:, None], seq_grad, jnp.zeros((), bf16))
    xhat, _ = normalize(seq_in.astype(f32))
    hidden_one = (xhat * gain_one + shift_one).astype(bf16)
    hidden_two = (xhat * gain_two + shift_two).astype(bf16)

    ffn_out, ffn_dh, g_fc, g_proj, g_bfc = ffn_branch(
        hidden_two, seq_grad, w_fc, w_proj, b_fc_j
    )
    attn_out, attn_dh, g_qkv, g_out, g_bqkv = attention_branch(
        length[None],
        hidden_one,
        seq_grad,
        w_qkv,
        w_out,
        b_qkv_j,
        rope_tables(total, head_size),
    )

    d_proj = reduce_rows(g_proj.reshape(n_fsdp, -1, width), place, parts)
    d_fc = reduce_rows(g_fc.reshape(n_fsdp, rows_here, -1), place, parts)
    q_rows = jnp.swapaxes(g_qkv.reshape(3, n_fsdp, rows_here, inner), 0, 1)
    q_rows = jnp.swapaxes(q_rows, 1, 2).reshape(n_fsdp, rows_here, 3 * inner)
    d_qkv = reduce_rows(q_rows, place, parts)
    d_proj = jnp.swapaxes(d_proj, 0, 1).reshape(weight_proj.shape)
    d_fc = d_fc.reshape(rows_here, parts, n_fsdp, -1)
    d_fc = jnp.swapaxes(d_fc, 1, 2).reshape(weight_fc.shape)
    d_qkv = d_qkv.reshape(rows_here, parts, 3, n_h, -1)
    d_qkv = jnp.transpose(d_qkv, (0, 2, 3, 1, 4)).reshape(weight_qkv.shape)
    if spread_heads:
        d_out = reduce_rows(g_out.reshape(n_fsdp, -1, width), place, parts)
        d_out = jnp.swapaxes(d_out, 0, 1).reshape(weight_out.shape)
    else:
        full = jnp.zeros((parts, inner, width), bf16)
        full = lax.dynamic_update_index_in_dim(full, g_out, j, 0).reshape(width, width)
        d_out = lax.psum_scatter(full, "fsdp", scatter_dimension=0, tiled=True)
        d_out = lax.psum(d_out, ("dp", "ctx")).astype(f32)

    own_grad = jnp.sum(seq_grad.astype(f32), axis=0) / parts
    g_bqkv_all = jnp.zeros((3, n_h, parts, inner // n_h), f32)
    g_bqkv_all = lax.dynamic_update_index_in_dim(
        g_bqkv_all, g_bqkv[:, 0].reshape(3, n_h, -1), j, 2
    )
    g_bfc_all = jnp.zeros((n_fsdp, parts, units // (n_fsdp * parts)), f32)
    g_bfc_all = lax.dynamic_update_index_in_dim(g_bfc_all, g_bfc[0].reshape(n_fsdp, -1), j, 1)
    rows_of = (
        jnp.sum(attn_dh * xhat, axis=0),
        jnp.sum(attn_dh, axis=0),
        jnp.sum(ffn_dh * xhat, axis=0),
        jnp.sum(ffn_dh, axis=0),
        own_grad,
        g_bqkv_all.reshape(-1),
        g_bfc_all.reshape(-1),
    )
    flat = sum_everywhere(jnp.concatenate(rows_of).reshape(-1, 128)).reshape(-1)
    small_grads = []
    at = 0
    for entry in rows_of:
        size = entry.shape[0]
        mine = lax.dynamic_slice_in_dim(flat, at + f * (size // n_fsdp), size // n_fsdp)
        small_grads.append(mine)
        at += size
    d_gain_one, d_shift_one, d_gain_two, d_shift_two, d_bias, d_bqkv, d_bfc = small_grads

    branch = return_blocks((attn_out + ffn_out).astype(bf16), place, parts, seqs)
    pulled = return_blocks(
        (attn_dh * gain_one + ffn_dh * gain_two).astype(bf16), place, parts, seqs
    )
    features = residual_in.astype(f32)
    residual_out = (features + branch + (b_out + b_proj)).astype(bf16)
    own_hat, own_inverse = normalize(features)
    pulled = own_inverse * (
        pulled
        - jnp.mean(pulled, axis=-1, keepdims=True)
        - own_hat * jnp.mean(pulled * own_hat, axis=-1, keepdims=True)
    )
    own_pos = c * block_rows + jnp.arange(block_rows, dtype=jnp.int32)
    valid = (own_pos[None, :] < lengths[:, None])[..., None]
    residual_grad = (jnp.where(valid, cotangent.astype(f32), 0.0) + pulled).astype(bf16)
    return (
        residual_out,
        residual_grad,
        d_gain_one,
        d_shift_one,
        d_qkv,
        d_bqkv,
        d_out,
        d_bias,
        d_gain_two,
        d_shift_two,
        d_fc,
        d_bfc,
        d_proj,
        d_bias,
    )


def solution(mesh):
    tokens = P(("dp", "fsdp"), "ctx", None)
    vector, matrix = P("fsdp"), P("fsdp", None)
    return jax.shard_map(
        per_device,
        mesh=mesh,
        in_specs=(
            tokens,
            P(("dp", "fsdp")),
            vector,
            vector,
            matrix,
            vector,
            matrix,
            vector,
            vector,
            vector,
            matrix,
            vector,
            matrix,
            vector,
            tokens,
        ),
        out_specs=(
            tokens,
            tokens,
            vector,
            vector,
            matrix,
            vector,
            matrix,
            vector,
            vector,
            vector,
            matrix,
            vector,
            matrix,
            vector,
        ),
        check_vma=False,
    )
```

```python
import functools
import math

import jax
import jax.numpy as jnp
from jax import lax
from jax.experimental import pallas as pl
from jax.experimental.pallas import tpu as pltpu
from jax.sharding import PartitionSpec as P

HEADS = 16
ROT = 16
LANES = 256
ROWS = 256

epsilon = 1e-05
rope_base = 10000.0
masked_score = -1e30

f32 = jnp.float32
bf16 = jnp.bfloat16


def dot_nn(a, b):
    return lax.dot_general(a, b, (((1,), (0,)), ((), ())), preferred_element_type=f32)


def dot_nt(a, b):
    return lax.dot_general(a, b, (((1,), (1,)), ((), ())), preferred_element_type=f32)


def slot_of(chunk, tiled):
    return chunk % 2 * 4 + chunk // 2 if tiled else chunk


def attn_kernel(
    tiled,
    length_ref,
    h_ref,
    dy_ref,
    wq_ref,
    wk_ref,
    wv_ref,
    wo_ref,
    b_ref,
    rope_ref,
    out_ref,
    dh_ref,
    gqkv_ref,
    gout_ref,
    gb_ref,
    ht_s,
    q_s,
    k_s,
    v_s,
    do_s,
    kt_s,
    vt_s,
    dot_s,
    ot_s,
    dqt_s,
    dk_s,
    dv_s,
    p_s,
    kb_s,
):
    group = pl.program_id(0)
    total, width = h_ref.shape
    blocks = total // ROWS
    head_size = 64
    heads_here = LANES // head_size
    length = length_ref[0]

    @pl.when(group == 0)
    def _():
        for r in range(blocks):
            ht_s[:, r * ROWS : (r + 1) * ROWS] = h_ref[r * ROWS : (r + 1) * ROWS, :].T
        key_pos = lax.broadcasted_iota(jnp.int32, (total, 128), 0)
        kb_s[...] = jnp.where(key_pos < length, 0.0, masked_score)

    def turn(v, rows):
        left = pltpu.roll(v, LANES - ROT // 2, 1)
        right = pltpu.roll(v, ROT // 2, 1)
        return v * rope_ref[0, rows, :] + left * rope_ref[1, rows, :] + right * rope_ref[2, rows, :]

    def turn_back(v, rows):
        left = pltpu.roll(v, LANES - ROT // 2, 1)
        right = pltpu.roll(v, ROT // 2, 1)
        return v * rope_ref[0, rows, :] - left * rope_ref[1, rows, :] - right * rope_ref[2, rows, :]

    for r in range(blocks):
        rows = slice(r * ROWS, (r + 1) * ROWS)
        hr = h_ref[rows, :]
        q = turn(dot_nn(hr, wq_ref[...]) + b_ref[0, 0:1, :], rows).astype(bf16)
        q_s[rows, :] = (q.astype(f32) * 0.125).astype(bf16)
        k = turn(dot_nn(hr, wk_ref[...]) + b_ref[1, 0:1, :], rows).astype(bf16)
        k_s[rows, :] = k
        kt_s[:, rows] = k.T
        v = (dot_nn(hr, wv_ref[...]) + b_ref[2, 0:1, :]).astype(bf16)
        v_s[rows, :] = v
        vt_s[:, rows] = v.T
        do = dot_nt(dy_ref[rows, :], wo_ref[...]).astype(bf16)
        do_s[rows, :] = do
        dot_s[:, rows] = do.T

    dk_s[...] = jnp.zeros_like(dk_s)
    dv_s[...] = jnp.zeros_like(dv_s)
    lane = lax.broadcasted_iota(jnp.int32, (ROWS, LANES), 1)
    causal = lax.broadcasted_iota(jnp.int32, (ROWS, ROWS), 0) <= lax.broadcasted_iota(
        jnp.int32, (ROWS, ROWS), 1
    )

    def one_head(head, carry):
        feats = pl.ds(pl.multiple_of(head * head_size, head_size), head_size)
        mine = (lane // head_size) == head
        zero = jnp.zeros((ROWS, LANES), bf16)
        for i in range(blocks):
            rows = slice(i * ROWS, (i + 1) * ROWS)
            qm = jnp.where(mine, q_s[rows, :], zero)
            dom = jnp.where(mine, do_s[rows, :], zero)
            scores = []
            top = None
            for b in range(i + 1):
                keys = slice(b * ROWS, (b + 1) * ROWS)
                sc = dot_nt(k_s[keys, :], qm)
                kb = kb_s[keys, :]
                sc = sc + jnp.concatenate([kb, kb], axis=1)
                if b == i:
                    sc = jnp.where(causal, sc, masked_score)
                best = jnp.max(sc, axis=0, keepdims=True)
                top = best if top is None else jnp.maximum(top, best)
                scores.append(sc)
            row_sum = None
            for b in range(i + 1):
                scores[b] = jnp.exp(scores[b] - top)
                part = jnp.sum(scores[b], axis=0, keepdims=True)
                row_sum = part if row_sum is None else row_sum + part
            inverse = 1.0 / row_sum
            o_t = None
            for b in range(i + 1):
                keys = slice(b * ROWS, (b + 1) * ROWS)
                scores[b] = scores[b] * inverse
                low = scores[b].astype(bf16)
                dv_s[keys, :] += dot_nn(low, dom)
                part = dot_nn(vt_s[feats, keys], low)
                o_t = part if o_t is None else o_t + part
            ot_s[feats, rows] = o_t
            delta = jnp.sum(dot_s[feats, rows].astype(f32) * o_t, axis=0, keepdims=True)
            dq_t = None
            for b in range(i + 1):
                keys = slice(b * ROWS, (b + 1) * ROWS)
                dp = dot_nt(v_s[keys, :], dom)
                ds = (scores[b] * (dp - delta)).astype(bf16)
                dk_s[keys, :] += dot_nn(ds, qm)
                part = dot_nn(kt_s[feats, keys], ds)
                dq_t = part if dq_t is None else dq_t + part
            dqt_s[feats, rows] = dq_t * 0.125
        return carry

    lax.fori_loop(0, heads_here, one_head, 0)

    sums = [jnp.zeros((1, LANES), f32) for _ in range(3)]
    for r in range(blocks):
        rows = slice(r * ROWS, (r + 1) * ROWS)
        dq = turn_back(dqt_s[:, rows].T, rows).astype(bf16)
        dk = turn_back(dk_s[rows, :], rows).astype(bf16)
        dv = dv_s[rows, :].astype(bf16)
        for at, grad in enumerate((dq, dk, dv)):
            sums[at] = sums[at] + jnp.sum(grad.astype(f32), axis=0, keepdims=True)
            p_s[at, rows, :] = grad
        o = ot_s[:, rows].T.astype(bf16)
        out_part = dot_nn(o, wo_ref[...])
        dh_part = (
            dot_nt(dq, wq_ref[...]) + dot_nt(dk, wk_ref[...]) + dot_nt(dv, wv_ref[...])
        )

        @pl.when(group == 0)
        def _():
            out_ref[rows, :] = out_part
            dh_ref[rows, :] = dh_part

        @pl.when(group > 0)
        def _():
            out_ref[rows, :] += out_part
            dh_ref[rows, :] += dh_part

    for at in range(3):
        gb_ref[at] = jnp.broadcast_to(sums[at], (8, LANES))
        for r in range(8):
            size = width // 8
            rows = slice(r * size, (r + 1) * size)
            gqkv_ref[at, slot_of(r, tiled)] = dot_nn(ht_s[rows, :], p_s[at]).astype(bf16)
    for r in range(4):
        rows = slice(r * 64, (r + 1) * 64)
        grad = dot_nn(ot_s[rows, :].astype(bf16), dy_ref[...]).astype(bf16)
        if tiled:
            gout_ref[r % 2, 0, r // 2] = grad
        else:
            gout_ref[rows, :] = grad


def attention_branch(length, hidden, out_grad, w_qkv, w_out, b_qkv, rope, tiled):
    total, width = hidden.shape
    inner = w_out.shape[0]
    groups = inner // LANES
    whole = lambda g: (0, 0)
    flops = 2 * total * width * inner * 12 + 2 * groups * 4 * total * total * LANES * 4
    if tiled:
        gout_spec = pl.BlockSpec((2, 1, 2, LANES // 4, width), lambda g: (0, g, 0, 0, 0))
        gout_shape = (2, groups, 2, LANES // 4, width)
    else:
        gout_spec = pl.BlockSpec((LANES, width), lambda g: (g, 0))
        gout_shape = (inner, width)
    return pl.pallas_call(
        functools.partial(attn_kernel, tiled),
        grid=(groups,),
        in_specs=[
            pl.BlockSpec(memory_space=pltpu.SMEM),
            pl.BlockSpec((total, width), whole),
            pl.BlockSpec((total, width), whole),
            pl.BlockSpec((width, LANES), lambda g: (0, g)),
            pl.BlockSpec((width, LANES), lambda g: (0, groups + g)),
            pl.BlockSpec((width, LANES), lambda g: (0, 2 * groups + g)),
            pl.BlockSpec((LANES, width), lambda g: (g, 0)),
            pl.BlockSpec((3, 8, LANES), lambda g: (0, 0, g)),
            pl.BlockSpec((3, total, LANES), lambda g: (0, 0, 0)),
        ],
        out_specs=[
            pl.BlockSpec((total, width), whole),
            pl.BlockSpec((total, width), whole),
            pl.BlockSpec((3, 8, width // 8, LANES), lambda g: (0, 0, 0, g)),
            gout_spec,
            pl.BlockSpec((3, 8, LANES), lambda g: (0, 0, g)),
        ],
        out_shape=[
            jax.ShapeDtypeStruct((total, width), f32),
            jax.ShapeDtypeStruct((total, width), f32),
            jax.ShapeDtypeStruct((3, 8, width // 8, inner), bf16),
            jax.ShapeDtypeStruct(gout_shape, bf16),
            jax.ShapeDtypeStruct((3, 8, inner), f32),
        ],
        scratch_shapes=[
            pltpu.VMEM((width, total), bf16),
            pltpu.VMEM((total, LANES), bf16),
            pltpu.VMEM((total, LANES), bf16),
            pltpu.VMEM((total, LANES), bf16),
            pltpu.VMEM((total, LANES), bf16),
            pltpu.VMEM((LANES, total), bf16),
            pltpu.VMEM((LANES, total), bf16),
            pltpu.VMEM((LANES, total), bf16),
            pltpu.VMEM((LANES, total), f32),
            pltpu.VMEM((LANES, total), f32),
            pltpu.VMEM((total, LANES), f32),
            pltpu.VMEM((total, LANES), f32),
            pltpu.VMEM((3, total, LANES), bf16),
            pltpu.VMEM((total, 128), f32),
        ],
        compiler_params=pltpu.CompilerParams(vmem_limit_bytes=60 * 2**20),
        cost_estimate=pl.CostEstimate(
            flops=flops, bytes_accessed=24 * 2**20, transcendentals=8 * total * total
        ),
        name="attention",
    )(length, hidden, out_grad, w_qkv, w_qkv, w_qkv, w_out, b_qkv, rope)


def ffn_kernel(
    tiled,
    h_ref,
    dy_ref,
    wf_ref,
    wp_ref,
    b_ref,
    out_ref,
    dh_ref,
    gf_ref,
    gp_ref,
    gb_ref,
    ht_s,
    act_s,
    dup_s,
):
    step = pl.program_id(0)
    total, width = h_ref.shape
    blocks = total // ROWS
    chunk = wf_ref.shape[1]

    @pl.when(step == 0)
    def _():
        for r in range(blocks):
            ht_s[:, r * ROWS : (r + 1) * ROWS] = h_ref[r * ROWS : (r + 1) * ROWS, :].T

    def one(r, total_grad):
        rows = pl.ds(pl.multiple_of(r * ROWS, ROWS), ROWS)
        up = dot_nn(h_ref[rows, :], wf_ref[...]) + b_ref[0:1, :]
        half = 0.5 + 0.5 * lax.erf(up * (1.0 / math.sqrt(2.0)))
        act = (up * half).astype(bf16)
        slope = half + up * (jnp.exp(-0.5 * up * up) * (1.0 / math.sqrt(2.0 * math.pi)))
        act_grad = dot_nt(dy_ref[rows, :], wp_ref[...])
        up_grad = (slope * act_grad).astype(bf16)
        act_s[rows, :] = act
        dup_s[rows, :] = up_grad
        out_part = dot_nn(act, wp_ref[...])
        dh_part = dot_nt(up_grad, wf_ref[...])

        @pl.when(step == 0)
        def _():
            out_ref[rows, :] = out_part
            dh_ref[rows, :] = dh_part

        @pl.when(step > 0)
        def _():
            out_ref[rows, :] += out_part
            dh_ref[rows, :] += dh_part

        return total_grad + jnp.sum(up_grad.astype(f32), axis=0, keepdims=True)

    sums = lax.fori_loop(0, blocks, one, jnp.zeros((1, chunk), f32))
    gb_ref[...] = jnp.broadcast_to(sums, (8, chunk))
    for r in range(8):
        size = width // 8
        rows = slice(r * size, (r + 1) * size)
        gf_ref[slot_of(r, tiled)] = dot_nn(ht_s[rows, :], dup_s[...]).astype(bf16)
    for r in range(chunk // ROWS):
        cols = slice(r * ROWS, (r + 1) * ROWS)
        grad = dot_nn(act_s[:, cols].T, dy_ref[...]).astype(bf16)
        if tiled:
            gp_ref[r, 0] = grad
        else:
            gp_ref[cols, :] = grad


def ffn_branch(hidden, out_grad, w_fc, w_proj, b_fc, tiled):
    total, width = hidden.shape
    units = w_proj.shape[0]
    chunk = min(512, units)
    whole = lambda s: (0, 0)
    if tiled:
        gp_spec = pl.BlockSpec((2, 1, ROWS, width), lambda s: (0, s, 0, 0))
        gp_shape = (2, units // chunk, ROWS, width)
    else:
        gp_spec = pl.BlockSpec((chunk, width), lambda s: (s, 0))
        gp_shape = (units, width)
    return pl.pallas_call(
        functools.partial(ffn_kernel, tiled),
        grid=(units // chunk,),
        in_specs=[
            pl.BlockSpec((total, width), whole),
            pl.BlockSpec((total, width), whole),
            pl.BlockSpec((width, chunk), lambda s: (0, s)),
            pl.BlockSpec((chunk, width), lambda s: (s, 0)),
            pl.BlockSpec((8, chunk), lambda s: (0, s)),
        ],
        out_specs=[
            pl.BlockSpec((total, width), whole),
            pl.BlockSpec((total, width), whole),
            pl.BlockSpec((8, width // 8, chunk), lambda s: (0, 0, s)),
            gp_spec,
            pl.BlockSpec((8, chunk), lambda s: (0, s)),
        ],
        out_shape=[
            jax.ShapeDtypeStruct((total, width), f32),
            jax.ShapeDtypeStruct((total, width), f32),
            jax.ShapeDtypeStruct((8, width // 8, units), bf16),
            jax.ShapeDtypeStruct(gp_shape, bf16),
            jax.ShapeDtypeStruct((8, units), f32),
        ],
        scratch_shapes=[
            pltpu.VMEM((width, total), bf16),
            pltpu.VMEM((total, chunk), bf16),
            pltpu.VMEM((total, chunk), bf16),
        ],
        compiler_params=pltpu.CompilerParams(vmem_limit_bytes=60 * 2**20),
        cost_estimate=pl.CostEstimate(
            flops=2 * total * width * units * 6,
            bytes_accessed=28 * 2**20,
            transcendentals=2 * total * units,
        ),
        name="feed_forward",
    )(hidden, out_grad, w_fc, w_proj, b_fc)


def shift(block, axis, distance):
    count = lax.axis_size(axis)
    return lax.ppermute(block, axis, [(i, (i + distance) % count) for i in range(count)])


def swap_bit(block, axis, bit):
    return lax.ppermute(block, axis, [(i, i ^ bit) for i in range(lax.axis_size(axis))])


def shift_within(block, axis, size, distance):
    count = lax.axis_size(axis)
    return lax.ppermute(
        block,
        axis,
        [(i, i // size * size + (i % size + distance) % size) for i in range(count)],
    )


def pick(array, index, axis=0):
    return lax.dynamic_index_in_dim(array, index, axis, keepdims=False)


def order_two(flag, mine, other):
    first = flag == 0
    return jnp.stack([jnp.where(first, mine, other), jnp.where(first, other, mine)])


def gather_rows(local, place):
    dp, y, core, f = place["dp"], place["y"], place["core"], place["f"]
    count = lax.axis_size("fsdp")
    rows, cols = local.shape
    share = rows // lax.axis_size("dp")
    mine = lax.dynamic_slice_in_dim(local, dp * share, share, 0)
    got = jnp.stack([shift(mine, "fsdp", e) for e in range(1, count)])
    got = order_two(y, got, swap_bit(got, "dp", 2))
    got = order_two(core, got, swap_bit(got, "dp", 1))
    got = jnp.transpose(got, (2, 1, 0, 3, 4)).reshape(count - 1, rows, cols)
    if count == 2:
        return order_two(f, local, got[0])
    whole = jnp.zeros((count, rows, cols), local.dtype)
    whole = lax.dynamic_update_index_in_dim(whole, local, f, 0)
    for e in range(1, count):
        whole = lax.dynamic_update_index_in_dim(whole, got[e - 1], (f - e) % count, 0)
    return whole


def reduce_rows(partial, place, parts):
    dp, y, core, f, j = (place[k] for k in ("dp", "y", "core", "f", "j"))
    count, rows, cols = partial.shape
    share = rows // 4
    a = partial.reshape(count, 2, 2, share, cols)
    a = pick(a, core, 2) + swap_bit(pick(a, 1 - core, 2), "dp", 1)
    total = pick(a, f)
    for e in range(1, count):
        total = total + shift(pick(a, (f + e) % count), "fsdp", e)
    total = pick(total, y) + swap_bit(pick(total, 1 - y), "dp", 2)
    total = total + shift(total, "ctx", parts)
    if parts == 2:
        both = order_two(j, total, shift_within(total, "ctx", 2, 1))
    else:
        both = jnp.zeros((parts,) + total.shape, total.dtype)
        both = lax.dynamic_update_index_in_dim(both, total, j, 0)
        for e in range(1, parts):
            got = shift_within(total, "ctx", parts, e)
            both = lax.dynamic_update_index_in_dim(both, got, (j - e) % parts, 0)
    both = order_two(y, both, swap_bit(both, "dp", 2))
    both = order_two(core, both, swap_bit(both, "dp", 1))
    return jnp.transpose(both, (1, 0, 3, 2, 4)).reshape(rows, parts, cols).astype(f32)


def sum_everywhere(vector):
    for bit in (1, 2):
        vector = vector + swap_bit(vector, "dp", bit)
    for axis in ("fsdp", "ctx"):
        bit = 1
        while bit < lax.axis_size(axis):
            vector = vector + swap_bit(vector, axis, bit)
            bit *= 2
    return vector


def gather_sequence(blocks, place, parts):
    s, c = place["s"], place["c"]
    count = lax.axis_size("ctx")
    seqs, rows, width = blocks.shape
    pieces = [(c, pick(blocks, s))]
    for d in range(1, seqs):
        got = shift(pick(blocks, (s + d) % seqs), "ctx", d * parts)
        pieces.append(((c - d * parts) % count, got))
    arrived = []
    for d in range(seqs):
        arrived.append(pieces[d])
        for e in range(1, parts):
            source = s * parts + (place["j"] - e) % parts
            got = shift_within(pieces[d][1], "ctx", parts, e)
            arrived.append(((source - d * parts) % count, got))
    whole = jnp.zeros((count, rows, width), blocks.dtype)
    for at, piece in arrived:
        whole = lax.dynamic_update_index_in_dim(whole, piece, at, 0)
    return whole.reshape(count * rows, width)


def return_blocks(partial, place, parts, seqs):
    s, c, j = place["s"], place["c"], place["j"]
    count = lax.axis_size("ctx")
    rows = partial.shape[0] // count
    blocks = partial.reshape(seqs, parts, rows, -1)
    total = pick(blocks, j, 1).astype(f32)
    for e in range(1, parts):
        total = total + shift_within(pick(blocks, (j + e) % parts, 1), "ctx", parts, e).astype(f32)
    mine = [pick(total, s)]
    for d in range(1, seqs):
        mine.append(shift(pick(total, (s + d) % seqs).astype(bf16), "ctx", d * parts).astype(f32))
    if seqs == 2:
        return order_two(s, mine[0], mine[1])
    whole = jnp.zeros((seqs, rows, partial.shape[1]), f32)
    for d in range(seqs):
        whole = lax.dynamic_update_index_in_dim(whole, mine[d], (s - d) % seqs, 0)
    return whole


class Mover:
    def __init__(self, send, recv, local):
        self.send, self.recv, self.local = send, recv, local
        self.copies, self.left, self.started = [], [], 0

    def to(self, src, dst, axis, index):
        at = len(self.copies)
        copy = pltpu.make_async_remote_copy(
            src_ref=src,
            dst_ref=dst,
            send_sem=self.send.at[at],
            recv_sem=self.recv.at[at],
            device_id={axis: index},
            device_id_type=pl.DeviceIdType.MESH,
        )
        copy.start()
        self.copies.append(copy)
        return copy

    def here(self, src, dst):
        copy = pltpu.make_async_copy(src, dst, self.local.at[self.started])
        self.started += 1
        copy.start()
        return copy

    def out(self, src, dst):
        self.left.append(self.here(src, dst))

    def finish(self):
        for copy in self.copies:
            copy.wait_send()
        for copy in self.left:
            copy.wait()


class Spot:
    def __init__(self):
        self.dp, self.c, self.f = (lax.axis_index(a) for a in ("dp", "ctx", "fsdp"))
        self.y, self.core = self.dp // 2, self.dp % 2
        self.s, self.j = self.c // 2, self.c % 2
        flip = lambda v: v + 1 - 2 * (v % 2)
        self.x_to = ("fsdp", 1 - self.f)
        self.y_to = ("dp", (1 - self.y) * 2 + self.core)
        self.core_to = ("dp", flip(self.dp))
        self.pair_to = ("ctx", flip(self.c))
        self.far_to = ("ctx", (1 - self.s) * 2 + self.j)

    def greet(self):
        barrier = pltpu.get_barrier_semaphore()
        partners = (self.x_to, self.y_to, self.core_to, self.pair_to, self.far_to)
        for axis, index in partners:
            pl.semaphore_signal(
                barrier, inc=1, device_id={axis: index}, device_id_type=pl.DeviceIdType.MESH
            )
        pl.semaphore_wait(barrier, len(partners))


def block(index, size):
    return pl.ds(pl.multiple_of(index * size, size), size)


def gather_kernel(
    x_ref,
    cot_ref,
    fc_ref,
    proj_ref,
    qkv_ref,
    out_ref,
    small_ref,
    seq_in,
    seq_grad,
    w_fc,
    w_proj,
    w_qkv,
    w_out,
    small,
    hold_act,
    hold_fc,
    hold_proj,
    hold_qkv,
    hold_out,
    hold_small,
    send,
    recv,
    local,
):
    at = Spot()
    mover = Mover(send, recv, local)
    at.greet()
    rows = x_ref.shape[1]
    other = 1 - at.f
    turns = []
    through = []

    def keep(src, held, dst):
        through.append((mover.here(src, held), held, dst))

    mover.to(small_ref, small.at[at.f], *at.x_to)
    keep(small_ref, hold_small, small.at[at.f])

    first = {}
    for slot, (name, src, dst) in enumerate((("in", x_ref, seq_in), ("grad", cot_ref, seq_grad))):
        mine = dst.at[block(at.c, rows)]
        far = mover.to(src.at[1 - at.s], mine, *at.far_to)
        near = mover.to(src.at[at.s], mine, *at.pair_to)
        keep(src.at[at.s], hold_act.at[slot], mine)
        first[name] = (far, near, dst)

    def fc_spans(r):
        width = w_fc.shape[1] // 2
        return [
            (fc_ref.at[r, block(2 * k + at.j, width)], pl.ds(k * width, width)) for k in range(2)
        ]

    def qkv_spans(r):
        width = w_qkv.shape[1] // 6
        return [
            (qkv_ref.at[r, block(2 * k + at.j, width)], pl.ds(k * width, width)) for k in range(6)
        ]

    def row_spans(ref, held):
        count = held.shape[0] // 2

        def spans(r):
            start = pl.multiple_of(at.j * count + r.start, r.size)
            return [(ref.at[pl.ds(start, r.size)], slice(None))]

        return spans

    weights = (
        (w_fc, fc_spans),
        (w_proj, row_spans(proj_ref, w_proj)),
        (w_qkv, qkv_spans),
        (w_out, row_spans(out_ref, w_out)),
    )
    holds = (hold_fc, hold_proj, hold_qkv, hold_out)
    for held, spans in weights:
        count = held.shape[0] // 2
        share = count // 4
        span = pl.ds(pl.multiple_of(at.dp * share, share), share)
        there = pl.ds(pl.multiple_of(at.f * count + at.dp * share, share), share)
        turns.append([mover.to(src, held.at[there, cols], *at.x_to) for src, cols in spans(span)])
    for (held, spans), hold in zip(weights, holds):
        count = held.shape[0] // 2
        there = block(at.f, count)
        for src, cols in spans(pl.ds(0, count)):
            keep(src, hold if isinstance(cols, slice) else hold.at[:, cols], held.at[there, cols])
    for copy, hold, dst in through:
        copy.wait()
        mover.out(hold, dst)

    def quarter(held, dp):
        count = held.shape[0] // 2
        share = count // 4
        return held.at[pl.ds(pl.multiple_of(other * count + dp * share, share), share)]

    y_turns, last = [], []
    for (held, _), copies in zip(weights, turns):
        for copy in copies:
            copy.wait_recv()
        part = quarter(held, at.dp)
        y_turns.append(mover.to(part, part, *at.y_to))
        last.append(mover.to(part, part, *at.core_to))
    for name in ("in", "grad"):
        far, _, dst = first[name]
        far.wait_recv()
        part = dst.at[block(at.far_to[1], rows)]
        last.append(mover.to(part, part, *at.pair_to))
    for (held, _), copy in zip(weights, y_turns):
        copy.wait_recv()
        part = quarter(held, at.y_to[1])
        last.append(mover.to(part, part, *at.core_to))
    for name in ("in", "grad"):
        first[name][1].wait_recv()
    for copy in last:
        copy.wait_recv()
    mover.copies[0].wait_recv()
    mover.finish()


def gather_all(x, cot, fc, proj, qkv, out, small):
    seqs, rows, width = x.shape
    total = 4 * rows
    hbm = pl.BlockSpec(memory_space=pl.ANY)
    shape = lambda *dims: jax.ShapeDtypeStruct(dims, bf16)
    return pl.pallas_call(
        gather_kernel,
        in_specs=[hbm] * 7,
        out_specs=[hbm] * 7,
        out_shape=[
            shape(total, width),
            shape(total, width),
            shape(width, fc.shape[1] // 2),
            shape(proj.shape[0], width),
            shape(width, qkv.shape[1] // 2),
            shape(out.shape[0], width),
            shape(2, *small.shape),
        ],
        scratch_shapes=[
            pltpu.VMEM((2, rows, width), bf16),
            pltpu.VMEM((width // 2, fc.shape[1] // 2), bf16),
            pltpu.VMEM((proj.shape[0] // 2, width), bf16),
            pltpu.VMEM((width // 2, qkv.shape[1] // 2), bf16),
            pltpu.VMEM((out.shape[0] // 2, width), bf16),
            pltpu.VMEM(small.shape, bf16),
            pltpu.SemaphoreType.DMA((32,)),
            pltpu.SemaphoreType.DMA((32,)),
            pltpu.SemaphoreType.DMA((32,)),
        ],
        compiler_params=pltpu.CompilerParams(
            collective_id=0, has_side_effects=True, vmem_limit_bytes=40 * 2**20
        ),
        name="gather",
    )(x, cot, fc, proj, qkv, out, small)


def reduce_kernel(
    gfc_ref,
    gproj_ref,
    gqkv_ref,
    gout_ref,
    branch_ref,
    pull_ref,
    small_ref,
    d_fc,
    d_proj,
    d_qkv,
    d_out,
    branch,
    pull,
    small,
    *scratch,
):
    send, recv, local = scratch[-3:]
    at = Spot()
    mover = Mover(send, recv, local)
    bufs = list(scratch[:-3])
    take = lambda count: [bufs.pop(0) for _ in range(count)]
    at.greet()

    def fc_piece(k):
        width = d_fc.shape[1] // 4
        src = lambda core: gfc_ref.at[core, :, :, :, pl.ds(k * width, width)]

        def place(y, core, part):
            size = d_fc.shape[0] // 4
            return [(slice(None), d_fc.at[block(y * 2 + core, size), block(2 * k + part, width)])]

        return src, place

    def proj_piece(k):
        size = gproj_ref.shape[3] // 2
        src = lambda core: gproj_ref.at[core, :, :, pl.ds(k * size, size)]

        def place(y, core, part):
            return [(slice(None), d_proj.at[block(part * 8 + y * 4 + core * 2 + k, size)])]

        return src, place

    def qkv_piece(k):
        width = d_qkv.shape[1] // 12
        src = lambda core: gqkv_ref.at[k, core]

        def place(y, core, part):
            size = d_qkv.shape[0] // 4
            return [
                (pl.ds(h * width, width), d_qkv.at[block(y * 2 + core, size), block(4 * k + 2 * h + part, width)])
                for h in range(2)
            ]

        return src, place

    def out_piece():
        size = gout_ref.shape[3]
        src = lambda core: gout_ref.at[core]

        def place(y, core, part):
            return [(slice(None), d_out.at[block(part * 4 + y * 2 + core, size)])]

        return src, place

    pieces = [proj_piece(0), proj_piece(1), fc_piece(0), fc_piece(1)]
    pieces += [qkv_piece(0), qkv_piece(1), qkv_piece(2), out_piece()]
    states = []
    for src, place in pieces:
        own, from_core, from_x, from_y, from_far, full = take(6)
        states.append(
            dict(src=src, place=place, own=own, rc=from_core, rx=from_x, ry=from_y, rz=from_far, full=full)
        )

    def step_start(p):
        p["load"] = mover.here(p["src"](at.core), p["own"])
        p["c"] = mover.to(p["src"](1 - at.core), p["rc"], *at.core_to)

    def step_core(p):
        p["load"].wait()
        p["c"].wait_recv()
        own, got = p["own"], p["rc"]
        own[1 - at.f] = own[1 - at.f] + got[1 - at.f]
        p["x"] = mover.to(own.at[1 - at.f], p["rx"], *at.x_to)
        own[at.f] = own[at.f] + got[at.f]

    def step_x(p):
        p["x"].wait_recv()
        own, got = p["own"], p["rx"]
        own[at.f, 1 - at.y] = own[at.f, 1 - at.y] + got[1 - at.y]
        p["y"] = mover.to(own.at[at.f, 1 - at.y], p["ry"], *at.y_to)
        own[at.f, at.y] = own[at.f, at.y] + got[at.y]

    def step_y(p):
        p["y"].wait_recv()
        own = p["own"]
        own[at.f, at.y] = own[at.f, at.y] + p["ry"][...]
        p["z"] = mover.to(own.at[at.f, at.y], p["rz"], *at.far_to)

    def step_far(p):
        p["z"].wait_recv()
        cell = p["full"].at[at.y, at.core, at.j]
        cell[...] = p["own"][at.f, at.y] + p["rz"][...]
        p["p"] = mover.to(cell, cell, *at.pair_to)

    def step_pair(p):
        p["p"].wait_recv()
        cells = p["full"].at[at.y, at.core]
        p["yy"] = mover.to(cells, cells, *at.y_to)
        p["c1"] = mover.to(cells, cells, *at.core_to)

    def step_yy(p):
        p["yy"].wait_recv()
        cells = p["full"].at[1 - at.y, at.core]
        p["c2"] = mover.to(cells, cells, *at.core_to)

    def step_done(p):
        p["c1"].wait_recv()
        p["c2"].wait_recv()
        for y in range(2):
            for core in range(2):
                for part in range(2):
                    for cols, dst in p["place"](y, core, part):
                        mover.out(p["full"].at[y, core, part, :, cols], dst)

    homes = []
    rows = branch.shape[1]
    for src, dst in ((branch_ref, branch), (pull_ref, pull)):
        mine, got, full = take(3)
        home = dict(mine=mine, got=got, full=full, dst=dst)
        home["loads"] = [mover.here(src.at[block(2 * t + at.j, rows)], mine.at[t]) for t in range(2)]
        home["near"] = [
            mover.to(src.at[block(2 * t + 1 - at.j, rows)], got.at[t], *at.pair_to) for t in range(2)
        ]
        homes.append(home)

    def home_near(h):
        for copy in h["loads"]:
            copy.wait()
        for copy in h["near"]:
            copy.wait_recv()
        mine, got, full = h["mine"], h["got"], h["full"]
        mine[1 - at.s] = mine[1 - at.s] + got[1 - at.s]
        h["far"] = mover.to(mine.at[1 - at.s], full.at[at.s], *at.far_to)
        full[at.s] = mine[at.s] + got[at.s]

    def home_far(h):
        h["far"].wait_recv()
        mover.out(h["full"], h["dst"])

    held, slots = take(2)
    mover.here(small_ref, held.at[0]).wait()
    trips = (at.core_to, at.x_to, at.y_to, at.far_to, at.pair_to)

    def small_send(i):
        return mover.to(held.at[i], slots.at[i], *trips[i])

    steps = [step_core, step_x, step_y, step_far, step_pair, step_yy, step_done]
    for p in states:
        step_start(p)
    small_copy = small_send(0)
    total = len(states) + len(steps) - 1
    for turn in range(total):
        for back, step in reversed(list(enumerate(steps))):
            if 0 <= turn - back < len(states):
                step(states[turn - back])
        if turn < 5:
            small_copy.wait_recv()
            held[turn + 1] = held[turn] + slots[turn]
            if turn < 4:
                small_copy = small_send(turn + 1)
            else:
                mover.out(held.at[5], small)
        if turn == 3:
            home_near(homes[0])
        if turn == 6:
            home_near(homes[1])
        if turn == 7:
            home_far(homes[0])
        if turn == 10:
            home_far(homes[1])
    mover.finish()


def reduce_all(gfc, gproj, gqkv, gout, branch, pull, small, sizes):
    rows_here, units, inner_rows, width, block_rows = sizes
    hbm = pl.BlockSpec(memory_space=pl.ANY)
    shape = lambda *dims: jax.ShapeDtypeStruct(dims, bf16)
    cells = [(gproj.shape[3] // 2, width)] * 2
    cells += [(gfc.shape[3], gfc.shape[4] // 2)] * 2
    cells += [gqkv.shape[4:]] * 3 + [gout.shape[3:]]
    scratch = []
    for cell in cells:
        scratch += [
            pltpu.VMEM((2, 2) + tuple(cell), bf16),
            pltpu.VMEM((2, 2) + tuple(cell), bf16),
            pltpu.VMEM((2,) + tuple(cell), bf16),
            pltpu.VMEM(tuple(cell), bf16),
            pltpu.VMEM(tuple(cell), bf16),
            pltpu.VMEM((2, 2, 2) + tuple(cell), bf16),
        ]
    for _ in range(2):
        scratch += [pltpu.VMEM((2, block_rows, width), bf16)] * 3
    scratch += [pltpu.VMEM((6,) + small.shape, f32), pltpu.VMEM((5,) + small.shape, f32)]
    return pl.pallas_call(
        reduce_kernel,
        in_specs=[hbm] * 7,
        out_specs=[hbm] * 7,
        out_shape=[
            shape(rows_here, units),
            shape(units // 2, width),
            shape(rows_here, 3 * width),
            shape(inner_rows, width),
            shape(2, block_rows, width),
            shape(2, block_rows, width),
            jax.ShapeDtypeStruct(small.shape, f32),
        ],
        scratch_shapes=scratch
        + [
            pltpu.SemaphoreType.DMA((96,)),
            pltpu.SemaphoreType.DMA((96,)),
            pltpu.SemaphoreType.DMA((128,)),
        ],
        compiler_params=pltpu.CompilerParams(
            collective_id=1, has_side_effects=True, vmem_limit_bytes=60 * 2**20
        ),
        name="reduce",
    )(gfc, gproj, gqkv, gout, branch, pull, small)


def normalize(features):
    center = features - jnp.mean(features, axis=-1, keepdims=True)
    spread = jnp.mean(center * center, axis=-1, keepdims=True)
    inverse = lax.rsqrt(spread + epsilon)
    return center * inverse, inverse


def rope_tables(total, head_size):
    half = ROT // 2
    inverse = rope_base ** (-(2.0 * jnp.arange(half, dtype=f32)) / ROT)
    angles = jnp.arange(total, dtype=jnp.int32).astype(f32)[:, None] * inverse[None, :]
    cosine, sine = jnp.cos(angles), jnp.sin(angles)
    rest = jnp.zeros((total, head_size - ROT), f32)
    none = jnp.zeros((total, half), f32)
    same = jnp.concatenate([cosine, cosine, rest + 1.0], axis=1)
    ahead = jnp.concatenate([-sine, none, rest], axis=1)
    behind = jnp.concatenate([none, sine, rest], axis=1)
    return jnp.tile(jnp.stack([same, ahead, behind]), (1, 1, LANES // head_size))


def per_device(
    residual_in,
    lengths,
    gain_attn,
    shift_attn,
    weight_qkv,
    bias_qkv,
    weight_out,
    bias_out,
    gain_ffn,
    shift_ffn,
    weight_fc,
    bias_fc,
    weight_proj,
    bias_proj,
    cotangent,
):
    seqs, block_rows, width = residual_in.shape
    n_ctx, n_fsdp = lax.axis_size("ctx"), lax.axis_size("fsdp")
    parts = n_ctx // seqs
    total = n_ctx * block_rows
    units = weight_fc.shape[1]
    head_size = width // HEADS
    c, f, dp = lax.axis_index("ctx"), lax.axis_index("fsdp"), lax.axis_index("dp")
    s, j = c // parts, c % parts
    place = dict(c=c, f=f, dp=dp, s=s, j=j, y=dp // 2, core=dp % 2)
    spread_heads = HEADS % (n_fsdp * parts) == 0
    n_h = n_fsdp if spread_heads else 1
    inner = width // parts

    rows_here = weight_qkv.shape[0]
    own_heads = lambda v: pick(v.reshape(3, n_h, parts, -1), j, 2)
    fast = (seqs, n_ctx, n_fsdp, lax.axis_size("dp")) == (2, 4, 2, 4)
    small_local = jnp.concatenate(
        [gain_attn, shift_attn, gain_ffn, shift_ffn, bias_out, bias_proj, bias_qkv, bias_fc]
    )
    part_width = width // n_fsdp
    if fast:
        packed = jnp.pad(small_local.reshape(13, -1), ((0, 3), (0, 0)))
        seq_in, seq_grad, w_fc, w_proj, w_qkv, w_out, small = gather_all(
            residual_in, cotangent, weight_fc, weight_proj, weight_qkv, weight_out, packed
        )
        small = small[:, :13].reshape(2, -1)
    else:
        small = lax.all_gather(small_local, "fsdp", axis=0)
    vec = lambda at, size: small[:, at : at + size].reshape(-1).astype(f32)
    gain_one, shift_one, gain_two, shift_two, b_out, b_proj = (
        vec(i * part_width, part_width) for i in range(6)
    )
    b_qkv = vec(6 * part_width, 3 * part_width)
    b_fc = vec(9 * part_width, units // n_fsdp)

    if not fast:
        fc_local = pick(weight_fc.reshape(rows_here, n_fsdp, parts, -1), j, 2).reshape(rows_here, -1)
        proj_local = pick(weight_proj.reshape(parts, -1, width), j)
        qkv_local = pick(weight_qkv.reshape(rows_here, 3, n_h, parts, -1), j, 3).reshape(rows_here, -1)
        seq_in = gather_sequence(residual_in, place, parts)
        w_fc = gather_rows(fc_local, place).reshape(width, -1)
        w_proj = gather_rows(proj_local, place).reshape(-1, width)
        seq_grad = gather_sequence(cotangent, place, parts)
        w_qkv = gather_rows(qkv_local, place).reshape(width, -1)
        if spread_heads:
            w_out = gather_rows(pick(weight_out.reshape(parts, -1, width), j), place).reshape(-1, width)
        else:
            w_out = lax.all_gather(weight_out, "fsdp", axis=0, tiled=True)
            w_out = pick(w_out.reshape(parts, -1, width), j)
    b_qkv_j = own_heads(b_qkv).reshape(3, 1, inner)
    b_qkv_j = jnp.broadcast_to(b_qkv_j, (3, 8, inner))
    b_fc_j = pick(b_fc.reshape(n_fsdp, parts, -1), j, 1).reshape(1, -1)
    b_fc_j = jnp.broadcast_to(b_fc_j, (8, b_fc_j.shape[1]))

    length = pick(lengths, s)
    positions = jnp.arange(total, dtype=jnp.int32)
    seq_grad = jnp.where((positions < length)[:, None], seq_grad, jnp.zeros((), bf16))
    xhat, _ = normalize(seq_in.astype(f32))
    hidden_one = (xhat * gain_one + shift_one).astype(bf16)
    hidden_two = (xhat * gain_two + shift_two).astype(bf16)

    ffn_out, ffn_dh, g_fc, g_proj, g_bfc = ffn_branch(
        hidden_two, seq_grad, w_fc, w_proj, b_fc_j, fast
    )
    attn_out, attn_dh, g_qkv, g_out, g_bqkv = attention_branch(
        length[None],
        hidden_one,
        seq_grad,
        w_qkv,
        w_out,
        b_qkv_j,
        rope_tables(total, head_size),
        fast,
    )

    own_grad = jnp.sum(seq_grad.astype(f32), axis=0) / parts
    g_bqkv_all = jnp.zeros((3, n_h, parts, inner // n_h), f32)
    g_bqkv_all = lax.dynamic_update_index_in_dim(
        g_bqkv_all, g_bqkv[:, 0].reshape(3, n_h, -1), j, 2
    )
    g_bfc_all = jnp.zeros((n_fsdp, parts, units // (n_fsdp * parts)), f32)
    g_bfc_all = lax.dynamic_update_index_in_dim(g_bfc_all, g_bfc[0].reshape(n_fsdp, -1), j, 1)
    rows_of = (
        jnp.sum(attn_dh * xhat, axis=0),
        jnp.sum(attn_dh, axis=0),
        jnp.sum(ffn_dh * xhat, axis=0),
        jnp.sum(ffn_dh, axis=0),
        own_grad,
        g_bqkv_all.reshape(-1),
        g_bfc_all.reshape(-1),
    )
    small_sums = jnp.concatenate(rows_of).reshape(-1, 128)
    branch_part = (attn_out + ffn_out).astype(bf16)
    pull_part = (attn_dh * gain_one + ffn_dh * gain_two).astype(bf16)
    if fast:
        cells = lambda grad: grad.reshape(2, 2, 2, -1, grad.shape[-1])
        d_fc, d_proj, d_qkv, d_out, branch, pulled, small_sums = reduce_all(
            cells(g_fc),
            cells(g_proj),
            g_qkv.reshape(3, 2, 2, 2, -1, inner),
            g_out,
            branch_part,
            pull_part,
            small_sums,
            (rows_here, units, weight_out.shape[0], width, block_rows),
        )
        d_fc, d_proj, d_qkv, d_out = (g.astype(f32) for g in (d_fc, d_proj, d_qkv, d_out))
        branch, pulled = branch.astype(f32), pulled.astype(f32)
    else:
        d_proj = reduce_rows(g_proj.reshape(n_fsdp, -1, width), place, parts)
        d_fc = reduce_rows(g_fc.reshape(n_fsdp, rows_here, -1), place, parts)
        q_rows = jnp.swapaxes(g_qkv.reshape(3, n_fsdp, rows_here, inner), 0, 1)
        q_rows = jnp.swapaxes(q_rows, 1, 2).reshape(n_fsdp, rows_here, 3 * inner)
        d_qkv = reduce_rows(q_rows, place, parts)
        d_proj = jnp.swapaxes(d_proj, 0, 1).reshape(weight_proj.shape)
        d_fc = d_fc.reshape(rows_here, parts, n_fsdp, -1)
        d_fc = jnp.swapaxes(d_fc, 1, 2).reshape(weight_fc.shape)
        d_qkv = d_qkv.reshape(rows_here, parts, 3, n_h, -1)
        d_qkv = jnp.transpose(d_qkv, (0, 2, 3, 1, 4)).reshape(weight_qkv.shape)
        if spread_heads:
            d_out = reduce_rows(g_out.reshape(n_fsdp, -1, width), place, parts)
            d_out = jnp.swapaxes(d_out, 0, 1).reshape(weight_out.shape)
        else:
            full = jnp.zeros((parts, inner, width), bf16)
            full = lax.dynamic_update_index_in_dim(full, g_out, j, 0).reshape(width, width)
            d_out = lax.psum_scatter(full, "fsdp", scatter_dimension=0, tiled=True)
            d_out = lax.psum(d_out, ("dp", "ctx")).astype(f32)
        small_sums = sum_everywhere(small_sums)
        branch = return_blocks(branch_part, place, parts, seqs)
        pulled = return_blocks(pull_part, place, parts, seqs)
    flat = small_sums.reshape(-1)
    small_grads = []
    at = 0
    for entry in rows_of:
        size = entry.shape[0]
        mine = lax.dynamic_slice_in_dim(flat, at + f * (size // n_fsdp), size // n_fsdp)
        small_grads.append(mine)
        at += size
    d_gain_one, d_shift_one, d_gain_two, d_shift_two, d_bias, d_bqkv, d_bfc = small_grads

    features = residual_in.astype(f32)
    residual_out = (features + branch + (b_out + b_proj)).astype(bf16)
    own_hat, own_inverse = normalize(features)
    pulled = own_inverse * (
        pulled
        - jnp.mean(pulled, axis=-1, keepdims=True)
        - own_hat * jnp.mean(pulled * own_hat, axis=-1, keepdims=True)
    )
    own_pos = c * block_rows + jnp.arange(block_rows, dtype=jnp.int32)
    valid = (own_pos[None, :] < lengths[:, None])[..., None]
    residual_grad = (jnp.where(valid, cotangent.astype(f32), 0.0) + pulled).astype(bf16)
    return (
        residual_out,
        residual_grad,
        d_gain_one,
        d_shift_one,
        d_qkv,
        d_bqkv,
        d_out,
        d_bias,
        d_gain_two,
        d_shift_two,
        d_fc,
        d_bfc,
        d_proj,
        d_bias,
    )


def solution(mesh):
    tokens = P(("dp", "fsdp"), "ctx", None)
    vector, matrix = P("fsdp"), P("fsdp", None)
    return jax.shard_map(
        per_device,
        mesh=mesh,
        in_specs=(
            tokens,
            P(("dp", "fsdp")),
            vector,
            vector,
            matrix,
            vector,
            matrix,
            vector,
            vector,
            vector,
            matrix,
            vector,
            matrix,
            vector,
            tokens,
        ),
        out_specs=(
            tokens,
            tokens,
            vector,
            vector,
            matrix,
            vector,
            matrix,
            vector,
            vector,
            vector,
            matrix,
            vector,
            matrix,
            vector,
        ),
        check_vma=False,
    )
```

```python
import functools
import math

import jax
import jax.numpy as jnp
from jax import lax
from jax.experimental import pallas as pl
from jax.experimental.pallas import tpu as pltpu
from jax.sharding import PartitionSpec as P

HEADS = 16
ROT = 16
LANES = 256
ROWS = 256

epsilon = 1e-05
rope_base = 10000.0
masked_score = -1e30

f32 = jnp.float32
bf16 = jnp.bfloat16


def dot_nn(a, b):
    return lax.dot_general(a, b, (((1,), (0,)), ((), ())), preferred_element_type=f32)


def dot_nt(a, b):
    return lax.dot_general(a, b, (((1,), (1,)), ((), ())), preferred_element_type=f32)


def slot_of(chunk):
    return chunk % 2 * 4 + chunk // 2


def attn_kernel(
    length_ref,
    h_ref,
    dy_ref,
    wq_ref,
    wk_ref,
    wv_ref,
    wo_ref,
    b_ref,
    rope_ref,
    out_ref,
    dh_ref,
    gqkv_ref,
    gout_ref,
    gb_ref,
    ht_s,
    q_s,
    k_s,
    v_s,
    do_s,
    kt_s,
    vt_s,
    dot_s,
    ot_s,
    dqt_s,
    dk_s,
    dv_s,
    p_s,
    kb_s,
):
    group = pl.program_id(0)
    total, width = h_ref.shape
    blocks = total // ROWS
    head_size = 64
    heads_here = LANES // head_size
    length = length_ref[0]

    @pl.when(group == 0)
    def _():
        for r in range(blocks):
            ht_s[:, r * ROWS : (r + 1) * ROWS] = h_ref[r * ROWS : (r + 1) * ROWS, :].T
        key_pos = lax.broadcasted_iota(jnp.int32, (total, 128), 0)
        kb_s[...] = jnp.where(key_pos < length, 0.0, masked_score)

    def turn(v, rows):
        left = pltpu.roll(v, LANES - ROT // 2, 1)
        right = pltpu.roll(v, ROT // 2, 1)
        return v * rope_ref[0, rows, :] + left * rope_ref[1, rows, :] + right * rope_ref[2, rows, :]

    def turn_back(v, rows):
        left = pltpu.roll(v, LANES - ROT // 2, 1)
        right = pltpu.roll(v, ROT // 2, 1)
        return v * rope_ref[0, rows, :] - left * rope_ref[1, rows, :] - right * rope_ref[2, rows, :]

    for r in range(blocks):
        rows = slice(r * ROWS, (r + 1) * ROWS)
        hr = h_ref[rows, :]
        q = turn(dot_nn(hr, wq_ref[...]) + b_ref[0, 0:1, :], rows).astype(bf16)
        q_s[rows, :] = (q.astype(f32) * 0.125).astype(bf16)
        k = turn(dot_nn(hr, wk_ref[...]) + b_ref[1, 0:1, :], rows).astype(bf16)
        k_s[rows, :] = k
        kt_s[:, rows] = k.T
        v = (dot_nn(hr, wv_ref[...]) + b_ref[2, 0:1, :]).astype(bf16)
        v_s[rows, :] = v
        vt_s[:, rows] = v.T
        do = dot_nt(dy_ref[rows, :], wo_ref[...]).astype(bf16)
        do_s[rows, :] = do
        dot_s[:, rows] = do.T

    dk_s[...] = jnp.zeros_like(dk_s)
    dv_s[...] = jnp.zeros_like(dv_s)
    lane = lax.broadcasted_iota(jnp.int32, (ROWS, LANES), 1)
    causal = lax.broadcasted_iota(jnp.int32, (ROWS, ROWS), 0) <= lax.broadcasted_iota(
        jnp.int32, (ROWS, ROWS), 1
    )

    def one_head(head, carry):
        feats = pl.ds(pl.multiple_of(head * head_size, head_size), head_size)
        mine = (lane // head_size) == head
        zero = jnp.zeros((ROWS, LANES), bf16)
        for i in range(blocks):
            rows = slice(i * ROWS, (i + 1) * ROWS)
            qm = jnp.where(mine, q_s[rows, :], zero)
            dom = jnp.where(mine, do_s[rows, :], zero)
            scores = []
            top = None
            for b in range(i + 1):
                keys = slice(b * ROWS, (b + 1) * ROWS)
                sc = dot_nt(k_s[keys, :], qm)
                kb = kb_s[keys, :]
                sc = sc + jnp.concatenate([kb, kb], axis=1)
                if b == i:
                    sc = jnp.where(causal, sc, masked_score)
                best = jnp.max(sc, axis=0, keepdims=True)
                top = best if top is None else jnp.maximum(top, best)
                scores.append(sc)
            row_sum = None
            for b in range(i + 1):
                scores[b] = jnp.exp(scores[b] - top)
                part = jnp.sum(scores[b], axis=0, keepdims=True)
                row_sum = part if row_sum is None else row_sum + part
            inverse = 1.0 / row_sum
            o_t = None
            for b in range(i + 1):
                keys = slice(b * ROWS, (b + 1) * ROWS)
                scores[b] = scores[b] * inverse
                low = scores[b].astype(bf16)
                dv_s[keys, :] += dot_nn(low, dom)
                part = dot_nn(vt_s[feats, keys], low)
                o_t = part if o_t is None else o_t + part
            ot_s[feats, rows] = o_t
            delta = jnp.sum(dot_s[feats, rows].astype(f32) * o_t, axis=0, keepdims=True)
            dq_t = None
            for b in range(i + 1):
                keys = slice(b * ROWS, (b + 1) * ROWS)
                dp = dot_nt(v_s[keys, :], dom)
                ds = (scores[b] * (dp - delta)).astype(bf16)
                dk_s[keys, :] += dot_nn(ds, qm)
                part = dot_nn(kt_s[feats, keys], ds)
                dq_t = part if dq_t is None else dq_t + part
            dqt_s[feats, rows] = dq_t * 0.125
        return carry

    lax.fori_loop(0, heads_here, one_head, 0)

    sums = [jnp.zeros((1, LANES), f32) for _ in range(3)]
    for r in range(blocks):
        rows = slice(r * ROWS, (r + 1) * ROWS)
        dq = turn_back(dqt_s[:, rows].T, rows).astype(bf16)
        dk = turn_back(dk_s[rows, :], rows).astype(bf16)
        dv = dv_s[rows, :].astype(bf16)
        for at, grad in enumerate((dq, dk, dv)):
            sums[at] = sums[at] + jnp.sum(grad.astype(f32), axis=0, keepdims=True)
            p_s[at, rows, :] = grad
        o = ot_s[:, rows].T.astype(bf16)
        out_part = dot_nn(o, wo_ref[...])
        dh_part = (
            dot_nt(dq, wq_ref[...]) + dot_nt(dk, wk_ref[...]) + dot_nt(dv, wv_ref[...])
        )

        @pl.when(group == 0)
        def _():
            out_ref[rows, :] = out_part
            dh_ref[rows, :] = dh_part

        @pl.when(group > 0)
        def _():
            out_ref[rows, :] += out_part
            dh_ref[rows, :] += dh_part

    for at in range(3):
        gb_ref[at] = jnp.broadcast_to(sums[at], (8, LANES))
        for r in range(width // ROWS):
            rows = slice(r * ROWS, (r + 1) * ROWS)
            gqkv_ref[at, rows, :] = dot_nn(ht_s[rows, :], p_s[at]).astype(bf16)
    gout_ref[...] = dot_nn(ot_s[...].astype(bf16), dy_ref[...]).astype(bf16)


def attention_branch(length, hidden, out_grad, w_qkv, w_out, b_qkv, rope):
    total, width = hidden.shape
    inner = w_out.shape[0]
    groups = inner // LANES
    whole = lambda g: (0, 0)
    flops = 2 * total * width * inner * 12 + 2 * groups * 4 * total * total * LANES * 4
    return pl.pallas_call(
        attn_kernel,
        grid=(groups,),
        in_specs=[
            pl.BlockSpec(memory_space=pltpu.SMEM),
            pl.BlockSpec((total, width), whole),
            pl.BlockSpec((total, width), whole),
            pl.BlockSpec((width, LANES), lambda g: (0, g)),
            pl.BlockSpec((width, LANES), lambda g: (0, groups + g)),
            pl.BlockSpec((width, LANES), lambda g: (0, 2 * groups + g)),
            pl.BlockSpec((LANES, width), lambda g: (g, 0)),
            pl.BlockSpec((3, 8, LANES), lambda g: (0, 0, g)),
            pl.BlockSpec((3, total, LANES), lambda g: (0, 0, 0)),
        ],
        out_specs=[
            pl.BlockSpec((total, width), whole),
            pl.BlockSpec((total, width), whole),
            pl.BlockSpec((3, width, LANES), lambda g: (0, 0, g)),
            pl.BlockSpec((LANES, width), lambda g: (g, 0)),
            pl.BlockSpec((3, 8, LANES), lambda g: (0, 0, g)),
        ],
        out_shape=[
            jax.ShapeDtypeStruct((total, width), f32),
            jax.ShapeDtypeStruct((total, width), f32),
            jax.ShapeDtypeStruct((3, width, inner), bf16),
            jax.ShapeDtypeStruct((inner, width), bf16),
            jax.ShapeDtypeStruct((3, 8, inner), f32),
        ],
        scratch_shapes=[
            pltpu.VMEM((width, total), bf16),
            pltpu.VMEM((total, LANES), bf16),
            pltpu.VMEM((total, LANES), bf16),
            pltpu.VMEM((total, LANES), bf16),
            pltpu.VMEM((total, LANES), bf16),
            pltpu.VMEM((LANES, total), bf16),
            pltpu.VMEM((LANES, total), bf16),
            pltpu.VMEM((LANES, total), bf16),
            pltpu.VMEM((LANES, total), f32),
            pltpu.VMEM((LANES, total), f32),
            pltpu.VMEM((total, LANES), f32),
            pltpu.VMEM((total, LANES), f32),
            pltpu.VMEM((3, total, LANES), bf16),
            pltpu.VMEM((total, 128), f32),
        ],
        compiler_params=pltpu.CompilerParams(vmem_limit_bytes=60 * 2**20),
        cost_estimate=pl.CostEstimate(
            flops=flops, bytes_accessed=24 * 2**20, transcendentals=8 * total * total
        ),
        name="attention",
    )(length, hidden, out_grad, w_qkv, w_qkv, w_qkv, w_out, b_qkv, rope)


def ffn_kernel(
    tiled,
    h_ref,
    dy_ref,
    wf_ref,
    wp_ref,
    b_ref,
    out_ref,
    dh_ref,
    gf_ref,
    gp_ref,
    gb_ref,
    ht_s,
    act_s,
    dup_s,
):
    step = pl.program_id(0)
    total, width = h_ref.shape
    blocks = total // ROWS
    chunk = wf_ref.shape[1]

    @pl.when(step == 0)
    def _():
        for r in range(blocks):
            ht_s[:, r * ROWS : (r + 1) * ROWS] = h_ref[r * ROWS : (r + 1) * ROWS, :].T

    def one(r, total_grad):
        rows = pl.ds(pl.multiple_of(r * ROWS, ROWS), ROWS)
        up = dot_nn(h_ref[rows, :], wf_ref[...]) + b_ref[0:1, :]
        half = 0.5 + 0.5 * lax.erf(up * (1.0 / math.sqrt(2.0)))
        act = (up * half).astype(bf16)
        slope = half + up * (jnp.exp(-0.5 * up * up) * (1.0 / math.sqrt(2.0 * math.pi)))
        act_grad = dot_nt(dy_ref[rows, :], wp_ref[...])
        up_grad = (slope * act_grad).astype(bf16)
        act_s[rows, :] = act
        dup_s[rows, :] = up_grad
        out_part = dot_nn(act, wp_ref[...])
        dh_part = dot_nt(up_grad, wf_ref[...])

        @pl.when(step == 0)
        def _():
            out_ref[rows, :] = out_part
            dh_ref[rows, :] = dh_part

        @pl.when(step > 0)
        def _():
            out_ref[rows, :] += out_part
            dh_ref[rows, :] += dh_part

        return total_grad + jnp.sum(up_grad.astype(f32), axis=0, keepdims=True)

    sums = lax.fori_loop(0, blocks, one, jnp.zeros((1, chunk), f32))
    gb_ref[...] = jnp.broadcast_to(sums, (8, chunk))
    for r in range(8):
        size = width // 8
        rows = slice(r * size, (r + 1) * size)
        grad = dot_nn(ht_s[rows, :], dup_s[...]).astype(bf16)
        if tiled:
            gf_ref[0, slot_of(r)] = grad
        else:
            gf_ref[rows, :] = grad
    for r in range(chunk // ROWS):
        cols = slice(r * ROWS, (r + 1) * ROWS)
        grad = dot_nn(act_s[:, cols].T, dy_ref[...]).astype(bf16)
        if tiled:
            gp_ref[0, r, 0] = grad[: ROWS // 2]
            gp_ref[1, r, 0] = grad[ROWS // 2 :]
        else:
            gp_ref[cols, :] = grad


def ffn_branch(hidden, out_grad, w_fc, w_proj, b_fc, tiled):
    total, width = hidden.shape
    units = w_proj.shape[0]
    chunk = min(512, units)
    whole = lambda s: (0, 0)
    if tiled:
        gp_spec = pl.BlockSpec((2, 2, 1, ROWS // 2, width), lambda s: (0, 0, s, 0, 0))
        gp_shape = (2, 2, units // chunk, ROWS // 2, width)
        gf_spec = pl.BlockSpec((1, 8, width // 8, chunk), lambda s: (s // 2, 0, 0, s % 2))
        gf_shape = (2, 8, width // 8, units // 2)
    else:
        gp_spec = pl.BlockSpec((chunk, width), lambda s: (s, 0))
        gp_shape = (units, width)
        gf_spec = pl.BlockSpec((width, chunk), lambda s: (0, s))
        gf_shape = (width, units)
    return pl.pallas_call(
        functools.partial(ffn_kernel, tiled),
        grid=(units // chunk,),
        in_specs=[
            pl.BlockSpec((total, width), whole),
            pl.BlockSpec((total, width), whole),
            pl.BlockSpec((width, chunk), lambda s: (0, s)),
            pl.BlockSpec((chunk, width), lambda s: (s, 0)),
            pl.BlockSpec((8, chunk), lambda s: (0, s)),
        ],
        out_specs=[
            pl.BlockSpec((total, width), whole),
            pl.BlockSpec((total, width), whole),
            gf_spec,
            gp_spec,
            pl.BlockSpec((8, chunk), lambda s: (0, s)),
        ],
        out_shape=[
            jax.ShapeDtypeStruct((total, width), f32),
            jax.ShapeDtypeStruct((total, width), f32),
            jax.ShapeDtypeStruct(gf_shape, bf16),
            jax.ShapeDtypeStruct(gp_shape, bf16),
            jax.ShapeDtypeStruct((8, units), f32),
        ],
        scratch_shapes=[
            pltpu.VMEM((width, total), bf16),
            pltpu.VMEM((total, chunk), bf16),
            pltpu.VMEM((total, chunk), bf16),
        ],
        compiler_params=pltpu.CompilerParams(vmem_limit_bytes=60 * 2**20),
        cost_estimate=pl.CostEstimate(
            flops=2 * total * width * units * 6,
            bytes_accessed=28 * 2**20,
            transcendentals=2 * total * units,
        ),
        name="feed_forward",
    )(hidden, out_grad, w_fc, w_proj, b_fc)


def shift(block, axis, distance):
    count = lax.axis_size(axis)
    return lax.ppermute(block, axis, [(i, (i + distance) % count) for i in range(count)])


def swap_bit(block, axis, bit):
    return lax.ppermute(block, axis, [(i, i ^ bit) for i in range(lax.axis_size(axis))])


def shift_within(block, axis, size, distance):
    count = lax.axis_size(axis)
    return lax.ppermute(
        block,
        axis,
        [(i, i // size * size + (i % size + distance) % size) for i in range(count)],
    )


def pick(array, index, axis=0):
    return lax.dynamic_index_in_dim(array, index, axis, keepdims=False)


def order_two(flag, mine, other):
    first = flag == 0
    return jnp.stack([jnp.where(first, mine, other), jnp.where(first, other, mine)])


def gather_rows(local, place):
    dp, y, core, f = place["dp"], place["y"], place["core"], place["f"]
    count = lax.axis_size("fsdp")
    rows, cols = local.shape
    share = rows // lax.axis_size("dp")
    mine = lax.dynamic_slice_in_dim(local, dp * share, share, 0)
    got = jnp.stack([shift(mine, "fsdp", e) for e in range(1, count)])
    got = order_two(y, got, swap_bit(got, "dp", 2))
    got = order_two(core, got, swap_bit(got, "dp", 1))
    got = jnp.transpose(got, (2, 1, 0, 3, 4)).reshape(count - 1, rows, cols)
    if count == 2:
        return order_two(f, local, got[0])
    whole = jnp.zeros((count, rows, cols), local.dtype)
    whole = lax.dynamic_update_index_in_dim(whole, local, f, 0)
    for e in range(1, count):
        whole = lax.dynamic_update_index_in_dim(whole, got[e - 1], (f - e) % count, 0)
    return whole


def reduce_rows(partial, place, parts):
    dp, y, core, f, j = (place[k] for k in ("dp", "y", "core", "f", "j"))
    count, rows, cols = partial.shape
    share = rows // 4
    a = partial.reshape(count, 2, 2, share, cols)
    a = pick(a, core, 2) + swap_bit(pick(a, 1 - core, 2), "dp", 1)
    total = pick(a, f)
    for e in range(1, count):
        total = total + shift(pick(a, (f + e) % count), "fsdp", e)
    total = pick(total, y) + swap_bit(pick(total, 1 - y), "dp", 2)
    total = total + shift(total, "ctx", parts)
    if parts == 2:
        both = order_two(j, total, shift_within(total, "ctx", 2, 1))
    else:
        both = jnp.zeros((parts,) + total.shape, total.dtype)
        both = lax.dynamic_update_index_in_dim(both, total, j, 0)
        for e in range(1, parts):
            got = shift_within(total, "ctx", parts, e)
            both = lax.dynamic_update_index_in_dim(both, got, (j - e) % parts, 0)
    both = order_two(y, both, swap_bit(both, "dp", 2))
    both = order_two(core, both, swap_bit(both, "dp", 1))
    return jnp.transpose(both, (1, 0, 3, 2, 4)).reshape(rows, parts, cols).astype(f32)


def sum_everywhere(vector):
    for bit in (1, 2):
        vector = vector + swap_bit(vector, "dp", bit)
    for axis in ("fsdp", "ctx"):
        bit = 1
        while bit < lax.axis_size(axis):
            vector = vector + swap_bit(vector, axis, bit)
            bit *= 2
    return vector


def gather_sequence(blocks, place, parts):
    s, c = place["s"], place["c"]
    count = lax.axis_size("ctx")
    seqs, rows, width = blocks.shape
    pieces = [(c, pick(blocks, s))]
    for d in range(1, seqs):
        got = shift(pick(blocks, (s + d) % seqs), "ctx", d * parts)
        pieces.append(((c - d * parts) % count, got))
    arrived = []
    for d in range(seqs):
        arrived.append(pieces[d])
        for e in range(1, parts):
            source = s * parts + (place["j"] - e) % parts
            got = shift_within(pieces[d][1], "ctx", parts, e)
            arrived.append(((source - d * parts) % count, got))
    whole = jnp.zeros((count, rows, width), blocks.dtype)
    for at, piece in arrived:
        whole = lax.dynamic_update_index_in_dim(whole, piece, at, 0)
    return whole.reshape(count * rows, width)


def return_blocks(partial, place, parts, seqs):
    s, c, j = place["s"], place["c"], place["j"]
    count = lax.axis_size("ctx")
    rows = partial.shape[0] // count
    blocks = partial.reshape(seqs, parts, rows, -1)
    total = pick(blocks, j, 1).astype(f32)
    for e in range(1, parts):
        total = total + shift_within(pick(blocks, (j + e) % parts, 1), "ctx", parts, e).astype(f32)
    mine = [pick(total, s)]
    for d in range(1, seqs):
        mine.append(shift(pick(total, (s + d) % seqs).astype(bf16), "ctx", d * parts).astype(f32))
    if seqs == 2:
        return order_two(s, mine[0], mine[1])
    whole = jnp.zeros((seqs, rows, partial.shape[1]), f32)
    for d in range(seqs):
        whole = lax.dynamic_update_index_in_dim(whole, mine[d], (s - d) % seqs, 0)
    return whole


class Mover:
    def __init__(self, send, recv, local):
        self.send, self.recv, self.local = send, recv, local
        self.copies, self.left, self.started = [], [], 0

    def to(self, src, dst, axis, index):
        copy = self.remote(src, dst, len(self.copies), (axis, index))
        copy.start()
        self.copies.append(copy)
        return copy

    def here(self, src, dst):
        copy = pltpu.make_async_copy(src, dst, self.local.at[self.started])
        self.started += 1
        copy.start()
        return copy

    def out(self, src, dst):
        self.left.append(self.here(src, dst))

    def remote(self, src, dst, slot, to):
        return pltpu.make_async_remote_copy(
            src_ref=src,
            dst_ref=dst,
            send_sem=self.send.at[slot],
            recv_sem=self.recv.at[slot],
            device_id={to[0]: to[1]},
            device_id_type=pl.DeviceIdType.MESH,
        )

    def stay(self, src, dst, slot):
        return pltpu.make_async_copy(src, dst, self.local.at[slot])

    def finish(self):
        for copy in self.copies:
            copy.wait_send()
        for copy in self.left:
            copy.wait()


class Spot:
    def __init__(self):
        self.dp, self.c, self.f = (lax.axis_index(a) for a in ("dp", "ctx", "fsdp"))
        self.y, self.core = self.dp // 2, self.dp % 2
        self.s, self.j = self.c // 2, self.c % 2
        flip = lambda v: v + 1 - 2 * (v % 2)
        self.x_to = ("fsdp", 1 - self.f)
        self.y_to = ("dp", (1 - self.y) * 2 + self.core)
        self.core_to = ("dp", flip(self.dp))
        self.pair_to = ("ctx", flip(self.c))
        self.far_to = ("ctx", (1 - self.s) * 2 + self.j)

    def greet(self):
        barrier = pltpu.get_barrier_semaphore()
        partners = (self.x_to, self.y_to, self.core_to, self.pair_to, self.far_to)
        for axis, index in partners:
            pl.semaphore_signal(
                barrier, inc=1, device_id={axis: index}, device_id_type=pl.DeviceIdType.MESH
            )
        pl.semaphore_wait(barrier, len(partners))


def block(index, size):
    return pl.ds(pl.multiple_of(index * size, size), size)


def gather_kernel(
    x_ref,
    cot_ref,
    fc_ref,
    proj_ref,
    qkv_ref,
    out_ref,
    small_ref,
    seq_in,
    seq_grad,
    w_fc,
    w_proj,
    w_qkv,
    w_out,
    small,
    hold_act,
    hold_fc,
    hold_proj,
    hold_qkv,
    hold_out,
    hold_small,
    send,
    recv,
    local,
):
    at = Spot()
    mover = Mover(send, recv, local)
    at.greet()
    rows = x_ref.shape[1]
    other = 1 - at.f
    turns = []
    through = []

    def keep(src, held, dst):
        through.append((mover.here(src, held), held, dst))

    mover.to(small_ref, small.at[at.f], *at.x_to)
    keep(small_ref, hold_small, small.at[at.f])

    first = {}
    for slot, (name, src, dst) in enumerate((("in", x_ref, seq_in), ("grad", cot_ref, seq_grad))):
        mine = dst.at[block(at.c, rows)]
        far = mover.to(src.at[1 - at.s], mine, *at.far_to)
        near = mover.to(src.at[at.s], mine, *at.pair_to)
        keep(src.at[at.s], hold_act.at[slot], mine)
        first[name] = (far, near, dst)

    def fc_spans(r):
        width = w_fc.shape[1] // 2
        return [
            (fc_ref.at[r, block(2 * k + at.j, width)], pl.ds(k * width, width)) for k in range(2)
        ]

    def qkv_spans(r):
        width = w_qkv.shape[1] // 12
        return [
            (
                qkv_ref.at[r, block(t * 8 + h * 4 + at.j * 2 + g, width)],
                pl.ds((t * 4 + g * 2 + h) * width, width),
            )
            for t in range(3)
            for g in range(2)
            for h in range(2)
        ]

    def row_spans(ref, held):
        count = held.shape[0] // 2

        def spans(r):
            start = pl.multiple_of(at.j * count + r.start, r.size)
            return [(ref.at[pl.ds(start, r.size)], slice(None))]

        return spans

    weights = (
        (w_fc, fc_spans),
        (w_proj, row_spans(proj_ref, w_proj)),
        (w_qkv, qkv_spans),
        (w_out, row_spans(out_ref, w_out)),
    )
    holds = (hold_fc, hold_proj, hold_qkv, hold_out)
    for held, spans in weights:
        count = held.shape[0] // 2
        share = count // 4
        span = pl.ds(pl.multiple_of(at.dp * share, share), share)
        there = pl.ds(pl.multiple_of(at.f * count + at.dp * share, share), share)
        turns.append([mover.to(src, held.at[there, cols], *at.x_to) for src, cols in spans(span)])
    for (held, spans), hold in zip(weights, holds):
        count = held.shape[0] // 2
        there = block(at.f, count)
        for src, cols in spans(pl.ds(0, count)):
            keep(src, hold if isinstance(cols, slice) else hold.at[:, cols], held.at[there, cols])
    for copy, hold, dst in through:
        copy.wait()
        mover.out(hold, dst)

    def quarter(held, dp):
        count = held.shape[0] // 2
        share = count // 4
        return held.at[pl.ds(pl.multiple_of(other * count + dp * share, share), share)]

    y_turns, last = [], []
    for (held, _), copies in zip(weights, turns):
        for copy in copies:
            copy.wait_recv()
        part = quarter(held, at.dp)
        y_turns.append(mover.to(part, part, *at.y_to))
        last.append(mover.to(part, part, *at.core_to))
    for name in ("in", "grad"):
        far, _, dst = first[name]
        far.wait_recv()
        part = dst.at[block(at.far_to[1], rows)]
        last.append(mover.to(part, part, *at.pair_to))
    for (held, _), copy in zip(weights, y_turns):
        copy.wait_recv()
        part = quarter(held, at.y_to[1])
        last.append(mover.to(part, part, *at.core_to))
    for name in ("in", "grad"):
        first[name][1].wait_recv()
    for copy in last:
        copy.wait_recv()
    mover.copies[0].wait_recv()
    mover.finish()


def gather_all(x, cot, fc, proj, qkv, out, small):
    seqs, rows, width = x.shape
    total = 4 * rows
    hbm = pl.BlockSpec(memory_space=pl.ANY)
    shape = lambda *dims: jax.ShapeDtypeStruct(dims, bf16)
    return pl.pallas_call(
        gather_kernel,
        in_specs=[hbm] * 7,
        out_specs=[hbm] * 7,
        out_shape=[
            shape(total, width),
            shape(total, width),
            shape(width, fc.shape[1] // 2),
            shape(proj.shape[0], width),
            shape(width, qkv.shape[1] // 2),
            shape(out.shape[0], width),
            shape(2, *small.shape),
        ],
        scratch_shapes=[
            pltpu.VMEM((2, rows, width), bf16),
            pltpu.VMEM((width // 2, fc.shape[1] // 2), bf16),
            pltpu.VMEM((proj.shape[0] // 2, width), bf16),
            pltpu.VMEM((width // 2, qkv.shape[1] // 2), bf16),
            pltpu.VMEM((out.shape[0] // 2, width), bf16),
            pltpu.VMEM(small.shape, bf16),
            pltpu.SemaphoreType.DMA((40,)),
            pltpu.SemaphoreType.DMA((40,)),
            pltpu.SemaphoreType.DMA((40,)),
        ],
        compiler_params=pltpu.CompilerParams(
            collective_id=0, has_side_effects=True, vmem_limit_bytes=40 * 2**20
        ),
        name="gather",
    )(x, cot, fc, proj, qkv, out, small)


def branch_kernel(
    length_ref,
    x_ref,
    dy_ref,
    wqkv_ref,
    wo_ref,
    bias_ref,
    rope_ref,
    ffn_out_ref,
    ffn_pull_ref,
    gp_ref,
    gf_ref,
    small_ref,
    summed,
    branch,
    pull,
    small,
    x_s,
    dy_s,
    h_s,
    ht_s,
    wqkv_s,
    wo_s,
    rope_s,
    q_s,
    k_s,
    v_s,
    do_s,
    kt_s,
    vt_s,
    dot_s,
    ot_s,
    dqt_s,
    dk_s,
    dv_s,
    dp_s,
    o_s,
    kb_s,
    own_s,
    mine_s,
    core_s,
    x_got,
    y_got,
    far_got,
    home_s,
    home_got,
    small_s,
    small_got,
    send,
    recv,
    local,
):
    at = Spot()
    mover = Mover(send, recv, local)
    total, width = x_s.shape
    blocks = total // ROWS
    inner = wo_s.shape[0]
    head_size = 64
    length = length_ref[0]

    load_x = mover.here(x_ref, x_s)
    load_w = mover.here(wqkv_ref, wqkv_s)
    load_rope = mover.here(rope_ref, rope_s)
    load_dy = mover.here(dy_ref, dy_s)
    half = LANES // 2
    load_wo = [
        mover.here(
            wo_ref.at[pl.ds(h * LANES + g * half, half)],
            wo_s.at[pl.ds(g * LANES + h * half, half)],
        )
        for g in range(2)
        for h in range(2)
    ]
    load_small = mover.here(small_ref, small_s.at[0])
    at.greet()

    links = ("c", "x", "y", "z", "p", "yy", "c1", "c2")

    def own_of(n):
        return own_s.at[n] if n < 4 else mine_s.at[n - 4, at.core]

    def whole_of(n):
        return gp_ref.at[n] if n < 2 else gf_ref.at[n - 2]

    def link(n, name):
        own = own_of(n)
        mine, other = summed.at[n, at.y, at.core], summed.at[n, 1 - at.y, at.core]
        if name == "c":
            src = (whole_of(n) if n < 4 else mine_s.at[n - 4]).at[1 - at.core]
            ends = (src, core_s.at[n], at.core_to)
        elif name == "x":
            ends = (own.at[1 - at.f], x_got.at[n], at.x_to)
        elif name == "y":
            ends = (own.at[at.f, 1 - at.y], y_got.at[n], at.y_to)
        elif name == "z":
            ends = (own.at[at.f, at.y], far_got.at[n], at.far_to)
        elif name == "p":
            ends = (y_got.at[n], summed.at[n, at.y, at.core, at.j], at.pair_to)
        elif name == "yy":
            ends = (mine, mine, at.y_to)
        elif name == "c1":
            ends = (mine, mine, at.core_to)
        else:
            ends = (other, other, at.core_to)
        return mover.remote(ends[0], ends[1], n * len(links) + links.index(name), ends[2])

    def load(n):
        return mover.stay(whole_of(n).at[at.core], own_s.at[n], 24 + n)

    def keep(n):
        return mover.stay(y_got.at[n], summed.at[n, at.y, at.core, at.j], 28 + n)

    def step_start(n):
        if n < 4:
            load(n).start()
        link(n, "c").start()

    def step_core(n):
        if n < 4:
            load(n).wait()
        link(n, "c").wait_recv()
        own, got = own_of(n), core_s.at[n]
        own[1 - at.f] = own[1 - at.f] + got[1 - at.f]
        link(n, "x").start()
        own[at.f] = own[at.f] + got[at.f]

    def step_x(n):
        link(n, "x").wait_recv()
        own, got = own_of(n), x_got.at[n]
        own[at.f, 1 - at.y] = own[at.f, 1 - at.y] + got[1 - at.y]
        link(n, "y").start()
        own[at.f, at.y] = own[at.f, at.y] + got[at.y]

    def step_y(n):
        link(n, "y").wait_recv()
        own = own_of(n)
        own[at.f, at.y] = own[at.f, at.y] + y_got[n]
        link(n, "z").start()

    def step_far(n):
        link(n, "z").wait_recv()
        y_got[n] = own_of(n)[at.f, at.y] + far_got[n]
        link(n, "p").start()
        keep(n).start()

    def step_pair(n):
        link(n, "p").wait_recv()
        keep(n).wait()
        link(n, "yy").start()
        link(n, "c1").start()

    def step_yy(n):
        link(n, "yy").wait_recv()
        link(n, "c2").start()

    base = 6 * len(links)

    def near(k):
        t, n = k // 2, k % 2
        return mover.remote(
            home_s.at[n, 2 * t + 1 - at.j], home_got.at[n, t], base + k, at.pair_to
        )

    def last(k):
        t, n = k // 2, k % 2
        mine, dst = home_s.at[n, 2 * t + at.j], (branch, pull)[n].at[at.s]
        return mover.remote(mine, dst, base + 4 + n, at.far_to), mover.stay(mine, dst, 34 + n)

    def home_near(k):
        near(k).start()

    def home_sum(k):
        t, n = k // 2, k % 2
        near(k).wait_recv()
        mine = home_s.at[n, 2 * t + at.j]
        mine[...] = (mine[...].astype(f32) + home_got[n, t].astype(f32)).astype(bf16)
        far, stay = last(k)
        pl.when(at.s == t)(stay.start)
        pl.when(at.s != t)(far.start)

    trips = (at.core_to, at.x_to, at.y_to, at.far_to, at.pair_to)

    def small_trip(n):
        return mover.remote(small_s.at[n], small_got.at[n], base + 6 + n, trips[n])

    def small_step(n):
        if n > 0:
            small_trip(n - 1).wait_recv()
            small_s[n] = small_s[n - 1] + small_got[n - 1]
        if n < 5:
            small_trip(n).start()
        else:
            mover.out(small_s.at[5], small)

    def end():
        for n in range(6):
            link(n, "c1").wait_recv()
            link(n, "c2").wait_recv()
            for name in links:
                link(n, name).wait_send()
        for n in range(2):
            far, stay = last(n)
            far.wait()
            stay.wait()
        for n in range(4):
            near(n).wait_send()
        for n in range(5):
            small_trip(n).wait_send()

    acts = dict(
        start=step_start,
        core=step_core,
        x=step_x,
        y=step_y,
        far=step_far,
        pair=step_pair,
        yy=step_yy,
        near=home_near,
        sum=home_sum,
        small=small_step,
    )

    def turn(*place):
        for word in PLAN.get(",".join(str(v) for v in place), ()):
            name, n = word.split(":")
            acts[name](int(n))

    for n in range(4):
        step_start(n)

    def normal(rows):
        v = x_s[rows, :].astype(f32)
        center = v - jnp.mean(v, axis=-1, keepdims=True)
        spread = jnp.mean(center * center, axis=-1, keepdims=True)
        return center * lax.rsqrt(spread + epsilon)

    def table(n, rows):
        part = rope_s[n, rows, :]
        return jnp.concatenate([part, part], axis=1)

    def turned(v, rows, sign):
        left = pltpu.roll(v, LANES - ROT // 2, 1)
        right = pltpu.roll(v, ROT // 2, 1)
        moved = left * table(1, rows) + right * table(2, rows)
        return v * table(0, rows) + moved if sign > 0 else v * table(0, rows) - moved

    key_pos = lax.broadcasted_iota(jnp.int32, (total, 128), 0)
    kb_s[...] = jnp.where(key_pos < length, 0.0, masked_score)
    lane = lax.broadcasted_iota(jnp.int32, (ROWS, LANES), 1)
    causal = lax.broadcasted_iota(jnp.int32, (ROWS, ROWS), 0) <= lax.broadcasted_iota(
        jnp.int32, (ROWS, ROWS), 1
    )
    gain, offset = bias_ref[3:4, :], bias_ref[4:5, :]

    def span(b):
        return slice(b * ROWS, (b + 1) * ROWS)

    def project(g):
        cols = lambda t: slice(t * inner + g * LANES, t * inner + (g + 1) * LANES)
        bias = lambda t: bias_ref[t : t + 1, g * LANES : (g + 1) * LANES]
        for r in range(blocks):
            rows = span(r)
            if g == 0:
                hr = (normal(rows) * gain + offset).astype(bf16)
                h_s[rows, :] = hr
                ht_s[:, rows] = hr.T
                if r == 0:
                    load_w.wait()
                    load_rope.wait()
                    load_dy.wait()
                    for copy in load_wo:
                        copy.wait()
            else:
                hr = h_s[rows, :]
            q = turned(dot_nn(hr, wqkv_s[:, cols(0)]) + bias(0), rows, 1).astype(bf16)
            q_s[rows, :] = (q.astype(f32) * 0.125).astype(bf16)
            k = turned(dot_nn(hr, wqkv_s[:, cols(1)]) + bias(1), rows, 1).astype(bf16)
            k_s[rows, :] = k
            kt_s[:, rows] = k.T
            v = (dot_nn(hr, wqkv_s[:, cols(2)]) + bias(2)).astype(bf16)
            v_s[rows, :] = v
            vt_s[:, rows] = v.T
            do = dot_nt(dy_s[rows, :], wo_s[g * LANES : (g + 1) * LANES, :]).astype(bf16)
            do_s[rows, :] = do
            dot_s[:, rows] = do.T
            turn("p%d" % g, r)
        dk_s[...] = jnp.zeros_like(dk_s)
        dv_s[...] = jnp.zeros_like(dv_s)

    def one_head(g, i, head, carry):
        feats = pl.ds(pl.multiple_of(head * head_size, head_size), head_size)
        mine = (lane // head_size) == head
        zero = jnp.zeros((ROWS, LANES), bf16)
        rows = span(i)
        qm = jnp.where(mine, q_s[rows, :], zero)
        dom = jnp.where(mine, do_s[rows, :], zero)
        scores = []
        top = None
        for b in range(i + 1):
            sc = dot_nt(k_s[span(b), :], qm)
            kb = kb_s[span(b), :]
            sc = sc + jnp.concatenate([kb, kb], axis=1)
            if b == i:
                sc = jnp.where(causal, sc, masked_score)
            best = jnp.max(sc, axis=0, keepdims=True)
            top = best if top is None else jnp.maximum(top, best)
            scores.append(sc)
        row_sum = None
        for b in range(i + 1):
            scores[b] = jnp.exp(scores[b] - top)
            part = jnp.sum(scores[b], axis=0, keepdims=True)
            row_sum = part if row_sum is None else row_sum + part
        inverse = 1.0 / row_sum
        o_t = None
        for b in range(i + 1):
            scores[b] = scores[b] * inverse
            low = scores[b].astype(bf16)
            dv_s[span(b), :] += dot_nn(low, dom)
            part = dot_nn(vt_s[feats, span(b)], low)
            o_t = part if o_t is None else o_t + part
        ot_s[feats, rows] = o_t
        delta = jnp.sum(dot_s[feats, rows].astype(f32) * o_t, axis=0, keepdims=True)
        dq_t = None
        for b in range(i + 1):
            dp = dot_nt(v_s[span(b), :], dom)
            ds = (scores[b] * (dp - delta)).astype(bf16)
            dk_s[span(b), :] += dot_nn(ds, qm)
            part = dot_nn(kt_s[feats, span(b)], ds)
            dq_t = part if dq_t is None else dq_t + part
        dqt_s[feats, rows] = dq_t * 0.125
        for h in range(LANES // head_size):
            if "%d,%d,%d" % (g, i, h) in PLAN:
                pl.when(head == h)(functools.partial(turn, g, i, h))
        return carry

    def finish_block(g, i, sums):
        rows = span(i)
        cols = slice(g * LANES, (g + 1) * LANES)
        dq = turned(dqt_s[:, rows].T, rows, -1).astype(bf16)
        dk = turned(dk_s[rows, :], rows, -1).astype(bf16)
        dv = dv_s[rows, :].astype(bf16)
        for t, grad in enumerate((dq, dk, dv)):
            sums[t] = sums[t] + jnp.sum(grad.astype(f32), axis=0, keepdims=True)
            dp_s[t, rows, cols] = grad
        o_s[rows, cols] = ot_s[:, rows].T.astype(bf16)

    def finish_rows(i, gain_sum, shift_sum):
        rows = span(i)
        out = dot_nn(o_s[rows, :], wo_s[...])
        home_s[0, i] = (out + home_s[0, i].astype(f32)).astype(bf16)
        dh = dot_nt(dp_s[0, rows, :], wqkv_s[:, :inner])
        dh = dh + dot_nt(dp_s[1, rows, :], wqkv_s[:, inner : 2 * inner])
        dh = dh + dot_nt(dp_s[2, rows, :], wqkv_s[:, 2 * inner :])
        home_s[1, i] = (dh * gain + home_s[1, i].astype(f32)).astype(bf16)
        gain_sum = gain_sum + jnp.sum(dh * normal(rows), axis=0, keepdims=True)
        return gain_sum, shift_sum + jnp.sum(dh, axis=0, keepdims=True)

    def weight_grads(g):
        cols = slice(g * LANES, (g + 1) * LANES)
        size = width // 8
        for t in range(3):
            for r in range(8):
                grad = dot_nn(ht_s[r * size : (r + 1) * size, :], dp_s[t, :, cols])
                mine_s[g, r % 2, r // 4, r // 2 % 2, :, t * LANES : (t + 1) * LANES] = grad.astype(bf16)
        grad = dot_nn(ot_s[...].astype(bf16), dy_s[...]).astype(bf16)
        size = LANES // 8
        for r in range(8):
            for b in range(4):
                mine_s[
                    g, r % 2, r // 4, r // 2 % 2, b * size : (b + 1) * size, 3 * LANES :
                ] = grad[r * size : (r + 1) * size, b * LANES : (b + 1) * LANES]

    load_x.wait()
    loads_home = [
        mover.here(ref.at[block(b, ROWS)], home_s.at[n, b])
        for n, ref in ((0, ffn_out_ref), (1, ffn_pull_ref))
        for b in range(blocks)
    ]
    load_small.wait()
    gain_sum = jnp.zeros((1, width), f32)
    shift_sum = jnp.zeros((1, width), f32)
    for g in range(2):
        project(g)
        sums = [jnp.zeros((1, LANES), f32) for _ in range(3)]
        for i in reversed(range(blocks)):
            lax.fori_loop(0, LANES // head_size, functools.partial(one_head, g, i), 0)
            finish_block(g, i, sums)
            if g == 1:
                if i == blocks - 1:
                    for copy in loads_home:
                        copy.wait()
                gain_sum, shift_sum = finish_rows(i, gain_sum, shift_sum)
            turn(g, i)
        weight_grads(g)
        line = pl.ds(pl.multiple_of(8 + at.j * 8, 8), 8)
        first_row = lax.broadcasted_iota(jnp.int32, (8, LANES), 0) == 0
        for t in range(3):
            cols = slice(t * inner + g * LANES, t * inner + (g + 1) * LANES)
            small_s[0, line, cols] = jnp.where(first_row, sums[t], small_s[0, line, cols])
        if g == 0:
            turn("grads")
    small_s[0, 0:1, :width] = gain_sum
    small_s[0, 1:2, :width] = shift_sum
    turn("tail")
    end()
    mover.finish()


PLAN = {
    "p0,2": ("core:1",),
    "0,3,3": ("core:0",),
    "0,3": ("x:1",),
    "0,2,3": ("y:1",),
    "0,1,0": ("core:3", "x:0",),
    "0,0,0": ("y:0",),
    "0,0,1": ("far:1",),
    "0,0,2": ("core:2", "x:3",),
    "p1,0": ("start:4",),
    "p1,2": ("y:3", "far:0",),
    "1,3,0": ("x:2",),
    "1,3,3": ("far:3", "y:2", "core:4",),
    "1,2,0": ("pair:0",),
    "1,2": ("near:2",),
    "1,1,3": ("yy:0", "pair:3", "near:3",),
    "1,0,1": ("sum:2",),
    "1,0,2": ("far:2",),
    "1,0,3": ("x:4",),
    "tail": ("near:1", "start:5", "y:4", "core:5", "pair:1", "x:5", "small:0", "y:5", "far:4", "small:1", "small:2", "far:5", "near:0", "sum:1", "pair:4", "sum:3", "pair:2", "pair:5", "small:3", "small:4", "sum:0", "yy:3", "yy:1", "yy:2", "yy:4", "small:5", "yy:5",),
}


def branch_and_sums(length, x, dy, w_qkv, w_out, bias, rope, ffn_out, ffn_pull, gp, gf, small):
    total, width = x.shape
    inner = w_out.shape[0]
    cell = (ROWS // 2, width)
    hbm = pl.BlockSpec(memory_space=pl.ANY)
    vmem = pl.BlockSpec(memory_space=pltpu.VMEM)
    home = jax.ShapeDtypeStruct((2, ROWS, width), bf16)
    buf = lambda dims, kind=bf16: pltpu.VMEM(tuple(dims), kind)
    return pl.pallas_call(
        branch_kernel,
        in_specs=[pl.BlockSpec(memory_space=pltpu.SMEM)] + [hbm] * 4 + [vmem] + [hbm] * 6,
        out_specs=[hbm] * 4,
        out_shape=[
            jax.ShapeDtypeStruct((6, 2, 2, 2) + cell, bf16),
            home,
            home,
            jax.ShapeDtypeStruct(small.shape, f32),
        ],
        scratch_shapes=[
            buf((total, width)),
            buf((total, width)),
            buf((total, width)),
            buf((width, total)),
            buf((width, 3 * inner)),
            buf((inner, width)),
            buf((3, total, 128), f32),
            buf((total, LANES)),
            buf((total, LANES)),
            buf((total, LANES)),
            buf((total, LANES)),
            buf((LANES, total)),
            buf((LANES, total)),
            buf((LANES, total)),
            buf((LANES, total), f32),
            buf((LANES, total), f32),
            buf((total, LANES), f32),
            buf((total, LANES), f32),
            buf((3, total, inner)),
            buf((total, inner)),
            buf((total, 128), f32),
            buf((4, 2, 2) + cell),
            buf((2, 2, 2, 2) + cell),
            buf((6, 2, 2) + cell),
            buf((6, 2) + cell),
            buf((6,) + cell),
            buf((6,) + cell),
            buf((2, total // ROWS, ROWS, width)),
            buf((2, 2, ROWS, width)),
            buf((6,) + small.shape, f32),
            buf((5,) + small.shape, f32),
            pltpu.SemaphoreType.DMA((80,)),
            pltpu.SemaphoreType.DMA((80,)),
            pltpu.SemaphoreType.DMA((40,)),
        ],
        compiler_params=pltpu.CompilerParams(
            collective_id=1, has_side_effects=True, vmem_limit_bytes=62 * 2**20
        ),
        name="branch",
    )(length, x, dy, w_qkv, w_out, bias, rope, ffn_out, ffn_pull, gp, gf, small)


def widen_proj_kernel(src_ref, dst_ref):
    for k in range(2):
        for p in range(2):
            dst_ref[p, 0, 0, k] = src_ref[k, 0, 0, p].astype(f32)


def widen_proj(summed, shape):
    size, width = summed.shape[4:]
    return pl.pallas_call(
        widen_proj_kernel,
        grid=(2, 2),
        in_specs=[pl.BlockSpec((2, 1, 1, 2, size, width), lambda y, c: (0, y, c, 0, 0, 0))],
        out_specs=pl.BlockSpec((2, 1, 1, 2, size, width), lambda y, c: (0, y, c, 0, 0, 0)),
        out_shape=jax.ShapeDtypeStruct((2, 2, 2, 2, size, width), f32),
        name="widen_proj",
    )(summed).reshape(shape)


def widen_fc_kernel(src_ref, dst_ref):
    width = src_ref.shape[5]
    for k in range(2):
        for p in range(2):
            at = (2 * k + p) * width
            dst_ref[:, at : at + width] = src_ref[k, 0, 0, p].astype(f32)


def widen_fc(summed, shape):
    size, width = summed.shape[4:]
    return pl.pallas_call(
        widen_fc_kernel,
        grid=(2, 2),
        in_specs=[pl.BlockSpec((2, 1, 1, 2, size, width), lambda y, c: (1, y, c, 0, 0, 0))],
        out_specs=pl.BlockSpec((size, 4 * width), lambda y, c: (y * 2 + c, 0)),
        out_shape=jax.ShapeDtypeStruct(shape, f32),
        name="widen_fc",
    )(summed)


def widen_heads_kernel(src_ref, qkv_ref, out_ref):
    size = src_ref.shape[4]
    for g in range(2):
        for p in range(2):
            for t in range(3):
                for h in range(2):
                    got = src_ref[g, 0, 0, p, :, (t * 2 + h) * 128 : (t * 2 + h + 1) * 128]
                    to = t * 8 + h * 4 + p * 2 + g
                    qkv_ref[:, to * 128 : (to + 1) * 128] = got.astype(f32)
            for b in range(4):
                got = src_ref[g, 0, 0, p, b * size // 4 : (b + 1) * size // 4, 3 * LANES :]
                out_ref[p, g, 0, 0, :, b * LANES : (b + 1) * LANES] = got.astype(f32)


def widen_heads(summed, qkv_shape, out_shape):
    size, width = summed.shape[4:]
    qkv, out = pl.pallas_call(
        widen_heads_kernel,
        grid=(2, 2),
        in_specs=[
            pl.BlockSpec((2, 1, 1, 2, size, width), lambda y, c: (2, y, c, 0, 0, 0))
        ],
        out_specs=[
            pl.BlockSpec((size, qkv_shape[1]), lambda y, c: (y * 2 + c, 0)),
            pl.BlockSpec((2, 2, 1, 1, size // 4, width), lambda y, c: (0, 0, y, c, 0, 0)),
        ],
        out_shape=[
            jax.ShapeDtypeStruct(qkv_shape, f32),
            jax.ShapeDtypeStruct((2, 2, 2, 2, size // 4, width), f32),
        ],
        name="widen_heads",
    )(summed)
    return qkv, out.reshape(out_shape)


def normalize(features):
    center = features - jnp.mean(features, axis=-1, keepdims=True)
    spread = jnp.mean(center * center, axis=-1, keepdims=True)
    inverse = lax.rsqrt(spread + epsilon)
    return center * inverse, inverse


def rope_tables(total, head_size):
    half = ROT // 2
    inverse = rope_base ** (-(2.0 * jnp.arange(half, dtype=f32)) / ROT)
    angles = jnp.arange(total, dtype=jnp.int32).astype(f32)[:, None] * inverse[None, :]
    cosine, sine = jnp.cos(angles), jnp.sin(angles)
    rest = jnp.zeros((total, head_size - ROT), f32)
    none = jnp.zeros((total, half), f32)
    same = jnp.concatenate([cosine, cosine, rest + 1.0], axis=1)
    ahead = jnp.concatenate([-sine, none, rest], axis=1)
    behind = jnp.concatenate([none, sine, rest], axis=1)
    return jnp.tile(jnp.stack([same, ahead, behind]), (1, 1, LANES // head_size))


def per_device(
    residual_in,
    lengths,
    gain_attn,
    shift_attn,
    weight_qkv,
    bias_qkv,
    weight_out,
    bias_out,
    gain_ffn,
    shift_ffn,
    weight_fc,
    bias_fc,
    weight_proj,
    bias_proj,
    cotangent,
):
    seqs, block_rows, width = residual_in.shape
    n_ctx, n_fsdp = lax.axis_size("ctx"), lax.axis_size("fsdp")
    parts = n_ctx // seqs
    total = n_ctx * block_rows
    units = weight_fc.shape[1]
    head_size = width // HEADS
    c, f, dp = lax.axis_index("ctx"), lax.axis_index("fsdp"), lax.axis_index("dp")
    s, j = c // parts, c % parts
    place = dict(c=c, f=f, dp=dp, s=s, j=j, y=dp // 2, core=dp % 2)
    spread_heads = HEADS % (n_fsdp * parts) == 0
    n_h = n_fsdp if spread_heads else 1
    inner = width // parts

    rows_here = weight_qkv.shape[0]
    own_heads = lambda v: pick(v.reshape(3, n_h, parts, -1), j, 2)
    fast = (seqs, n_ctx, n_fsdp, lax.axis_size("dp")) == (2, 4, 2, 4)
    small_local = jnp.concatenate(
        [gain_attn, shift_attn, gain_ffn, shift_ffn, bias_out, bias_proj, bias_qkv, bias_fc]
    )
    part_width = width // n_fsdp
    if fast:
        packed = jnp.pad(small_local.reshape(13, -1), ((0, 3), (0, 0)))
        seq_in, seq_grad, w_fc, w_proj, w_qkv, w_out, small = gather_all(
            residual_in, cotangent, weight_fc, weight_proj, weight_qkv, weight_out, packed
        )
        small = small[:, :13].reshape(2, -1)
    else:
        small = lax.all_gather(small_local, "fsdp", axis=0)
    vec = lambda at, size: small[:, at : at + size].reshape(-1).astype(f32)
    gain_one, shift_one, gain_two, shift_two, b_out, b_proj = (
        vec(i * part_width, part_width) for i in range(6)
    )
    b_qkv = vec(6 * part_width, 3 * part_width)
    b_fc = vec(9 * part_width, units // n_fsdp)

    if not fast:
        fc_local = pick(weight_fc.reshape(rows_here, n_fsdp, parts, -1), j, 2).reshape(rows_here, -1)
        proj_local = pick(weight_proj.reshape(parts, -1, width), j)
        qkv_local = pick(weight_qkv.reshape(rows_here, 3, n_h, parts, -1), j, 3).reshape(rows_here, -1)
        seq_in = gather_sequence(residual_in, place, parts)
        w_fc = gather_rows(fc_local, place).reshape(width, -1)
        w_proj = gather_rows(proj_local, place).reshape(-1, width)
        seq_grad = gather_sequence(cotangent, place, parts)
        w_qkv = gather_rows(qkv_local, place).reshape(width, -1)
        if spread_heads:
            w_out = gather_rows(pick(weight_out.reshape(parts, -1, width), j), place).reshape(-1, width)
        else:
            w_out = lax.all_gather(weight_out, "fsdp", axis=0, tiled=True)
            w_out = pick(w_out.reshape(parts, -1, width), j)
    b_qkv_j = own_heads(b_qkv).reshape(3, 1, inner)
    b_fc_j = pick(b_fc.reshape(n_fsdp, parts, -1), j, 1).reshape(1, -1)
    b_fc_j = jnp.broadcast_to(b_fc_j, (8, b_fc_j.shape[1]))

    length = pick(lengths, s)
    positions = jnp.arange(total, dtype=jnp.int32)
    seq_grad = jnp.where((positions < length)[:, None], seq_grad, jnp.zeros((), bf16))
    xhat, _ = normalize(seq_in.astype(f32))
    hidden_one = (xhat * gain_one + shift_one).astype(bf16)
    hidden_two = (xhat * gain_two + shift_two).astype(bf16)

    ffn_out, ffn_dh, g_fc, g_proj, g_bfc = ffn_branch(
        hidden_two, seq_grad, w_fc, w_proj, b_fc_j, fast
    )
    ffn_sums = (jnp.sum(ffn_dh * xhat, axis=0), jnp.sum(ffn_dh, axis=0))
    own_grad = jnp.sum(seq_grad.astype(f32), axis=0) / parts
    rope = rope_tables(total, head_size)
    own_part = lambda v, size=part_width: lax.dynamic_slice_in_dim(v, f * size, size)

    if fast:
        row = lambda v: v.reshape(1, -1)
        widen = lambda v: jnp.pad(v, ((0, 0), (0, 2 * width - v.shape[1])))
        shared = widen(jnp.concatenate([jnp.zeros((2, width), f32)] + [row(v) for v in (*ffn_sums, own_grad)]))
        shared = jnp.pad(shared, ((0, 3), (0, 0)))
        of_part = jnp.pad(widen(g_bfc[:1]), ((1, 6), (0, 0)))
        nothing = jnp.zeros((8, 2 * width), f32)
        small_in = jnp.concatenate(
            [shared, jnp.where(j == 0, of_part, nothing), jnp.where(j == 1, of_part, nothing)]
        )
        heads = b_qkv_j.reshape(3, n_h, 2, -1)
        heads = jnp.swapaxes(heads, 1, 2).reshape(3, inner)
        heads = jnp.pad(heads, ((0, 0), (0, width - inner)))
        vectors = jnp.concatenate([heads, row(gain_one), row(shift_one), jnp.zeros((3, width), f32)])
        summed, branch, pulled, small_sums = branch_and_sums(
            length[None],
            seq_in,
            seq_grad,
            w_qkv,
            w_out,
            vectors,
            rope[:, :, :128],
            ffn_out.astype(bf16),
            (ffn_dh * gain_two).astype(bf16),
            g_proj.reshape(2, 2, 2, 2, -1, width),
            g_fc.reshape(2, 2, 2, 2, -1, width),
            small_in,
        )
        d_proj = widen_proj(summed, weight_proj.shape)
        d_fc = widen_fc(summed, weight_fc.shape)
        d_qkv, d_out = widen_heads(summed, weight_qkv.shape, weight_out.shape)
        d_gain_one, d_shift_one, d_gain_two, d_shift_two, d_bias = (
            own_part(small_sums[i, :width]) for i in range(5)
        )
        d_bqkv = small_sums[8::8, : 3 * inner].reshape(parts, 3, 2, n_h, -1)
        d_bqkv = own_part(jnp.transpose(d_bqkv, (1, 3, 0, 2, 4)).reshape(-1), 3 * part_width)
        d_bfc = jnp.swapaxes(small_sums[9::8].reshape(parts, n_fsdp, -1), 0, 1).reshape(-1)
        d_bfc = own_part(d_bfc, units // n_fsdp)
        branch, pulled = branch.astype(f32), pulled.astype(f32)
    else:
        attn_out, attn_dh, g_qkv, g_out, g_bqkv = attention_branch(
            length[None],
            hidden_one,
            seq_grad,
            w_qkv,
            w_out,
            jnp.broadcast_to(b_qkv_j, (3, 8, inner)),
            rope,
        )
        g_bqkv_all = jnp.zeros((3, n_h, parts, inner // n_h), f32)
        g_bqkv_all = lax.dynamic_update_index_in_dim(
            g_bqkv_all, g_bqkv[:, 0].reshape(3, n_h, -1), j, 2
        )
        g_bfc_all = jnp.zeros((n_fsdp, parts, units // (n_fsdp * parts)), f32)
        g_bfc_all = lax.dynamic_update_index_in_dim(g_bfc_all, g_bfc[0].reshape(n_fsdp, -1), j, 1)
        rows_of = (
            jnp.sum(attn_dh * xhat, axis=0),
            jnp.sum(attn_dh, axis=0),
            *ffn_sums,
            own_grad,
            g_bqkv_all.reshape(-1),
            g_bfc_all.reshape(-1),
        )
        flat = sum_everywhere(jnp.concatenate(rows_of).reshape(-1, 128)).reshape(-1)
        small_grads = []
        at = 0
        for entry in rows_of:
            size = entry.shape[0]
            small_grads.append(own_part(flat[at : at + size], size // n_fsdp))
            at += size
        d_gain_one, d_shift_one, d_gain_two, d_shift_two, d_bias, d_bqkv, d_bfc = small_grads
        branch_part = (attn_out + ffn_out).astype(bf16)
        pull_part = (attn_dh * gain_one + ffn_dh * gain_two).astype(bf16)
        d_proj = reduce_rows(g_proj.reshape(n_fsdp, -1, width), place, parts)
        d_fc = reduce_rows(g_fc.reshape(n_fsdp, rows_here, -1), place, parts)
        q_rows = jnp.swapaxes(g_qkv.reshape(3, n_fsdp, rows_here, inner), 0, 1)
        q_rows = jnp.swapaxes(q_rows, 1, 2).reshape(n_fsdp, rows_here, 3 * inner)
        d_qkv = reduce_rows(q_rows, place, parts)
        d_proj = jnp.swapaxes(d_proj, 0, 1).reshape(weight_proj.shape)
        d_fc = d_fc.reshape(rows_here, parts, n_fsdp, -1)
        d_fc = jnp.swapaxes(d_fc, 1, 2).reshape(weight_fc.shape)
        d_qkv = d_qkv.reshape(rows_here, parts, 3, n_h, -1)
        d_qkv = jnp.transpose(d_qkv, (0, 2, 3, 1, 4)).reshape(weight_qkv.shape)
        if spread_heads:
            d_out = reduce_rows(g_out.reshape(n_fsdp, -1, width), place, parts)
            d_out = jnp.swapaxes(d_out, 0, 1).reshape(weight_out.shape)
        else:
            full = jnp.zeros((parts, inner, width), bf16)
            full = lax.dynamic_update_index_in_dim(full, g_out, j, 0).reshape(width, width)
            d_out = lax.psum_scatter(full, "fsdp", scatter_dimension=0, tiled=True)
            d_out = lax.psum(d_out, ("dp", "ctx")).astype(f32)
        branch = return_blocks(branch_part, place, parts, seqs)
        pulled = return_blocks(pull_part, place, parts, seqs)

    features = residual_in.astype(f32)
    residual_out = (features + branch + (b_out + b_proj)).astype(bf16)
    own_hat, own_inverse = normalize(features)
    pulled = own_inverse * (
        pulled
        - jnp.mean(pulled, axis=-1, keepdims=True)
        - own_hat * jnp.mean(pulled * own_hat, axis=-1, keepdims=True)
    )
    own_pos = c * block_rows + jnp.arange(block_rows, dtype=jnp.int32)
    valid = (own_pos[None, :] < lengths[:, None])[..., None]
    residual_grad = (jnp.where(valid, cotangent.astype(f32), 0.0) + pulled).astype(bf16)
    return (
        residual_out,
        residual_grad,
        d_gain_one,
        d_shift_one,
        d_qkv,
        d_bqkv,
        d_out,
        d_bias,
        d_gain_two,
        d_shift_two,
        d_fc,
        d_bfc,
        d_proj,
        d_bias,
    )


def solution(mesh):
    tokens = P(("dp", "fsdp"), "ctx", None)
    vector, matrix = P("fsdp"), P("fsdp", None)
    return jax.shard_map(
        per_device,
        mesh=mesh,
        in_specs=(
            tokens,
            P(("dp", "fsdp")),
            vector,
            vector,
            matrix,
            vector,
            matrix,
            vector,
            vector,
            vector,
            matrix,
            vector,
            matrix,
            vector,
            tokens,
        ),
        out_specs=(
            tokens,
            tokens,
            vector,
            vector,
            matrix,
            vector,
            matrix,
            vector,
            vector,
            vector,
            matrix,
            vector,
            matrix,
            vector,
        ),
        check_vma=False,
    )
```

```python
import functools
import math

import jax
import jax.numpy as jnp
import numpy as np
from jax import lax
from jax.experimental import pallas as pl
from jax.experimental.pallas import tpu as pltpu
from jax.sharding import PartitionSpec as P

HEADS = 16
ROT = 16
LANES = 256
ROWS = 256

epsilon = 1e-05
rope_base = 10000.0
masked_score = -1e30

f32 = jnp.float32
bf16 = jnp.bfloat16


def dot_nn(a, b):
    return lax.dot_general(a, b, (((1,), (0,)), ((), ())), preferred_element_type=f32)


def dot_nt(a, b):
    return lax.dot_general(a, b, (((1,), (1,)), ((), ())), preferred_element_type=f32)


def attn_kernel(
    length_ref,
    h_ref,
    dy_ref,
    wq_ref,
    wk_ref,
    wv_ref,
    wo_ref,
    b_ref,
    rope_ref,
    out_ref,
    dh_ref,
    gqkv_ref,
    gout_ref,
    gb_ref,
    ht_s,
    q_s,
    k_s,
    v_s,
    do_s,
    kt_s,
    vt_s,
    dot_s,
    ot_s,
    dqt_s,
    dk_s,
    dv_s,
    p_s,
    kb_s,
):
    group = pl.program_id(0)
    total, width = h_ref.shape
    blocks = total // ROWS
    head_size = 64
    heads_here = LANES // head_size
    length = length_ref[0]

    @pl.when(group == 0)
    def _():
        for r in range(blocks):
            ht_s[:, r * ROWS : (r + 1) * ROWS] = h_ref[r * ROWS : (r + 1) * ROWS, :].T
        key_pos = lax.broadcasted_iota(jnp.int32, (total, 128), 0)
        kb_s[...] = jnp.where(key_pos < length, 0.0, masked_score)

    def turn(v, rows):
        left = pltpu.roll(v, LANES - ROT // 2, 1)
        right = pltpu.roll(v, ROT // 2, 1)
        return v * rope_ref[0, rows, :] + left * rope_ref[1, rows, :] + right * rope_ref[2, rows, :]

    def turn_back(v, rows):
        left = pltpu.roll(v, LANES - ROT // 2, 1)
        right = pltpu.roll(v, ROT // 2, 1)
        return v * rope_ref[0, rows, :] - left * rope_ref[1, rows, :] - right * rope_ref[2, rows, :]

    for r in range(blocks):
        rows = slice(r * ROWS, (r + 1) * ROWS)
        hr = h_ref[rows, :]
        q = turn(dot_nn(hr, wq_ref[...]) + b_ref[0, 0:1, :], rows).astype(bf16)
        q_s[rows, :] = (q.astype(f32) * 0.125).astype(bf16)
        k = turn(dot_nn(hr, wk_ref[...]) + b_ref[1, 0:1, :], rows).astype(bf16)
        k_s[rows, :] = k
        kt_s[:, rows] = k.T
        v = (dot_nn(hr, wv_ref[...]) + b_ref[2, 0:1, :]).astype(bf16)
        v_s[rows, :] = v
        vt_s[:, rows] = v.T
        do = dot_nt(dy_ref[rows, :], wo_ref[...]).astype(bf16)
        do_s[rows, :] = do
        dot_s[:, rows] = do.T

    dk_s[...] = jnp.zeros_like(dk_s)
    dv_s[...] = jnp.zeros_like(dv_s)
    lane = lax.broadcasted_iota(jnp.int32, (ROWS, LANES), 1)
    causal = lax.broadcasted_iota(jnp.int32, (ROWS, ROWS), 0) <= lax.broadcasted_iota(
        jnp.int32, (ROWS, ROWS), 1
    )

    def one_head(head, carry):
        feats = pl.ds(pl.multiple_of(head * head_size, head_size), head_size)
        mine = (lane // head_size) == head
        zero = jnp.zeros((ROWS, LANES), bf16)
        for i in range(blocks):
            rows = slice(i * ROWS, (i + 1) * ROWS)
            qm = jnp.where(mine, q_s[rows, :], zero)
            dom = jnp.where(mine, do_s[rows, :], zero)
            scores = []
            top = None
            for b in range(i + 1):
                keys = slice(b * ROWS, (b + 1) * ROWS)
                sc = dot_nt(k_s[keys, :], qm)
                kb = kb_s[keys, :]
                sc = sc + jnp.concatenate([kb, kb], axis=1)
                if b == i:
                    sc = jnp.where(causal, sc, masked_score)
                best = jnp.max(sc, axis=0, keepdims=True)
                top = best if top is None else jnp.maximum(top, best)
                scores.append(sc)
            row_sum = None
            for b in range(i + 1):
                scores[b] = jnp.exp(scores[b] - top)
                part = jnp.sum(scores[b], axis=0, keepdims=True)
                row_sum = part if row_sum is None else row_sum + part
            inverse = 1.0 / row_sum
            o_t = None
            for b in range(i + 1):
                keys = slice(b * ROWS, (b + 1) * ROWS)
                scores[b] = scores[b] * inverse
                low = scores[b].astype(bf16)
                dv_s[keys, :] += dot_nn(low, dom)
                part = dot_nn(vt_s[feats, keys], low)
                o_t = part if o_t is None else o_t + part
            ot_s[feats, rows] = o_t
            delta = jnp.sum(dot_s[feats, rows].astype(f32) * o_t, axis=0, keepdims=True)
            dq_t = None
            for b in range(i + 1):
                keys = slice(b * ROWS, (b + 1) * ROWS)
                dp = dot_nt(v_s[keys, :], dom)
                ds = (scores[b] * (dp - delta)).astype(bf16)
                dk_s[keys, :] += dot_nn(ds, qm)
                part = dot_nn(kt_s[feats, keys], ds)
                dq_t = part if dq_t is None else dq_t + part
            dqt_s[feats, rows] = dq_t * 0.125
        return carry

    lax.fori_loop(0, heads_here, one_head, 0)

    sums = [jnp.zeros((1, LANES), f32) for _ in range(3)]
    for r in range(blocks):
        rows = slice(r * ROWS, (r + 1) * ROWS)
        dq = turn_back(dqt_s[:, rows].T, rows).astype(bf16)
        dk = turn_back(dk_s[rows, :], rows).astype(bf16)
        dv = dv_s[rows, :].astype(bf16)
        for at, grad in enumerate((dq, dk, dv)):
            sums[at] = sums[at] + jnp.sum(grad.astype(f32), axis=0, keepdims=True)
            p_s[at, rows, :] = grad
        o = ot_s[:, rows].T.astype(bf16)
        out_part = dot_nn(o, wo_ref[...])
        dh_part = (
            dot_nt(dq, wq_ref[...]) + dot_nt(dk, wk_ref[...]) + dot_nt(dv, wv_ref[...])
        )

        @pl.when(group == 0)
        def _():
            out_ref[rows, :] = out_part
            dh_ref[rows, :] = dh_part

        @pl.when(group > 0)
        def _():
            out_ref[rows, :] += out_part
            dh_ref[rows, :] += dh_part

    for at in range(3):
        gb_ref[at] = jnp.broadcast_to(sums[at], (8, LANES))
        for r in range(width // ROWS):
            rows = slice(r * ROWS, (r + 1) * ROWS)
            gqkv_ref[at, rows, :] = dot_nn(ht_s[rows, :], p_s[at]).astype(bf16)
    gout_ref[...] = dot_nn(ot_s[...].astype(bf16), dy_ref[...]).astype(bf16)


def attention_branch(length, hidden, out_grad, w_qkv, w_out, b_qkv, rope):
    total, width = hidden.shape
    inner = w_out.shape[0]
    groups = inner // LANES
    whole = lambda g: (0, 0)
    flops = 2 * total * width * inner * 12 + 2 * groups * 4 * total * total * LANES * 4
    return pl.pallas_call(
        attn_kernel,
        grid=(groups,),
        in_specs=[
            pl.BlockSpec(memory_space=pltpu.SMEM),
            pl.BlockSpec((total, width), whole),
            pl.BlockSpec((total, width), whole),
            pl.BlockSpec((width, LANES), lambda g: (0, g)),
            pl.BlockSpec((width, LANES), lambda g: (0, groups + g)),
            pl.BlockSpec((width, LANES), lambda g: (0, 2 * groups + g)),
            pl.BlockSpec((LANES, width), lambda g: (g, 0)),
            pl.BlockSpec((3, 8, LANES), lambda g: (0, 0, g)),
            pl.BlockSpec((3, total, LANES), lambda g: (0, 0, 0)),
        ],
        out_specs=[
            pl.BlockSpec((total, width), whole),
            pl.BlockSpec((total, width), whole),
            pl.BlockSpec((3, width, LANES), lambda g: (0, 0, g)),
            pl.BlockSpec((LANES, width), lambda g: (g, 0)),
            pl.BlockSpec((3, 8, LANES), lambda g: (0, 0, g)),
        ],
        out_shape=[
            jax.ShapeDtypeStruct((total, width), f32),
            jax.ShapeDtypeStruct((total, width), f32),
            jax.ShapeDtypeStruct((3, width, inner), bf16),
            jax.ShapeDtypeStruct((inner, width), bf16),
            jax.ShapeDtypeStruct((3, 8, inner), f32),
        ],
        scratch_shapes=[
            pltpu.VMEM((width, total), bf16),
            pltpu.VMEM((total, LANES), bf16),
            pltpu.VMEM((total, LANES), bf16),
            pltpu.VMEM((total, LANES), bf16),
            pltpu.VMEM((total, LANES), bf16),
            pltpu.VMEM((LANES, total), bf16),
            pltpu.VMEM((LANES, total), bf16),
            pltpu.VMEM((LANES, total), bf16),
            pltpu.VMEM((LANES, total), f32),
            pltpu.VMEM((LANES, total), f32),
            pltpu.VMEM((total, LANES), f32),
            pltpu.VMEM((total, LANES), f32),
            pltpu.VMEM((3, total, LANES), bf16),
            pltpu.VMEM((total, 128), f32),
        ],
        compiler_params=pltpu.CompilerParams(vmem_limit_bytes=60 * 2**20),
        cost_estimate=pl.CostEstimate(
            flops=flops, bytes_accessed=24 * 2**20, transcendentals=8 * total * total
        ),
        name="attention",
    )(length, hidden, out_grad, w_qkv, w_qkv, w_qkv, w_out, b_qkv, rope)


def ffn_kernel(
    h_ref,
    dy_ref,
    wf_ref,
    wp_ref,
    b_ref,
    out_ref,
    dh_ref,
    gf_ref,
    gp_ref,
    gb_ref,
    ht_s,
    act_s,
    dup_s,
):
    step = pl.program_id(0)
    total, width = h_ref.shape
    blocks = total // ROWS
    chunk = wf_ref.shape[1]

    @pl.when(step == 0)
    def _():
        for r in range(blocks):
            ht_s[:, r * ROWS : (r + 1) * ROWS] = h_ref[r * ROWS : (r + 1) * ROWS, :].T

    def one(r, total_grad):
        rows = pl.ds(pl.multiple_of(r * ROWS, ROWS), ROWS)
        up = dot_nn(h_ref[rows, :], wf_ref[...]) + b_ref[0:1, :]
        half = 0.5 + 0.5 * lax.erf(up * (1.0 / math.sqrt(2.0)))
        act = (up * half).astype(bf16)
        slope = half + up * (jnp.exp(-0.5 * up * up) * (1.0 / math.sqrt(2.0 * math.pi)))
        act_grad = dot_nt(dy_ref[rows, :], wp_ref[...])
        up_grad = (slope * act_grad).astype(bf16)
        act_s[rows, :] = act
        dup_s[rows, :] = up_grad
        out_part = dot_nn(act, wp_ref[...])
        dh_part = dot_nt(up_grad, wf_ref[...])

        @pl.when(step == 0)
        def _():
            out_ref[rows, :] = out_part
            dh_ref[rows, :] = dh_part

        @pl.when(step > 0)
        def _():
            out_ref[rows, :] += out_part
            dh_ref[rows, :] += dh_part

        return total_grad + jnp.sum(up_grad.astype(f32), axis=0, keepdims=True)

    sums = lax.fori_loop(0, blocks, one, jnp.zeros((1, chunk), f32))
    gb_ref[...] = jnp.broadcast_to(sums, (8, chunk))
    for r in range(8):
        size = width // 8
        rows = slice(r * size, (r + 1) * size)
        grad = dot_nn(ht_s[rows, :], dup_s[...]).astype(bf16)
        gf_ref[rows, :] = grad
    for r in range(chunk // ROWS):
        cols = slice(r * ROWS, (r + 1) * ROWS)
        grad = dot_nn(act_s[:, cols].T, dy_ref[...]).astype(bf16)
        gp_ref[cols, :] = grad


def ffn_branch(hidden, out_grad, w_fc, w_proj, b_fc):
    total, width = hidden.shape
    units = w_proj.shape[0]
    chunk = min(512, units)
    whole = lambda s: (0, 0)
    return pl.pallas_call(
        ffn_kernel,
        grid=(units // chunk,),
        in_specs=[
            pl.BlockSpec((total, width), whole),
            pl.BlockSpec((total, width), whole),
            pl.BlockSpec((width, chunk), lambda s: (0, s)),
            pl.BlockSpec((chunk, width), lambda s: (s, 0)),
            pl.BlockSpec((8, chunk), lambda s: (0, s)),
        ],
        out_specs=[
            pl.BlockSpec((total, width), whole),
            pl.BlockSpec((total, width), whole),
            pl.BlockSpec((width, chunk), lambda s: (0, s)),
            pl.BlockSpec((chunk, width), lambda s: (s, 0)),
            pl.BlockSpec((8, chunk), lambda s: (0, s)),
        ],
        out_shape=[
            jax.ShapeDtypeStruct((total, width), f32),
            jax.ShapeDtypeStruct((total, width), f32),
            jax.ShapeDtypeStruct((width, units), bf16),
            jax.ShapeDtypeStruct((units, width), bf16),
            jax.ShapeDtypeStruct((8, units), f32),
        ],
        scratch_shapes=[
            pltpu.VMEM((width, total), bf16),
            pltpu.VMEM((total, chunk), bf16),
            pltpu.VMEM((total, chunk), bf16),
        ],
        compiler_params=pltpu.CompilerParams(vmem_limit_bytes=60 * 2**20),
        cost_estimate=pl.CostEstimate(
            flops=2 * total * width * units * 6,
            bytes_accessed=28 * 2**20,
            transcendentals=2 * total * units,
        ),
        name="feed_forward",
    )(hidden, out_grad, w_fc, w_proj, b_fc)


def shift(block, axis, distance):
    count = lax.axis_size(axis)
    return lax.ppermute(block, axis, [(i, (i + distance) % count) for i in range(count)])


def swap_bit(block, axis, bit):
    return lax.ppermute(block, axis, [(i, i ^ bit) for i in range(lax.axis_size(axis))])


def shift_within(block, axis, size, distance):
    count = lax.axis_size(axis)
    return lax.ppermute(
        block,
        axis,
        [(i, i // size * size + (i % size + distance) % size) for i in range(count)],
    )


def pick(array, index, axis=0):
    return lax.dynamic_index_in_dim(array, index, axis, keepdims=False)


def order_two(flag, mine, other):
    first = flag == 0
    return jnp.stack([jnp.where(first, mine, other), jnp.where(first, other, mine)])


def gather_rows(local, place):
    dp, y, core, f = place["dp"], place["y"], place["core"], place["f"]
    count = lax.axis_size("fsdp")
    rows, cols = local.shape
    share = rows // lax.axis_size("dp")
    mine = lax.dynamic_slice_in_dim(local, dp * share, share, 0)
    got = jnp.stack([shift(mine, "fsdp", e) for e in range(1, count)])
    got = order_two(y, got, swap_bit(got, "dp", 2))
    got = order_two(core, got, swap_bit(got, "dp", 1))
    got = jnp.transpose(got, (2, 1, 0, 3, 4)).reshape(count - 1, rows, cols)
    if count == 2:
        return order_two(f, local, got[0])
    whole = jnp.zeros((count, rows, cols), local.dtype)
    whole = lax.dynamic_update_index_in_dim(whole, local, f, 0)
    for e in range(1, count):
        whole = lax.dynamic_update_index_in_dim(whole, got[e - 1], (f - e) % count, 0)
    return whole


def reduce_rows(partial, place, parts):
    dp, y, core, f, j = (place[k] for k in ("dp", "y", "core", "f", "j"))
    count, rows, cols = partial.shape
    share = rows // 4
    a = partial.reshape(count, 2, 2, share, cols)
    a = pick(a, core, 2) + swap_bit(pick(a, 1 - core, 2), "dp", 1)
    total = pick(a, f)
    for e in range(1, count):
        total = total + shift(pick(a, (f + e) % count), "fsdp", e)
    total = pick(total, y) + swap_bit(pick(total, 1 - y), "dp", 2)
    total = total + shift(total, "ctx", parts)
    if parts == 2:
        both = order_two(j, total, shift_within(total, "ctx", 2, 1))
    else:
        both = jnp.zeros((parts,) + total.shape, total.dtype)
        both = lax.dynamic_update_index_in_dim(both, total, j, 0)
        for e in range(1, parts):
            got = shift_within(total, "ctx", parts, e)
            both = lax.dynamic_update_index_in_dim(both, got, (j - e) % parts, 0)
    both = order_two(y, both, swap_bit(both, "dp", 2))
    both = order_two(core, both, swap_bit(both, "dp", 1))
    return jnp.transpose(both, (1, 0, 3, 2, 4)).reshape(rows, parts, cols).astype(f32)


def sum_everywhere(vector):
    for bit in (1, 2):
        vector = vector + swap_bit(vector, "dp", bit)
    for axis in ("fsdp", "ctx"):
        bit = 1
        while bit < lax.axis_size(axis):
            vector = vector + swap_bit(vector, axis, bit)
            bit *= 2
    return vector


def gather_sequence(blocks, place, parts):
    s, c = place["s"], place["c"]
    count = lax.axis_size("ctx")
    seqs, rows, width = blocks.shape
    pieces = [(c, pick(blocks, s))]
    for d in range(1, seqs):
        got = shift(pick(blocks, (s + d) % seqs), "ctx", d * parts)
        pieces.append(((c - d * parts) % count, got))
    arrived = []
    for d in range(seqs):
        arrived.append(pieces[d])
        for e in range(1, parts):
            source = s * parts + (place["j"] - e) % parts
            got = shift_within(pieces[d][1], "ctx", parts, e)
            arrived.append(((source - d * parts) % count, got))
    whole = jnp.zeros((count, rows, width), blocks.dtype)
    for at, piece in arrived:
        whole = lax.dynamic_update_index_in_dim(whole, piece, at, 0)
    return whole.reshape(count * rows, width)


def return_blocks(partial, place, parts, seqs):
    s, c, j = place["s"], place["c"], place["j"]
    count = lax.axis_size("ctx")
    rows = partial.shape[0] // count
    blocks = partial.reshape(seqs, parts, rows, -1)
    total = pick(blocks, j, 1).astype(f32)
    for e in range(1, parts):
        total = total + shift_within(pick(blocks, (j + e) % parts, 1), "ctx", parts, e).astype(f32)
    mine = [pick(total, s)]
    for d in range(1, seqs):
        mine.append(shift(pick(total, (s + d) % seqs).astype(bf16), "ctx", d * parts).astype(f32))
    if seqs == 2:
        return order_two(s, mine[0], mine[1])
    whole = jnp.zeros((seqs, rows, partial.shape[1]), f32)
    for d in range(seqs):
        whole = lax.dynamic_update_index_in_dim(whole, mine[d], (s - d) % seqs, 0)
    return whole


class Mover:
    def __init__(self, send, recv, local):
        self.send, self.recv, self.local = send, recv, local
        self.copies, self.left, self.started = [], [], 0

    def to(self, src, dst, axis, index):
        copy = self.remote(src, dst, len(self.copies), (axis, index))
        copy.start()
        self.copies.append(copy)
        return copy

    def here(self, src, dst):
        copy = pltpu.make_async_copy(src, dst, self.local.at[self.started])
        self.started += 1
        copy.start()
        return copy

    def out(self, src, dst):
        self.left.append(self.here(src, dst))

    def remote(self, src, dst, slot, to):
        return pltpu.make_async_remote_copy(
            src_ref=src,
            dst_ref=dst,
            send_sem=self.send.at[slot],
            recv_sem=self.recv.at[slot],
            device_id={to[0]: to[1]},
            device_id_type=pl.DeviceIdType.MESH,
        )

    def stay(self, src, dst, slot):
        return pltpu.make_async_copy(src, dst, self.local.at[slot])

    def finish(self):
        for copy in self.copies:
            copy.wait_send()
        for copy in self.left:
            copy.wait()


class Spot:
    def __init__(self):
        self.dp, self.c, self.f = (lax.axis_index(a) for a in ("dp", "ctx", "fsdp"))
        self.y, self.core = self.dp // 2, self.dp % 2
        self.s, self.j = self.c // 2, self.c % 2
        flip = lambda v: v + 1 - 2 * (v % 2)
        self.x_to = ("fsdp", 1 - self.f)
        self.y_to = ("dp", (1 - self.y) * 2 + self.core)
        self.core_to = ("dp", flip(self.dp))
        self.pair_to = ("ctx", flip(self.c))
        self.far_to = ("ctx", (1 - self.s) * 2 + self.j)

    def greet(self):
        barrier = pltpu.get_barrier_semaphore()
        partners = (self.x_to, self.y_to, self.core_to, self.pair_to, self.far_to)
        for axis, index in partners:
            pl.semaphore_signal(
                barrier, inc=1, device_id={axis: index}, device_id_type=pl.DeviceIdType.MESH
            )
        pl.semaphore_wait(barrier, len(partners))


def block(index, size):
    return pl.ds(pl.multiple_of(index * size, size), size)


def front_kernel(
    info_ref,
    x_ref,
    cot_ref,
    fc_ref,
    proj_ref,
    qkv_ref,
    out_ref,
    small_ref,
    rope_ref,
    seq_in,
    seq_grad,
    w_qkv,
    w_out,
    pull,
    home,
    gp,
    gf,
    part,
    vectors,
    x_s,
    dy_s,
    cot_s,
    small_s,
    wf_s,
    wp_s,
    wq_s,
    wo_s,
    h_s,
    ht_s,
    act_s,
    dup_s,
    rope_s,
    q_s,
    k_s,
    vt_s,
    o_s,
    ot_s,
    kb_s,
    home_s,
    got_s,
    pull_s,
    gp_s,
    gf_s,
    core_got,
    x_got,
    vec_s,
    bfc_s,
    part_s,
    send,
    recv,
    local,
):
    at = Spot()
    mover = Mover(send, recv, local)
    total, width = x_s.shape
    blocks = total // ROWS
    units = wp_s.shape[0]
    inner = wo_s.shape[0]
    head_size = 64
    length = info_ref[2]
    other = 1 - at.f
    far_c, pair_c = at.far_to[1], at.pair_to[1]
    last_c = (1 - at.s) * 2 + 1 - at.j

    load_x = mover.here(x_ref.at[at.s], x_s.at[block(at.c, ROWS)])
    load_small = mover.here(small_ref, small_s.at[at.f])
    load_cot = mover.here(cot_ref, cot_s)
    load_rope = mover.here(rope_ref, rope_s)
    at.greet()

    small_copy = mover.to(small_ref, small_s.at[at.f], *at.x_to)
    x_far = mover.to(x_ref.at[1 - at.s], x_s.at[block(at.c, ROWS)], *at.far_to)
    x_near = mover.to(x_ref.at[at.s], x_s.at[block(at.c, ROWS)], *at.pair_to)

    def fc_spans(r):
        size = units // 2
        return [(fc_ref.at[r, block(2 * k + at.j, size)], pl.ds(k * size, size)) for k in range(2)]

    def qkv_spans(r):
        size = wq_s.shape[1] // 12
        return [
            (
                qkv_ref.at[r, block(t * 8 + h * 4 + at.j * 2 + g, size)],
                pl.ds((t * 4 + g * 2 + h) * size, size),
            )
            for t in range(3)
            for g in range(2)
            for h in range(2)
        ]

    def row_spans(ref, held):
        count = held.shape[0] // 2

        def spans(r):
            start = pl.multiple_of(at.j * count + r.start, r.size)
            return [(ref.at[pl.ds(start, r.size)], pl.ds(0, width))]

        return spans

    weights = dict(
        fc=(wf_s, fc_spans),
        proj=(wp_s, row_spans(proj_ref, wp_s)),
        qkv=(wq_s, qkv_spans),
        out=(wo_s, row_spans(out_ref, wo_s)),
    )
    got_x, got_y, got_core, stays = {}, {}, {}, {}

    def send_x(name):
        held, spans = weights[name]
        count = held.shape[0] // 2
        share = count // 4
        mine = pl.ds(pl.multiple_of(at.dp * share, share), share)
        there = pl.ds(pl.multiple_of(at.f * count + at.dp * share, share), share)
        got_x[name] = [mover.to(src, held.at[there, cols], *at.x_to) for src, cols in spans(mine)]

    def keep(name):
        held, spans = weights[name]
        count = held.shape[0] // 2
        there = block(at.f, count)
        stays[name] = [
            mover.here(src, held.at[there, cols]) for src, cols in spans(pl.ds(0, count))
        ]

    def quarter(name, dp):
        held = weights[name][0]
        count = held.shape[0] // 2
        share = count // 4
        return held.at[pl.ds(pl.multiple_of(other * count + dp * share, share), share)]

    def pass_x(name):
        for copy in got_x[name]:
            copy.wait_recv()
        mine = quarter(name, at.dp)
        got_y[name] = mover.to(mine, mine, *at.y_to)
        got_core[name] = [mover.to(mine, mine, *at.core_to)]

    def pass_y(name):
        got_y[name].wait_recv()
        mine = quarter(name, at.y_to[1])
        got_core[name].append(mover.to(mine, mine, *at.core_to))

    def arrived(name):
        for copy in got_core[name]:
            copy.wait_recv()
        for copy in stays[name]:
            copy.wait()

    send_x("fc")
    for name in weights:
        keep(name)

    load_small.wait()
    small_copy.wait_recv()

    def line(shard, r):
        return small_s[shard].astype(f32)[r : r + 1, :]

    def joined(r):
        return jnp.concatenate([line(0, r), line(1, r)], axis=1)

    first = at.j == 0
    vec_s[...] = jnp.zeros_like(vec_s)
    part_s[...] = jnp.zeros_like(part_s)
    size = LANES // 2
    for t in range(3):
        for h in range(2):
            row = line((t * 2 + h) // 3, 6 + (t * 2 + h) % 3)
            row = jnp.where(first, row[:, :LANES], row[:, LANES:])
            for g in range(2):
                to = g * LANES + h * size
                vec_s[t : t + 1, to : to + size] = row[:, g * size : (g + 1) * size]
    vec_s[3:4, :] = joined(0)
    vec_s[4:5, :] = joined(1)
    vec_s[5:6, :] = joined(4) + joined(5)
    for h in range(2):
        for n in range(2):
            to = h * units // 2 + n * 512
            bfc_s[0:1, to : to + 512] = jnp.where(first, line(h, 9 + n), line(h, 11 + n))
    gain_one, shift_one = vec_s[3:4, :], vec_s[4:5, :]
    gain_two, shift_two = joined(2), joined(3)
    bfc_s[1:2, :width] = gain_two
    mover.out(vec_s, vectors)

    def normal(rows):
        v = x_s[rows, :].astype(f32)
        center = v - jnp.mean(v, axis=-1, keepdims=True)
        spread = jnp.mean(center * center, axis=-1, keepdims=True)
        return center * lax.rsqrt(spread + epsilon)

    def arrive(c):
        rows = block(c, ROWS)
        h = (normal(rows) * gain_two + shift_two).astype(bf16)
        h_s[rows, :] = h
        ht_s[:, rows] = h.T

    load_x.wait()
    arrive(at.c)
    load_cot.wait()
    for t in range(2):
        pos = at.c * ROWS + lax.broadcasted_iota(jnp.int32, (ROWS, width), 0)
        cot_s[t] = jnp.where(pos < info_ref[t], cot_s[t].astype(f32), 0.0).astype(bf16)
    dy_s[block(at.c, ROWS), :] = cot_s[at.s]
    pass_x("fc")
    send_x("proj")
    x_far.wait_recv()
    mine = x_s.at[block(far_c, ROWS)]
    x_last = mover.to(mine, mine, *at.pair_to)
    grad_far = mover.to(cot_s.at[1 - at.s], dy_s.at[block(at.c, ROWS)], *at.far_to)
    arrive(far_c)
    x_near.wait_recv()
    arrive(pair_c)
    pass_x("proj")
    send_x("qkv")
    pass_y("fc")
    arrived("fc")

    def span(b):
        return slice(b * ROWS, (b + 1) * ROWS)

    chunk = 512

    def forward(c):
        rows = block(c, ROWS)

        def one(q, carry):
            cols = block(q, chunk)
            up = dot_nn(h_s[rows, :], wf_s[:, cols]) + bfc_s[0:1, cols]
            half = 0.5 + 0.5 * lax.erf(up * (1.0 / math.sqrt(2.0)))
            act_s[rows, cols] = (up * half).astype(bf16)
            slope = half + up * (jnp.exp(-0.5 * up * up) * (1.0 / math.sqrt(2.0 * math.pi)))
            dup_s[rows, cols] = slope.astype(bf16)
            return carry

        lax.fori_loop(0, units // chunk, one, 0)

    forward(at.c)
    forward(far_c)
    pass_x("qkv")
    send_x("out")
    x_last.wait_recv()
    arrive(last_c)
    grad_near = mover.to(cot_s.at[at.s], dy_s.at[block(at.c, ROWS)], *at.pair_to)
    pass_y("proj")
    forward(pair_c)
    pass_x("out")
    forward(last_c)
    pass_y("qkv")
    pass_y("out")
    grad_far.wait_recv()
    mine = dy_s.at[block(far_c, ROWS)]
    grad_last = mover.to(mine, mine, *at.pair_to)
    mover.out(x_s, seq_in)
    arrived("qkv")
    arrived("out")
    mover.out(wq_s, w_qkv)
    mover.out(wo_s, w_out)

    load_rope.wait()

    def table(n, rows):
        piece = rope_s[n, rows, :]
        return jnp.concatenate([piece] * (inner // 128), axis=1)

    def turned(v, rows):
        left = pltpu.roll(v, inner - ROT // 2, 1)
        right = pltpu.roll(v, ROT // 2, 1)
        return v * table(0, rows) + left * table(1, rows) + right * table(2, rows)

    for r in range(blocks):
        rows = span(r)
        h = (normal(rows) * gain_one + shift_one).astype(bf16)
        q = turned(dot_nn(h, wq_s[:, :inner]) + vec_s[0:1, :inner], rows).astype(bf16)
        q_s[rows, :] = (q.astype(f32) * 0.125).astype(bf16)
        k = dot_nn(h, wq_s[:, inner : 2 * inner]) + vec_s[1:2, :inner]
        k_s[rows, :] = turned(k, rows).astype(bf16)
        v = dot_nn(h, wq_s[:, 2 * inner :]) + vec_s[2:3, :inner]
        vt_s[:, rows] = v.astype(bf16).T
    key_pos = lax.broadcasted_iota(jnp.int32, (total, 128), 0)
    kb_s[...] = jnp.where(key_pos < length, 0.0, masked_score)
    lane = lax.broadcasted_iota(jnp.int32, (ROWS, LANES), 1)
    causal = lax.broadcasted_iota(jnp.int32, (ROWS, ROWS), 0) <= lax.broadcasted_iota(
        jnp.int32, (ROWS, ROWS), 1
    )

    def one_head(g, i, head, carry):
        feats = pl.ds(pl.multiple_of(head * head_size, head_size), head_size)
        from_v = pl.ds(pl.multiple_of(g * LANES + head * head_size, head_size), head_size)
        cols = slice(g * LANES, (g + 1) * LANES)
        mine = (lane // head_size) == head
        qm = jnp.where(mine, q_s[span(i), cols], jnp.zeros((ROWS, LANES), bf16))
        scores = []
        top = None
        for b in range(i + 1):
            sc = dot_nt(k_s[span(b), cols], qm)
            kb = kb_s[span(b), :]
            sc = sc + jnp.concatenate([kb, kb], axis=1)
            if b == i:
                sc = jnp.where(causal, sc, masked_score)
            best = jnp.max(sc, axis=0, keepdims=True)
            top = best if top is None else jnp.maximum(top, best)
            scores.append(sc)
        row_sum = None
        o_t = None
        for b in range(i + 1):
            e = jnp.exp(scores[b] - top)
            add = jnp.sum(e, axis=0, keepdims=True)
            row_sum = add if row_sum is None else row_sum + add
            add = dot_nn(vt_s[from_v, span(b)], e.astype(bf16))
            o_t = add if o_t is None else o_t + add
        ot_s[feats, :] = o_t / row_sum
        return carry

    for i in range(blocks):
        for g in range(2):
            lax.fori_loop(0, LANES // head_size, functools.partial(one_head, g, i), 0)
            if i == 0 and g == 0:
                arrived("proj")
            o = ot_s[...].T.astype(bf16)
            for h in range(2):
                to = h * LANES + g * size
                o_s[span(i), to : to + size] = o[:, h * size : (h + 1) * size]
        both = dot_nn(act_s[span(i), :], wp_s[...]) + dot_nn(o_s[span(i), :], wo_s[...])
        home_s[i] = both.astype(bf16)
    nears = [
        mover.to(home_s.at[2 * t + 1 - at.j], got_s.at[t], *at.pair_to) for t in range(2)
    ]

    grad_near.wait_recv()
    grad_last.wait_recv()
    mover.out(dy_s, seq_grad)
    bfc_s[2:3, :] = jnp.zeros((1, units), f32)
    for r in range(8):
        grad = dot_nn(act_s[:, r * ROWS : (r + 1) * ROWS].T, dy_s[...]).astype(bf16)
        for k in range(2):
            gp_s[k, r % 2, r // 4, r // 2 % 2] = grad[k * ROWS // 2 : (k + 1) * ROWS // 2]
    to_core = [mover.to(gp_s.at[k, 1 - at.core], core_got.at[k], *at.core_to) for k in range(2)]
    to_x = []

    def step_core(k):
        to_core[k].wait_recv()
        own, got = gp_s.at[k, at.core], core_got.at[k]
        own[1 - at.f] = own[1 - at.f] + got[1 - at.f]
        to_x.append(mover.to(own.at[1 - at.f], x_got.at[k], *at.x_to))
        own[at.f] = own[at.f] + got[at.f]

    def step_x(k):
        to_x[k].wait_recv()
        own = gp_s.at[k, at.core, at.f]
        own[...] = own[...] + x_got[k]
        mover.out(own, gp.at[k])

    gain_sum = jnp.zeros((1, width), f32)
    shift_sum = jnp.zeros((1, width), f32)
    dy_sum = jnp.zeros((1, width), f32)
    for i in range(blocks):
        rows = span(i)

        def one(q, carry):
            cols = block(q, chunk)
            act_grad = dot_nt(dy_s[rows, :], wp_s[cols, :])
            up_grad = (dup_s[rows, cols].astype(f32) * act_grad).astype(bf16)
            dup_s[rows, cols] = up_grad
            bfc_s[2:3, cols] += jnp.sum(up_grad.astype(f32), axis=0, keepdims=True)
            return carry

        lax.fori_loop(0, units // chunk, one, 0)
        dh = dot_nt(dup_s[rows, :], wf_s[...])
        pull_s[rows, :] = (dh * gain_two).astype(bf16)
        gain_sum = gain_sum + jnp.sum(dh * normal(rows), axis=0, keepdims=True)
        shift_sum = shift_sum + jnp.sum(dh, axis=0, keepdims=True)
        dy_sum = dy_sum + jnp.sum(dy_s[rows, :].astype(f32), axis=0, keepdims=True)
        if i == 0:
            step_core(0)
        if i == 3:
            step_x(0)
            step_core(1)
    mover.out(pull_s, pull)
    part_s[2:3, :width] = gain_sum
    part_s[3:4, :width] = shift_sum
    part_s[4:5, :width] = dy_sum * 0.5
    second = lax.broadcasted_iota(jnp.int32, (8, units), 0) == 1
    part_s[block(1 + at.j, 8), :] = jnp.where(second, bfc_s[2:3, :], 0.0)
    mover.out(part_s, part)
    rows_each = width // 8
    for k in range(2):
        for r in range(8):
            cols = slice(k * units // 2, (k + 1) * units // 2)
            grad = dot_nn(ht_s[r * rows_each : (r + 1) * rows_each, :], dup_s[:, cols])
            gf_s[k, r % 2, r // 4, r // 2 % 2] = grad.astype(bf16)
        mover.out(gf_s.at[k], gf.at[k])

    for t in range(2):
        nears[t].wait_recv()
        mine = home_s.at[2 * t + at.j]
        mine[...] = (mine[...].astype(f32) + got_s[t].astype(f32)).astype(bf16)
        mover.out(mine, home.at[t])
    step_x(1)
    mover.finish()


def front(info, x, cot, fc, proj, qkv, out, small, rope):
    seqs, rows, width = x.shape
    total = 4 * rows
    units = proj.shape[0]
    inner = out.shape[0]
    cell = (rows // 2, width)
    hbm = pl.BlockSpec(memory_space=pl.ANY)
    shape = lambda *dims: jax.ShapeDtypeStruct(dims, bf16)
    buf = lambda *dims: pltpu.VMEM(dims, bf16)
    wide = lambda *dims: pltpu.VMEM(dims, f32)
    return pl.pallas_call(
        front_kernel,
        in_specs=[pl.BlockSpec(memory_space=pltpu.SMEM)] + [hbm] * 8,
        out_specs=[hbm] * 10,
        out_shape=[
            shape(total, width),
            shape(total, width),
            shape(width, 3 * inner),
            shape(inner, width),
            shape(total, width),
            shape(2, rows, width),
            shape(2, 2, *cell),
            shape(2, 2, 2, 2, *cell),
            jax.ShapeDtypeStruct((24, units), f32),
            jax.ShapeDtypeStruct((8, width), f32),
        ],
        scratch_shapes=[
            buf(total, width),
            buf(total, width),
            buf(2, rows, width),
            buf(2, *small.shape),
            buf(width, units),
            buf(units, width),
            buf(width, 3 * inner),
            buf(inner, width),
            buf(total, width),
            buf(width, total),
            buf(total, units),
            buf(total, units),
            wide(*rope.shape),
            buf(total, inner),
            buf(total, inner),
            buf(inner, total),
            buf(total, inner),
            wide(LANES, ROWS),
            wide(total, 128),
            buf(4, rows, width),
            buf(2, rows, width),
            buf(total, width),
            buf(2, 2, 2, 2, *cell),
            buf(2, 2, 2, 2, *cell),
            buf(2, 2, 2, *cell),
            buf(2, 2, *cell),
            wide(8, width),
            wide(8, units),
            wide(24, units),
            pltpu.SemaphoreType.DMA((48,)),
            pltpu.SemaphoreType.DMA((48,)),
            pltpu.SemaphoreType.DMA((48,)),
        ],
        compiler_params=pltpu.CompilerParams(
            collective_id=0, has_side_effects=True, vmem_limit_bytes=62 * 2**20
        ),
        name="front",
    )(info, x, cot, fc, proj, qkv, out, small, rope)


def branch_kernel(
    length_ref,
    x_ref,
    dy_ref,
    wqkv_ref,
    wo_ref,
    bias_ref,
    rope_ref,
    out_ref,
    ffn_pull_ref,
    gp_ref,
    gf_ref,
    small_ref,
    summed,
    branch,
    pull,
    small,
    x_s,
    dy_s,
    h_s,
    ht_s,
    wqkv_s,
    wo_s,
    rope_s,
    q_s,
    k_s,
    v_s,
    do_s,
    kt_s,
    vt_s,
    dot_s,
    ot_s,
    dqt_s,
    dk_s,
    dv_s,
    dp_s,
    kb_s,
    begun_s,
    own_s,
    mine_s,
    core_s,
    x_got,
    y_got,
    far_got,
    home_s,
    home_got,
    out_s,
    small_s,
    small_got,
    send,
    recv,
    local,
):
    at = Spot()
    mover = Mover(send, recv, local)
    total, width = x_s.shape
    blocks = total // ROWS
    inner = wo_s.shape[0]
    head_size = 64
    length = length_ref[0]

    load_x = mover.here(x_ref, x_s)
    load_w = mover.here(wqkv_ref, wqkv_s)
    load_rope = mover.here(rope_ref, rope_s)
    load_dy = mover.here(dy_ref, dy_s)
    half = LANES // 2
    load_wo = [
        mover.here(
            wo_ref.at[pl.ds(h * LANES + g * half, half)],
            wo_s.at[pl.ds(g * LANES + h * half, half)],
        )
        for g in range(2)
        for h in range(2)
    ]
    load_small = mover.here(small_ref, small_s.at[0])
    load_out = mover.here(out_ref, out_s)
    at.greet()

    links = ("c", "x", "y", "z", "p", "yy", "c1", "c2")

    def own_of(n):
        return own_s.at[n - 2] if n < 4 else mine_s.at[n - 4, at.core]

    def cell(n, y):
        return begun_s.at[n, y] if n < 2 else own_of(n).at[at.f, y]

    def link(n, name):
        mine, other = summed.at[n, at.y, at.core], summed.at[n, 1 - at.y, at.core]
        if name == "c":
            src = (gf_ref.at[n - 2] if n < 4 else mine_s.at[n - 4]).at[1 - at.core]
            ends = (src, core_s.at[n - 2], at.core_to)
        elif name == "x":
            ends = (own_of(n).at[1 - at.f], x_got.at[n - 2], at.x_to)
        elif name == "y":
            ends = (cell(n, 1 - at.y), y_got.at[n], at.y_to)
        elif name == "z":
            ends = (cell(n, at.y), far_got.at[n], at.far_to)
        elif name == "p":
            ends = (y_got.at[n], summed.at[n, at.y, at.core, at.j], at.pair_to)
        elif name == "yy":
            ends = (mine, mine, at.y_to)
        elif name == "c1":
            ends = (mine, mine, at.core_to)
        else:
            ends = (other, other, at.core_to)
        return mover.remote(ends[0], ends[1], n * len(links) + links.index(name), ends[2])

    def load(n):
        if n < 2:
            return mover.stay(gp_ref.at[n], begun_s.at[n], 24 + n)
        return mover.stay(gf_ref.at[n - 2, at.core], own_s.at[n - 2], 24 + n)

    def keep(n):
        return mover.stay(y_got.at[n], summed.at[n, at.y, at.core, at.j], 28 + n)

    def step_start(n):
        if n < 4:
            load(n).start()
        link(n, "c").start()

    def step_core(n):
        if n < 4:
            load(n).wait()
        link(n, "c").wait_recv()
        own, got = own_of(n), core_s.at[n - 2]
        own[1 - at.f] = own[1 - at.f] + got[1 - at.f]
        link(n, "x").start()
        own[at.f] = own[at.f] + got[at.f]

    def step_x(n):
        link(n, "x").wait_recv()
        own, got = own_of(n), x_got.at[n - 2]
        own[at.f, 1 - at.y] = own[at.f, 1 - at.y] + got[1 - at.y]
        link(n, "y").start()
        own[at.f, at.y] = own[at.f, at.y] + got[at.y]

    def step_y(n):
        link(n, "y").wait_recv()
        mine = cell(n, at.y)
        mine[...] = mine[...] + y_got[n]
        link(n, "z").start()

    def step_far(n):
        link(n, "z").wait_recv()
        y_got[n] = cell(n, at.y)[...] + far_got[n]
        link(n, "p").start()
        keep(n).start()

    def step_pair(n):
        link(n, "p").wait_recv()
        keep(n).wait()
        link(n, "yy").start()
        link(n, "c1").start()

    def step_yy(n):
        link(n, "yy").wait_recv()
        link(n, "c2").start()

    base = 6 * len(links)

    def near(t):
        return mover.remote(home_s.at[2 * t + 1 - at.j], home_got.at[t], base + t, at.pair_to)

    def last(t):
        mine, dst = home_s.at[2 * t + at.j], pull.at[at.s]
        return mover.remote(mine, dst, base + 2, at.far_to), mover.stay(mine, dst, 34)

    def out_home():
        far = mover.remote(out_s.at[1 - at.s], branch.at[at.s], base + 3, at.far_to)
        return far, mover.stay(out_s.at[at.s], branch.at[at.s], 35)

    def home_near(t):
        near(t).start()

    def home_sum(t):
        near(t).wait_recv()
        mine = home_s.at[2 * t + at.j]
        mine[...] = (mine[...].astype(f32) + home_got[t].astype(f32)).astype(bf16)
        far, stay = last(t)
        pl.when(at.s == t)(stay.start)
        pl.when(at.s != t)(far.start)

    trips = (at.core_to, at.x_to, at.y_to, at.far_to, at.pair_to)

    def small_trip(n):
        return mover.remote(small_s.at[n], small_got.at[n], base + 4 + n, trips[n])

    def small_step(n):
        if n > 0:
            small_trip(n - 1).wait_recv()
            small_s[n] = small_s[n - 1] + small_got[n - 1]
        if n < 5:
            small_trip(n).start()
        else:
            mover.out(small_s.at[5], small)

    def end():
        for n in range(6):
            link(n, "c1").wait_recv()
            link(n, "c2").wait_recv()
            for name in links[2 if n < 2 else 0 :]:
                link(n, name).wait_send()
        for far, stay in (last(0), out_home()):
            far.wait()
            stay.wait()
        for t in range(2):
            near(t).wait_send()
        for n in range(5):
            small_trip(n).wait_send()

    acts = dict(
        start=step_start,
        core=step_core,
        x=step_x,
        y=step_y,
        far=step_far,
        pair=step_pair,
        yy=step_yy,
        near=home_near,
        sum=home_sum,
        small=small_step,
    )

    def turn(*place):
        for word in PLAN.get(",".join(str(v) for v in place), ()):
            name, n = word.split(":")
            acts[name](int(n))

    for n in range(2):
        load(n).start()
    for n in range(2, 4):
        step_start(n)
    for n in range(2):
        load(n).wait()
        link(n, "y").start()
    load_out.wait()
    for copy in out_home():
        copy.start()

    def normal(rows):
        v = x_s[rows, :].astype(f32)
        center = v - jnp.mean(v, axis=-1, keepdims=True)
        spread = jnp.mean(center * center, axis=-1, keepdims=True)
        return center * lax.rsqrt(spread + epsilon)

    def table(n, rows):
        part = rope_s[n, rows, :]
        return jnp.concatenate([part, part], axis=1)

    def turned(v, rows, sign):
        left = pltpu.roll(v, LANES - ROT // 2, 1)
        right = pltpu.roll(v, ROT // 2, 1)
        moved = left * table(1, rows) + right * table(2, rows)
        return v * table(0, rows) + moved if sign > 0 else v * table(0, rows) - moved

    key_pos = lax.broadcasted_iota(jnp.int32, (total, 128), 0)
    kb_s[...] = jnp.where(key_pos < length, 0.0, masked_score)
    lane = lax.broadcasted_iota(jnp.int32, (ROWS, LANES), 1)
    causal = lax.broadcasted_iota(jnp.int32, (ROWS, ROWS), 0) <= lax.broadcasted_iota(
        jnp.int32, (ROWS, ROWS), 1
    )
    gain, offset = bias_ref[3:4, :], bias_ref[4:5, :]

    def span(b):
        return slice(b * ROWS, (b + 1) * ROWS)

    def project(g):
        cols = lambda t: slice(t * inner + g * LANES, t * inner + (g + 1) * LANES)
        bias = lambda t: bias_ref[t : t + 1, g * LANES : (g + 1) * LANES]
        for r in range(blocks):
            rows = span(r)
            if g == 0:
                hr = (normal(rows) * gain + offset).astype(bf16)
                h_s[rows, :] = hr
                ht_s[:, rows] = hr.T
                if r == 0:
                    load_w.wait()
                    load_rope.wait()
                    load_dy.wait()
                    for copy in load_wo:
                        copy.wait()
            else:
                hr = h_s[rows, :]
            q = turned(dot_nn(hr, wqkv_s[:, cols(0)]) + bias(0), rows, 1).astype(bf16)
            q_s[rows, :] = (q.astype(f32) * 0.125).astype(bf16)
            k = turned(dot_nn(hr, wqkv_s[:, cols(1)]) + bias(1), rows, 1).astype(bf16)
            k_s[rows, :] = k
            kt_s[:, rows] = k.T
            v = (dot_nn(hr, wqkv_s[:, cols(2)]) + bias(2)).astype(bf16)
            v_s[rows, :] = v
            vt_s[:, rows] = v.T
            do = dot_nt(dy_s[rows, :], wo_s[g * LANES : (g + 1) * LANES, :]).astype(bf16)
            do_s[rows, :] = do
            dot_s[:, rows] = do.T
            turn("p%d" % g, r)
        dk_s[...] = jnp.zeros_like(dk_s)
        dv_s[...] = jnp.zeros_like(dv_s)

    def one_head(g, i, head, carry):
        feats = pl.ds(pl.multiple_of(head * head_size, head_size), head_size)
        mine = (lane // head_size) == head
        zero = jnp.zeros((ROWS, LANES), bf16)
        rows = span(i)
        qm = jnp.where(mine, q_s[rows, :], zero)
        dom = jnp.where(mine, do_s[rows, :], zero)
        scores = []
        top = None
        for b in range(i + 1):
            sc = dot_nt(k_s[span(b), :], qm)
            kb = kb_s[span(b), :]
            sc = sc + jnp.concatenate([kb, kb], axis=1)
            if b == i:
                sc = jnp.where(causal, sc, masked_score)
            best = jnp.max(sc, axis=0, keepdims=True)
            top = best if top is None else jnp.maximum(top, best)
            scores.append(sc)
        row_sum = None
        for b in range(i + 1):
            scores[b] = jnp.exp(scores[b] - top)
            part = jnp.sum(scores[b], axis=0, keepdims=True)
            row_sum = part if row_sum is None else row_sum + part
        inverse = 1.0 / row_sum
        o_t = None
        for b in range(i + 1):
            scores[b] = scores[b] * inverse
            low = scores[b].astype(bf16)
            dv_s[span(b), :] += dot_nn(low, dom)
            part = dot_nn(vt_s[feats, span(b)], low)
            o_t = part if o_t is None else o_t + part
        ot_s[feats, rows] = o_t
        delta = jnp.sum(dot_s[feats, rows].astype(f32) * o_t, axis=0, keepdims=True)
        dq_t = None
        for b in range(i + 1):
            dp = dot_nt(v_s[span(b), :], dom)
            ds = (scores[b] * (dp - delta)).astype(bf16)
            dk_s[span(b), :] += dot_nn(ds, qm)
            part = dot_nn(kt_s[feats, span(b)], ds)
            dq_t = part if dq_t is None else dq_t + part
        dqt_s[feats, rows] = dq_t * 0.125
        for h in range(LANES // head_size):
            if "%d,%d,%d" % (g, i, h) in PLAN:
                pl.when(head == h)(functools.partial(turn, g, i, h))
        return carry

    def finish_block(g, i, sums):
        rows = span(i)
        cols = slice(g * LANES, (g + 1) * LANES)
        dq = turned(dqt_s[:, rows].T, rows, -1).astype(bf16)
        dk = turned(dk_s[rows, :], rows, -1).astype(bf16)
        dv = dv_s[rows, :].astype(bf16)
        for t, grad in enumerate((dq, dk, dv)):
            sums[t] = sums[t] + jnp.sum(grad.astype(f32), axis=0, keepdims=True)
            dp_s[t, rows, cols] = grad

    def finish_rows(i, gain_sum, shift_sum):
        rows = span(i)
        dh = dot_nt(dp_s[0, rows, :], wqkv_s[:, :inner])
        dh = dh + dot_nt(dp_s[1, rows, :], wqkv_s[:, inner : 2 * inner])
        dh = dh + dot_nt(dp_s[2, rows, :], wqkv_s[:, 2 * inner :])
        home_s[i] = (dh * gain + home_s[i].astype(f32)).astype(bf16)
        gain_sum = gain_sum + jnp.sum(dh * normal(rows), axis=0, keepdims=True)
        return gain_sum, shift_sum + jnp.sum(dh, axis=0, keepdims=True)

    def weight_grads(g):
        cols = slice(g * LANES, (g + 1) * LANES)
        size = width // 8
        for t in range(3):
            for r in range(8):
                grad = dot_nn(ht_s[r * size : (r + 1) * size, :], dp_s[t, :, cols])
                mine_s[g, r % 2, r // 4, r // 2 % 2, :, t * LANES : (t + 1) * LANES] = grad.astype(bf16)
        grad = dot_nn(ot_s[...].astype(bf16), dy_s[...]).astype(bf16)
        size = LANES // 8
        for r in range(8):
            for b in range(4):
                mine_s[
                    g, r % 2, r // 4, r // 2 % 2, b * size : (b + 1) * size, 3 * LANES :
                ] = grad[r * size : (r + 1) * size, b * LANES : (b + 1) * LANES]

    load_x.wait()
    loads_home = [
        mover.here(ffn_pull_ref.at[block(b, ROWS)], home_s.at[b]) for b in range(blocks)
    ]
    load_small.wait()
    gain_sum = jnp.zeros((1, width), f32)
    shift_sum = jnp.zeros((1, width), f32)
    for g in range(2):
        project(g)
        sums = [jnp.zeros((1, LANES), f32) for _ in range(3)]
        for i in reversed(range(blocks)):
            lax.fori_loop(0, LANES // head_size, functools.partial(one_head, g, i), 0)
            finish_block(g, i, sums)
            if g == 1:
                if i == blocks - 1:
                    for copy in loads_home:
                        copy.wait()
                gain_sum, shift_sum = finish_rows(i, gain_sum, shift_sum)
            turn(g, i)
        weight_grads(g)
        line = pl.ds(pl.multiple_of(8 + at.j * 8, 8), 8)
        first_row = lax.broadcasted_iota(jnp.int32, (8, LANES), 0) == 0
        for t in range(3):
            cols = slice(t * inner + g * LANES, t * inner + (g + 1) * LANES)
            small_s[0, line, cols] = jnp.where(first_row, sums[t], small_s[0, line, cols])
        if g == 0:
            turn("grads")
    small_s[0, 0:1, :width] = gain_sum
    small_s[0, 1:2, :width] = shift_sum
    turn("tail")
    end()
    mover.finish()


PLAN = {
    "p0,0": ("core:2",),
    "0,3,0": ("y:0", "core:3",),
    "0,1,2": ("x:2",),
    "0,1,3": ("y:1", "far:0",),
    "0,0,2": ("x:3",),
    "p1,0": ("start:4",),
    "p1,2": ("y:2", "far:1",),
    "p1,3": ("pair:0",),
    "1,3,0": ("core:4",),
    "1,3,3": ("y:3", "far:2",),
    "1,2": ("yy:0", "near:1",),
    "1,1,0": ("x:4",),
    "1,0,0": ("y:4", "pair:2",),
    "tail": ("start:5", "core:5", "pair:1", "far:3", "sum:1", "x:5", "far:4", "yy:2", "small:0", "small:1", "small:2", "pair:3", "near:0", "y:5", "pair:4", "far:5", "small:3", "sum:0", "pair:5", "yy:1", "small:4", "yy:3", "yy:4", "yy:5", "small:5",),
}


def branch_and_sums(length, x, dy, w_qkv, w_out, bias, rope, out, ffn_pull, gp, gf, small):
    total, width = x.shape
    inner = w_out.shape[0]
    cell = (ROWS // 2, width)
    hbm = pl.BlockSpec(memory_space=pl.ANY)
    vmem = pl.BlockSpec(memory_space=pltpu.VMEM)
    home = jax.ShapeDtypeStruct((2, ROWS, width), bf16)
    buf = lambda dims, kind=bf16: pltpu.VMEM(tuple(dims), kind)
    return pl.pallas_call(
        branch_kernel,
        in_specs=[pl.BlockSpec(memory_space=pltpu.SMEM)] + [hbm] * 4 + [vmem] + [hbm] * 6,
        out_specs=[hbm] * 4,
        out_shape=[
            jax.ShapeDtypeStruct((6, 2, 2, 2) + cell, bf16),
            home,
            home,
            jax.ShapeDtypeStruct(small.shape, f32),
        ],
        scratch_shapes=[
            buf((total, width)),
            buf((total, width)),
            buf((total, width)),
            buf((width, total)),
            buf((width, 3 * inner)),
            buf((inner, width)),
            buf((3, total, 128), f32),
            buf((total, LANES)),
            buf((total, LANES)),
            buf((total, LANES)),
            buf((total, LANES)),
            buf((LANES, total)),
            buf((LANES, total)),
            buf((LANES, total)),
            buf((LANES, total), f32),
            buf((LANES, total), f32),
            buf((total, LANES), f32),
            buf((total, LANES), f32),
            buf((3, total, inner)),
            buf((total, 128), f32),
            buf((2, 2) + cell),
            buf((2, 2, 2) + cell),
            buf((2, 2, 2, 2) + cell),
            buf((4, 2, 2) + cell),
            buf((4, 2) + cell),
            buf((6,) + cell),
            buf((6,) + cell),
            buf((total // ROWS, ROWS, width)),
            buf((2, ROWS, width)),
            buf((2, ROWS, width)),
            buf((6,) + small.shape, f32),
            buf((5,) + small.shape, f32),
            pltpu.SemaphoreType.DMA((80,)),
            pltpu.SemaphoreType.DMA((80,)),
            pltpu.SemaphoreType.DMA((40,)),
        ],
        compiler_params=pltpu.CompilerParams(
            collective_id=1, has_side_effects=True, vmem_limit_bytes=62 * 2**20
        ),
        name="branch",
    )(length, x, dy, w_qkv, w_out, bias, rope, out, ffn_pull, gp, gf, small)


def widen_kernel(proj_ref, fc_ref, heads_ref, d_proj, d_fc, d_qkv, d_out):
    size, width = proj_ref.shape[4:]
    for p in range(2):
        d_proj[p, 0, 0, 0] = proj_ref[0, 0, 0, p].astype(f32)
        d_fc[:, p * width : (p + 1) * width] = fc_ref[0, 0, 0, p].astype(f32)
    second = pl.program_id(2)

    @pl.when(second == 0)
    def _():
        for g in range(2):
            for p in range(2):
                for t in range(3):
                    for h in range(2):
                        got = heads_ref[g, 0, 0, p, :, (t * 2 + h) * 128 : (t * 2 + h + 1) * 128]
                        to = t * 8 + h * 4 + p * 2 + g
                        d_qkv[:, to * 128 : (to + 1) * 128] = got.astype(f32)

    @pl.when(second == 1)
    def _():
        for g in range(2):
            for p in range(2):
                for b in range(4):
                    got = heads_ref[g, 0, 0, p, b * size // 4 : (b + 1) * size // 4, 3 * LANES :]
                    d_out[p, g, 0, 0, :, b * LANES : (b + 1) * LANES] = got.astype(f32)


def widen(summed, proj_shape, fc_shape, qkv_shape, out_shape):
    size, width = summed.shape[4:]
    shape = lambda *dims: jax.ShapeDtypeStruct(dims, f32)
    pair = (1, 1, 1, 2, size, width)
    d_proj, d_fc, d_qkv, d_out = pl.pallas_call(
        widen_kernel,
        grid=(2, 2, 2),
        in_specs=[
            pl.BlockSpec(pair, lambda y, c, k: (k, y, c, 0, 0, 0)),
            pl.BlockSpec(pair, lambda y, c, k: (2 + k, y, c, 0, 0, 0)),
            pl.BlockSpec((2, 1, 1, 2, size, width), lambda y, c, k: (2, y, c, 0, 0, 0)),
        ],
        out_specs=[
            pl.BlockSpec((2, 1, 1, 1, size, width), lambda y, c, k: (0, y, c, k, 0, 0)),
            pl.BlockSpec((size, 2 * width), lambda y, c, k: (y * 2 + c, k)),
            pl.BlockSpec((size, qkv_shape[1]), lambda y, c, k: (y * 2 + c, 0)),
            pl.BlockSpec((2, 2, 1, 1, size // 4, width), lambda y, c, k: (0, 0, y, c, 0, 0)),
        ],
        out_shape=[
            shape(2, 2, 2, 2, size, width),
            shape(*fc_shape),
            shape(*qkv_shape),
            shape(2, 2, 2, 2, size // 4, width),
        ],
        compiler_params=pltpu.CompilerParams(vmem_limit_bytes=40 * 2**20),
        name="widen",
    )(summed, summed, summed)
    return d_proj.reshape(proj_shape), d_fc, d_qkv, d_out.reshape(out_shape)


def normalize(features):
    center = features - jnp.mean(features, axis=-1, keepdims=True)
    spread = jnp.mean(center * center, axis=-1, keepdims=True)
    inverse = lax.rsqrt(spread + epsilon)
    return center * inverse, inverse


def rope_tables(total, head_size):
    half = ROT // 2
    inverse = (rope_base ** (-(2.0 * np.arange(half)) / ROT)).astype(np.float32)
    angles = np.arange(total, dtype=np.float32)[:, None] * inverse[None, :]
    cosine, sine = np.cos(angles), np.sin(angles)
    rest = np.zeros((total, head_size - ROT), np.float32)
    none = np.zeros((total, half), np.float32)
    same = np.concatenate([cosine, cosine, rest + 1.0], axis=1)
    ahead = np.concatenate([-sine, none, rest], axis=1)
    behind = np.concatenate([none, sine, rest], axis=1)
    return jnp.asarray(np.tile(np.stack([same, ahead, behind]), (1, 1, 128 // head_size)), f32)


def pack_rows(vectors, width):
    packed, at = 0.0, 0
    for vector in vectors:
        rows = vector.astype(f32).reshape(-1, width)
        packed = packed + jnp.pad(rows, ((at, 16 - at - rows.shape[0]), (0, 0)))
        at += rows.shape[0]
    return packed.astype(bf16)


def finish(residual_in, cotangent, lengths, start, branch, pulled, bias):
    features = residual_in.astype(f32)
    residual_out = (features + branch + bias).astype(bf16)
    own_hat, own_inverse = normalize(features)
    pulled = own_inverse * (
        pulled
        - jnp.mean(pulled, axis=-1, keepdims=True)
        - own_hat * jnp.mean(pulled * own_hat, axis=-1, keepdims=True)
    )
    own_pos = start + jnp.arange(residual_in.shape[1], dtype=jnp.int32)
    valid = (own_pos[None, :] < lengths[:, None])[..., None]
    residual_grad = (jnp.where(valid, cotangent.astype(f32), 0.0) + pulled).astype(bf16)
    return residual_out, residual_grad


def fast_block(residual_in, lengths, cotangent, info, weights, packed, rope, own_part):
    weight_fc, weight_proj, weight_qkv, weight_out = weights
    width = residual_in.shape[2]
    units = weight_fc.shape[1]
    inner = weight_out.shape[0]
    seq_in, seq_grad, w_qkv, w_out, pull, home, gp, gf, part, vectors = front(
        info, residual_in, cotangent, *weights, packed, rope
    )
    summed, branch, pulled, sums = branch_and_sums(
        info[2:], seq_in, seq_grad, w_qkv, w_out, vectors, rope, home, pull, gp, gf, part
    )
    d_proj, d_fc, d_qkv, d_out = widen(
        summed, weight_proj.shape, weight_fc.shape, weight_qkv.shape, weight_out.shape
    )
    d_gain_one, d_shift_one, d_gain_two, d_shift_two, d_bias = (
        own_part(sums[i, :width]) for i in range(5)
    )
    d_bqkv = sums[8::8, : 3 * inner].reshape(2, 3, 2, 2, -1)
    d_bqkv = own_part(jnp.transpose(d_bqkv, (1, 3, 0, 2, 4)).reshape(-1), 3 * width // 2)
    d_bfc = jnp.swapaxes(sums[9::8].reshape(2, 2, -1), 0, 1).reshape(-1)
    d_bfc = own_part(d_bfc, units // 2)
    residual_out, residual_grad = finish(
        residual_in,
        cotangent,
        lengths,
        lax.axis_index("ctx") * residual_in.shape[1],
        branch.astype(f32),
        pulled.astype(f32),
        vectors[5],
    )
    return (
        residual_out,
        residual_grad,
        d_gain_one,
        d_shift_one,
        d_qkv,
        d_bqkv,
        d_out,
        d_bias,
        d_gain_two,
        d_shift_two,
        d_fc,
        d_bfc,
        d_proj,
        d_bias,
    )


def per_device(
    residual_in,
    lengths,
    gain_attn,
    shift_attn,
    weight_qkv,
    bias_qkv,
    weight_out,
    bias_out,
    gain_ffn,
    shift_ffn,
    weight_fc,
    bias_fc,
    weight_proj,
    bias_proj,
    cotangent,
):
    seqs, block_rows, width = residual_in.shape
    n_ctx, n_fsdp = lax.axis_size("ctx"), lax.axis_size("fsdp")
    parts = n_ctx // seqs
    total = n_ctx * block_rows
    units = weight_fc.shape[1]
    head_size = width // HEADS
    c, f, dp = lax.axis_index("ctx"), lax.axis_index("fsdp"), lax.axis_index("dp")
    s, j = c // parts, c % parts
    place = dict(c=c, f=f, dp=dp, s=s, j=j, y=dp // 2, core=dp % 2)
    spread_heads = HEADS % (n_fsdp * parts) == 0
    n_h = n_fsdp if spread_heads else 1
    inner = width // parts

    rows_here = weight_qkv.shape[0]
    own_heads = lambda v: pick(v.reshape(3, n_h, parts, -1), j, 2)
    fast = (seqs, n_ctx, n_fsdp, lax.axis_size("dp")) == (2, 4, 2, 4)
    small_local = jnp.concatenate(
        [gain_attn, shift_attn, gain_ffn, shift_ffn, bias_out, bias_proj, bias_qkv, bias_fc]
    )
    part_width = width // n_fsdp
    length = pick(lengths, s)
    rope = rope_tables(total, head_size)
    own_part = lambda v, size=part_width: lax.dynamic_slice_in_dim(v, f * size, size)
    if fast:
        return fast_block(
            residual_in,
            lengths,
            cotangent,
            jnp.concatenate([lengths, length[None]]),
            (weight_fc, weight_proj, weight_qkv, weight_out),
            pack_rows(
                (gain_attn, shift_attn, gain_ffn, shift_ffn, bias_out, bias_proj, bias_qkv, bias_fc),
                part_width,
            ),
            rope,
            own_part,
        )
    small = lax.all_gather(small_local, "fsdp", axis=0)
    vec = lambda at, size: small[:, at : at + size].reshape(-1).astype(f32)
    gain_one, shift_one, gain_two, shift_two, b_out, b_proj = (
        vec(i * part_width, part_width) for i in range(6)
    )
    b_qkv = vec(6 * part_width, 3 * part_width)
    b_fc = vec(9 * part_width, units // n_fsdp)

    fc_local = pick(weight_fc.reshape(rows_here, n_fsdp, parts, -1), j, 2).reshape(rows_here, -1)
    proj_local = pick(weight_proj.reshape(parts, -1, width), j)
    qkv_local = pick(weight_qkv.reshape(rows_here, 3, n_h, parts, -1), j, 3).reshape(rows_here, -1)
    seq_in = gather_sequence(residual_in, place, parts)
    w_fc = gather_rows(fc_local, place).reshape(width, -1)
    w_proj = gather_rows(proj_local, place).reshape(-1, width)
    seq_grad = gather_sequence(cotangent, place, parts)
    w_qkv = gather_rows(qkv_local, place).reshape(width, -1)
    if spread_heads:
        w_out = gather_rows(pick(weight_out.reshape(parts, -1, width), j), place).reshape(-1, width)
    else:
        w_out = lax.all_gather(weight_out, "fsdp", axis=0, tiled=True)
        w_out = pick(w_out.reshape(parts, -1, width), j)
    b_qkv_j = own_heads(b_qkv).reshape(3, 1, inner)
    b_fc_j = pick(b_fc.reshape(n_fsdp, parts, -1), j, 1).reshape(1, -1)
    b_fc_j = jnp.broadcast_to(b_fc_j, (8, b_fc_j.shape[1]))

    positions = jnp.arange(total, dtype=jnp.int32)
    seq_grad = jnp.where((positions < length)[:, None], seq_grad, jnp.zeros((), bf16))
    xhat, _ = normalize(seq_in.astype(f32))
    hidden_one = (xhat * gain_one + shift_one).astype(bf16)
    hidden_two = (xhat * gain_two + shift_two).astype(bf16)

    ffn_out, ffn_dh, g_fc, g_proj, g_bfc = ffn_branch(
        hidden_two, seq_grad, w_fc, w_proj, b_fc_j
    )
    ffn_sums = (jnp.sum(ffn_dh * xhat, axis=0), jnp.sum(ffn_dh, axis=0))
    own_grad = jnp.sum(seq_grad.astype(f32), axis=0) / parts
    attn_out, attn_dh, g_qkv, g_out, g_bqkv = attention_branch(
        length[None],
        hidden_one,
        seq_grad,
        w_qkv,
        w_out,
        jnp.broadcast_to(b_qkv_j, (3, 8, inner)),
        jnp.tile(rope, (1, 1, LANES // 128)),
    )
    g_bqkv_all = jnp.zeros((3, n_h, parts, inner // n_h), f32)
    g_bqkv_all = lax.dynamic_update_index_in_dim(
        g_bqkv_all, g_bqkv[:, 0].reshape(3, n_h, -1), j, 2
    )
    g_bfc_all = jnp.zeros((n_fsdp, parts, units // (n_fsdp * parts)), f32)
    g_bfc_all = lax.dynamic_update_index_in_dim(g_bfc_all, g_bfc[0].reshape(n_fsdp, -1), j, 1)
    rows_of = (
        jnp.sum(attn_dh * xhat, axis=0),
        jnp.sum(attn_dh, axis=0),
        *ffn_sums,
        own_grad,
        g_bqkv_all.reshape(-1),
        g_bfc_all.reshape(-1),
    )
    flat = sum_everywhere(jnp.concatenate(rows_of).reshape(-1, 128)).reshape(-1)
    small_grads = []
    at = 0
    for entry in rows_of:
        size = entry.shape[0]
        small_grads.append(own_part(flat[at : at + size], size // n_fsdp))
        at += size
    d_gain_one, d_shift_one, d_gain_two, d_shift_two, d_bias, d_bqkv, d_bfc = small_grads
    branch_part = (attn_out + ffn_out).astype(bf16)
    pull_part = (attn_dh * gain_one + ffn_dh * gain_two).astype(bf16)
    d_proj = reduce_rows(g_proj.reshape(n_fsdp, -1, width), place, parts)
    d_fc = reduce_rows(g_fc.reshape(n_fsdp, rows_here, -1), place, parts)
    q_rows = jnp.swapaxes(g_qkv.reshape(3, n_fsdp, rows_here, inner), 0, 1)
    q_rows = jnp.swapaxes(q_rows, 1, 2).reshape(n_fsdp, rows_here, 3 * inner)
    d_qkv = reduce_rows(q_rows, place, parts)
    d_proj = jnp.swapaxes(d_proj, 0, 1).reshape(weight_proj.shape)
    d_fc = d_fc.reshape(rows_here, parts, n_fsdp, -1)
    d_fc = jnp.swapaxes(d_fc, 1, 2).reshape(weight_fc.shape)
    d_qkv = d_qkv.reshape(rows_here, parts, 3, n_h, -1)
    d_qkv = jnp.transpose(d_qkv, (0, 2, 3, 1, 4)).reshape(weight_qkv.shape)
    if spread_heads:
        d_out = reduce_rows(g_out.reshape(n_fsdp, -1, width), place, parts)
        d_out = jnp.swapaxes(d_out, 0, 1).reshape(weight_out.shape)
    else:
        full = jnp.zeros((parts, inner, width), bf16)
        full = lax.dynamic_update_index_in_dim(full, g_out, j, 0).reshape(width, width)
        d_out = lax.psum_scatter(full, "fsdp", scatter_dimension=0, tiled=True)
        d_out = lax.psum(d_out, ("dp", "ctx")).astype(f32)
    branch = return_blocks(branch_part, place, parts, seqs)
    pulled = return_blocks(pull_part, place, parts, seqs)

    residual_out, residual_grad = finish(
        residual_in, cotangent, lengths, c * block_rows, branch, pulled, b_out + b_proj
    )
    return (
        residual_out,
        residual_grad,
        d_gain_one,
        d_shift_one,
        d_qkv,
        d_bqkv,
        d_out,
        d_bias,
        d_gain_two,
        d_shift_two,
        d_fc,
        d_bfc,
        d_proj,
        d_bias,
    )


def solution(mesh):
    tokens = P(("dp", "fsdp"), "ctx", None)
    vector, matrix = P("fsdp"), P("fsdp", None)
    return jax.shard_map(
        per_device,
        mesh=mesh,
        in_specs=(
            tokens,
            P(("dp", "fsdp")),
            vector,
            vector,
            matrix,
            vector,
            matrix,
            vector,
            vector,
            vector,
            matrix,
            vector,
            matrix,
            vector,
            tokens,
        ),
        out_specs=(
            tokens,
            tokens,
            vector,
            vector,
            matrix,
            vector,
            matrix,
            vector,
            vector,
            vector,
            matrix,
            vector,
            matrix,
            vector,
        ),
        check_vma=False,
    )
```

```python
import functools
import math

import jax
import jax.numpy as jnp
import numpy as np
from jax import lax
from jax.experimental import pallas as pl
from jax.experimental.pallas import tpu as pltpu
from jax.sharding import PartitionSpec as P

HEADS = 16
ROT = 16
LANES = 256
ROWS = 256

epsilon = 1e-05
rope_base = 10000.0
masked_score = -1e30

f32 = jnp.float32
bf16 = jnp.bfloat16


def dot_nn(a, b):
    return lax.dot_general(a, b, (((1,), (0,)), ((), ())), preferred_element_type=f32)


def dot_nt(a, b):
    return lax.dot_general(a, b, (((1,), (1,)), ((), ())), preferred_element_type=f32)


def attn_kernel(
    length_ref,
    h_ref,
    dy_ref,
    wq_ref,
    wk_ref,
    wv_ref,
    wo_ref,
    b_ref,
    rope_ref,
    out_ref,
    dh_ref,
    gqkv_ref,
    gout_ref,
    gb_ref,
    ht_s,
    q_s,
    k_s,
    v_s,
    do_s,
    kt_s,
    vt_s,
    dot_s,
    ot_s,
    dqt_s,
    dk_s,
    dv_s,
    p_s,
    kb_s,
):
    group = pl.program_id(0)
    total, width = h_ref.shape
    blocks = total // ROWS
    head_size = 64
    heads_here = LANES // head_size
    length = length_ref[0]

    @pl.when(group == 0)
    def _():
        for r in range(blocks):
            ht_s[:, r * ROWS : (r + 1) * ROWS] = h_ref[r * ROWS : (r + 1) * ROWS, :].T
        key_pos = lax.broadcasted_iota(jnp.int32, (total, 128), 0)
        kb_s[...] = jnp.where(key_pos < length, 0.0, masked_score)

    def turn(v, rows):
        left = pltpu.roll(v, LANES - ROT // 2, 1)
        right = pltpu.roll(v, ROT // 2, 1)
        return v * rope_ref[0, rows, :] + left * rope_ref[1, rows, :] + right * rope_ref[2, rows, :]

    def turn_back(v, rows):
        left = pltpu.roll(v, LANES - ROT // 2, 1)
        right = pltpu.roll(v, ROT // 2, 1)
        return v * rope_ref[0, rows, :] - left * rope_ref[1, rows, :] - right * rope_ref[2, rows, :]

    for r in range(blocks):
        rows = slice(r * ROWS, (r + 1) * ROWS)
        hr = h_ref[rows, :]
        q = turn(dot_nn(hr, wq_ref[...]) + b_ref[0, 0:1, :], rows).astype(bf16)
        q_s[rows, :] = (q.astype(f32) * 0.125).astype(bf16)
        k = turn(dot_nn(hr, wk_ref[...]) + b_ref[1, 0:1, :], rows).astype(bf16)
        k_s[rows, :] = k
        kt_s[:, rows] = k.T
        v = (dot_nn(hr, wv_ref[...]) + b_ref[2, 0:1, :]).astype(bf16)
        v_s[rows, :] = v
        vt_s[:, rows] = v.T
        do = dot_nt(dy_ref[rows, :], wo_ref[...]).astype(bf16)
        do_s[rows, :] = do
        dot_s[:, rows] = do.T

    dk_s[...] = jnp.zeros_like(dk_s)
    dv_s[...] = jnp.zeros_like(dv_s)
    lane = lax.broadcasted_iota(jnp.int32, (ROWS, LANES), 1)
    causal = lax.broadcasted_iota(jnp.int32, (ROWS, ROWS), 0) <= lax.broadcasted_iota(
        jnp.int32, (ROWS, ROWS), 1
    )

    def one_head(head, carry):
        feats = pl.ds(pl.multiple_of(head * head_size, head_size), head_size)
        mine = (lane // head_size) == head
        zero = jnp.zeros((ROWS, LANES), bf16)
        for i in range(blocks):
            rows = slice(i * ROWS, (i + 1) * ROWS)
            qm = jnp.where(mine, q_s[rows, :], zero)
            dom = jnp.where(mine, do_s[rows, :], zero)
            scores = []
            top = None
            for b in range(i + 1):
                keys = slice(b * ROWS, (b + 1) * ROWS)
                sc = dot_nt(k_s[keys, :], qm)
                kb = kb_s[keys, :]
                sc = sc + jnp.concatenate([kb, kb], axis=1)
                if b == i:
                    sc = jnp.where(causal, sc, masked_score)
                best = jnp.max(sc, axis=0, keepdims=True)
                top = best if top is None else jnp.maximum(top, best)
                scores.append(sc)
            row_sum = None
            for b in range(i + 1):
                scores[b] = jnp.exp(scores[b] - top)
                part = jnp.sum(scores[b], axis=0, keepdims=True)
                row_sum = part if row_sum is None else row_sum + part
            inverse = 1.0 / row_sum
            o_t = None
            for b in range(i + 1):
                keys = slice(b * ROWS, (b + 1) * ROWS)
                scores[b] = scores[b] * inverse
                low = scores[b].astype(bf16)
                dv_s[keys, :] += dot_nn(low, dom)
                part = dot_nn(vt_s[feats, keys], low)
                o_t = part if o_t is None else o_t + part
            ot_s[feats, rows] = o_t
            delta = jnp.sum(dot_s[feats, rows].astype(f32) * o_t, axis=0, keepdims=True)
            dq_t = None
            for b in range(i + 1):
                keys = slice(b * ROWS, (b + 1) * ROWS)
                dp = dot_nt(v_s[keys, :], dom)
                ds = (scores[b] * (dp - delta)).astype(bf16)
                dk_s[keys, :] += dot_nn(ds, qm)
                part = dot_nn(kt_s[feats, keys], ds)
                dq_t = part if dq_t is None else dq_t + part
            dqt_s[feats, rows] = dq_t * 0.125
        return carry

    lax.fori_loop(0, heads_here, one_head, 0)

    sums = [jnp.zeros((1, LANES), f32) for _ in range(3)]
    for r in range(blocks):
        rows = slice(r * ROWS, (r + 1) * ROWS)
        dq = turn_back(dqt_s[:, rows].T, rows).astype(bf16)
        dk = turn_back(dk_s[rows, :], rows).astype(bf16)
        dv = dv_s[rows, :].astype(bf16)
        for at, grad in enumerate((dq, dk, dv)):
            sums[at] = sums[at] + jnp.sum(grad.astype(f32), axis=0, keepdims=True)
            p_s[at, rows, :] = grad
        o = ot_s[:, rows].T.astype(bf16)
        out_part = dot_nn(o, wo_ref[...])
        dh_part = (
            dot_nt(dq, wq_ref[...]) + dot_nt(dk, wk_ref[...]) + dot_nt(dv, wv_ref[...])
        )

        @pl.when(group == 0)
        def _():
            out_ref[rows, :] = out_part
            dh_ref[rows, :] = dh_part

        @pl.when(group > 0)
        def _():
            out_ref[rows, :] += out_part
            dh_ref[rows, :] += dh_part

    for at in range(3):
        gb_ref[at] = jnp.broadcast_to(sums[at], (8, LANES))
        for r in range(width // ROWS):
            rows = slice(r * ROWS, (r + 1) * ROWS)
            gqkv_ref[at, rows, :] = dot_nn(ht_s[rows, :], p_s[at]).astype(bf16)
    gout_ref[...] = dot_nn(ot_s[...].astype(bf16), dy_ref[...]).astype(bf16)


def attention_branch(length, hidden, out_grad, w_qkv, w_out, b_qkv, rope):
    total, width = hidden.shape
    inner = w_out.shape[0]
    groups = inner // LANES
    whole = lambda g: (0, 0)
    flops = 2 * total * width * inner * 12 + 2 * groups * 4 * total * total * LANES * 4
    return pl.pallas_call(
        attn_kernel,
        grid=(groups,),
        in_specs=[
            pl.BlockSpec(memory_space=pltpu.SMEM),
            pl.BlockSpec((total, width), whole),
            pl.BlockSpec((total, width), whole),
            pl.BlockSpec((width, LANES), lambda g: (0, g)),
            pl.BlockSpec((width, LANES), lambda g: (0, groups + g)),
            pl.BlockSpec((width, LANES), lambda g: (0, 2 * groups + g)),
            pl.BlockSpec((LANES, width), lambda g: (g, 0)),
            pl.BlockSpec((3, 8, LANES), lambda g: (0, 0, g)),
            pl.BlockSpec((3, total, LANES), lambda g: (0, 0, 0)),
        ],
        out_specs=[
            pl.BlockSpec((total, width), whole),
            pl.BlockSpec((total, width), whole),
            pl.BlockSpec((3, width, LANES), lambda g: (0, 0, g)),
            pl.BlockSpec((LANES, width), lambda g: (g, 0)),
            pl.BlockSpec((3, 8, LANES), lambda g: (0, 0, g)),
        ],
        out_shape=[
            jax.ShapeDtypeStruct((total, width), f32),
            jax.ShapeDtypeStruct((total, width), f32),
            jax.ShapeDtypeStruct((3, width, inner), bf16),
            jax.ShapeDtypeStruct((inner, width), bf16),
            jax.ShapeDtypeStruct((3, 8, inner), f32),
        ],
        scratch_shapes=[
            pltpu.VMEM((width, total), bf16),
            pltpu.VMEM((total, LANES), bf16),
            pltpu.VMEM((total, LANES), bf16),
            pltpu.VMEM((total, LANES), bf16),
            pltpu.VMEM((total, LANES), bf16),
            pltpu.VMEM((LANES, total), bf16),
            pltpu.VMEM((LANES, total), bf16),
            pltpu.VMEM((LANES, total), bf16),
            pltpu.VMEM((LANES, total), f32),
            pltpu.VMEM((LANES, total), f32),
            pltpu.VMEM((total, LANES), f32),
            pltpu.VMEM((total, LANES), f32),
            pltpu.VMEM((3, total, LANES), bf16),
            pltpu.VMEM((total, 128), f32),
        ],
        compiler_params=pltpu.CompilerParams(vmem_limit_bytes=60 * 2**20),
        cost_estimate=pl.CostEstimate(
            flops=flops, bytes_accessed=24 * 2**20, transcendentals=8 * total * total
        ),
        name="attention",
    )(length, hidden, out_grad, w_qkv, w_qkv, w_qkv, w_out, b_qkv, rope)


def ffn_kernel(
    h_ref,
    dy_ref,
    wf_ref,
    wp_ref,
    b_ref,
    out_ref,
    dh_ref,
    gf_ref,
    gp_ref,
    gb_ref,
    ht_s,
    act_s,
    dup_s,
):
    step = pl.program_id(0)
    total, width = h_ref.shape
    blocks = total // ROWS
    chunk = wf_ref.shape[1]

    @pl.when(step == 0)
    def _():
        for r in range(blocks):
            ht_s[:, r * ROWS : (r + 1) * ROWS] = h_ref[r * ROWS : (r + 1) * ROWS, :].T

    def one(r, total_grad):
        rows = pl.ds(pl.multiple_of(r * ROWS, ROWS), ROWS)
        up = dot_nn(h_ref[rows, :], wf_ref[...]) + b_ref[0:1, :]
        half = 0.5 + 0.5 * lax.erf(up * (1.0 / math.sqrt(2.0)))
        act = (up * half).astype(bf16)
        slope = half + up * (jnp.exp(-0.5 * up * up) * (1.0 / math.sqrt(2.0 * math.pi)))
        act_grad = dot_nt(dy_ref[rows, :], wp_ref[...])
        up_grad = (slope * act_grad).astype(bf16)
        act_s[rows, :] = act
        dup_s[rows, :] = up_grad
        out_part = dot_nn(act, wp_ref[...])
        dh_part = dot_nt(up_grad, wf_ref[...])

        @pl.when(step == 0)
        def _():
            out_ref[rows, :] = out_part
            dh_ref[rows, :] = dh_part

        @pl.when(step > 0)
        def _():
            out_ref[rows, :] += out_part
            dh_ref[rows, :] += dh_part

        return total_grad + jnp.sum(up_grad.astype(f32), axis=0, keepdims=True)

    sums = lax.fori_loop(0, blocks, one, jnp.zeros((1, chunk), f32))
    gb_ref[...] = jnp.broadcast_to(sums, (8, chunk))
    for r in range(8):
        size = width // 8
        rows = slice(r * size, (r + 1) * size)
        grad = dot_nn(ht_s[rows, :], dup_s[...]).astype(bf16)
        gf_ref[rows, :] = grad
    for r in range(chunk // ROWS):
        cols = slice(r * ROWS, (r + 1) * ROWS)
        grad = dot_nn(act_s[:, cols].T, dy_ref[...]).astype(bf16)
        gp_ref[cols, :] = grad


def ffn_branch(hidden, out_grad, w_fc, w_proj, b_fc):
    total, width = hidden.shape
    units = w_proj.shape[0]
    chunk = min(512, units)
    whole = lambda s: (0, 0)
    return pl.pallas_call(
        ffn_kernel,
        grid=(units // chunk,),
        in_specs=[
            pl.BlockSpec((total, width), whole),
            pl.BlockSpec((total, width), whole),
            pl.BlockSpec((width, chunk), lambda s: (0, s)),
            pl.BlockSpec((chunk, width), lambda s: (s, 0)),
            pl.BlockSpec((8, chunk), lambda s: (0, s)),
        ],
        out_specs=[
            pl.BlockSpec((total, width), whole),
            pl.BlockSpec((total, width), whole),
            pl.BlockSpec((width, chunk), lambda s: (0, s)),
            pl.BlockSpec((chunk, width), lambda s: (s, 0)),
            pl.BlockSpec((8, chunk), lambda s: (0, s)),
        ],
        out_shape=[
            jax.ShapeDtypeStruct((total, width), f32),
            jax.ShapeDtypeStruct((total, width), f32),
            jax.ShapeDtypeStruct((width, units), bf16),
            jax.ShapeDtypeStruct((units, width), bf16),
            jax.ShapeDtypeStruct((8, units), f32),
        ],
        scratch_shapes=[
            pltpu.VMEM((width, total), bf16),
            pltpu.VMEM((total, chunk), bf16),
            pltpu.VMEM((total, chunk), bf16),
        ],
        compiler_params=pltpu.CompilerParams(vmem_limit_bytes=60 * 2**20),
        cost_estimate=pl.CostEstimate(
            flops=2 * total * width * units * 6,
            bytes_accessed=28 * 2**20,
            transcendentals=2 * total * units,
        ),
        name="feed_forward",
    )(hidden, out_grad, w_fc, w_proj, b_fc)


def shift(block, axis, distance):
    count = lax.axis_size(axis)
    return lax.ppermute(block, axis, [(i, (i + distance) % count) for i in range(count)])


def swap_bit(block, axis, bit):
    return lax.ppermute(block, axis, [(i, i ^ bit) for i in range(lax.axis_size(axis))])


def shift_within(block, axis, size, distance):
    count = lax.axis_size(axis)
    return lax.ppermute(
        block,
        axis,
        [(i, i // size * size + (i % size + distance) % size) for i in range(count)],
    )


def pick(array, index, axis=0):
    return lax.dynamic_index_in_dim(array, index, axis, keepdims=False)


def order_two(flag, mine, other):
    first = flag == 0
    return jnp.stack([jnp.where(first, mine, other), jnp.where(first, other, mine)])


def gather_rows(local, place):
    dp, y, core, f = place["dp"], place["y"], place["core"], place["f"]
    count = lax.axis_size("fsdp")
    rows, cols = local.shape
    share = rows // lax.axis_size("dp")
    mine = lax.dynamic_slice_in_dim(local, dp * share, share, 0)
    got = jnp.stack([shift(mine, "fsdp", e) for e in range(1, count)])
    got = order_two(y, got, swap_bit(got, "dp", 2))
    got = order_two(core, got, swap_bit(got, "dp", 1))
    got = jnp.transpose(got, (2, 1, 0, 3, 4)).reshape(count - 1, rows, cols)
    if count == 2:
        return order_two(f, local, got[0])
    whole = jnp.zeros((count, rows, cols), local.dtype)
    whole = lax.dynamic_update_index_in_dim(whole, local, f, 0)
    for e in range(1, count):
        whole = lax.dynamic_update_index_in_dim(whole, got[e - 1], (f - e) % count, 0)
    return whole


def reduce_rows(partial, place, parts):
    dp, y, core, f, j = (place[k] for k in ("dp", "y", "core", "f", "j"))
    count, rows, cols = partial.shape
    share = rows // 4
    a = partial.reshape(count, 2, 2, share, cols)
    a = pick(a, core, 2) + swap_bit(pick(a, 1 - core, 2), "dp", 1)
    total = pick(a, f)
    for e in range(1, count):
        total = total + shift(pick(a, (f + e) % count), "fsdp", e)
    total = pick(total, y) + swap_bit(pick(total, 1 - y), "dp", 2)
    total = total + shift(total, "ctx", parts)
    if parts == 2:
        both = order_two(j, total, shift_within(total, "ctx", 2, 1))
    else:
        both = jnp.zeros((parts,) + total.shape, total.dtype)
        both = lax.dynamic_update_index_in_dim(both, total, j, 0)
        for e in range(1, parts):
            got = shift_within(total, "ctx", parts, e)
            both = lax.dynamic_update_index_in_dim(both, got, (j - e) % parts, 0)
    both = order_two(y, both, swap_bit(both, "dp", 2))
    both = order_two(core, both, swap_bit(both, "dp", 1))
    return jnp.transpose(both, (1, 0, 3, 2, 4)).reshape(rows, parts, cols).astype(f32)


def sum_everywhere(vector):
    for bit in (1, 2):
        vector = vector + swap_bit(vector, "dp", bit)
    for axis in ("fsdp", "ctx"):
        bit = 1
        while bit < lax.axis_size(axis):
            vector = vector + swap_bit(vector, axis, bit)
            bit *= 2
    return vector


def gather_sequence(blocks, place, parts):
    s, c = place["s"], place["c"]
    count = lax.axis_size("ctx")
    seqs, rows, width = blocks.shape
    pieces = [(c, pick(blocks, s))]
    for d in range(1, seqs):
        got = shift(pick(blocks, (s + d) % seqs), "ctx", d * parts)
        pieces.append(((c - d * parts) % count, got))
    arrived = []
    for d in range(seqs):
        arrived.append(pieces[d])
        for e in range(1, parts):
            source = s * parts + (place["j"] - e) % parts
            got = shift_within(pieces[d][1], "ctx", parts, e)
            arrived.append(((source - d * parts) % count, got))
    whole = jnp.zeros((count, rows, width), blocks.dtype)
    for at, piece in arrived:
        whole = lax.dynamic_update_index_in_dim(whole, piece, at, 0)
    return whole.reshape(count * rows, width)


def return_blocks(partial, place, parts, seqs):
    s, c, j = place["s"], place["c"], place["j"]
    count = lax.axis_size("ctx")
    rows = partial.shape[0] // count
    blocks = partial.reshape(seqs, parts, rows, -1)
    total = pick(blocks, j, 1).astype(f32)
    for e in range(1, parts):
        total = total + shift_within(pick(blocks, (j + e) % parts, 1), "ctx", parts, e).astype(f32)
    mine = [pick(total, s)]
    for d in range(1, seqs):
        mine.append(shift(pick(total, (s + d) % seqs).astype(bf16), "ctx", d * parts).astype(f32))
    if seqs == 2:
        return order_two(s, mine[0], mine[1])
    whole = jnp.zeros((seqs, rows, partial.shape[1]), f32)
    for d in range(seqs):
        whole = lax.dynamic_update_index_in_dim(whole, mine[d], (s - d) % seqs, 0)
    return whole


class Mover:
    def __init__(self, send, recv, local):
        self.send, self.recv, self.local = send, recv, local
        self.copies, self.left, self.started = [], [], 0

    def to(self, src, dst, axis, index):
        copy = self.remote(src, dst, len(self.copies), (axis, index))
        copy.start()
        self.copies.append(copy)
        return copy

    def here(self, src, dst):
        copy = pltpu.make_async_copy(src, dst, self.local.at[self.started])
        self.started += 1
        copy.start()
        return copy

    def out(self, src, dst):
        self.left.append(self.here(src, dst))

    def remote(self, src, dst, slot, to):
        return pltpu.make_async_remote_copy(
            src_ref=src,
            dst_ref=dst,
            send_sem=self.send.at[slot],
            recv_sem=self.recv.at[slot],
            device_id={to[0]: to[1]},
            device_id_type=pl.DeviceIdType.MESH,
        )

    def stay(self, src, dst, slot):
        return pltpu.make_async_copy(src, dst, self.local.at[slot])

    def finish(self):
        for copy in self.copies:
            copy.wait_send()
        for copy in self.left:
            copy.wait()


class Spot:
    def __init__(self):
        self.dp, self.c, self.f = (lax.axis_index(a) for a in ("dp", "ctx", "fsdp"))
        self.y, self.core = self.dp // 2, self.dp % 2
        self.s, self.j = self.c // 2, self.c % 2
        flip = lambda v: v + 1 - 2 * (v % 2)
        self.x_to = ("fsdp", 1 - self.f)
        self.y_to = ("dp", (1 - self.y) * 2 + self.core)
        self.core_to = ("dp", flip(self.dp))
        self.pair_to = ("ctx", flip(self.c))
        self.far_to = ("ctx", (1 - self.s) * 2 + self.j)

    def greet(self):
        barrier = pltpu.get_barrier_semaphore()
        partners = (self.x_to, self.y_to, self.core_to, self.pair_to, self.far_to)
        for axis, index in partners:
            pl.semaphore_signal(
                barrier, inc=1, device_id={axis: index}, device_id_type=pl.DeviceIdType.MESH
            )
        pl.semaphore_wait(barrier, len(partners))


def block(index, size):
    return pl.ds(pl.multiple_of(index * size, size), size)


def front_kernel(
    info_ref,
    x_ref,
    cot_ref,
    fc_ref,
    proj_ref,
    qkv_ref,
    out_ref,
    rope_ref,
    *rest,
):
    vector_refs, rest = rest[:8], rest[8:]
    (
        seq_in,
        seq_grad,
        w_qkv,
        w_out,
        pull,
        home,
        gp,
        gf,
        part,
        vectors,
        x_s,
        dy_s,
        cot_s,
        held_s,
        small_s,
        wf_s,
        wp_s,
        wq_s,
        wo_s,
        h_s,
        ht_s,
        act_s,
        dup_s,
        rope_s,
        q_s,
        k_s,
        vt_s,
        o_s,
        ot_s,
        kb_s,
        home_s,
        got_s,
        pull_s,
        gp_s,
        gf_s,
        core_got,
        x_got,
        vec_s,
        bfc_s,
        part_s,
        send,
        recv,
        local,
    ) = rest
    at = Spot()
    mover = Mover(send, recv, local)
    total, width = x_s.shape
    blocks = total // ROWS
    units = wp_s.shape[0]
    inner = wo_s.shape[0]
    head_size = 64
    length = jnp.where(at.s == 0, info_ref[0], info_ref[1])
    other = 1 - at.f
    far_c, pair_c = at.far_to[1], at.pair_to[1]
    last_c = (1 - at.s) * 2 + 1 - at.j

    load_x = mover.here(x_ref.at[at.s], x_s.at[block(at.c, ROWS)])
    load_cot = mover.here(cot_ref, cot_s)
    held_s[...] = jnp.zeros_like(held_s)
    row = 0
    for ref in vector_refs:
        size = small_s.shape[2]
        vector = ref[...].astype(f32).reshape(1, ref.shape[0])
        for start in range(0, ref.shape[0], size):
            held_s[row : row + 1, :] = vector[:, start : start + size]
            row += 1
    small_s[at.f] = held_s[...]
    load_rope = mover.here(rope_ref, rope_s)
    at.greet()

    small_copy = mover.to(held_s, small_s.at[at.f], *at.x_to)
    x_far = mover.to(x_ref.at[1 - at.s], x_s.at[block(at.c, ROWS)], *at.far_to)
    x_near = mover.to(x_ref.at[at.s], x_s.at[block(at.c, ROWS)], *at.pair_to)

    def fc_spans(r):
        size = units // 2
        return [(fc_ref.at[r, block(2 * k + at.j, size)], pl.ds(k * size, size)) for k in range(2)]

    def qkv_spans(r):
        size = wq_s.shape[1] // 12
        return [
            (
                qkv_ref.at[r, block(t * 8 + h * 4 + at.j * 2 + g, size)],
                pl.ds((t * 4 + g * 2 + h) * size, size),
            )
            for t in range(3)
            for g in range(2)
            for h in range(2)
        ]

    def row_spans(ref, held):
        count = held.shape[0] // 2

        def spans(r):
            start = pl.multiple_of(at.j * count + r.start, r.size)
            return [(ref.at[pl.ds(start, r.size)], pl.ds(0, width))]

        return spans

    weights = dict(
        fc=(wf_s, fc_spans),
        proj=(wp_s, row_spans(proj_ref, wp_s)),
        qkv=(wq_s, qkv_spans),
        out=(wo_s, row_spans(out_ref, wo_s)),
    )
    got_x, got_y, got_core, stays = {}, {}, {}, {}

    def send_x(name):
        held, spans = weights[name]
        count = held.shape[0] // 2
        share = count // 4
        mine = pl.ds(pl.multiple_of(at.dp * share, share), share)
        there = pl.ds(pl.multiple_of(at.f * count + at.dp * share, share), share)
        got_x[name] = [mover.to(src, held.at[there, cols], *at.x_to) for src, cols in spans(mine)]

    def keep(name):
        held, spans = weights[name]
        count = held.shape[0] // 2
        there = block(at.f, count)
        stays[name] = [
            mover.here(src, held.at[there, cols]) for src, cols in spans(pl.ds(0, count))
        ]

    def quarter(name, dp):
        held = weights[name][0]
        count = held.shape[0] // 2
        share = count // 4
        return held.at[pl.ds(pl.multiple_of(other * count + dp * share, share), share)]

    def pass_x(name):
        for copy in got_x[name]:
            copy.wait_recv()
        mine = quarter(name, at.dp)
        got_y[name] = mover.to(mine, mine, *at.y_to)
        got_core[name] = [mover.to(mine, mine, *at.core_to)]

    def pass_y(name):
        got_y[name].wait_recv()
        mine = quarter(name, at.y_to[1])
        got_core[name].append(mover.to(mine, mine, *at.core_to))

    def arrived(name):
        for copy in got_core[name]:
            copy.wait_recv()
        for copy in stays[name]:
            copy.wait()

    send_x("fc")
    for name in weights:
        keep(name)

    small_copy.wait_recv()

    def line(shard, r):
        return small_s[shard, r : r + 1, :]

    def joined(r):
        return jnp.concatenate([line(0, r), line(1, r)], axis=1)

    first = at.j == 0
    vec_s[...] = jnp.zeros_like(vec_s)
    part_s[...] = jnp.zeros_like(part_s)
    size = LANES // 2
    for t in range(3):
        for h in range(2):
            row = line((t * 2 + h) // 3, 6 + (t * 2 + h) % 3)
            row = jnp.where(first, row[:, :LANES], row[:, LANES:])
            for g in range(2):
                to = g * LANES + h * size
                vec_s[t : t + 1, to : to + size] = row[:, g * size : (g + 1) * size]
    vec_s[3:4, :] = joined(0)
    vec_s[4:5, :] = joined(1)
    vec_s[5:6, :] = joined(4) + joined(5)
    for h in range(2):
        for n in range(2):
            to = h * units // 2 + n * 512
            bfc_s[0:1, to : to + 512] = jnp.where(first, line(h, 9 + n), line(h, 11 + n))
    gain_one, shift_one = vec_s[3:4, :], vec_s[4:5, :]
    gain_two, shift_two = joined(2), joined(3)
    bfc_s[1:2, :width] = gain_two
    mover.out(vec_s, vectors)

    def normal(rows):
        v = x_s[rows, :].astype(f32)
        center = v - jnp.mean(v, axis=-1, keepdims=True)
        spread = jnp.mean(center * center, axis=-1, keepdims=True)
        return center * lax.rsqrt(spread + epsilon)

    def arrive(c):
        rows = block(c, ROWS)
        h = (normal(rows) * gain_two + shift_two).astype(bf16)
        h_s[rows, :] = h
        ht_s[:, rows] = h.T

    load_x.wait()
    arrive(at.c)
    load_cot.wait()
    for t in range(2):
        pos = at.c * ROWS + lax.broadcasted_iota(jnp.int32, (ROWS, width), 0)
        cot_s[t] = jnp.where(pos < info_ref[t], cot_s[t].astype(f32), 0.0).astype(bf16)
    dy_s[block(at.c, ROWS), :] = cot_s[at.s]
    pass_x("fc")
    send_x("proj")
    x_far.wait_recv()
    mine = x_s.at[block(far_c, ROWS)]
    x_last = mover.to(mine, mine, *at.pair_to)
    grad_far = mover.to(cot_s.at[1 - at.s], dy_s.at[block(at.c, ROWS)], *at.far_to)
    arrive(far_c)
    x_near.wait_recv()
    arrive(pair_c)
    pass_x("proj")
    send_x("qkv")
    pass_y("fc")
    arrived("fc")

    def span(b):
        return slice(b * ROWS, (b + 1) * ROWS)

    chunk = 512

    def forward(c):
        rows = block(c, ROWS)

        def one(q, carry):
            cols = block(q, chunk)
            up = dot_nn(h_s[rows, :], wf_s[:, cols]) + bfc_s[0:1, cols]
            half = 0.5 + 0.5 * lax.erf(up * (1.0 / math.sqrt(2.0)))
            act_s[rows, cols] = (up * half).astype(bf16)
            slope = half + up * (jnp.exp(-0.5 * up * up) * (1.0 / math.sqrt(2.0 * math.pi)))
            dup_s[rows, cols] = slope.astype(bf16)
            return carry

        lax.fori_loop(0, units // chunk, one, 0)

    forward(at.c)
    forward(far_c)
    pass_x("qkv")
    send_x("out")
    x_last.wait_recv()
    arrive(last_c)
    grad_near = mover.to(cot_s.at[at.s], dy_s.at[block(at.c, ROWS)], *at.pair_to)
    pass_y("proj")
    forward(pair_c)
    pass_x("out")
    forward(last_c)
    pass_y("qkv")
    pass_y("out")
    grad_far.wait_recv()
    mine = dy_s.at[block(far_c, ROWS)]
    grad_last = mover.to(mine, mine, *at.pair_to)
    mover.out(x_s, seq_in)
    arrived("qkv")
    arrived("out")
    mover.out(wq_s, w_qkv)
    mover.out(wo_s, w_out)

    load_rope.wait()

    def table(n, rows):
        piece = rope_s[n, rows, :]
        return jnp.concatenate([piece] * (inner // 128), axis=1)

    def turned(v, rows):
        left = pltpu.roll(v, inner - ROT // 2, 1)
        right = pltpu.roll(v, ROT // 2, 1)
        return v * table(0, rows) + left * table(1, rows) + right * table(2, rows)

    for r in range(blocks):
        rows = span(r)
        h = (normal(rows) * gain_one + shift_one).astype(bf16)
        q = turned(dot_nn(h, wq_s[:, :inner]) + vec_s[0:1, :inner], rows).astype(bf16)
        q_s[rows, :] = (q.astype(f32) * 0.125).astype(bf16)
        k = dot_nn(h, wq_s[:, inner : 2 * inner]) + vec_s[1:2, :inner]
        k_s[rows, :] = turned(k, rows).astype(bf16)
        v = dot_nn(h, wq_s[:, 2 * inner :]) + vec_s[2:3, :inner]
        vt_s[:, rows] = v.astype(bf16).T
    key_pos = lax.broadcasted_iota(jnp.int32, (total, 128), 0)
    kb_s[...] = jnp.where(key_pos < length, 0.0, masked_score)
    lane = lax.broadcasted_iota(jnp.int32, (ROWS, LANES), 1)
    causal = lax.broadcasted_iota(jnp.int32, (ROWS, ROWS), 0) <= lax.broadcasted_iota(
        jnp.int32, (ROWS, ROWS), 1
    )

    def one_head(g, i, head, carry):
        feats = pl.ds(pl.multiple_of(head * head_size, head_size), head_size)
        from_v = pl.ds(pl.multiple_of(g * LANES + head * head_size, head_size), head_size)
        cols = slice(g * LANES, (g + 1) * LANES)
        mine = (lane // head_size) == head
        qm = jnp.where(mine, q_s[span(i), cols], jnp.zeros((ROWS, LANES), bf16))
        scores = []
        top = None
        for b in range(i + 1):
            sc = dot_nt(k_s[span(b), cols], qm)
            kb = kb_s[span(b), :]
            sc = sc + jnp.concatenate([kb, kb], axis=1)
            if b == i:
                sc = jnp.where(causal, sc, masked_score)
            best = jnp.max(sc, axis=0, keepdims=True)
            top = best if top is None else jnp.maximum(top, best)
            scores.append(sc)
        row_sum = None
        o_t = None
        for b in range(i + 1):
            e = jnp.exp(scores[b] - top)
            add = jnp.sum(e, axis=0, keepdims=True)
            row_sum = add if row_sum is None else row_sum + add
            add = dot_nn(vt_s[from_v, span(b)], e.astype(bf16))
            o_t = add if o_t is None else o_t + add
        ot_s[feats, :] = o_t / row_sum
        return carry

    for i in range(blocks):
        for g in range(2):
            lax.fori_loop(0, LANES // head_size, functools.partial(one_head, g, i), 0)
            if i == 0 and g == 0:
                arrived("proj")
            o = ot_s[...].T.astype(bf16)
            for h in range(2):
                to = h * LANES + g * size
                o_s[span(i), to : to + size] = o[:, h * size : (h + 1) * size]
        both = dot_nn(act_s[span(i), :], wp_s[...]) + dot_nn(o_s[span(i), :], wo_s[...])
        home_s[i] = both.astype(bf16)
    nears = [
        mover.to(home_s.at[2 * t + 1 - at.j], got_s.at[t], *at.pair_to) for t in range(2)
    ]

    grad_near.wait_recv()
    grad_last.wait_recv()
    mover.out(dy_s, seq_grad)
    bfc_s[2:3, :] = jnp.zeros((1, units), f32)
    for r in range(8):
        grad = dot_nn(act_s[:, r * ROWS : (r + 1) * ROWS].T, dy_s[...]).astype(bf16)
        for k in range(2):
            gp_s[k, r % 2, r // 4, r // 2 % 2] = grad[k * ROWS // 2 : (k + 1) * ROWS // 2]
    to_core = [mover.to(gp_s.at[k, 1 - at.core], core_got.at[k], *at.core_to) for k in range(2)]
    to_x = []

    def step_core(k):
        to_core[k].wait_recv()
        own, got = gp_s.at[k, at.core], core_got.at[k]
        own[1 - at.f] = own[1 - at.f] + got[1 - at.f]
        if k == 0:
            to_x.append(mover.to(own.at[1 - at.f], x_got, *at.x_to))
        own[at.f] = own[at.f] + got[at.f]

    def step_x():
        to_x[0].wait_recv()
        own = gp_s.at[0, at.core, at.f]
        own[...] = own[...] + x_got[...]
        mover.out(own, gp.at[0, 0])

    gain_sum = jnp.zeros((1, width), f32)
    shift_sum = jnp.zeros((1, width), f32)
    dy_sum = jnp.zeros((1, width), f32)
    for i in range(blocks):
        rows = span(i)

        def one(q, carry):
            cols = block(q, chunk)
            act_grad = dot_nt(dy_s[rows, :], wp_s[cols, :])
            up_grad = (dup_s[rows, cols].astype(f32) * act_grad).astype(bf16)
            dup_s[rows, cols] = up_grad
            bfc_s[2:3, cols] += jnp.sum(up_grad.astype(f32), axis=0, keepdims=True)
            return carry

        lax.fori_loop(0, units // chunk, one, 0)
        dh = dot_nt(dup_s[rows, :], wf_s[...])
        pull_s[rows, :] = (dh * gain_two).astype(bf16)
        gain_sum = gain_sum + jnp.sum(dh * normal(rows), axis=0, keepdims=True)
        shift_sum = shift_sum + jnp.sum(dh, axis=0, keepdims=True)
        dy_sum = dy_sum + jnp.sum(dy_s[rows, :].astype(f32), axis=0, keepdims=True)
        if i == 0:
            step_core(0)
        if i == 1:
            step_core(1)
            mover.out(gp_s.at[1, at.core], gp.at[1])
    mover.out(pull_s, pull)
    part_s[2:3, :] = gain_sum
    part_s[3:4, :] = shift_sum
    part_s[4:5, :] = dy_sum * 0.5
    none = jnp.zeros((2, width), f32)
    sums = jnp.concatenate([none, bfc_s[2:3, :width], bfc_s[2:3, width:], none, none], axis=0)
    part_s[8:16, :] = jnp.where(first, sums, jnp.concatenate([sums[4:], sums[:4]], axis=0))
    mover.out(part_s, part)
    rows_each = width // 8
    for k in range(2):
        for r in range(8):
            cols = slice(k * units // 2, (k + 1) * units // 2)
            grad = dot_nn(ht_s[r * rows_each : (r + 1) * rows_each, :], dup_s[:, cols])
            gf_s[k, r % 2, r // 4, r // 2 % 2] = grad.astype(bf16)
        mover.out(gf_s.at[k], gf.at[k])
        if k == 0:
            step_x()

    for t in range(2):
        nears[t].wait_recv()
        mine = home_s.at[2 * t + at.j]
        mine[...] = (mine[...].astype(f32) + got_s[t].astype(f32)).astype(bf16)
        mover.out(mine, home.at[t])
    mover.finish()


def front(info, x, cot, fc, proj, qkv, out, rope, vectors):
    seqs, rows, width = x.shape
    total = 4 * rows
    units = proj.shape[0]
    inner = out.shape[0]
    cell = (rows // 2, width)
    hbm = pl.BlockSpec(memory_space=pl.ANY)
    shape = lambda *dims: jax.ShapeDtypeStruct(dims, bf16)
    buf = lambda *dims: pltpu.VMEM(dims, bf16)
    wide = lambda *dims: pltpu.VMEM(dims, f32)
    return pl.pallas_call(
        front_kernel,
        in_specs=[pl.BlockSpec(memory_space=pltpu.SMEM)]
        + [hbm] * 7
        + [pl.BlockSpec(memory_space=pltpu.VMEM)] * 8,
        out_specs=[hbm] * 10,
        out_shape=[
            shape(total, width),
            shape(total, width),
            shape(width, 3 * inner),
            shape(inner, width),
            shape(total, width),
            shape(2, rows, width),
            shape(2, 2, 2, *cell),
            shape(2, 2, 2, 2, *cell),
            jax.ShapeDtypeStruct((16, width), f32),
            jax.ShapeDtypeStruct((8, width), f32),
        ],
        scratch_shapes=[
            buf(total, width),
            buf(total, width),
            buf(2, rows, width),
            wide(16, width // 2),
            wide(2, 16, width // 2),
            buf(width, units),
            buf(units, width),
            buf(width, 3 * inner),
            buf(inner, width),
            buf(total, width),
            buf(width, total),
            buf(total, units),
            buf(total, units),
            wide(*rope.shape),
            buf(total, inner),
            buf(total, inner),
            buf(inner, total),
            buf(total, inner),
            wide(LANES, ROWS),
            wide(total, 128),
            buf(4, rows, width),
            buf(2, rows, width),
            buf(total, width),
            buf(2, 2, 2, 2, *cell),
            buf(2, 2, 2, 2, *cell),
            buf(2, 2, 2, *cell),
            buf(2, *cell),
            wide(8, width),
            wide(8, units),
            wide(16, width),
            pltpu.SemaphoreType.DMA((48,)),
            pltpu.SemaphoreType.DMA((48,)),
            pltpu.SemaphoreType.DMA((48,)),
        ],
        compiler_params=pltpu.CompilerParams(
            collective_id=0, has_side_effects=True, vmem_limit_bytes=62 * 2**20
        ),
        name="front",
    )(info, x, cot, fc, proj, qkv, out, rope, *vectors)


def branch_kernel(
    length_ref,
    x_ref,
    dy_ref,
    wqkv_ref,
    wo_ref,
    bias_ref,
    rope_ref,
    out_ref,
    ffn_pull_ref,
    gp_ref,
    gf_ref,
    small_ref,
    summed,
    branch,
    pull,
    small,
    x_s,
    dy_s,
    h_s,
    ht_s,
    wqkv_s,
    wo_s,
    rope_s,
    q_s,
    k_s,
    v_s,
    do_s,
    kt_s,
    vt_s,
    dot_s,
    ot_s,
    dqt_s,
    dk_s,
    dv_s,
    dp_s,
    kb_s,
    begun_s,
    own_s,
    mine_s,
    core_s,
    x_got,
    y_got,
    far_got,
    home_s,
    home_got,
    out_s,
    small_s,
    small_got,
    send,
    recv,
    local,
):
    at = Spot()
    mover = Mover(send, recv, local)
    total, width = x_s.shape
    blocks = total // ROWS
    inner = wo_s.shape[0]
    head_size = 64
    length = jnp.where(at.s == 0, length_ref[0], length_ref[1])

    load_x = mover.here(x_ref, x_s)
    load_w = mover.here(wqkv_ref, wqkv_s)
    load_rope = mover.here(rope_ref, rope_s)
    load_dy = mover.here(dy_ref, dy_s)
    half = LANES // 2
    load_wo = [
        mover.here(
            wo_ref.at[pl.ds(h * LANES + g * half, half)],
            wo_s.at[pl.ds(g * LANES + h * half, half)],
        )
        for g in range(2)
        for h in range(2)
    ]
    load_small = mover.here(small_ref, small_s.at[0])
    load_out = mover.here(out_ref, out_s)
    at.greet()

    links = ("c", "x", "y", "z", "p", "yy", "c1", "c2")

    def own_of(n):
        return own_s.at[n - 1] if n < 4 else mine_s.at[n - 4, at.core]

    def cell(n, y):
        return begun_s.at[y] if n < 1 else own_of(n).at[at.f, y]

    def link(n, name):
        mine, other = summed.at[n, at.y, at.core], summed.at[n, 1 - at.y, at.core]
        if name == "c":
            src = (gf_ref.at[n - 2] if n < 4 else mine_s.at[n - 4]).at[1 - at.core]
            ends = (src, core_s.at[n - 2], at.core_to)
        elif name == "x":
            ends = (own_of(n).at[1 - at.f], x_got.at[n - 1], at.x_to)
        elif name == "y":
            ends = (cell(n, 1 - at.y), y_got.at[n], at.y_to)
        elif name == "z":
            ends = (cell(n, at.y), far_got.at[n], at.far_to)
        elif name == "p":
            ends = (y_got.at[n], summed.at[n, at.y, at.core, at.j], at.pair_to)
        elif name == "yy":
            ends = (mine, mine, at.y_to)
        elif name == "c1":
            ends = (mine, mine, at.core_to)
        else:
            ends = (other, other, at.core_to)
        return mover.remote(ends[0], ends[1], n * len(links) + links.index(name), ends[2])

    def load(n):
        if n == 0:
            return mover.stay(gp_ref.at[0, 0], begun_s, 24)
        src = gp_ref.at[1] if n == 1 else gf_ref.at[n - 2, at.core]
        return mover.stay(src, own_s.at[n - 1], 24 + n)

    def keep(n):
        return mover.stay(y_got.at[n], summed.at[n, at.y, at.core, at.j], 28 + n)

    def step_start(n):
        if n < 4:
            load(n).start()
        link(n, "c").start()

    def step_core(n):
        if n < 4:
            load(n).wait()
        link(n, "c").wait_recv()
        own, got = own_of(n), core_s.at[n - 2]
        own[1 - at.f] = own[1 - at.f] + got[1 - at.f]
        link(n, "x").start()
        own[at.f] = own[at.f] + got[at.f]

    def step_x(n):
        link(n, "x").wait_recv()
        own, got = own_of(n), x_got.at[n - 1]
        own[at.f, 1 - at.y] = own[at.f, 1 - at.y] + got[1 - at.y]
        link(n, "y").start()
        own[at.f, at.y] = own[at.f, at.y] + got[at.y]

    def step_y(n):
        link(n, "y").wait_recv()
        mine = cell(n, at.y)
        mine[...] = mine[...] + y_got[n]
        link(n, "z").start()

    def step_far(n):
        link(n, "z").wait_recv()
        y_got[n] = cell(n, at.y)[...] + far_got[n]
        link(n, "p").start()
        keep(n).start()

    def step_pair(n):
        link(n, "p").wait_recv()
        keep(n).wait()
        link(n, "yy").start()
        link(n, "c1").start()

    def step_yy(n):
        link(n, "yy").wait_recv()
        link(n, "c2").start()

    base = 6 * len(links)

    def near(t):
        return mover.remote(home_s.at[2 * t + 1 - at.j], home_got.at[t], base + t, at.pair_to)

    def last(t):
        mine, dst = home_s.at[2 * t + at.j], pull.at[at.s]
        return mover.remote(mine, dst, base + 2, at.far_to), mover.stay(mine, dst, 34)

    def out_home():
        far = mover.remote(out_s.at[1 - at.s], branch.at[at.s], base + 3, at.far_to)
        return far, mover.stay(out_s.at[at.s], branch.at[at.s], 35)

    def home_near(t):
        near(t).start()

    def home_sum(t):
        near(t).wait_recv()
        mine = home_s.at[2 * t + at.j]
        mine[...] = (mine[...].astype(f32) + home_got[t].astype(f32)).astype(bf16)
        far, stay = last(t)
        pl.when(at.s == t)(stay.start)
        pl.when(at.s != t)(far.start)

    trips = (at.core_to, at.x_to, at.y_to, at.far_to, at.pair_to)

    def small_trip(n):
        return mover.remote(small_s.at[n], small_got.at[n], base + 4 + n, trips[n])

    def small_step(n):
        if n > 0:
            small_trip(n - 1).wait_recv()
            small_s[n] = small_s[n - 1] + small_got[n - 1]
        if n < 5:
            small_trip(n).start()
        else:
            mover.out(small_s.at[5], small)

    def end():
        for n in range(6):
            link(n, "c1").wait_recv()
            link(n, "c2").wait_recv()
            for name in links[max(2 - n, 0) :]:
                link(n, name).wait_send()
        for far, stay in (last(0), out_home()):
            far.wait()
            stay.wait()
        for t in range(2):
            near(t).wait_send()
        for n in range(5):
            small_trip(n).wait_send()

    acts = dict(
        start=step_start,
        core=step_core,
        x=step_x,
        y=step_y,
        far=step_far,
        pair=step_pair,
        yy=step_yy,
        near=home_near,
        sum=home_sum,
        small=small_step,
    )

    def turn(*place):
        for word in PLAN.get(",".join(str(v) for v in place), ()):
            name, n = word.split(":")
            acts[name](int(n))

    for n in range(2):
        load(n).start()
    for n in range(2, 4):
        step_start(n)
    load(0).wait()
    link(0, "y").start()
    load(1).wait()
    link(1, "x").start()
    load_out.wait()
    for copy in out_home():
        copy.start()

    def normal(rows):
        v = x_s[rows, :].astype(f32)
        center = v - jnp.mean(v, axis=-1, keepdims=True)
        spread = jnp.mean(center * center, axis=-1, keepdims=True)
        return center * lax.rsqrt(spread + epsilon)

    def table(n, rows):
        part = rope_s[n, rows, :]
        return jnp.concatenate([part, part], axis=1)

    def turned(v, rows, sign):
        left = pltpu.roll(v, LANES - ROT // 2, 1)
        right = pltpu.roll(v, ROT // 2, 1)
        moved = left * table(1, rows) + right * table(2, rows)
        return v * table(0, rows) + moved if sign > 0 else v * table(0, rows) - moved

    key_pos = lax.broadcasted_iota(jnp.int32, (total, 128), 0)
    kb_s[...] = jnp.where(key_pos < length, 0.0, masked_score)
    lane = lax.broadcasted_iota(jnp.int32, (ROWS, LANES), 1)
    causal = lax.broadcasted_iota(jnp.int32, (ROWS, ROWS), 0) <= lax.broadcasted_iota(
        jnp.int32, (ROWS, ROWS), 1
    )
    gain, offset = bias_ref[3:4, :], bias_ref[4:5, :]

    def span(b):
        return slice(b * ROWS, (b + 1) * ROWS)

    def project(g):
        cols = lambda t: slice(t * inner + g * LANES, t * inner + (g + 1) * LANES)
        bias = lambda t: bias_ref[t : t + 1, g * LANES : (g + 1) * LANES]
        for r in range(blocks):
            rows = span(r)
            if g == 0:
                hr = (normal(rows) * gain + offset).astype(bf16)
                h_s[rows, :] = hr
                ht_s[:, rows] = hr.T
                if r == 0:
                    load_w.wait()
                    load_rope.wait()
                    load_dy.wait()
                    for copy in load_wo:
                        copy.wait()
            else:
                hr = h_s[rows, :]
            q = turned(dot_nn(hr, wqkv_s[:, cols(0)]) + bias(0), rows, 1).astype(bf16)
            q_s[rows, :] = (q.astype(f32) * 0.125).astype(bf16)
            k = turned(dot_nn(hr, wqkv_s[:, cols(1)]) + bias(1), rows, 1).astype(bf16)
            k_s[rows, :] = k
            kt_s[:, rows] = k.T
            v = (dot_nn(hr, wqkv_s[:, cols(2)]) + bias(2)).astype(bf16)
            v_s[rows, :] = v
            vt_s[:, rows] = v.T
            do = dot_nt(dy_s[rows, :], wo_s[g * LANES : (g + 1) * LANES, :]).astype(bf16)
            do_s[rows, :] = do
            dot_s[:, rows] = do.T
            turn("p%d" % g, r)
        dk_s[...] = jnp.zeros_like(dk_s)
        dv_s[...] = jnp.zeros_like(dv_s)

    def one_head(g, i, head, carry):
        feats = pl.ds(pl.multiple_of(head * head_size, head_size), head_size)
        mine = (lane // head_size) == head
        zero = jnp.zeros((ROWS, LANES), bf16)
        rows = span(i)
        qm = jnp.where(mine, q_s[rows, :], zero)
        dom = jnp.where(mine, do_s[rows, :], zero)
        scores = []
        top = None
        for b in range(i + 1):
            sc = dot_nt(k_s[span(b), :], qm)
            kb = kb_s[span(b), :]
            sc = sc + jnp.concatenate([kb, kb], axis=1)
            if b == i:
                sc = jnp.where(causal, sc, masked_score)
            best = jnp.max(sc, axis=0, keepdims=True)
            top = best if top is None else jnp.maximum(top, best)
            scores.append(sc)
        row_sum = None
        for b in range(i + 1):
            scores[b] = jnp.exp(scores[b] - top)
            part = jnp.sum(scores[b], axis=0, keepdims=True)
            row_sum = part if row_sum is None else row_sum + part
        inverse = 1.0 / row_sum
        o_t = None
        for b in range(i + 1):
            scores[b] = scores[b] * inverse
            low = scores[b].astype(bf16)
            dv_s[span(b), :] += dot_nn(low, dom)
            part = dot_nn(vt_s[feats, span(b)], low)
            o_t = part if o_t is None else o_t + part
        ot_s[feats, rows] = o_t
        delta = jnp.sum(dot_s[feats, rows].astype(f32) * o_t, axis=0, keepdims=True)
        dq_t = None
        for b in range(i + 1):
            dp = dot_nt(v_s[span(b), :], dom)
            ds = (scores[b] * (dp - delta)).astype(bf16)
            dk_s[span(b), :] += dot_nn(ds, qm)
            part = dot_nn(kt_s[feats, span(b)], ds)
            dq_t = part if dq_t is None else dq_t + part
        dqt_s[feats, rows] = dq_t * 0.125
        for h in range(LANES // head_size):
            if "%d,%d,%d" % (g, i, h) in PLAN:
                pl.when(head == h)(functools.partial(turn, g, i, h))
        return carry

    def finish_block(g, i, sums):
        rows = span(i)
        cols = slice(g * LANES, (g + 1) * LANES)
        dq = turned(dqt_s[:, rows].T, rows, -1).astype(bf16)
        dk = turned(dk_s[rows, :], rows, -1).astype(bf16)
        dv = dv_s[rows, :].astype(bf16)
        for t, grad in enumerate((dq, dk, dv)):
            sums[t] = sums[t] + jnp.sum(grad.astype(f32), axis=0, keepdims=True)
            dp_s[t, rows, cols] = grad

    def finish_rows(i, gain_sum, shift_sum):
        rows = span(i)
        dh = dot_nt(dp_s[0, rows, :], wqkv_s[:, :inner])
        dh = dh + dot_nt(dp_s[1, rows, :], wqkv_s[:, inner : 2 * inner])
        dh = dh + dot_nt(dp_s[2, rows, :], wqkv_s[:, 2 * inner :])
        home_s[i] = (dh * gain + home_s[i].astype(f32)).astype(bf16)
        gain_sum = gain_sum + jnp.sum(dh * normal(rows), axis=0, keepdims=True)
        return gain_sum, shift_sum + jnp.sum(dh, axis=0, keepdims=True)

    def weight_grads(g):
        cols = slice(g * LANES, (g + 1) * LANES)
        size = width // 8
        for t in range(3):
            for r in range(8):
                grad = dot_nn(ht_s[r * size : (r + 1) * size, :], dp_s[t, :, cols])
                mine_s[g, r % 2, r // 4, r // 2 % 2, :, t * LANES : (t + 1) * LANES] = grad.astype(bf16)
        grad = dot_nn(ot_s[...].astype(bf16), dy_s[...]).astype(bf16)
        size = LANES // 8
        for r in range(8):
            for b in range(4):
                mine_s[
                    g, r % 2, r // 4, r // 2 % 2, b * size : (b + 1) * size, 3 * LANES :
                ] = grad[r * size : (r + 1) * size, b * LANES : (b + 1) * LANES]

    load_x.wait()
    loads_home = [
        mover.here(ffn_pull_ref.at[block(b, ROWS)], home_s.at[b]) for b in range(blocks)
    ]
    load_small.wait()
    gain_sum = jnp.zeros((1, width), f32)
    shift_sum = jnp.zeros((1, width), f32)
    for g in range(2):
        project(g)
        sums = [jnp.zeros((1, LANES), f32) for _ in range(3)]
        for i in reversed(range(blocks)):
            lax.fori_loop(0, LANES // head_size, functools.partial(one_head, g, i), 0)
            finish_block(g, i, sums)
            if g == 1:
                if i == blocks - 1:
                    for copy in loads_home:
                        copy.wait()
                gain_sum, shift_sum = finish_rows(i, gain_sum, shift_sum)
            turn(g, i)
        weight_grads(g)
        row = lax.broadcasted_iota(jnp.int32, (8, LANES), 0)
        for t in range(3):
            start = t % 2 * inner + g * LANES
            cols = slice(start, start + LANES)
            here = row == 4 * at.j + t // 2
            small_s[0, 8:16, cols] = jnp.where(here, sums[t], small_s[0, 8:16, cols])
        if g == 0:
            turn("grads")
    small_s[0, 0:1, :] = gain_sum
    small_s[0, 1:2, :] = shift_sum
    turn("tail")
    end()
    mover.finish()


PLAN = {
    "p0,3": ("y:0",),
    "0,3,0": ("core:3",),
    "0,2": ("x:1",),
    "0,1,3": ("x:3",),
    "grads": ("start:4", "y:1",),
    "p1,0": ("far:0",),
    "p1,2": ("core:2",),
    "1,3,3": ("far:1", "y:3", "core:4", "x:2",),
    "1,1,0": ("near:1",),
    "1,1,1": ("x:4", "y:2",),
    "1,0,0": ("pair:1",),
    "1,0,3": ("pair:0",),
    "tail": ("far:2", "far:3", "start:5", "small:0", "core:5", "y:4", "x:5", "near:0", "y:5", "far:4", "pair:2", "sum:1", "pair:3", "pair:4", "small:1", "far:5", "sum:0", "small:2", "yy:1", "pair:5", "yy:2", "yy:0", "yy:4", "yy:3", "small:3", "small:4", "yy:5", "small:5",),
}


def branch_and_sums(length, x, dy, w_qkv, w_out, bias, rope, out, ffn_pull, gp, gf, small):
    total, width = x.shape
    inner = w_out.shape[0]
    cell = (ROWS // 2, width)
    hbm = pl.BlockSpec(memory_space=pl.ANY)
    vmem = pl.BlockSpec(memory_space=pltpu.VMEM)
    home = jax.ShapeDtypeStruct((2, ROWS, width), bf16)
    buf = lambda dims, kind=bf16: pltpu.VMEM(tuple(dims), kind)
    return pl.pallas_call(
        branch_kernel,
        in_specs=[pl.BlockSpec(memory_space=pltpu.SMEM)] + [hbm] * 4 + [vmem] + [hbm] * 6,
        out_specs=[hbm] * 4,
        out_shape=[
            jax.ShapeDtypeStruct((6, 2, 2, 2) + cell, bf16),
            home,
            home,
            jax.ShapeDtypeStruct(small.shape, f32),
        ],
        scratch_shapes=[
            buf((total, width)),
            buf((total, width)),
            buf((total, width)),
            buf((width, total)),
            buf((width, 3 * inner)),
            buf((inner, width)),
            buf((3, total, 128), f32),
            buf((total, LANES)),
            buf((total, LANES)),
            buf((total, LANES)),
            buf((total, LANES)),
            buf((LANES, total)),
            buf((LANES, total)),
            buf((LANES, total)),
            buf((LANES, total), f32),
            buf((LANES, total), f32),
            buf((total, LANES), f32),
            buf((total, LANES), f32),
            buf((3, total, inner)),
            buf((total, 128), f32),
            buf((2,) + cell),
            buf((3, 2, 2) + cell),
            buf((2, 2, 2, 2) + cell),
            buf((4, 2, 2) + cell),
            buf((5, 2) + cell),
            buf((6,) + cell),
            buf((6,) + cell),
            buf((total // ROWS, ROWS, width)),
            buf((2, ROWS, width)),
            buf((2, ROWS, width)),
            buf((6,) + small.shape, f32),
            buf((5,) + small.shape, f32),
            pltpu.SemaphoreType.DMA((80,)),
            pltpu.SemaphoreType.DMA((80,)),
            pltpu.SemaphoreType.DMA((40,)),
        ],
        compiler_params=pltpu.CompilerParams(
            collective_id=1, has_side_effects=True, vmem_limit_bytes=62 * 2**20
        ),
        name="branch",
    )(length, x, dy, w_qkv, w_out, bias, rope, out, ffn_pull, gp, gf, small)


def last_kernel(
    lengths_ref,
    proj_ref,
    fc_ref,
    heads_ref,
    x_ref,
    cot_ref,
    branch_ref,
    pull_ref,
    vectors_ref,
    sums_ref,
    residual_out,
    residual_grad,
    d_proj,
    d_fc,
    d_qkv,
    d_out,
    d_gain_one,
    d_shift_one,
    d_gain_two,
    d_shift_two,
    d_bias_out,
    d_bias_proj,
    d_bqkv,
    d_bfc,
):
    size, width = proj_ref.shape[4:]
    for p in range(2):
        d_proj[p, 0, 0, 0] = proj_ref[0, 0, 0, p].astype(f32)
        d_fc[:, p * width : (p + 1) * width] = fc_ref[0, 0, 0, p].astype(f32)
    y, core, second = (pl.program_id(n) for n in range(3))

    rows = x_ref.shape[1]
    features = x_ref[0].astype(f32)
    residual_out[0] = (features + branch_ref[0].astype(f32) + vectors_ref[5:6, :]).astype(bf16)
    hat, inverse = normalize(features)
    pulled = pull_ref[0].astype(f32)
    pulled = inverse * (
        pulled
        - jnp.mean(pulled, axis=-1, keepdims=True)
        - hat * jnp.mean(pulled * hat, axis=-1, keepdims=True)
    )
    start = (lax.axis_index("ctx") * 4 + core * 2 + second) * rows
    valid = start + lax.broadcasted_iota(jnp.int32, (rows, width), 0) < lengths_ref[y]
    own = jnp.where(valid, cot_ref[0].astype(f32), 0.0)
    residual_grad[0] = (own + pulled).astype(bf16)

    @pl.when(second == 0)
    def _():
        for g in range(2):
            for p in range(2):
                for t in range(3):
                    for h in range(2):
                        got = heads_ref[g, 0, 0, p, :, (t * 2 + h) * 128 : (t * 2 + h + 1) * 128]
                        to = t * 8 + h * 4 + p * 2 + g
                        d_qkv[:, to * 128 : (to + 1) * 128] = got.astype(f32)

    @pl.when(second == 1)
    def _():
        for g in range(2):
            for p in range(2):
                for b in range(4):
                    got = heads_ref[g, 0, 0, p, b * size // 4 : (b + 1) * size // 4, 3 * LANES :]
                    d_out[p, g, 0, 0, :, b * LANES : (b + 1) * LANES] = got.astype(f32)

    @pl.when(y * 4 + core * 2 + second == 0)
    def _():
        first = lax.axis_index("fsdp") == 0
        half = width // 2
        gains = (d_gain_one, d_shift_one, d_gain_two, d_shift_two, d_bias_out)
        for r, ref in (*enumerate(gains), (4, d_bias_proj)):
            line = sums_ref[r : r + 1, :]
            ref[...] = jnp.where(first, line[:, :half], line[:, half:]).reshape(half)
        pieces = []
        for t in range(3):
            for h in range(2):
                for p in range(2):
                    for g in range(2):
                        at = t % 2 * half + (g * 2 + h) * 128
                        pieces.append(sums_ref[8 + 4 * p + t // 2 : 9 + 4 * p + t // 2, at : at + 128])
        line = jnp.concatenate(pieces, axis=1)
        count = 3 * half
        d_bqkv[...] = jnp.where(first, line[:, :count], line[:, count:]).reshape(count)
        line = jnp.concatenate(
            [jnp.where(first, sums_ref[r : r + 1, :], sums_ref[r + 1 : r + 2, :]) for r in (10, 14)],
            axis=1,
        )
        d_bfc[...] = line.reshape(2 * width)


def last_pass(lengths, summed, x, cot, branch, pull, vectors, sums, proj_shape, fc_shape, qkv_shape, out_shape):
    size, width = summed.shape[4:]
    rows = x.shape[1] // 4
    shape = lambda *dims: jax.ShapeDtypeStruct(dims, f32)
    pair = (1, 1, 1, 2, size, width)
    token = pl.BlockSpec((1, rows, width), lambda y, c, k: (y, c * 2 + k, 0))
    line = lambda count: pl.BlockSpec((count,), lambda y, c, k: (0,))
    table = lambda count: pl.BlockSpec((count, width), lambda y, c, k: (0, 0))
    counts = [width // 2] * 6 + [3 * width // 2, 2 * width]
    residual_out, residual_grad, d_proj, d_fc, d_qkv, d_out, *vectors_out = pl.pallas_call(
        last_kernel,
        grid=(2, 2, 2),
        in_specs=[
            pl.BlockSpec(memory_space=pltpu.SMEM),
            pl.BlockSpec(pair, lambda y, c, k: (k, y, c, 0, 0, 0)),
            pl.BlockSpec(pair, lambda y, c, k: (2 + k, y, c, 0, 0, 0)),
            pl.BlockSpec((2, 1, 1, 2, size, width), lambda y, c, k: (2, y, c, 0, 0, 0)),
            token,
            token,
            token,
            token,
            table(8),
            table(16),
        ],
        out_specs=[
            token,
            token,
            pl.BlockSpec((2, 1, 1, 1, size, width), lambda y, c, k: (0, y, c, k, 0, 0)),
            pl.BlockSpec((size, 2 * width), lambda y, c, k: (y * 2 + c, k)),
            pl.BlockSpec((size, qkv_shape[1]), lambda y, c, k: (y * 2 + c, 0)),
            pl.BlockSpec((2, 2, 1, 1, size // 4, width), lambda y, c, k: (0, 0, y, c, 0, 0)),
        ]
        + [line(count) for count in counts],
        out_shape=[
            jax.ShapeDtypeStruct(x.shape, bf16),
            jax.ShapeDtypeStruct(x.shape, bf16),
            shape(2, 2, 2, 2, size, width),
            shape(*fc_shape),
            shape(*qkv_shape),
            shape(2, 2, 2, 2, size // 4, width),
        ]
        + [shape(count) for count in counts],
        compiler_params=pltpu.CompilerParams(vmem_limit_bytes=62 * 2**20),
        name="last",
    )(lengths, summed, summed, summed, x, cot, branch, pull, vectors, sums)
    grads = (d_proj.reshape(proj_shape), d_fc, d_qkv, d_out.reshape(out_shape))
    return residual_out, residual_grad, grads, vectors_out


def normalize(features):
    center = features - jnp.mean(features, axis=-1, keepdims=True)
    spread = jnp.mean(center * center, axis=-1, keepdims=True)
    inverse = lax.rsqrt(spread + epsilon)
    return center * inverse, inverse


def rope_tables(total, head_size):
    half = ROT // 2
    inverse = (rope_base ** (-(2.0 * np.arange(half)) / ROT)).astype(np.float32)
    angles = np.arange(total, dtype=np.float32)[:, None] * inverse[None, :]
    cosine, sine = np.cos(angles), np.sin(angles)
    rest = np.zeros((total, head_size - ROT), np.float32)
    none = np.zeros((total, half), np.float32)
    same = np.concatenate([cosine, cosine, rest + 1.0], axis=1)
    ahead = np.concatenate([-sine, none, rest], axis=1)
    behind = np.concatenate([none, sine, rest], axis=1)
    return jnp.asarray(np.tile(np.stack([same, ahead, behind]), (1, 1, 128 // head_size)), f32)


def finish(residual_in, cotangent, lengths, start, branch, pulled, bias):
    features = residual_in.astype(f32)
    residual_out = (features + branch + bias).astype(bf16)
    own_hat, own_inverse = normalize(features)
    pulled = own_inverse * (
        pulled
        - jnp.mean(pulled, axis=-1, keepdims=True)
        - own_hat * jnp.mean(pulled * own_hat, axis=-1, keepdims=True)
    )
    own_pos = start + jnp.arange(residual_in.shape[1], dtype=jnp.int32)
    valid = (own_pos[None, :] < lengths[:, None])[..., None]
    residual_grad = (jnp.where(valid, cotangent.astype(f32), 0.0) + pulled).astype(bf16)
    return residual_out, residual_grad


def fast_block(residual_in, lengths, cotangent, weights, small, rope):
    weight_fc, weight_proj, weight_qkv, weight_out = weights
    seq_in, seq_grad, w_qkv, w_out, pull, home, gp, gf, part, vectors = front(
        lengths, residual_in, cotangent, *weights, rope, small
    )
    summed, branch, pulled, sums = branch_and_sums(
        lengths, seq_in, seq_grad, w_qkv, w_out, vectors, rope, home, pull, gp, gf, part
    )
    residual_out, residual_grad, grads, vectors_out = last_pass(
        lengths,
        summed,
        residual_in,
        cotangent,
        branch,
        pulled,
        vectors,
        sums,
        weight_proj.shape,
        weight_fc.shape,
        weight_qkv.shape,
        weight_out.shape,
    )
    d_proj, d_fc, d_qkv, d_out = grads
    d_gain_one, d_shift_one, d_gain_two, d_shift_two, d_bout, d_bproj, d_bqkv, d_bfc = vectors_out
    return (
        residual_out,
        residual_grad,
        d_gain_one,
        d_shift_one,
        d_qkv,
        d_bqkv,
        d_out,
        d_bout,
        d_gain_two,
        d_shift_two,
        d_fc,
        d_bfc,
        d_proj,
        d_bproj,
    )


def per_device(
    residual_in,
    lengths,
    gain_attn,
    shift_attn,
    weight_qkv,
    bias_qkv,
    weight_out,
    bias_out,
    gain_ffn,
    shift_ffn,
    weight_fc,
    bias_fc,
    weight_proj,
    bias_proj,
    cotangent,
):
    seqs, block_rows, width = residual_in.shape
    n_ctx, n_fsdp = lax.axis_size("ctx"), lax.axis_size("fsdp")
    parts = n_ctx // seqs
    total = n_ctx * block_rows
    units = weight_fc.shape[1]
    head_size = width // HEADS
    c, f, dp = lax.axis_index("ctx"), lax.axis_index("fsdp"), lax.axis_index("dp")
    s, j = c // parts, c % parts
    place = dict(c=c, f=f, dp=dp, s=s, j=j, y=dp // 2, core=dp % 2)
    spread_heads = HEADS % (n_fsdp * parts) == 0
    n_h = n_fsdp if spread_heads else 1
    inner = width // parts

    rows_here = weight_qkv.shape[0]
    own_heads = lambda v: pick(v.reshape(3, n_h, parts, -1), j, 2)
    fast = (seqs, n_ctx, n_fsdp, lax.axis_size("dp")) == (2, 4, 2, 4)
    small_local = jnp.concatenate(
        [gain_attn, shift_attn, gain_ffn, shift_ffn, bias_out, bias_proj, bias_qkv, bias_fc]
    )
    part_width = width // n_fsdp
    length = pick(lengths, s)
    rope = rope_tables(total, head_size)
    own_part = lambda v, size=part_width: lax.dynamic_slice_in_dim(v, f * size, size)
    if fast:
        return fast_block(
            residual_in,
            lengths,
            cotangent,
            (weight_fc, weight_proj, weight_qkv, weight_out),
            (gain_attn, shift_attn, gain_ffn, shift_ffn, bias_out, bias_proj, bias_qkv, bias_fc),
            rope,
        )
    small = lax.all_gather(small_local, "fsdp", axis=0)
    vec = lambda at, size: small[:, at : at + size].reshape(-1).astype(f32)
    gain_one, shift_one, gain_two, shift_two, b_out, b_proj = (
        vec(i * part_width, part_width) for i in range(6)
    )
    b_qkv = vec(6 * part_width, 3 * part_width)
    b_fc = vec(9 * part_width, units // n_fsdp)

    fc_local = pick(weight_fc.reshape(rows_here, n_fsdp, parts, -1), j, 2).reshape(rows_here, -1)
    proj_local = pick(weight_proj.reshape(parts, -1, width), j)
    qkv_local = pick(weight_qkv.reshape(rows_here, 3, n_h, parts, -1), j, 3).reshape(rows_here, -1)
    seq_in = gather_sequence(residual_in, place, parts)
    w_fc = gather_rows(fc_local, place).reshape(width, -1)
    w_proj = gather_rows(proj_local, place).reshape(-1, width)
    seq_grad = gather_sequence(cotangent, place, parts)
    w_qkv = gather_rows(qkv_local, place).reshape(width, -1)
    if spread_heads:
        w_out = gather_rows(pick(weight_out.reshape(parts, -1, width), j), place).reshape(-1, width)
    else:
        w_out = lax.all_gather(weight_out, "fsdp", axis=0, tiled=True)
        w_out = pick(w_out.reshape(parts, -1, width), j)
    b_qkv_j = own_heads(b_qkv).reshape(3, 1, inner)
    b_fc_j = pick(b_fc.reshape(n_fsdp, parts, -1), j, 1).reshape(1, -1)
    b_fc_j = jnp.broadcast_to(b_fc_j, (8, b_fc_j.shape[1]))

    positions = jnp.arange(total, dtype=jnp.int32)
    seq_grad = jnp.where((positions < length)[:, None], seq_grad, jnp.zeros((), bf16))
    xhat, _ = normalize(seq_in.astype(f32))
    hidden_one = (xhat * gain_one + shift_one).astype(bf16)
    hidden_two = (xhat * gain_two + shift_two).astype(bf16)

    ffn_out, ffn_dh, g_fc, g_proj, g_bfc = ffn_branch(
        hidden_two, seq_grad, w_fc, w_proj, b_fc_j
    )
    ffn_sums = (jnp.sum(ffn_dh * xhat, axis=0), jnp.sum(ffn_dh, axis=0))
    own_grad = jnp.sum(seq_grad.astype(f32), axis=0) / parts
    attn_out, attn_dh, g_qkv, g_out, g_bqkv = attention_branch(
        length[None],
        hidden_one,
        seq_grad,
        w_qkv,
        w_out,
        jnp.broadcast_to(b_qkv_j, (3, 8, inner)),
        jnp.tile(rope, (1, 1, LANES // 128)),
    )
    g_bqkv_all = jnp.zeros((3, n_h, parts, inner // n_h), f32)
    g_bqkv_all = lax.dynamic_update_index_in_dim(
        g_bqkv_all, g_bqkv[:, 0].reshape(3, n_h, -1), j, 2
    )
    g_bfc_all = jnp.zeros((n_fsdp, parts, units // (n_fsdp * parts)), f32)
    g_bfc_all = lax.dynamic_update_index_in_dim(g_bfc_all, g_bfc[0].reshape(n_fsdp, -1), j, 1)
    rows_of = (
        jnp.sum(attn_dh * xhat, axis=0),
        jnp.sum(attn_dh, axis=0),
        *ffn_sums,
        own_grad,
        g_bqkv_all.reshape(-1),
        g_bfc_all.reshape(-1),
    )
    flat = sum_everywhere(jnp.concatenate(rows_of).reshape(-1, 128)).reshape(-1)
    small_grads = []
    at = 0
    for entry in rows_of:
        size = entry.shape[0]
        small_grads.append(own_part(flat[at : at + size], size // n_fsdp))
        at += size
    d_gain_one, d_shift_one, d_gain_two, d_shift_two, d_bias, d_bqkv, d_bfc = small_grads
    branch_part = (attn_out + ffn_out).astype(bf16)
    pull_part = (attn_dh * gain_one + ffn_dh * gain_two).astype(bf16)
    d_proj = reduce_rows(g_proj.reshape(n_fsdp, -1, width), place, parts)
    d_fc = reduce_rows(g_fc.reshape(n_fsdp, rows_here, -1), place, parts)
    q_rows = jnp.swapaxes(g_qkv.reshape(3, n_fsdp, rows_here, inner), 0, 1)
    q_rows = jnp.swapaxes(q_rows, 1, 2).reshape(n_fsdp, rows_here, 3 * inner)
    d_qkv = reduce_rows(q_rows, place, parts)
    d_proj = jnp.swapaxes(d_proj, 0, 1).reshape(weight_proj.shape)
    d_fc = d_fc.reshape(rows_here, parts, n_fsdp, -1)
    d_fc = jnp.swapaxes(d_fc, 1, 2).reshape(weight_fc.shape)
    d_qkv = d_qkv.reshape(rows_here, parts, 3, n_h, -1)
    d_qkv = jnp.transpose(d_qkv, (0, 2, 3, 1, 4)).reshape(weight_qkv.shape)
    if spread_heads:
        d_out = reduce_rows(g_out.reshape(n_fsdp, -1, width), place, parts)
        d_out = jnp.swapaxes(d_out, 0, 1).reshape(weight_out.shape)
    else:
        full = jnp.zeros((parts, inner, width), bf16)
        full = lax.dynamic_update_index_in_dim(full, g_out, j, 0).reshape(width, width)
        d_out = lax.psum_scatter(full, "fsdp", scatter_dimension=0, tiled=True)
        d_out = lax.psum(d_out, ("dp", "ctx")).astype(f32)
    branch = return_blocks(branch_part, place, parts, seqs)
    pulled = return_blocks(pull_part, place, parts, seqs)

    residual_out, residual_grad = finish(
        residual_in, cotangent, lengths, c * block_rows, branch, pulled, b_out + b_proj
    )
    return (
        residual_out,
        residual_grad,
        d_gain_one,
        d_shift_one,
        d_qkv,
        d_bqkv,
        d_out,
        d_bias,
        d_gain_two,
        d_shift_two,
        d_fc,
        d_bfc,
        d_proj,
        d_bias,
    )


def solution(mesh):
    tokens = P(("dp", "fsdp"), "ctx", None)
    vector, matrix = P("fsdp"), P("fsdp", None)
    return jax.shard_map(
        per_device,
        mesh=mesh,
        in_specs=(
            tokens,
            P(("dp", "fsdp")),
            vector,
            vector,
            matrix,
            vector,
            matrix,
            vector,
            vector,
            vector,
            matrix,
            vector,
            matrix,
            vector,
            tokens,
        ),
        out_specs=(
            tokens,
            tokens,
            vector,
            vector,
            matrix,
            vector,
            matrix,
            vector,
            vector,
            vector,
            matrix,
            vector,
            matrix,
            vector,
        ),
        check_vma=False,
    )
```

```python
import functools
import math

import jax
import jax.numpy as jnp
import numpy as np
from jax import lax
from jax.experimental import pallas as pl
from jax.experimental.pallas import tpu as pltpu
from jax.sharding import PartitionSpec as P

HEADS = 16
ROT = 16
LANES = 256
ROWS = 256

epsilon = 1e-05
rope_base = 10000.0
masked_score = -1e30

f32 = jnp.float32
bf16 = jnp.bfloat16


def dot_nn(a, b):
    return lax.dot_general(a, b, (((1,), (0,)), ((), ())), preferred_element_type=f32)


def dot_nt(a, b):
    return lax.dot_general(a, b, (((1,), (1,)), ((), ())), preferred_element_type=f32)


def attn_kernel(
    length_ref,
    h_ref,
    dy_ref,
    wq_ref,
    wk_ref,
    wv_ref,
    wo_ref,
    b_ref,
    rope_ref,
    out_ref,
    dh_ref,
    gqkv_ref,
    gout_ref,
    gb_ref,
    ht_s,
    q_s,
    k_s,
    v_s,
    do_s,
    kt_s,
    vt_s,
    dot_s,
    ot_s,
    dqt_s,
    dk_s,
    dv_s,
    p_s,
    kb_s,
):
    group = pl.program_id(0)
    total, width = h_ref.shape
    blocks = total // ROWS
    head_size = 64
    heads_here = LANES // head_size
    length = length_ref[0]

    @pl.when(group == 0)
    def _():
        for r in range(blocks):
            ht_s[:, r * ROWS : (r + 1) * ROWS] = h_ref[r * ROWS : (r + 1) * ROWS, :].T
        key_pos = lax.broadcasted_iota(jnp.int32, (total, 128), 0)
        kb_s[...] = jnp.where(key_pos < length, 0.0, masked_score)

    def turn(v, rows):
        left = pltpu.roll(v, LANES - ROT // 2, 1)
        right = pltpu.roll(v, ROT // 2, 1)
        return v * rope_ref[0, rows, :] + left * rope_ref[1, rows, :] + right * rope_ref[2, rows, :]

    def turn_back(v, rows):
        left = pltpu.roll(v, LANES - ROT // 2, 1)
        right = pltpu.roll(v, ROT // 2, 1)
        return v * rope_ref[0, rows, :] - left * rope_ref[1, rows, :] - right * rope_ref[2, rows, :]

    for r in range(blocks):
        rows = slice(r * ROWS, (r + 1) * ROWS)
        hr = h_ref[rows, :]
        q = turn(dot_nn(hr, wq_ref[...]) + b_ref[0, 0:1, :], rows).astype(bf16)
        q_s[rows, :] = (q.astype(f32) * 0.125).astype(bf16)
        k = turn(dot_nn(hr, wk_ref[...]) + b_ref[1, 0:1, :], rows).astype(bf16)
        k_s[rows, :] = k
        kt_s[:, rows] = k.T
        v = (dot_nn(hr, wv_ref[...]) + b_ref[2, 0:1, :]).astype(bf16)
        v_s[rows, :] = v
        vt_s[:, rows] = v.T
        do = dot_nt(dy_ref[rows, :], wo_ref[...]).astype(bf16)
        do_s[rows, :] = do
        dot_s[:, rows] = do.T

    dk_s[...] = jnp.zeros_like(dk_s)
    dv_s[...] = jnp.zeros_like(dv_s)
    lane = lax.broadcasted_iota(jnp.int32, (ROWS, LANES), 1)
    causal = lax.broadcasted_iota(jnp.int32, (ROWS, ROWS), 0) <= lax.broadcasted_iota(
        jnp.int32, (ROWS, ROWS), 1
    )

    def one_head(head, carry):
        feats = pl.ds(pl.multiple_of(head * head_size, head_size), head_size)
        mine = (lane // head_size) == head
        zero = jnp.zeros((ROWS, LANES), bf16)
        for i in range(blocks):
            rows = slice(i * ROWS, (i + 1) * ROWS)
            qm = jnp.where(mine, q_s[rows, :], zero)
            dom = jnp.where(mine, do_s[rows, :], zero)
            scores = []
            top = None
            for b in range(i + 1):
                keys = slice(b * ROWS, (b + 1) * ROWS)
                sc = dot_nt(k_s[keys, :], qm)
                kb = kb_s[keys, :]
                sc = sc + jnp.concatenate([kb, kb], axis=1)
                if b == i:
                    sc = jnp.where(causal, sc, masked_score)
                best = jnp.max(sc, axis=0, keepdims=True)
                top = best if top is None else jnp.maximum(top, best)
                scores.append(sc)
            row_sum = None
            for b in range(i + 1):
                scores[b] = jnp.exp(scores[b] - top)
                part = jnp.sum(scores[b], axis=0, keepdims=True)
                row_sum = part if row_sum is None else row_sum + part
            inverse = 1.0 / row_sum
            o_t = None
            for b in range(i + 1):
                keys = slice(b * ROWS, (b + 1) * ROWS)
                scores[b] = scores[b] * inverse
                low = scores[b].astype(bf16)
                dv_s[keys, :] += dot_nn(low, dom)
                part = dot_nn(vt_s[feats, keys], low)
                o_t = part if o_t is None else o_t + part
            ot_s[feats, rows] = o_t
            delta = jnp.sum(dot_s[feats, rows].astype(f32) * o_t, axis=0, keepdims=True)
            dq_t = None
            for b in range(i + 1):
                keys = slice(b * ROWS, (b + 1) * ROWS)
                dp = dot_nt(v_s[keys, :], dom)
                ds = (scores[b] * (dp - delta)).astype(bf16)
                dk_s[keys, :] += dot_nn(ds, qm)
                part = dot_nn(kt_s[feats, keys], ds)
                dq_t = part if dq_t is None else dq_t + part
            dqt_s[feats, rows] = dq_t * 0.125
        return carry

    lax.fori_loop(0, heads_here, one_head, 0)

    sums = [jnp.zeros((1, LANES), f32) for _ in range(3)]
    for r in range(blocks):
        rows = slice(r * ROWS, (r + 1) * ROWS)
        dq = turn_back(dqt_s[:, rows].T, rows).astype(bf16)
        dk = turn_back(dk_s[rows, :], rows).astype(bf16)
        dv = dv_s[rows, :].astype(bf16)
        for at, grad in enumerate((dq, dk, dv)):
            sums[at] = sums[at] + jnp.sum(grad.astype(f32), axis=0, keepdims=True)
            p_s[at, rows, :] = grad
        o = ot_s[:, rows].T.astype(bf16)
        out_part = dot_nn(o, wo_ref[...])
        dh_part = (
            dot_nt(dq, wq_ref[...]) + dot_nt(dk, wk_ref[...]) + dot_nt(dv, wv_ref[...])
        )

        @pl.when(group == 0)
        def _():
            out_ref[rows, :] = out_part
            dh_ref[rows, :] = dh_part

        @pl.when(group > 0)
        def _():
            out_ref[rows, :] += out_part
            dh_ref[rows, :] += dh_part

    for at in range(3):
        gb_ref[at] = jnp.broadcast_to(sums[at], (8, LANES))
        for r in range(width // ROWS):
            rows = slice(r * ROWS, (r + 1) * ROWS)
            gqkv_ref[at, rows, :] = dot_nn(ht_s[rows, :], p_s[at]).astype(bf16)
    gout_ref[...] = dot_nn(ot_s[...].astype(bf16), dy_ref[...]).astype(bf16)


def attention_branch(length, hidden, out_grad, w_qkv, w_out, b_qkv, rope):
    total, width = hidden.shape
    inner = w_out.shape[0]
    groups = inner // LANES
    whole = lambda g: (0, 0)
    flops = 2 * total * width * inner * 12 + 2 * groups * 4 * total * total * LANES * 4
    return pl.pallas_call(
        attn_kernel,
        grid=(groups,),
        in_specs=[
            pl.BlockSpec(memory_space=pltpu.SMEM),
            pl.BlockSpec((total, width), whole),
            pl.BlockSpec((total, width), whole),
            pl.BlockSpec((width, LANES), lambda g: (0, g)),
            pl.BlockSpec((width, LANES), lambda g: (0, groups + g)),
            pl.BlockSpec((width, LANES), lambda g: (0, 2 * groups + g)),
            pl.BlockSpec((LANES, width), lambda g: (g, 0)),
            pl.BlockSpec((3, 8, LANES), lambda g: (0, 0, g)),
            pl.BlockSpec((3, total, LANES), lambda g: (0, 0, 0)),
        ],
        out_specs=[
            pl.BlockSpec((total, width), whole),
            pl.BlockSpec((total, width), whole),
            pl.BlockSpec((3, width, LANES), lambda g: (0, 0, g)),
            pl.BlockSpec((LANES, width), lambda g: (g, 0)),
            pl.BlockSpec((3, 8, LANES), lambda g: (0, 0, g)),
        ],
        out_shape=[
            jax.ShapeDtypeStruct((total, width), f32),
            jax.ShapeDtypeStruct((total, width), f32),
            jax.ShapeDtypeStruct((3, width, inner), bf16),
            jax.ShapeDtypeStruct((inner, width), bf16),
            jax.ShapeDtypeStruct((3, 8, inner), f32),
        ],
        scratch_shapes=[
            pltpu.VMEM((width, total), bf16),
            pltpu.VMEM((total, LANES), bf16),
            pltpu.VMEM((total, LANES), bf16),
            pltpu.VMEM((total, LANES), bf16),
            pltpu.VMEM((total, LANES), bf16),
            pltpu.VMEM((LANES, total), bf16),
            pltpu.VMEM((LANES, total), bf16),
            pltpu.VMEM((LANES, total), bf16),
            pltpu.VMEM((LANES, total), f32),
            pltpu.VMEM((LANES, total), f32),
            pltpu.VMEM((total, LANES), f32),
            pltpu.VMEM((total, LANES), f32),
            pltpu.VMEM((3, total, LANES), bf16),
            pltpu.VMEM((total, 128), f32),
        ],
        compiler_params=pltpu.CompilerParams(vmem_limit_bytes=60 * 2**20),
        cost_estimate=pl.CostEstimate(
            flops=flops, bytes_accessed=24 * 2**20, transcendentals=8 * total * total
        ),
        name="attention",
    )(length, hidden, out_grad, w_qkv, w_qkv, w_qkv, w_out, b_qkv, rope)


def ffn_kernel(
    h_ref,
    dy_ref,
    wf_ref,
    wp_ref,
    b_ref,
    out_ref,
    dh_ref,
    gf_ref,
    gp_ref,
    gb_ref,
    ht_s,
    act_s,
    dup_s,
):
    step = pl.program_id(0)
    total, width = h_ref.shape
    blocks = total // ROWS
    chunk = wf_ref.shape[1]

    @pl.when(step == 0)
    def _():
        for r in range(blocks):
            ht_s[:, r * ROWS : (r + 1) * ROWS] = h_ref[r * ROWS : (r + 1) * ROWS, :].T

    def one(r, total_grad):
        rows = pl.ds(pl.multiple_of(r * ROWS, ROWS), ROWS)
        up = dot_nn(h_ref[rows, :], wf_ref[...]) + b_ref[0:1, :]
        half = 0.5 + 0.5 * lax.erf(up * (1.0 / math.sqrt(2.0)))
        act = (up * half).astype(bf16)
        slope = half + up * (jnp.exp(-0.5 * up * up) * (1.0 / math.sqrt(2.0 * math.pi)))
        act_grad = dot_nt(dy_ref[rows, :], wp_ref[...])
        up_grad = (slope * act_grad).astype(bf16)
        act_s[rows, :] = act
        dup_s[rows, :] = up_grad
        out_part = dot_nn(act, wp_ref[...])
        dh_part = dot_nt(up_grad, wf_ref[...])

        @pl.when(step == 0)
        def _():
            out_ref[rows, :] = out_part
            dh_ref[rows, :] = dh_part

        @pl.when(step > 0)
        def _():
            out_ref[rows, :] += out_part
            dh_ref[rows, :] += dh_part

        return total_grad + jnp.sum(up_grad.astype(f32), axis=0, keepdims=True)

    sums = lax.fori_loop(0, blocks, one, jnp.zeros((1, chunk), f32))
    gb_ref[...] = jnp.broadcast_to(sums, (8, chunk))
    for r in range(8):
        size = width // 8
        rows = slice(r * size, (r + 1) * size)
        grad = dot_nn(ht_s[rows, :], dup_s[...]).astype(bf16)
        gf_ref[rows, :] = grad
    for r in range(chunk // ROWS):
        cols = slice(r * ROWS, (r + 1) * ROWS)
        grad = dot_nn(act_s[:, cols].T, dy_ref[...]).astype(bf16)
        gp_ref[cols, :] = grad


def ffn_branch(hidden, out_grad, w_fc, w_proj, b_fc):
    total, width = hidden.shape
    units = w_proj.shape[0]
    chunk = min(512, units)
    whole = lambda s: (0, 0)
    return pl.pallas_call(
        ffn_kernel,
        grid=(units // chunk,),
        in_specs=[
            pl.BlockSpec((total, width), whole),
            pl.BlockSpec((total, width), whole),
            pl.BlockSpec((width, chunk), lambda s: (0, s)),
            pl.BlockSpec((chunk, width), lambda s: (s, 0)),
            pl.BlockSpec((8, chunk), lambda s: (0, s)),
        ],
        out_specs=[
            pl.BlockSpec((total, width), whole),
            pl.BlockSpec((total, width), whole),
            pl.BlockSpec((width, chunk), lambda s: (0, s)),
            pl.BlockSpec((chunk, width), lambda s: (s, 0)),
            pl.BlockSpec((8, chunk), lambda s: (0, s)),
        ],
        out_shape=[
            jax.ShapeDtypeStruct((total, width), f32),
            jax.ShapeDtypeStruct((total, width), f32),
            jax.ShapeDtypeStruct((width, units), bf16),
            jax.ShapeDtypeStruct((units, width), bf16),
            jax.ShapeDtypeStruct((8, units), f32),
        ],
        scratch_shapes=[
            pltpu.VMEM((width, total), bf16),
            pltpu.VMEM((total, chunk), bf16),
            pltpu.VMEM((total, chunk), bf16),
        ],
        compiler_params=pltpu.CompilerParams(vmem_limit_bytes=60 * 2**20),
        cost_estimate=pl.CostEstimate(
            flops=2 * total * width * units * 6,
            bytes_accessed=28 * 2**20,
            transcendentals=2 * total * units,
        ),
        name="feed_forward",
    )(hidden, out_grad, w_fc, w_proj, b_fc)


def shift(block, axis, distance):
    count = lax.axis_size(axis)
    return lax.ppermute(block, axis, [(i, (i + distance) % count) for i in range(count)])


def swap_bit(block, axis, bit):
    return lax.ppermute(block, axis, [(i, i ^ bit) for i in range(lax.axis_size(axis))])


def shift_within(block, axis, size, distance):
    count = lax.axis_size(axis)
    return lax.ppermute(
        block,
        axis,
        [(i, i // size * size + (i % size + distance) % size) for i in range(count)],
    )


def pick(array, index, axis=0):
    return lax.dynamic_index_in_dim(array, index, axis, keepdims=False)


def order_two(flag, mine, other):
    first = flag == 0
    return jnp.stack([jnp.where(first, mine, other), jnp.where(first, other, mine)])


def gather_rows(local, place):
    dp, y, core, f = place["dp"], place["y"], place["core"], place["f"]
    count = lax.axis_size("fsdp")
    rows, cols = local.shape
    share = rows // lax.axis_size("dp")
    mine = lax.dynamic_slice_in_dim(local, dp * share, share, 0)
    got = jnp.stack([shift(mine, "fsdp", e) for e in range(1, count)])
    got = order_two(y, got, swap_bit(got, "dp", 2))
    got = order_two(core, got, swap_bit(got, "dp", 1))
    got = jnp.transpose(got, (2, 1, 0, 3, 4)).reshape(count - 1, rows, cols)
    if count == 2:
        return order_two(f, local, got[0])
    whole = jnp.zeros((count, rows, cols), local.dtype)
    whole = lax.dynamic_update_index_in_dim(whole, local, f, 0)
    for e in range(1, count):
        whole = lax.dynamic_update_index_in_dim(whole, got[e - 1], (f - e) % count, 0)
    return whole


def reduce_rows(partial, place, parts):
    dp, y, core, f, j = (place[k] for k in ("dp", "y", "core", "f", "j"))
    count, rows, cols = partial.shape
    share = rows // 4
    a = partial.reshape(count, 2, 2, share, cols)
    a = pick(a, core, 2) + swap_bit(pick(a, 1 - core, 2), "dp", 1)
    total = pick(a, f)
    for e in range(1, count):
        total = total + shift(pick(a, (f + e) % count), "fsdp", e)
    total = pick(total, y) + swap_bit(pick(total, 1 - y), "dp", 2)
    total = total + shift(total, "ctx", parts)
    if parts == 2:
        both = order_two(j, total, shift_within(total, "ctx", 2, 1))
    else:
        both = jnp.zeros((parts,) + total.shape, total.dtype)
        both = lax.dynamic_update_index_in_dim(both, total, j, 0)
        for e in range(1, parts):
            got = shift_within(total, "ctx", parts, e)
            both = lax.dynamic_update_index_in_dim(both, got, (j - e) % parts, 0)
    both = order_two(y, both, swap_bit(both, "dp", 2))
    both = order_two(core, both, swap_bit(both, "dp", 1))
    return jnp.transpose(both, (1, 0, 3, 2, 4)).reshape(rows, parts, cols).astype(f32)


def sum_everywhere(vector):
    for bit in (1, 2):
        vector = vector + swap_bit(vector, "dp", bit)
    for axis in ("fsdp", "ctx"):
        bit = 1
        while bit < lax.axis_size(axis):
            vector = vector + swap_bit(vector, axis, bit)
            bit *= 2
    return vector


def gather_sequence(blocks, place, parts):
    s, c = place["s"], place["c"]
    count = lax.axis_size("ctx")
    seqs, rows, width = blocks.shape
    pieces = [(c, pick(blocks, s))]
    for d in range(1, seqs):
        got = shift(pick(blocks, (s + d) % seqs), "ctx", d * parts)
        pieces.append(((c - d * parts) % count, got))
    arrived = []
    for d in range(seqs):
        arrived.append(pieces[d])
        for e in range(1, parts):
            source = s * parts + (place["j"] - e) % parts
            got = shift_within(pieces[d][1], "ctx", parts, e)
            arrived.append(((source - d * parts) % count, got))
    whole = jnp.zeros((count, rows, width), blocks.dtype)
    for at, piece in arrived:
        whole = lax.dynamic_update_index_in_dim(whole, piece, at, 0)
    return whole.reshape(count * rows, width)


def return_blocks(partial, place, parts, seqs):
    s, c, j = place["s"], place["c"], place["j"]
    count = lax.axis_size("ctx")
    rows = partial.shape[0] // count
    blocks = partial.reshape(seqs, parts, rows, -1)
    total = pick(blocks, j, 1).astype(f32)
    for e in range(1, parts):
        total = total + shift_within(pick(blocks, (j + e) % parts, 1), "ctx", parts, e).astype(f32)
    mine = [pick(total, s)]
    for d in range(1, seqs):
        mine.append(shift(pick(total, (s + d) % seqs).astype(bf16), "ctx", d * parts).astype(f32))
    if seqs == 2:
        return order_two(s, mine[0], mine[1])
    whole = jnp.zeros((seqs, rows, partial.shape[1]), f32)
    for d in range(seqs):
        whole = lax.dynamic_update_index_in_dim(whole, mine[d], (s - d) % seqs, 0)
    return whole


class Mover:
    def __init__(self, send, recv, local):
        self.send, self.recv, self.local = send, recv, local
        self.copies, self.left, self.started = [], [], 0

    def to(self, src, dst, axis, index):
        copy = self.remote(src, dst, len(self.copies), (axis, index))
        copy.start()
        self.copies.append(copy)
        return copy

    def here(self, src, dst):
        copy = pltpu.make_async_copy(src, dst, self.local.at[self.started])
        self.started += 1
        copy.start()
        return copy

    def out(self, src, dst):
        self.left.append(self.here(src, dst))

    def remote(self, src, dst, slot, to):
        return pltpu.make_async_remote_copy(
            src_ref=src,
            dst_ref=dst,
            send_sem=self.send.at[slot],
            recv_sem=self.recv.at[slot],
            device_id={to[0]: to[1]},
            device_id_type=pl.DeviceIdType.MESH,
        )

    def stay(self, src, dst, slot):
        return pltpu.make_async_copy(src, dst, self.local.at[slot])

    def finish(self):
        for copy in self.copies:
            copy.wait_send()
        for copy in self.left:
            copy.wait()


class Spot:
    def __init__(self):
        self.dp, self.c, self.f = (lax.axis_index(a) for a in ("dp", "ctx", "fsdp"))
        self.y, self.core = self.dp // 2, self.dp % 2
        self.s, self.j = self.c // 2, self.c % 2
        flip = lambda v: v + 1 - 2 * (v % 2)
        self.x_to = ("fsdp", 1 - self.f)
        self.y_to = ("dp", (1 - self.y) * 2 + self.core)
        self.core_to = ("dp", flip(self.dp))
        self.pair_to = ("ctx", flip(self.c))
        self.far_to = ("ctx", (1 - self.s) * 2 + self.j)

    def greet(self):
        barrier = pltpu.get_barrier_semaphore()
        partners = (self.x_to, self.y_to, self.core_to, self.pair_to, self.far_to)
        for axis, index in partners:
            pl.semaphore_signal(
                barrier, inc=1, device_id={axis: index}, device_id_type=pl.DeviceIdType.MESH
            )
        pl.semaphore_wait(barrier, len(partners))


def block(index, size):
    return pl.ds(pl.multiple_of(index * size, size), size)


def front_kernel(
    info_ref,
    x_ref,
    cot_ref,
    fc_ref,
    proj_ref,
    qkv_ref,
    out_ref,
    rope_ref,
    *rest,
):
    vector_refs, rest = rest[:8], rest[8:]
    (
        seq_in,
        seq_grad,
        w_qkv,
        w_out,
        pull,
        home,
        gp,
        gf,
        part,
        vectors,
        x_s,
        dy_s,
        cot_s,
        held_s,
        small_s,
        wf_s,
        wp_s,
        wq_s,
        wo_s,
        h_s,
        ht_s,
        act_s,
        dup_s,
        rope_s,
        q_s,
        k_s,
        vt_s,
        o_s,
        ot_s,
        kb_s,
        home_s,
        got_s,
        pull_s,
        gp_s,
        gf_s,
        core_got,
        x_got,
        vec_s,
        bfc_s,
        part_s,
        send,
        recv,
        local,
    ) = rest
    at = Spot()
    mover = Mover(send, recv, local)
    total, width = x_s.shape
    blocks = total // ROWS
    units = wp_s.shape[0]
    inner = wo_s.shape[0]
    head_size = 64
    length = jnp.where(at.s == 0, info_ref[0], info_ref[1])
    other = 1 - at.f
    far_c, pair_c = at.far_to[1], at.pair_to[1]
    last_c = (1 - at.s) * 2 + 1 - at.j

    load_x = mover.here(x_ref.at[at.s], x_s.at[block(at.c, ROWS)])
    load_cot = mover.here(cot_ref, cot_s)
    held_s[...] = jnp.zeros_like(held_s)
    row = 0
    for ref in vector_refs:
        size = small_s.shape[2]
        vector = ref[...].astype(f32).reshape(1, ref.shape[0])
        for start in range(0, ref.shape[0], size):
            held_s[row : row + 1, :] = vector[:, start : start + size]
            row += 1
    small_s[at.f] = held_s[...]
    load_rope = mover.here(rope_ref, rope_s)
    at.greet()

    small_copy = mover.to(held_s, small_s.at[at.f], *at.x_to)
    x_far = mover.to(x_ref.at[1 - at.s], x_s.at[block(at.c, ROWS)], *at.far_to)
    x_near = mover.to(x_ref.at[at.s], x_s.at[block(at.c, ROWS)], *at.pair_to)

    def fc_spans(k):
        size = units // 2
        return lambda r: [(fc_ref.at[r, block(2 * k + at.j, size)], pl.ds(0, size))]

    def qkv_spans(r):
        size = wq_s.shape[1] // 12
        return [
            (
                qkv_ref.at[r, block(t * 8 + h * 4 + at.j * 2 + g, size)],
                pl.ds((t * 4 + g * 2 + h) * size, size),
            )
            for t in range(3)
            for g in range(2)
            for h in range(2)
        ]

    def row_spans(ref, held):
        count = held.shape[0] // 2

        def spans(r):
            start = pl.multiple_of(at.j * count + r.start, r.size)
            return [(ref.at[pl.ds(start, r.size)], pl.ds(0, width))]

        return spans

    weights = dict(
        fc0=(wf_s.at[:, pl.ds(0, units // 2)], fc_spans(0)),
        fc1=(wf_s.at[:, pl.ds(units // 2, units // 2)], fc_spans(1)),
        qkv=(wq_s, qkv_spans),
        out=(wo_s, row_spans(out_ref, wo_s)),
        proj=(wp_s, row_spans(proj_ref, wp_s)),
    )
    got_x, got_y, got_core, stays = {}, {}, {}, {}

    def send_x(name):
        held, spans = weights[name]
        count = held.shape[0] // 2
        share = count // 4
        mine = pl.ds(pl.multiple_of(at.dp * share, share), share)
        there = pl.ds(pl.multiple_of(at.f * count + at.dp * share, share), share)
        got_x[name] = [mover.to(src, held.at[there, cols], *at.x_to) for src, cols in spans(mine)]

    def keep(name):
        held, spans = weights[name]
        count = held.shape[0] // 2
        there = block(at.f, count)
        stays[name] = [
            mover.here(src, held.at[there, cols]) for src, cols in spans(pl.ds(0, count))
        ]

    def quarter(name, dp):
        held = weights[name][0]
        count = held.shape[0] // 2
        share = count // 4
        return held.at[pl.ds(pl.multiple_of(other * count + dp * share, share), share)]

    def pass_x(name):
        for copy in got_x[name]:
            copy.wait_recv()
        mine = quarter(name, at.dp)
        got_y[name] = mover.to(mine, mine, *at.y_to)
        got_core[name] = [mover.to(mine, mine, *at.core_to)]

    def pass_y(name):
        got_y[name].wait_recv()
        mine = quarter(name, at.y_to[1])
        got_core[name].append(mover.to(mine, mine, *at.core_to))

    def arrived(name):
        for copy in got_core[name]:
            copy.wait_recv()
        for copy in stays[name]:
            copy.wait()

    send_x("fc0")
    for name in weights:
        keep(name)

    small_copy.wait_recv()

    def line(shard, r):
        return small_s[shard, r : r + 1, :]

    def joined(r):
        return jnp.concatenate([line(0, r), line(1, r)], axis=1)

    first = at.j == 0
    vec_s[...] = jnp.zeros_like(vec_s)
    part_s[...] = jnp.zeros_like(part_s)
    size = LANES // 2
    for t in range(3):
        for h in range(2):
            row = line((t * 2 + h) // 3, 6 + (t * 2 + h) % 3)
            row = jnp.where(first, row[:, :LANES], row[:, LANES:])
            for g in range(2):
                to = g * LANES + h * size
                vec_s[t : t + 1, to : to + size] = row[:, g * size : (g + 1) * size]
    vec_s[3:4, :] = joined(0)
    vec_s[4:5, :] = joined(1)
    vec_s[5:6, :] = joined(4) + joined(5)
    for h in range(2):
        for n in range(2):
            to = h * units // 2 + n * 512
            bfc_s[0:1, to : to + 512] = jnp.where(first, line(h, 9 + n), line(h, 11 + n))
    gain_one, shift_one = vec_s[3:4, :], vec_s[4:5, :]
    gain_two, shift_two = joined(2), joined(3)
    bfc_s[1:2, :width] = gain_two
    mover.out(vec_s, vectors)

    def normal(rows):
        v = x_s[rows, :].astype(f32)
        center = v - jnp.mean(v, axis=-1, keepdims=True)
        spread = jnp.mean(center * center, axis=-1, keepdims=True)
        return center * lax.rsqrt(spread + epsilon)

    def arrive(c):
        rows = block(c, ROWS)
        h = (normal(rows) * gain_two + shift_two).astype(bf16)
        h_s[rows, :] = h
        ht_s[:, rows] = h.T

    load_x.wait()
    arrive(at.c)
    load_cot.wait()
    for t in range(2):
        pos = at.c * ROWS + lax.broadcasted_iota(jnp.int32, (ROWS, width), 0)
        cot_s[t] = jnp.where(pos < info_ref[t], cot_s[t].astype(f32), 0.0).astype(bf16)
    dy_s[block(at.c, ROWS), :] = cot_s[at.s]
    pass_x("fc0")
    send_x("fc1")
    pass_x("fc1")
    send_x("qkv")
    pass_y("fc0")

    def span(b):
        return slice(b * ROWS, (b + 1) * ROWS)

    chunk = 512

    def forward(c, half):
        rows = block(c, ROWS)
        steps = units // chunk // 2

        def one(q, carry):
            cols = block(q, chunk)
            up = dot_nn(h_s[rows, :], wf_s[:, cols]) + bfc_s[0:1, cols]
            part = 0.5 + 0.5 * lax.erf(up * (1.0 / math.sqrt(2.0)))
            act_s[rows, cols] = (up * part).astype(bf16)
            slope = part + up * (jnp.exp(-0.5 * up * up) * (1.0 / math.sqrt(2.0 * math.pi)))
            dup_s[rows, cols] = slope.astype(bf16)
            return carry

        lax.fori_loop(half * steps, (half + 1) * steps, one, 0, unroll=steps)

    arrived("fc0")
    forward(at.c, 0)
    pass_y("fc1")
    pass_x("qkv")
    send_x("out")
    x_far.wait_recv()
    mine = x_s.at[block(far_c, ROWS)]
    x_last = mover.to(mine, mine, *at.pair_to)
    grad_far = mover.to(cot_s.at[1 - at.s], dy_s.at[block(at.c, ROWS)], *at.far_to)
    arrive(far_c)
    x_near.wait_recv()
    arrive(pair_c)
    arrived("fc1")
    pass_x("out")
    send_x("proj")
    forward(at.c, 1)
    for c in (far_c, pair_c):
        forward(c, 0)
        forward(c, 1)
    x_last.wait_recv()
    grad_near = mover.to(cot_s.at[at.s], dy_s.at[block(at.c, ROWS)], *at.pair_to)
    arrive(last_c)
    pass_y("qkv")
    pass_y("out")
    forward(last_c, 0)
    forward(last_c, 1)
    mover.out(x_s, seq_in)
    arrived("qkv")
    arrived("out")
    mover.out(wq_s, w_qkv)
    mover.out(wo_s, w_out)

    load_rope.wait()

    def table(n, rows):
        piece = rope_s[n, rows, :]
        return jnp.concatenate([piece] * (inner // 128), axis=1)

    def turned(v, rows):
        left = pltpu.roll(v, inner - ROT // 2, 1)
        right = pltpu.roll(v, ROT // 2, 1)
        return v * table(0, rows) + left * table(1, rows) + right * table(2, rows)

    for r in range(blocks):
        rows = span(r)
        h = (normal(rows) * gain_one + shift_one).astype(bf16)
        q = turned(dot_nn(h, wq_s[:, :inner]) + vec_s[0:1, :inner], rows).astype(bf16)
        q_s[rows, :] = (q.astype(f32) * 0.125).astype(bf16)
        k = dot_nn(h, wq_s[:, inner : 2 * inner]) + vec_s[1:2, :inner]
        k_s[rows, :] = turned(k, rows).astype(bf16)
        v = dot_nn(h, wq_s[:, 2 * inner :]) + vec_s[2:3, :inner]
        vt_s[:, rows] = v.astype(bf16).T
    pass_x("proj")
    grad_far.wait_recv()
    mine = dy_s.at[block(far_c, ROWS)]
    grad_last = mover.to(mine, mine, *at.pair_to)
    key_pos = lax.broadcasted_iota(jnp.int32, (total, 128), 0)
    kb_s[...] = jnp.where(key_pos < length, 0.0, masked_score)
    lane = lax.broadcasted_iota(jnp.int32, (ROWS, LANES), 1)
    causal = lax.broadcasted_iota(jnp.int32, (ROWS, ROWS), 0) <= lax.broadcasted_iota(
        jnp.int32, (ROWS, ROWS), 1
    )

    def one_head(g, i, head, carry):
        feats = pl.ds(pl.multiple_of(head * head_size, head_size), head_size)
        from_v = pl.ds(pl.multiple_of(g * LANES + head * head_size, head_size), head_size)
        cols = slice(g * LANES, (g + 1) * LANES)
        mine = (lane // head_size) == head
        qm = jnp.where(mine, q_s[span(i), cols], jnp.zeros((ROWS, LANES), bf16))
        scores = []
        top = None
        for b in range(i + 1):
            sc = dot_nt(k_s[span(b), cols], qm)
            kb = kb_s[span(b), :]
            sc = sc + jnp.concatenate([kb, kb], axis=1)
            if b == i:
                sc = jnp.where(causal, sc, masked_score)
            best = jnp.max(sc, axis=0, keepdims=True)
            top = best if top is None else jnp.maximum(top, best)
            scores.append(sc)
        row_sum = None
        o_t = None
        for b in range(i + 1):
            e = jnp.exp(scores[b] - top)
            add = jnp.sum(e, axis=0, keepdims=True)
            row_sum = add if row_sum is None else row_sum + add
            add = dot_nn(vt_s[from_v, span(b)], e.astype(bf16))
            o_t = add if o_t is None else o_t + add
        ot_s[feats, :] = o_t / row_sum
        return carry

    for i in range(blocks):
        for g in range(2):
            lax.fori_loop(0, LANES // head_size, functools.partial(one_head, g, i), 0, unroll=2)
            o = ot_s[...].T.astype(bf16)
            for h in range(2):
                to = h * LANES + g * size
                o_s[span(i), to : to + size] = o[:, h * size : (h + 1) * size]
        if i == 1:
            pass_y("proj")
    arrived("proj")
    for i in range(blocks):
        both = dot_nn(act_s[span(i), :], wp_s[...]) + dot_nn(o_s[span(i), :], wo_s[...])
        home_s[i] = both.astype(bf16)
    nears = [
        mover.to(home_s.at[2 * t + 1 - at.j], got_s.at[t], *at.pair_to) for t in range(2)
    ]

    grad_near.wait_recv()
    grad_last.wait_recv()
    mover.out(dy_s, seq_grad)
    bfc_s[2:3, :] = jnp.zeros((1, units), f32)
    for r in range(8):
        grad = dot_nn(act_s[:, r * ROWS : (r + 1) * ROWS].T, dy_s[...]).astype(bf16)
        for k in range(2):
            gp_s[k, r % 2, r // 4, r // 2 % 2] = grad[k * ROWS // 2 : (k + 1) * ROWS // 2]
    to_core = [mover.to(gp_s.at[k, 1 - at.core], core_got.at[k], *at.core_to) for k in range(2)]
    to_x = []

    def step_core(k):
        to_core[k].wait_recv()
        own, got = gp_s.at[k, at.core], core_got.at[k]
        own[1 - at.f] = own[1 - at.f] + got[1 - at.f]
        if k == 0:
            to_x.append(mover.to(own.at[1 - at.f], x_got, *at.x_to))
        own[at.f] = own[at.f] + got[at.f]

    def step_x():
        to_x[0].wait_recv()
        own = gp_s.at[0, at.core, at.f]
        own[...] = own[...] + x_got[...]
        mover.out(own, gp.at[0, 0])

    gain_sum = jnp.zeros((1, width), f32)
    shift_sum = jnp.zeros((1, width), f32)
    dy_sum = jnp.zeros((1, width), f32)
    for i in range(blocks):
        rows = span(i)

        def one(q, carry):
            cols = block(q, chunk)
            act_grad = dot_nt(dy_s[rows, :], wp_s[cols, :])
            up_grad = (dup_s[rows, cols].astype(f32) * act_grad).astype(bf16)
            dup_s[rows, cols] = up_grad
            bfc_s[2:3, cols] += jnp.sum(up_grad.astype(f32), axis=0, keepdims=True)
            return carry

        lax.fori_loop(0, units // chunk, one, 0, unroll=4)
        dh = dot_nt(dup_s[rows, :], wf_s[...])
        pull_s[rows, :] = (dh * gain_two).astype(bf16)
        gain_sum = gain_sum + jnp.sum(dh * normal(rows), axis=0, keepdims=True)
        shift_sum = shift_sum + jnp.sum(dh, axis=0, keepdims=True)
        dy_sum = dy_sum + jnp.sum(dy_s[rows, :].astype(f32), axis=0, keepdims=True)
        if i == 0:
            step_core(0)
        if i == 1:
            step_core(1)
            mover.out(gp_s.at[1, at.core], gp.at[1])
    mover.out(pull_s, pull)
    part_s[2:3, :] = gain_sum
    part_s[3:4, :] = shift_sum
    part_s[4:5, :] = dy_sum * 0.5
    none = jnp.zeros((2, width), f32)
    sums = jnp.concatenate([none, bfc_s[2:3, :width], bfc_s[2:3, width:], none, none], axis=0)
    part_s[8:16, :] = jnp.where(first, sums, jnp.concatenate([sums[4:], sums[:4]], axis=0))
    mover.out(part_s, part)
    rows_each = width // 8
    for k in range(2):
        for r in range(8):
            cols = slice(k * units // 2, (k + 1) * units // 2)
            grad = dot_nn(ht_s[r * rows_each : (r + 1) * rows_each, :], dup_s[:, cols])
            gf_s[k, r % 2, r // 4, r // 2 % 2] = grad.astype(bf16)
        mover.out(gf_s.at[k], gf.at[k])
        if k == 0:
            step_x()

    for t in range(2):
        nears[t].wait_recv()
        mine = home_s.at[2 * t + at.j]
        mine[...] = (mine[...].astype(f32) + got_s[t].astype(f32)).astype(bf16)
        mover.out(mine, home.at[t])
    mover.finish()


def front(info, x, cot, fc, proj, qkv, out, rope, vectors):
    seqs, rows, width = x.shape
    total = 4 * rows
    units = proj.shape[0]
    inner = out.shape[0]
    cell = (rows // 2, width)
    hbm = pl.BlockSpec(memory_space=pl.ANY)
    shape = lambda *dims: jax.ShapeDtypeStruct(dims, bf16)
    buf = lambda *dims: pltpu.VMEM(dims, bf16)
    wide = lambda *dims: pltpu.VMEM(dims, f32)
    return pl.pallas_call(
        front_kernel,
        in_specs=[pl.BlockSpec(memory_space=pltpu.SMEM)]
        + [hbm] * 7
        + [pl.BlockSpec(memory_space=pltpu.VMEM)] * 8,
        out_specs=[hbm] * 10,
        out_shape=[
            shape(total, width),
            shape(total, width),
            shape(width, 3 * inner),
            shape(inner, width),
            shape(total, width),
            shape(2, rows, width),
            shape(2, 2, 2, *cell),
            shape(2, 2, 2, 2, *cell),
            jax.ShapeDtypeStruct((16, width), f32),
            jax.ShapeDtypeStruct((8, width), f32),
        ],
        scratch_shapes=[
            buf(total, width),
            buf(total, width),
            buf(2, rows, width),
            wide(16, width // 2),
            wide(2, 16, width // 2),
            buf(width, units),
            buf(units, width),
            buf(width, 3 * inner),
            buf(inner, width),
            buf(total, width),
            buf(width, total),
            buf(total, units),
            buf(total, units),
            wide(*rope.shape),
            buf(total, inner),
            buf(total, inner),
            buf(inner, total),
            buf(total, inner),
            wide(LANES, ROWS),
            wide(total, 128),
            buf(4, rows, width),
            buf(2, rows, width),
            buf(total, width),
            buf(2, 2, 2, 2, *cell),
            buf(2, 2, 2, 2, *cell),
            buf(2, 2, 2, *cell),
            buf(2, *cell),
            wide(8, width),
            wide(8, units),
            wide(16, width),
            pltpu.SemaphoreType.DMA((48,)),
            pltpu.SemaphoreType.DMA((48,)),
            pltpu.SemaphoreType.DMA((48,)),
        ],
        compiler_params=pltpu.CompilerParams(
            collective_id=0, has_side_effects=True, vmem_limit_bytes=62 * 2**20
        ),
        name="front",
    )(info, x, cot, fc, proj, qkv, out, rope, *vectors)


def branch_kernel(
    length_ref,
    x_ref,
    dy_ref,
    wqkv_ref,
    wo_ref,
    bias_ref,
    rope_ref,
    out_ref,
    ffn_pull_ref,
    gp_ref,
    gf_ref,
    small_ref,
    summed,
    branch,
    pull,
    small,
    x_s,
    dy_s,
    h_s,
    ht_s,
    wqkv_s,
    wo_s,
    rope_s,
    q_s,
    k_s,
    v_s,
    do_s,
    kt_s,
    vt_s,
    dot_s,
    ot_s,
    dqt_s,
    dk_s,
    dv_s,
    dp_s,
    kb_s,
    begun_s,
    own_s,
    mine_s,
    core_s,
    x_got,
    y_got,
    far_got,
    home_s,
    home_got,
    out_s,
    small_s,
    small_got,
    send,
    recv,
    local,
):
    at = Spot()
    mover = Mover(send, recv, local)
    total, width = x_s.shape
    blocks = total // ROWS
    inner = wo_s.shape[0]
    head_size = 64
    length = jnp.where(at.s == 0, length_ref[0], length_ref[1])

    load_x = mover.here(x_ref, x_s)
    load_w = mover.here(wqkv_ref, wqkv_s)
    load_rope = mover.here(rope_ref, rope_s)
    load_dy = mover.here(dy_ref, dy_s)
    half = LANES // 2
    load_wo = [
        mover.here(
            wo_ref.at[pl.ds(h * LANES + g * half, half)],
            wo_s.at[pl.ds(g * LANES + h * half, half)],
        )
        for g in range(2)
        for h in range(2)
    ]
    load_small = mover.here(small_ref, small_s.at[0])
    load_out = mover.here(out_ref, out_s)
    at.greet()

    links = ("c", "x", "y", "z", "p", "yy", "c1", "c2")

    def own_of(n):
        return own_s.at[n - 1] if n < 4 else mine_s.at[n - 4, at.core]

    def cell(n, y):
        return begun_s.at[y] if n < 1 else own_of(n).at[at.f, y]

    def link(n, name):
        mine, other = summed.at[n, at.y, at.core], summed.at[n, 1 - at.y, at.core]
        if name == "c":
            src = (gf_ref.at[n - 2] if n < 4 else mine_s.at[n - 4]).at[1 - at.core]
            ends = (src, core_s.at[n - 2], at.core_to)
        elif name == "x":
            ends = (own_of(n).at[1 - at.f], x_got.at[n - 1], at.x_to)
        elif name == "y":
            ends = (cell(n, 1 - at.y), y_got.at[n], at.y_to)
        elif name == "z":
            ends = (cell(n, at.y), far_got.at[n], at.far_to)
        elif name == "p":
            ends = (y_got.at[n], summed.at[n, at.y, at.core, at.j], at.pair_to)
        elif name == "yy":
            ends = (mine, mine, at.y_to)
        elif name == "c1":
            ends = (mine, mine, at.core_to)
        else:
            ends = (other, other, at.core_to)
        return mover.remote(ends[0], ends[1], n * len(links) + links.index(name), ends[2])

    def load(n):
        if n == 0:
            return mover.stay(gp_ref.at[0, 0], begun_s, 24)
        src = gp_ref.at[1] if n == 1 else gf_ref.at[n - 2, at.core]
        return mover.stay(src, own_s.at[n - 1], 24 + n)

    def keep(n):
        return mover.stay(y_got.at[n], summed.at[n, at.y, at.core, at.j], 28 + n)

    def step_start(n):
        if n < 4:
            load(n).start()
        link(n, "c").start()

    def step_core(n):
        if n < 4:
            load(n).wait()
        link(n, "c").wait_recv()
        own, got = own_of(n), core_s.at[n - 2]
        own[1 - at.f] = own[1 - at.f] + got[1 - at.f]
        link(n, "x").start()
        own[at.f] = own[at.f] + got[at.f]

    def step_x(n):
        link(n, "x").wait_recv()
        own, got = own_of(n), x_got.at[n - 1]
        own[at.f, 1 - at.y] = own[at.f, 1 - at.y] + got[1 - at.y]
        link(n, "y").start()
        own[at.f, at.y] = own[at.f, at.y] + got[at.y]

    def step_y(n):
        link(n, "y").wait_recv()
        mine = cell(n, at.y)
        mine[...] = mine[...] + y_got[n]
        link(n, "z").start()

    def step_far(n):
        link(n, "z").wait_recv()
        y_got[n] = cell(n, at.y)[...] + far_got[n]
        link(n, "p").start()
        keep(n).start()

    def step_pair(n):
        link(n, "p").wait_recv()
        keep(n).wait()
        link(n, "yy").start()
        link(n, "c1").start()

    def step_yy(n):
        link(n, "yy").wait_recv()
        link(n, "c2").start()

    base = 6 * len(links)

    def near(t):
        return mover.remote(home_s.at[2 * t + 1 - at.j], home_got.at[t], base + t, at.pair_to)

    def last(t):
        mine, dst = home_s.at[2 * t + at.j], pull.at[at.s]
        return mover.remote(mine, dst, base + 2, at.far_to), mover.stay(mine, dst, 34)

    def out_home():
        far = mover.remote(out_s.at[1 - at.s], branch.at[at.s], base + 3, at.far_to)
        return far, mover.stay(out_s.at[at.s], branch.at[at.s], 35)

    def out_start(_):
        load_out.wait()
        for copy in out_home():
            copy.start()

    def home_near(t):
        near(t).start()

    def home_sum(t):
        near(t).wait_recv()
        mine = home_s.at[2 * t + at.j]
        mine[...] = (mine[...].astype(f32) + home_got[t].astype(f32)).astype(bf16)
        far, stay = last(t)
        pl.when(at.s == t)(stay.start)
        pl.when(at.s != t)(far.start)

    trips = (at.core_to, at.x_to, at.y_to, at.far_to, at.pair_to)

    def small_trip(n):
        return mover.remote(small_s.at[n], small_got.at[n], base + 4 + n, trips[n])

    def small_step(n):
        if n > 0:
            small_trip(n - 1).wait_recv()
            small_s[n] = small_s[n - 1] + small_got[n - 1]
        if n < 5:
            small_trip(n).start()
        else:
            mover.out(small_s.at[5], small)

    def end():
        for n in range(6):
            link(n, "c1").wait_recv()
            link(n, "c2").wait_recv()
            for name in links[max(2 - n, 0) :]:
                link(n, name).wait_send()
        for far, stay in (last(0), out_home()):
            far.wait()
            stay.wait()
        for t in range(2):
            near(t).wait_send()
        for n in range(5):
            small_trip(n).wait_send()

    acts = dict(
        start=step_start,
        core=step_core,
        x=step_x,
        y=step_y,
        far=step_far,
        pair=step_pair,
        yy=step_yy,
        near=home_near,
        sum=home_sum,
        oh=out_start,
        small=small_step,
    )

    def turn(*place):
        for word in PLAN.get(",".join(str(v) for v in place), ()):
            name, n = word.split(":")
            acts[name](int(n))

    for n in range(2):
        load(n).start()
    for n in range(2, 4):
        step_start(n)
    load(0).wait()
    link(0, "y").start()
    load(1).wait()
    link(1, "x").start()

    def normal(rows):
        v = x_s[rows, :].astype(f32)
        center = v - jnp.mean(v, axis=-1, keepdims=True)
        spread = jnp.mean(center * center, axis=-1, keepdims=True)
        return center * lax.rsqrt(spread + epsilon)

    def table(n, rows):
        part = rope_s[n, rows, :]
        return jnp.concatenate([part, part], axis=1)

    def turned(v, rows, sign):
        left = pltpu.roll(v, LANES - ROT // 2, 1)
        right = pltpu.roll(v, ROT // 2, 1)
        moved = left * table(1, rows) + right * table(2, rows)
        return v * table(0, rows) + moved if sign > 0 else v * table(0, rows) - moved

    key_pos = lax.broadcasted_iota(jnp.int32, (total, 128), 0)
    kb_s[...] = jnp.where(key_pos < length, 0.0, masked_score)
    lane = lax.broadcasted_iota(jnp.int32, (ROWS, LANES), 1)
    causal = lax.broadcasted_iota(jnp.int32, (ROWS, ROWS), 0) <= lax.broadcasted_iota(
        jnp.int32, (ROWS, ROWS), 1
    )
    gain, offset = bias_ref[3:4, :], bias_ref[4:5, :]

    def span(b):
        return slice(b * ROWS, (b + 1) * ROWS)

    def project(g):
        cols = lambda t: slice(t * inner + g * LANES, t * inner + (g + 1) * LANES)
        bias = lambda t: bias_ref[t : t + 1, g * LANES : (g + 1) * LANES]
        for r in range(blocks):
            rows = span(r)
            if g == 0:
                hr = (normal(rows) * gain + offset).astype(bf16)
                h_s[rows, :] = hr
                ht_s[:, rows] = hr.T
                if r == 0:
                    load_w.wait()
                    load_rope.wait()
                    load_dy.wait()
                    for copy in load_wo:
                        copy.wait()
            else:
                hr = h_s[rows, :]
            q = turned(dot_nn(hr, wqkv_s[:, cols(0)]) + bias(0), rows, 1).astype(bf16)
            q_s[rows, :] = (q.astype(f32) * 0.125).astype(bf16)
            k = turned(dot_nn(hr, wqkv_s[:, cols(1)]) + bias(1), rows, 1).astype(bf16)
            k_s[rows, :] = k
            kt_s[:, rows] = k.T
            v = (dot_nn(hr, wqkv_s[:, cols(2)]) + bias(2)).astype(bf16)
            v_s[rows, :] = v
            vt_s[:, rows] = v.T
            do = dot_nt(dy_s[rows, :], wo_s[g * LANES : (g + 1) * LANES, :]).astype(bf16)
            do_s[rows, :] = do
            dot_s[:, rows] = do.T
            turn("p%d" % g, r)
        dk_s[...] = jnp.zeros_like(dk_s)
        dv_s[...] = jnp.zeros_like(dv_s)

    def one_head(g, i, head, carry):
        feats = pl.ds(pl.multiple_of(head * head_size, head_size), head_size)
        mine = (lane // head_size) == head
        zero = jnp.zeros((ROWS, LANES), bf16)
        rows = span(i)
        qm = jnp.where(mine, q_s[rows, :], zero)
        dom = jnp.where(mine, do_s[rows, :], zero)
        scores = []
        top = None
        for b in range(i + 1):
            sc = dot_nt(k_s[span(b), :], qm)
            kb = kb_s[span(b), :]
            sc = sc + jnp.concatenate([kb, kb], axis=1)
            if b == i:
                sc = jnp.where(causal, sc, masked_score)
            best = jnp.max(sc, axis=0, keepdims=True)
            top = best if top is None else jnp.maximum(top, best)
            scores.append(sc)
        row_sum = None
        for b in range(i + 1):
            scores[b] = jnp.exp(scores[b] - top)
            part = jnp.sum(scores[b], axis=0, keepdims=True)
            row_sum = part if row_sum is None else row_sum + part
        inverse = 1.0 / row_sum
        o_t = None
        for b in range(i + 1):
            scores[b] = scores[b] * inverse
            low = scores[b].astype(bf16)
            dv_s[span(b), :] += dot_nn(low, dom)
            part = dot_nn(vt_s[feats, span(b)], low)
            o_t = part if o_t is None else o_t + part
        ot_s[feats, rows] = o_t
        delta = jnp.sum(dot_s[feats, rows].astype(f32) * o_t, axis=0, keepdims=True)
        dq_t = None
        for b in range(i + 1):
            dp = dot_nt(v_s[span(b), :], dom)
            ds = (scores[b] * (dp - delta)).astype(bf16)
            dk_s[span(b), :] += dot_nn(ds, qm)
            part = dot_nn(kt_s[feats, span(b)], ds)
            dq_t = part if dq_t is None else dq_t + part
        dqt_s[feats, rows] = dq_t * 0.125
        for h in range(LANES // head_size):
            if "%d,%d,%d" % (g, i, h) in PLAN:
                pl.when(head == h)(functools.partial(turn, g, i, h))
        return carry

    def finish_block(g, i, sums):
        rows = span(i)
        cols = slice(g * LANES, (g + 1) * LANES)
        dq = turned(dqt_s[:, rows].T, rows, -1).astype(bf16)
        dk = turned(dk_s[rows, :], rows, -1).astype(bf16)
        dv = dv_s[rows, :].astype(bf16)
        for t, grad in enumerate((dq, dk, dv)):
            sums[t] = sums[t] + jnp.sum(grad.astype(f32), axis=0, keepdims=True)
            dp_s[t, rows, cols] = grad

    def finish_rows(i, gain_sum, shift_sum):
        rows = span(i)
        dh = dot_nt(dp_s[0, rows, :], wqkv_s[:, :inner])
        dh = dh + dot_nt(dp_s[1, rows, :], wqkv_s[:, inner : 2 * inner])
        dh = dh + dot_nt(dp_s[2, rows, :], wqkv_s[:, 2 * inner :])
        home_s[i] = (dh * gain + home_s[i].astype(f32)).astype(bf16)
        gain_sum = gain_sum + jnp.sum(dh * normal(rows), axis=0, keepdims=True)
        return gain_sum, shift_sum + jnp.sum(dh, axis=0, keepdims=True)

    def weight_grads(g):
        cols = slice(g * LANES, (g + 1) * LANES)
        size = width // 8
        for t in range(3):
            for r in range(8):
                grad = dot_nn(ht_s[r * size : (r + 1) * size, :], dp_s[t, :, cols])
                mine_s[g, r % 2, r // 4, r // 2 % 2, :, t * LANES : (t + 1) * LANES] = grad.astype(bf16)
        grad = dot_nn(ot_s[...].astype(bf16), dy_s[...]).astype(bf16)
        size = LANES // 8
        for r in range(8):
            for b in range(4):
                mine_s[
                    g, r % 2, r // 4, r // 2 % 2, b * size : (b + 1) * size, 3 * LANES :
                ] = grad[r * size : (r + 1) * size, b * LANES : (b + 1) * LANES]

    load_x.wait()
    loads_home = [
        mover.here(ffn_pull_ref.at[block(b, ROWS)], home_s.at[b]) for b in range(blocks)
    ]
    load_small.wait()
    gain_sum = jnp.zeros((1, width), f32)
    shift_sum = jnp.zeros((1, width), f32)
    for g in range(2):
        project(g)
        sums = [jnp.zeros((1, LANES), f32) for _ in range(3)]
        for i in reversed(range(blocks)):
            lax.fori_loop(0, LANES // head_size, functools.partial(one_head, g, i), 0)
            finish_block(g, i, sums)
            if g == 1:
                if i == blocks - 1:
                    for copy in loads_home:
                        copy.wait()
                gain_sum, shift_sum = finish_rows(i, gain_sum, shift_sum)
            turn(g, i)
        weight_grads(g)
        row = lax.broadcasted_iota(jnp.int32, (8, LANES), 0)
        for t in range(3):
            start = t % 2 * inner + g * LANES
            cols = slice(start, start + LANES)
            here = row == 4 * at.j + t // 2
            small_s[0, 8:16, cols] = jnp.where(here, sums[t], small_s[0, 8:16, cols])
        if g == 0:
            turn("grads")
    small_s[0, 0:1, :] = gain_sum
    small_s[0, 1:2, :] = shift_sum
    turn("tail")
    end()
    mover.finish()


PLAN = {
    "p0,3": ("y:0",),
    "0,3,1": ("core:2",),
    "0,3,2": ("x:1",),
    "0,2,2": ("y:1",),
    "0,2": ("far:0", "core:3",),
    "0,1,1": ("x:2",),
    "grads": ("y:2",),
    "p1,0": ("far:1",),
    "p1,2": ("x:3",),
    "1,3,3": ("far:2", "pair:0", "y:3",),
    "1,2,3": ("start:4",),
    "1,2": ("near:1",),
    "1,1,1": ("core:4",),
    "1,1,2": ("pair:1",),
    "1,0,0": ("oh:0",),
    "1,0,1": ("x:4",),
    "1,0": ("yy:1",),
    "tail": ("far:3", "small:0", "start:5", "pair:2", "y:4", "small:1", "near:0", "core:5", "x:5", "y:5", "pair:3", "small:2", "far:4", "small:3", "sum:0", "yy:0", "yy:3", "far:5", "pair:4", "yy:2", "pair:5", "sum:1", "small:4", "yy:4", "yy:5", "small:5",),
}


def branch_and_sums(length, x, dy, w_qkv, w_out, bias, rope, out, ffn_pull, gp, gf, small):
    total, width = x.shape
    inner = w_out.shape[0]
    cell = (ROWS // 2, width)
    hbm = pl.BlockSpec(memory_space=pl.ANY)
    vmem = pl.BlockSpec(memory_space=pltpu.VMEM)
    home = jax.ShapeDtypeStruct((2, ROWS, width), bf16)
    buf = lambda dims, kind=bf16: pltpu.VMEM(tuple(dims), kind)
    return pl.pallas_call(
        branch_kernel,
        in_specs=[pl.BlockSpec(memory_space=pltpu.SMEM)] + [hbm] * 4 + [vmem] + [hbm] * 6,
        out_specs=[hbm] * 4,
        out_shape=[
            jax.ShapeDtypeStruct((6, 2, 2, 2) + cell, bf16),
            home,
            home,
            jax.ShapeDtypeStruct(small.shape, f32),
        ],
        scratch_shapes=[
            buf((total, width)),
            buf((total, width)),
            buf((total, width)),
            buf((width, total)),
            buf((width, 3 * inner)),
            buf((inner, width)),
            buf((3, total, 128), f32),
            buf((total, LANES)),
            buf((total, LANES)),
            buf((total, LANES)),
            buf((total, LANES)),
            buf((LANES, total)),
            buf((LANES, total)),
            buf((LANES, total)),
            buf((LANES, total), f32),
            buf((LANES, total), f32),
            buf((total, LANES), f32),
            buf((total, LANES), f32),
            buf((3, total, inner)),
            buf((total, 128), f32),
            buf((2,) + cell),
            buf((3, 2, 2) + cell),
            buf((2, 2, 2, 2) + cell),
            buf((4, 2, 2) + cell),
            buf((5, 2) + cell),
            buf((6,) + cell),
            buf((6,) + cell),
            buf((total // ROWS, ROWS, width)),
            buf((2, ROWS, width)),
            buf((2, ROWS, width)),
            buf((6,) + small.shape, f32),
            buf((5,) + small.shape, f32),
            pltpu.SemaphoreType.DMA((80,)),
            pltpu.SemaphoreType.DMA((80,)),
            pltpu.SemaphoreType.DMA((40,)),
        ],
        compiler_params=pltpu.CompilerParams(
            collective_id=1, has_side_effects=True, vmem_limit_bytes=62 * 2**20
        ),
        name="branch",
    )(length, x, dy, w_qkv, w_out, bias, rope, out, ffn_pull, gp, gf, small)


def last_kernel(
    lengths_ref,
    summed_ref,
    x_ref,
    cot_ref,
    branch_ref,
    pull_ref,
    vectors_ref,
    sums_ref,
    residual_out,
    residual_grad,
    d_proj,
    d_fc,
    d_qkv,
    d_out,
    d_gain_one,
    d_shift_one,
    d_gain_two,
    d_shift_two,
    d_bias_out,
    d_bias_proj,
    d_bqkv,
    d_bfc,
):
    size, width = summed_ref.shape[4:]
    y, core = pl.program_id(0), pl.program_id(1)
    for k in range(2):
        for p in range(2):
            d_proj[p, 0, 0, k] = summed_ref[k, 0, 0, p].astype(f32)
            to = (2 * k + p) * width
            d_fc[:, to : to + width] = summed_ref[2 + k, 0, 0, p].astype(f32)

    rows = x_ref.shape[1]
    features = x_ref[0].astype(f32)
    residual_out[0] = (features + branch_ref[0].astype(f32) + vectors_ref[5:6, :]).astype(bf16)
    hat, inverse = normalize(features)
    pulled = pull_ref[0].astype(f32)
    pulled = inverse * (
        pulled
        - jnp.mean(pulled, axis=-1, keepdims=True)
        - hat * jnp.mean(pulled * hat, axis=-1, keepdims=True)
    )
    start = (lax.axis_index("ctx") * 2 + core) * rows
    valid = start + lax.broadcasted_iota(jnp.int32, (rows, width), 0) < lengths_ref[y]
    own = jnp.where(valid, cot_ref[0].astype(f32), 0.0)
    residual_grad[0] = (own + pulled).astype(bf16)

    for g in range(2):
        for p in range(2):
            for t in range(3):
                for h in range(2):
                    cols = slice((t * 2 + h) * 128, (t * 2 + h + 1) * 128)
                    to = t * 8 + h * 4 + p * 2 + g
                    got = summed_ref[4 + g, 0, 0, p, :, cols]
                    d_qkv[:, to * 128 : (to + 1) * 128] = got.astype(f32)
            for b in range(4):
                got = summed_ref[4 + g, 0, 0, p, b * size // 4 : (b + 1) * size // 4, 3 * LANES :]
                d_out[p, g, 0, 0, :, b * LANES : (b + 1) * LANES] = got.astype(f32)

    @pl.when(y * 2 + core == 0)
    def _():
        first = lax.axis_index("fsdp") == 0
        half = width // 2
        gains = (d_gain_one, d_shift_one, d_gain_two, d_shift_two, d_bias_out)
        for r, ref in (*enumerate(gains), (4, d_bias_proj)):
            line = sums_ref[r : r + 1, :]
            ref[...] = jnp.where(first, line[:, :half], line[:, half:]).reshape(half)
        pieces = []
        for t in range(3):
            for h in range(2):
                for p in range(2):
                    for g in range(2):
                        at = t % 2 * half + (g * 2 + h) * 128
                        pieces.append(sums_ref[8 + 4 * p + t // 2 : 9 + 4 * p + t // 2, at : at + 128])
        line = jnp.concatenate(pieces, axis=1)
        count = 3 * half
        d_bqkv[...] = jnp.where(first, line[:, :count], line[:, count:]).reshape(count)
        line = jnp.concatenate(
            [jnp.where(first, sums_ref[r : r + 1, :], sums_ref[r + 1 : r + 2, :]) for r in (10, 14)],
            axis=1,
        )
        d_bfc[...] = line.reshape(2 * width)


def last_pass(lengths, summed, x, cot, branch, pull, vectors, sums, proj_shape, fc_shape, qkv_shape, out_shape):
    size, width = summed.shape[4:]
    rows = x.shape[1] // 2
    shape = lambda *dims: jax.ShapeDtypeStruct(dims, f32)
    token = pl.BlockSpec((1, rows, width), lambda y, c: (y, c, 0))
    line = lambda count: pl.BlockSpec((count,), lambda y, c: (0,))
    table = lambda count: pl.BlockSpec((count, width), lambda y, c: (0, 0))
    counts = [width // 2] * 6 + [3 * width // 2, 2 * width]
    residual_out, residual_grad, d_proj, d_fc, d_qkv, d_out, *vectors_out = pl.pallas_call(
        last_kernel,
        grid=(2, 2),
        in_specs=[
            pl.BlockSpec(memory_space=pltpu.SMEM),
            pl.BlockSpec((6, 1, 1, 2, size, width), lambda y, c: (0, y, c, 0, 0, 0)),
            token,
            token,
            token,
            token,
            table(8),
            table(16),
        ],
        out_specs=[
            token,
            token,
            pl.BlockSpec((2, 1, 1, 2, size, width), lambda y, c: (0, y, c, 0, 0, 0)),
            pl.BlockSpec((size, 4 * width), lambda y, c: (y * 2 + c, 0)),
            pl.BlockSpec((size, qkv_shape[1]), lambda y, c: (y * 2 + c, 0)),
            pl.BlockSpec((2, 2, 1, 1, size // 4, width), lambda y, c: (0, 0, y, c, 0, 0)),
        ]
        + [line(count) for count in counts],
        out_shape=[
            jax.ShapeDtypeStruct(x.shape, bf16),
            jax.ShapeDtypeStruct(x.shape, bf16),
            shape(2, 2, 2, 2, size, width),
            shape(*fc_shape),
            shape(*qkv_shape),
            shape(2, 2, 2, 2, size // 4, width),
        ]
        + [shape(count) for count in counts],
        compiler_params=pltpu.CompilerParams(vmem_limit_bytes=62 * 2**20),
        name="last",
    )(lengths, summed, x, cot, branch, pull, vectors, sums)
    grads = (d_proj.reshape(proj_shape), d_fc, d_qkv, d_out.reshape(out_shape))
    return residual_out, residual_grad, grads, vectors_out


def normalize(features):
    center = features - jnp.mean(features, axis=-1, keepdims=True)
    spread = jnp.mean(center * center, axis=-1, keepdims=True)
    inverse = lax.rsqrt(spread + epsilon)
    return center * inverse, inverse


def rope_tables(total, head_size):
    half = ROT // 2
    inverse = (rope_base ** (-(2.0 * np.arange(half)) / ROT)).astype(np.float32)
    angles = np.arange(total, dtype=np.float32)[:, None] * inverse[None, :]
    cosine, sine = np.cos(angles), np.sin(angles)
    rest = np.zeros((total, head_size - ROT), np.float32)
    none = np.zeros((total, half), np.float32)
    same = np.concatenate([cosine, cosine, rest + 1.0], axis=1)
    ahead = np.concatenate([-sine, none, rest], axis=1)
    behind = np.concatenate([none, sine, rest], axis=1)
    return jnp.asarray(np.tile(np.stack([same, ahead, behind]), (1, 1, 128 // head_size)), f32)


def finish(residual_in, cotangent, lengths, start, branch, pulled, bias):
    features = residual_in.astype(f32)
    residual_out = (features + branch + bias).astype(bf16)
    own_hat, own_inverse = normalize(features)
    pulled = own_inverse * (
        pulled
        - jnp.mean(pulled, axis=-1, keepdims=True)
        - own_hat * jnp.mean(pulled * own_hat, axis=-1, keepdims=True)
    )
    own_pos = start + jnp.arange(residual_in.shape[1], dtype=jnp.int32)
    valid = (own_pos[None, :] < lengths[:, None])[..., None]
    residual_grad = (jnp.where(valid, cotangent.astype(f32), 0.0) + pulled).astype(bf16)
    return residual_out, residual_grad


def fast_block(residual_in, lengths, cotangent, weights, small, rope):
    weight_fc, weight_proj, weight_qkv, weight_out = weights
    seq_in, seq_grad, w_qkv, w_out, pull, home, gp, gf, part, vectors = front(
        lengths, residual_in, cotangent, *weights, rope, small
    )
    summed, branch, pulled, sums = branch_and_sums(
        lengths, seq_in, seq_grad, w_qkv, w_out, vectors, rope, home, pull, gp, gf, part
    )
    residual_out, residual_grad, grads, vectors_out = last_pass(
        lengths,
        summed,
        residual_in,
        cotangent,
        branch,
        pulled,
        vectors,
        sums,
        weight_proj.shape,
        weight_fc.shape,
        weight_qkv.shape,
        weight_out.shape,
    )
    d_proj, d_fc, d_qkv, d_out = grads
    d_gain_one, d_shift_one, d_gain_two, d_shift_two, d_bout, d_bproj, d_bqkv, d_bfc = vectors_out
    return (
        residual_out,
        residual_grad,
        d_gain_one,
        d_shift_one,
        d_qkv,
        d_bqkv,
        d_out,
        d_bout,
        d_gain_two,
        d_shift_two,
        d_fc,
        d_bfc,
        d_proj,
        d_bproj,
    )


def per_device(
    residual_in,
    lengths,
    gain_attn,
    shift_attn,
    weight_qkv,
    bias_qkv,
    weight_out,
    bias_out,
    gain_ffn,
    shift_ffn,
    weight_fc,
    bias_fc,
    weight_proj,
    bias_proj,
    cotangent,
):
    seqs, block_rows, width = residual_in.shape
    n_ctx, n_fsdp = lax.axis_size("ctx"), lax.axis_size("fsdp")
    parts = n_ctx // seqs
    total = n_ctx * block_rows
    units = weight_fc.shape[1]
    head_size = width // HEADS
    c, f, dp = lax.axis_index("ctx"), lax.axis_index("fsdp"), lax.axis_index("dp")
    s, j = c // parts, c % parts
    place = dict(c=c, f=f, dp=dp, s=s, j=j, y=dp // 2, core=dp % 2)
    spread_heads = HEADS % (n_fsdp * parts) == 0
    n_h = n_fsdp if spread_heads else 1
    inner = width // parts

    rows_here = weight_qkv.shape[0]
    own_heads = lambda v: pick(v.reshape(3, n_h, parts, -1), j, 2)
    fast = (seqs, n_ctx, n_fsdp, lax.axis_size("dp")) == (2, 4, 2, 4)
    small_local = jnp.concatenate(
        [gain_attn, shift_attn, gain_ffn, shift_ffn, bias_out, bias_proj, bias_qkv, bias_fc]
    )
    part_width = width // n_fsdp
    length = pick(lengths, s)
    rope = rope_tables(total, head_size)
    own_part = lambda v, size=part_width: lax.dynamic_slice_in_dim(v, f * size, size)
    if fast:
        return fast_block(
            residual_in,
            lengths,
            cotangent,
            (weight_fc, weight_proj, weight_qkv, weight_out),
            (gain_attn, shift_attn, gain_ffn, shift_ffn, bias_out, bias_proj, bias_qkv, bias_fc),
            rope,
        )
    small = lax.all_gather(small_local, "fsdp", axis=0)
    vec = lambda at, size: small[:, at : at + size].reshape(-1).astype(f32)
    gain_one, shift_one, gain_two, shift_two, b_out, b_proj = (
        vec(i * part_width, part_width) for i in range(6)
    )
    b_qkv = vec(6 * part_width, 3 * part_width)
    b_fc = vec(9 * part_width, units // n_fsdp)

    fc_local = pick(weight_fc.reshape(rows_here, n_fsdp, parts, -1), j, 2).reshape(rows_here, -1)
    proj_local = pick(weight_proj.reshape(parts, -1, width), j)
    qkv_local = pick(weight_qkv.reshape(rows_here, 3, n_h, parts, -1), j, 3).reshape(rows_here, -1)
    seq_in = gather_sequence(residual_in, place, parts)
    w_fc = gather_rows(fc_local, place).reshape(width, -1)
    w_proj = gather_rows(proj_local, place).reshape(-1, width)
    seq_grad = gather_sequence(cotangent, place, parts)
    w_qkv = gather_rows(qkv_local, place).reshape(width, -1)
    if spread_heads:
        w_out = gather_rows(pick(weight_out.reshape(parts, -1, width), j), place).reshape(-1, width)
    else:
        w_out = lax.all_gather(weight_out, "fsdp", axis=0, tiled=True)
        w_out = pick(w_out.reshape(parts, -1, width), j)
    b_qkv_j = own_heads(b_qkv).reshape(3, 1, inner)
    b_fc_j = pick(b_fc.reshape(n_fsdp, parts, -1), j, 1).reshape(1, -1)
    b_fc_j = jnp.broadcast_to(b_fc_j, (8, b_fc_j.shape[1]))

    positions = jnp.arange(total, dtype=jnp.int32)
    seq_grad = jnp.where((positions < length)[:, None], seq_grad, jnp.zeros((), bf16))
    xhat, _ = normalize(seq_in.astype(f32))
    hidden_one = (xhat * gain_one + shift_one).astype(bf16)
    hidden_two = (xhat * gain_two + shift_two).astype(bf16)

    ffn_out, ffn_dh, g_fc, g_proj, g_bfc = ffn_branch(
        hidden_two, seq_grad, w_fc, w_proj, b_fc_j
    )
    ffn_sums = (jnp.sum(ffn_dh * xhat, axis=0), jnp.sum(ffn_dh, axis=0))
    own_grad = jnp.sum(seq_grad.astype(f32), axis=0) / parts
    attn_out, attn_dh, g_qkv, g_out, g_bqkv = attention_branch(
        length[None],
        hidden_one,
        seq_grad,
        w_qkv,
        w_out,
        jnp.broadcast_to(b_qkv_j, (3, 8, inner)),
        jnp.tile(rope, (1, 1, LANES // 128)),
    )
    g_bqkv_all = jnp.zeros((3, n_h, parts, inner // n_h), f32)
    g_bqkv_all = lax.dynamic_update_index_in_dim(
        g_bqkv_all, g_bqkv[:, 0].reshape(3, n_h, -1), j, 2
    )
    g_bfc_all = jnp.zeros((n_fsdp, parts, units // (n_fsdp * parts)), f32)
    g_bfc_all = lax.dynamic_update_index_in_dim(g_bfc_all, g_bfc[0].reshape(n_fsdp, -1), j, 1)
    rows_of = (
        jnp.sum(attn_dh * xhat, axis=0),
        jnp.sum(attn_dh, axis=0),
        *ffn_sums,
        own_grad,
        g_bqkv_all.reshape(-1),
        g_bfc_all.reshape(-1),
    )
    flat = sum_everywhere(jnp.concatenate(rows_of).reshape(-1, 128)).reshape(-1)
    small_grads = []
    at = 0
    for entry in rows_of:
        size = entry.shape[0]
        small_grads.append(own_part(flat[at : at + size], size // n_fsdp))
        at += size
    d_gain_one, d_shift_one, d_gain_two, d_shift_two, d_bias, d_bqkv, d_bfc = small_grads
    branch_part = (attn_out + ffn_out).astype(bf16)
    pull_part = (attn_dh * gain_one + ffn_dh * gain_two).astype(bf16)
    d_proj = reduce_rows(g_proj.reshape(n_fsdp, -1, width), place, parts)
    d_fc = reduce_rows(g_fc.reshape(n_fsdp, rows_here, -1), place, parts)
    q_rows = jnp.swapaxes(g_qkv.reshape(3, n_fsdp, rows_here, inner), 0, 1)
    q_rows = jnp.swapaxes(q_rows, 1, 2).reshape(n_fsdp, rows_here, 3 * inner)
    d_qkv = reduce_rows(q_rows, place, parts)
    d_proj = jnp.swapaxes(d_proj, 0, 1).reshape(weight_proj.shape)
    d_fc = d_fc.reshape(rows_here, parts, n_fsdp, -1)
    d_fc = jnp.swapaxes(d_fc, 1, 2).reshape(weight_fc.shape)
    d_qkv = d_qkv.reshape(rows_here, parts, 3, n_h, -1)
    d_qkv = jnp.transpose(d_qkv, (0, 2, 3, 1, 4)).reshape(weight_qkv.shape)
    if spread_heads:
        d_out = reduce_rows(g_out.reshape(n_fsdp, -1, width), place, parts)
        d_out = jnp.swapaxes(d_out, 0, 1).reshape(weight_out.shape)
    else:
        full = jnp.zeros((parts, inner, width), bf16)
        full = lax.dynamic_update_index_in_dim(full, g_out, j, 0).reshape(width, width)
        d_out = lax.psum_scatter(full, "fsdp", scatter_dimension=0, tiled=True)
        d_out = lax.psum(d_out, ("dp", "ctx")).astype(f32)
    branch = return_blocks(branch_part, place, parts, seqs)
    pulled = return_blocks(pull_part, place, parts, seqs)

    residual_out, residual_grad = finish(
        residual_in, cotangent, lengths, c * block_rows, branch, pulled, b_out + b_proj
    )
    return (
        residual_out,
        residual_grad,
        d_gain_one,
        d_shift_one,
        d_qkv,
        d_bqkv,
        d_out,
        d_bias,
        d_gain_two,
        d_shift_two,
        d_fc,
        d_bfc,
        d_proj,
        d_bias,
    )


def solution(mesh):
    tokens = P(("dp", "fsdp"), "ctx", None)
    vector, matrix = P("fsdp"), P("fsdp", None)
    return jax.shard_map(
        per_device,
        mesh=mesh,
        in_specs=(
            tokens,
            P(("dp", "fsdp")),
            vector,
            vector,
            matrix,
            vector,
            matrix,
            vector,
            vector,
            vector,
            matrix,
            vector,
            matrix,
            vector,
            tokens,
        ),
        out_specs=(
            tokens,
            tokens,
            vector,
            vector,
            matrix,
            vector,
            matrix,
            vector,
            vector,
            vector,
            matrix,
            vector,
            matrix,
            vector,
        ),
        check_vma=False,
    )
```

```python
import functools
import math

import jax
import jax.numpy as jnp
import numpy as np
from jax import lax
from jax.experimental import pallas as pl
from jax.experimental.pallas import tpu as pltpu
from jax.sharding import PartitionSpec as P

HEADS = 16
ROT = 16
LANES = 256
ROWS = 256

epsilon = 1e-05
rope_base = 10000.0
masked_score = -1e30

f32 = jnp.float32
bf16 = jnp.bfloat16


def dot_nn(a, b):
    return lax.dot_general(a, b, (((1,), (0,)), ((), ())), preferred_element_type=f32)


def dot_nt(a, b):
    return lax.dot_general(a, b, (((1,), (1,)), ((), ())), preferred_element_type=f32)


def attn_kernel(
    length_ref,
    h_ref,
    dy_ref,
    wq_ref,
    wk_ref,
    wv_ref,
    wo_ref,
    b_ref,
    rope_ref,
    out_ref,
    dh_ref,
    gqkv_ref,
    gout_ref,
    gb_ref,
    ht_s,
    q_s,
    k_s,
    v_s,
    do_s,
    kt_s,
    vt_s,
    dot_s,
    ot_s,
    dqt_s,
    dk_s,
    dv_s,
    p_s,
    kb_s,
):
    group = pl.program_id(0)
    total, width = h_ref.shape
    blocks = total // ROWS
    head_size = 64
    heads_here = LANES // head_size
    length = length_ref[0]

    @pl.when(group == 0)
    def _():
        for r in range(blocks):
            ht_s[:, r * ROWS : (r + 1) * ROWS] = h_ref[r * ROWS : (r + 1) * ROWS, :].T
        key_pos = lax.broadcasted_iota(jnp.int32, (total, 128), 0)
        kb_s[...] = jnp.where(key_pos < length, 0.0, masked_score)

    def turn(v, rows):
        left = pltpu.roll(v, LANES - ROT // 2, 1)
        right = pltpu.roll(v, ROT // 2, 1)
        return v * rope_ref[0, rows, :] + left * rope_ref[1, rows, :] + right * rope_ref[2, rows, :]

    def turn_back(v, rows):
        left = pltpu.roll(v, LANES - ROT // 2, 1)
        right = pltpu.roll(v, ROT // 2, 1)
        return v * rope_ref[0, rows, :] - left * rope_ref[1, rows, :] - right * rope_ref[2, rows, :]

    for r in range(blocks):
        rows = slice(r * ROWS, (r + 1) * ROWS)
        hr = h_ref[rows, :]
        q = turn(dot_nn(hr, wq_ref[...]) + b_ref[0, 0:1, :], rows).astype(bf16)
        q_s[rows, :] = (q.astype(f32) * 0.125).astype(bf16)
        k = turn(dot_nn(hr, wk_ref[...]) + b_ref[1, 0:1, :], rows).astype(bf16)
        k_s[rows, :] = k
        kt_s[:, rows] = k.T
        v = (dot_nn(hr, wv_ref[...]) + b_ref[2, 0:1, :]).astype(bf16)
        v_s[rows, :] = v
        vt_s[:, rows] = v.T
        do = dot_nt(dy_ref[rows, :], wo_ref[...]).astype(bf16)
        do_s[rows, :] = do
        dot_s[:, rows] = do.T

    dk_s[...] = jnp.zeros_like(dk_s)
    dv_s[...] = jnp.zeros_like(dv_s)
    lane = lax.broadcasted_iota(jnp.int32, (ROWS, LANES), 1)
    causal = lax.broadcasted_iota(jnp.int32, (ROWS, ROWS), 0) <= lax.broadcasted_iota(
        jnp.int32, (ROWS, ROWS), 1
    )

    def one_head(head, carry):
        feats = pl.ds(pl.multiple_of(head * head_size, head_size), head_size)
        mine = (lane // head_size) == head
        zero = jnp.zeros((ROWS, LANES), bf16)
        for i in range(blocks):
            rows = slice(i * ROWS, (i + 1) * ROWS)
            qm = jnp.where(mine, q_s[rows, :], zero)
            dom = jnp.where(mine, do_s[rows, :], zero)
            scores = []
            top = None
            for b in range(i + 1):
                keys = slice(b * ROWS, (b + 1) * ROWS)
                sc = dot_nt(k_s[keys, :], qm)
                kb = kb_s[keys, :]
                sc = sc + jnp.concatenate([kb, kb], axis=1)
                if b == i:
                    sc = jnp.where(causal, sc, masked_score)
                best = jnp.max(sc, axis=0, keepdims=True)
                top = best if top is None else jnp.maximum(top, best)
                scores.append(sc)
            row_sum = None
            for b in range(i + 1):
                scores[b] = jnp.exp(scores[b] - top)
                part = jnp.sum(scores[b], axis=0, keepdims=True)
                row_sum = part if row_sum is None else row_sum + part
            inverse = 1.0 / row_sum
            o_t = None
            for b in range(i + 1):
                keys = slice(b * ROWS, (b + 1) * ROWS)
                scores[b] = scores[b] * inverse
                low = scores[b].astype(bf16)
                dv_s[keys, :] += dot_nn(low, dom)
                part = dot_nn(vt_s[feats, keys], low)
                o_t = part if o_t is None else o_t + part
            ot_s[feats, rows] = o_t
            delta = jnp.sum(dot_s[feats, rows].astype(f32) * o_t, axis=0, keepdims=True)
            dq_t = None
            for b in range(i + 1):
                keys = slice(b * ROWS, (b + 1) * ROWS)
                dp = dot_nt(v_s[keys, :], dom)
                ds = (scores[b] * (dp - delta)).astype(bf16)
                dk_s[keys, :] += dot_nn(ds, qm)
                part = dot_nn(kt_s[feats, keys], ds)
                dq_t = part if dq_t is None else dq_t + part
            dqt_s[feats, rows] = dq_t * 0.125
        return carry

    lax.fori_loop(0, heads_here, one_head, 0)

    sums = [jnp.zeros((1, LANES), f32) for _ in range(3)]
    for r in range(blocks):
        rows = slice(r * ROWS, (r + 1) * ROWS)
        dq = turn_back(dqt_s[:, rows].T, rows).astype(bf16)
        dk = turn_back(dk_s[rows, :], rows).astype(bf16)
        dv = dv_s[rows, :].astype(bf16)
        for at, grad in enumerate((dq, dk, dv)):
            sums[at] = sums[at] + jnp.sum(grad.astype(f32), axis=0, keepdims=True)
            p_s[at, rows, :] = grad
        o = ot_s[:, rows].T.astype(bf16)
        out_part = dot_nn(o, wo_ref[...])
        dh_part = (
            dot_nt(dq, wq_ref[...]) + dot_nt(dk, wk_ref[...]) + dot_nt(dv, wv_ref[...])
        )

        @pl.when(group == 0)
        def _():
            out_ref[rows, :] = out_part
            dh_ref[rows, :] = dh_part

        @pl.when(group > 0)
        def _():
            out_ref[rows, :] += out_part
            dh_ref[rows, :] += dh_part

    for at in range(3):
        gb_ref[at] = jnp.broadcast_to(sums[at], (8, LANES))
        for r in range(width // ROWS):
            rows = slice(r * ROWS, (r + 1) * ROWS)
            gqkv_ref[at, rows, :] = dot_nn(ht_s[rows, :], p_s[at]).astype(bf16)
    gout_ref[...] = dot_nn(ot_s[...].astype(bf16), dy_ref[...]).astype(bf16)


def attention_branch(length, hidden, out_grad, w_qkv, w_out, b_qkv, rope):
    total, width = hidden.shape
    inner = w_out.shape[0]
    groups = inner // LANES
    whole = lambda g: (0, 0)
    flops = 2 * total * width * inner * 12 + 2 * groups * 4 * total * total * LANES * 4
    return pl.pallas_call(
        attn_kernel,
        grid=(groups,),
        in_specs=[
            pl.BlockSpec(memory_space=pltpu.SMEM),
            pl.BlockSpec((total, width), whole),
            pl.BlockSpec((total, width), whole),
            pl.BlockSpec((width, LANES), lambda g: (0, g)),
            pl.BlockSpec((width, LANES), lambda g: (0, groups + g)),
            pl.BlockSpec((width, LANES), lambda g: (0, 2 * groups + g)),
            pl.BlockSpec((LANES, width), lambda g: (g, 0)),
            pl.BlockSpec((3, 8, LANES), lambda g: (0, 0, g)),
            pl.BlockSpec((3, total, LANES), lambda g: (0, 0, 0)),
        ],
        out_specs=[
            pl.BlockSpec((total, width), whole),
            pl.BlockSpec((total, width), whole),
            pl.BlockSpec((3, width, LANES), lambda g: (0, 0, g)),
            pl.BlockSpec((LANES, width), lambda g: (g, 0)),
            pl.BlockSpec((3, 8, LANES), lambda g: (0, 0, g)),
        ],
        out_shape=[
            jax.ShapeDtypeStruct((total, width), f32),
            jax.ShapeDtypeStruct((total, width), f32),
            jax.ShapeDtypeStruct((3, width, inner), bf16),
            jax.ShapeDtypeStruct((inner, width), bf16),
            jax.ShapeDtypeStruct((3, 8, inner), f32),
        ],
        scratch_shapes=[
            pltpu.VMEM((width, total), bf16),
            pltpu.VMEM((total, LANES), bf16),
            pltpu.VMEM((total, LANES), bf16),
            pltpu.VMEM((total, LANES), bf16),
            pltpu.VMEM((total, LANES), bf16),
            pltpu.VMEM((LANES, total), bf16),
            pltpu.VMEM((LANES, total), bf16),
            pltpu.VMEM((LANES, total), bf16),
            pltpu.VMEM((LANES, total), f32),
            pltpu.VMEM((LANES, total), f32),
            pltpu.VMEM((total, LANES), f32),
            pltpu.VMEM((total, LANES), f32),
            pltpu.VMEM((3, total, LANES), bf16),
            pltpu.VMEM((total, 128), f32),
        ],
        compiler_params=pltpu.CompilerParams(vmem_limit_bytes=60 * 2**20),
        cost_estimate=pl.CostEstimate(
            flops=flops, bytes_accessed=24 * 2**20, transcendentals=8 * total * total
        ),
        name="attention",
    )(length, hidden, out_grad, w_qkv, w_qkv, w_qkv, w_out, b_qkv, rope)


def ffn_kernel(
    h_ref,
    dy_ref,
    wf_ref,
    wp_ref,
    b_ref,
    out_ref,
    dh_ref,
    gf_ref,
    gp_ref,
    gb_ref,
    ht_s,
    act_s,
    dup_s,
):
    step = pl.program_id(0)
    total, width = h_ref.shape
    blocks = total // ROWS
    chunk = wf_ref.shape[1]

    @pl.when(step == 0)
    def _():
        for r in range(blocks):
            ht_s[:, r * ROWS : (r + 1) * ROWS] = h_ref[r * ROWS : (r + 1) * ROWS, :].T

    def one(r, total_grad):
        rows = pl.ds(pl.multiple_of(r * ROWS, ROWS), ROWS)
        up = dot_nn(h_ref[rows, :], wf_ref[...]) + b_ref[0:1, :]
        half = 0.5 + 0.5 * lax.erf(up * (1.0 / math.sqrt(2.0)))
        act = (up * half).astype(bf16)
        slope = half + up * (jnp.exp(-0.5 * up * up) * (1.0 / math.sqrt(2.0 * math.pi)))
        act_grad = dot_nt(dy_ref[rows, :], wp_ref[...])
        up_grad = (slope * act_grad).astype(bf16)
        act_s[rows, :] = act
        dup_s[rows, :] = up_grad
        out_part = dot_nn(act, wp_ref[...])
        dh_part = dot_nt(up_grad, wf_ref[...])

        @pl.when(step == 0)
        def _():
            out_ref[rows, :] = out_part
            dh_ref[rows, :] = dh_part

        @pl.when(step > 0)
        def _():
            out_ref[rows, :] += out_part
            dh_ref[rows, :] += dh_part

        return total_grad + jnp.sum(up_grad.astype(f32), axis=0, keepdims=True)

    sums = lax.fori_loop(0, blocks, one, jnp.zeros((1, chunk), f32))
    gb_ref[...] = jnp.broadcast_to(sums, (8, chunk))
    for r in range(8):
        size = width // 8
        rows = slice(r * size, (r + 1) * size)
        grad = dot_nn(ht_s[rows, :], dup_s[...]).astype(bf16)
        gf_ref[rows, :] = grad
    for r in range(chunk // ROWS):
        cols = slice(r * ROWS, (r + 1) * ROWS)
        grad = dot_nn(act_s[:, cols].T, dy_ref[...]).astype(bf16)
        gp_ref[cols, :] = grad


def ffn_branch(hidden, out_grad, w_fc, w_proj, b_fc):
    total, width = hidden.shape
    units = w_proj.shape[0]
    chunk = min(512, units)
    whole = lambda s: (0, 0)
    return pl.pallas_call(
        ffn_kernel,
        grid=(units // chunk,),
        in_specs=[
            pl.BlockSpec((total, width), whole),
            pl.BlockSpec((total, width), whole),
            pl.BlockSpec((width, chunk), lambda s: (0, s)),
            pl.BlockSpec((chunk, width), lambda s: (s, 0)),
            pl.BlockSpec((8, chunk), lambda s: (0, s)),
        ],
        out_specs=[
            pl.BlockSpec((total, width), whole),
            pl.BlockSpec((total, width), whole),
            pl.BlockSpec((width, chunk), lambda s: (0, s)),
            pl.BlockSpec((chunk, width), lambda s: (s, 0)),
            pl.BlockSpec((8, chunk), lambda s: (0, s)),
        ],
        out_shape=[
            jax.ShapeDtypeStruct((total, width), f32),
            jax.ShapeDtypeStruct((total, width), f32),
            jax.ShapeDtypeStruct((width, units), bf16),
            jax.ShapeDtypeStruct((units, width), bf16),
            jax.ShapeDtypeStruct((8, units), f32),
        ],
        scratch_shapes=[
            pltpu.VMEM((width, total), bf16),
            pltpu.VMEM((total, chunk), bf16),
            pltpu.VMEM((total, chunk), bf16),
        ],
        compiler_params=pltpu.CompilerParams(vmem_limit_bytes=60 * 2**20),
        cost_estimate=pl.CostEstimate(
            flops=2 * total * width * units * 6,
            bytes_accessed=28 * 2**20,
            transcendentals=2 * total * units,
        ),
        name="feed_forward",
    )(hidden, out_grad, w_fc, w_proj, b_fc)


def shift(block, axis, distance):
    count = lax.axis_size(axis)
    return lax.ppermute(block, axis, [(i, (i + distance) % count) for i in range(count)])


def swap_bit(block, axis, bit):
    return lax.ppermute(block, axis, [(i, i ^ bit) for i in range(lax.axis_size(axis))])


def shift_within(block, axis, size, distance):
    count = lax.axis_size(axis)
    return lax.ppermute(
        block,
        axis,
        [(i, i // size * size + (i % size + distance) % size) for i in range(count)],
    )


def pick(array, index, axis=0):
    return lax.dynamic_index_in_dim(array, index, axis, keepdims=False)


def order_two(flag, mine, other):
    first = flag == 0
    return jnp.stack([jnp.where(first, mine, other), jnp.where(first, other, mine)])


def gather_rows(local, place):
    dp, y, core, f = place["dp"], place["y"], place["core"], place["f"]
    count = lax.axis_size("fsdp")
    rows, cols = local.shape
    share = rows // lax.axis_size("dp")
    mine = lax.dynamic_slice_in_dim(local, dp * share, share, 0)
    got = jnp.stack([shift(mine, "fsdp", e) for e in range(1, count)])
    got = order_two(y, got, swap_bit(got, "dp", 2))
    got = order_two(core, got, swap_bit(got, "dp", 1))
    got = jnp.transpose(got, (2, 1, 0, 3, 4)).reshape(count - 1, rows, cols)
    if count == 2:
        return order_two(f, local, got[0])
    whole = jnp.zeros((count, rows, cols), local.dtype)
    whole = lax.dynamic_update_index_in_dim(whole, local, f, 0)
    for e in range(1, count):
        whole = lax.dynamic_update_index_in_dim(whole, got[e - 1], (f - e) % count, 0)
    return whole


def reduce_rows(partial, place, parts):
    dp, y, core, f, j = (place[k] for k in ("dp", "y", "core", "f", "j"))
    count, rows, cols = partial.shape
    share = rows // 4
    a = partial.reshape(count, 2, 2, share, cols)
    a = pick(a, core, 2) + swap_bit(pick(a, 1 - core, 2), "dp", 1)
    total = pick(a, f)
    for e in range(1, count):
        total = total + shift(pick(a, (f + e) % count), "fsdp", e)
    total = pick(total, y) + swap_bit(pick(total, 1 - y), "dp", 2)
    total = total + shift(total, "ctx", parts)
    if parts == 2:
        both = order_two(j, total, shift_within(total, "ctx", 2, 1))
    else:
        both = jnp.zeros((parts,) + total.shape, total.dtype)
        both = lax.dynamic_update_index_in_dim(both, total, j, 0)
        for e in range(1, parts):
            got = shift_within(total, "ctx", parts, e)
            both = lax.dynamic_update_index_in_dim(both, got, (j - e) % parts, 0)
    both = order_two(y, both, swap_bit(both, "dp", 2))
    both = order_two(core, both, swap_bit(both, "dp", 1))
    return jnp.transpose(both, (1, 0, 3, 2, 4)).reshape(rows, parts, cols).astype(f32)


def sum_everywhere(vector):
    for bit in (1, 2):
        vector = vector + swap_bit(vector, "dp", bit)
    for axis in ("fsdp", "ctx"):
        bit = 1
        while bit < lax.axis_size(axis):
            vector = vector + swap_bit(vector, axis, bit)
            bit *= 2
    return vector


def gather_sequence(blocks, place, parts):
    s, c = place["s"], place["c"]
    count = lax.axis_size("ctx")
    seqs, rows, width = blocks.shape
    pieces = [(c, pick(blocks, s))]
    for d in range(1, seqs):
        got = shift(pick(blocks, (s + d) % seqs), "ctx", d * parts)
        pieces.append(((c - d * parts) % count, got))
    arrived = []
    for d in range(seqs):
        arrived.append(pieces[d])
        for e in range(1, parts):
            source = s * parts + (place["j"] - e) % parts
            got = shift_within(pieces[d][1], "ctx", parts, e)
            arrived.append(((source - d * parts) % count, got))
    whole = jnp.zeros((count, rows, width), blocks.dtype)
    for at, piece in arrived:
        whole = lax.dynamic_update_index_in_dim(whole, piece, at, 0)
    return whole.reshape(count * rows, width)


def return_blocks(partial, place, parts, seqs):
    s, c, j = place["s"], place["c"], place["j"]
    count = lax.axis_size("ctx")
    rows = partial.shape[0] // count
    blocks = partial.reshape(seqs, parts, rows, -1)
    total = pick(blocks, j, 1).astype(f32)
    for e in range(1, parts):
        total = total + shift_within(pick(blocks, (j + e) % parts, 1), "ctx", parts, e).astype(f32)
    mine = [pick(total, s)]
    for d in range(1, seqs):
        mine.append(shift(pick(total, (s + d) % seqs).astype(bf16), "ctx", d * parts).astype(f32))
    if seqs == 2:
        return order_two(s, mine[0], mine[1])
    whole = jnp.zeros((seqs, rows, partial.shape[1]), f32)
    for d in range(seqs):
        whole = lax.dynamic_update_index_in_dim(whole, mine[d], (s - d) % seqs, 0)
    return whole


class Mover:
    def __init__(self, send, recv, local):
        self.send, self.recv, self.local = send, recv, local
        self.copies, self.left, self.started = [], [], 0

    def to(self, src, dst, axis, index):
        copy = self.remote(src, dst, len(self.copies), (axis, index))
        copy.start()
        self.copies.append(copy)
        return copy

    def here(self, src, dst):
        copy = pltpu.make_async_copy(src, dst, self.local.at[self.started])
        self.started += 1
        copy.start()
        return copy

    def out(self, src, dst):
        self.left.append(self.here(src, dst))

    def remote(self, src, dst, slot, to):
        return pltpu.make_async_remote_copy(
            src_ref=src,
            dst_ref=dst,
            send_sem=self.send.at[slot],
            recv_sem=self.recv.at[slot],
            device_id={to[0]: to[1]},
            device_id_type=pl.DeviceIdType.MESH,
        )

    def stay(self, src, dst, slot):
        return pltpu.make_async_copy(src, dst, self.local.at[slot])

    def finish(self):
        for copy in self.copies:
            copy.wait_send()
        for copy in self.left:
            copy.wait()


class Spot:
    def __init__(self):
        self.dp, self.c, self.f = (lax.axis_index(a) for a in ("dp", "ctx", "fsdp"))
        self.y, self.core = self.dp // 2, self.dp % 2
        self.s, self.j = self.c // 2, self.c % 2
        flip = lambda v: v + 1 - 2 * (v % 2)
        self.x_to = ("fsdp", 1 - self.f)
        self.y_to = ("dp", (1 - self.y) * 2 + self.core)
        self.core_to = ("dp", flip(self.dp))
        self.pair_to = ("ctx", flip(self.c))
        self.far_to = ("ctx", (1 - self.s) * 2 + self.j)

    def greet(self):
        barrier = pltpu.get_barrier_semaphore()
        partners = (self.x_to, self.y_to, self.core_to, self.pair_to, self.far_to)
        for axis, index in partners:
            pl.semaphore_signal(
                barrier, inc=1, device_id={axis: index}, device_id_type=pl.DeviceIdType.MESH
            )
        pl.semaphore_wait(barrier, len(partners))


def block(index, size):
    return pl.ds(pl.multiple_of(index * size, size), size)


def front_kernel(
    info_ref,
    x_ref,
    cot_ref,
    fc_ref,
    proj_ref,
    qkv_ref,
    out_ref,
    rope_ref,
    *rest,
):
    vector_refs, rest = rest[:8], rest[8:]
    (
        seq_in,
        seq_grad,
        w_qkv,
        w_out,
        pull,
        home,
        gp,
        gf,
        part,
        vectors,
        x_s,
        dy_s,
        cot_s,
        held_s,
        small_s,
        wf_s,
        wp_s,
        wq_s,
        wo_s,
        h_s,
        ht_s,
        act_s,
        dup_s,
        rope_s,
        q_s,
        k_s,
        vt_s,
        o_s,
        ot_s,
        kb_s,
        home_s,
        got_s,
        pull_s,
        gp_s,
        gf_s,
        core_got,
        x_got,
        vec_s,
        bfc_s,
        part_s,
        send,
        recv,
        local,
    ) = rest
    at = Spot()
    mover = Mover(send, recv, local)
    total, width = x_s.shape
    blocks = total // ROWS
    units = wp_s.shape[0]
    inner = wo_s.shape[0]
    head_size = 64
    length = jnp.where(at.s == 0, info_ref[0], info_ref[1])
    other = 1 - at.f
    far_c, pair_c = at.far_to[1], at.pair_to[1]
    last_c = (1 - at.s) * 2 + 1 - at.j

    load_x = mover.here(x_ref.at[at.s], x_s.at[block(at.c, ROWS)])
    load_cot = mover.here(cot_ref, cot_s)
    held_s[...] = jnp.zeros_like(held_s)
    row = 0
    for ref in vector_refs:
        size = small_s.shape[2]
        vector = ref[...].astype(f32).reshape(1, ref.shape[0])
        for start in range(0, ref.shape[0], size):
            held_s[row : row + 1, :] = vector[:, start : start + size]
            row += 1
    small_s[at.f] = held_s[...]
    load_rope = mover.here(rope_ref, rope_s)
    at.greet()

    small_copy = mover.to(held_s, small_s.at[at.f], *at.x_to)
    x_far = mover.to(x_ref.at[1 - at.s], x_s.at[block(at.c, ROWS)], *at.far_to)
    x_near = mover.to(x_ref.at[at.s], x_s.at[block(at.c, ROWS)], *at.pair_to)

    def fc_spans(k):
        size = units // 2
        return lambda r: [(fc_ref.at[r, block(2 * k + at.j, size)], pl.ds(0, size))]

    def qkv_spans(r):
        size = wq_s.shape[1] // 12
        return [
            (
                qkv_ref.at[r, block(t * 8 + h * 4 + at.j * 2 + g, size)],
                pl.ds((t * 4 + g * 2 + h) * size, size),
            )
            for t in range(3)
            for g in range(2)
            for h in range(2)
        ]

    def row_spans(ref, held):
        count = held.shape[0] // 2

        def spans(r):
            start = pl.multiple_of(at.j * count + r.start, r.size)
            return [(ref.at[pl.ds(start, r.size)], pl.ds(0, width))]

        return spans

    weights = dict(
        fc0=(wf_s.at[:, pl.ds(0, units // 2)], fc_spans(0)),
        fc1=(wf_s.at[:, pl.ds(units // 2, units // 2)], fc_spans(1)),
        qkv=(wq_s, qkv_spans),
        out=(wo_s, row_spans(out_ref, wo_s)),
        proj=(wp_s, row_spans(proj_ref, wp_s)),
    )
    got_x, got_y, got_core, stays = {}, {}, {}, {}

    def send_x(name):
        held, spans = weights[name]
        count = held.shape[0] // 2
        share = count // 4
        mine = pl.ds(pl.multiple_of(at.dp * share, share), share)
        there = pl.ds(pl.multiple_of(at.f * count + at.dp * share, share), share)
        got_x[name] = [mover.to(src, held.at[there, cols], *at.x_to) for src, cols in spans(mine)]

    def keep(name):
        held, spans = weights[name]
        count = held.shape[0] // 2
        there = block(at.f, count)
        stays[name] = [
            mover.here(src, held.at[there, cols]) for src, cols in spans(pl.ds(0, count))
        ]

    def quarter(name, dp):
        held = weights[name][0]
        count = held.shape[0] // 2
        share = count // 4
        return held.at[pl.ds(pl.multiple_of(other * count + dp * share, share), share)]

    def pass_x(name):
        for copy in got_x[name]:
            copy.wait_recv()
        mine = quarter(name, at.dp)
        got_y[name] = mover.to(mine, mine, *at.y_to)
        got_core[name] = [mover.to(mine, mine, *at.core_to)]

    def pass_y(name):
        got_y[name].wait_recv()
        mine = quarter(name, at.y_to[1])
        got_core[name].append(mover.to(mine, mine, *at.core_to))

    def arrived(name):
        for copy in got_core[name]:
            copy.wait_recv()
        for copy in stays[name]:
            copy.wait()

    send_x("fc0")
    for name in weights:
        keep(name)

    small_copy.wait_recv()

    def line(shard, r):
        return small_s[shard, r : r + 1, :]

    def joined(r):
        return jnp.concatenate([line(0, r), line(1, r)], axis=1)

    first = at.j == 0
    vec_s[...] = jnp.zeros_like(vec_s)
    part_s[...] = jnp.zeros_like(part_s)
    size = LANES // 2
    for t in range(3):
        for h in range(2):
            row = line((t * 2 + h) // 3, 6 + (t * 2 + h) % 3)
            row = jnp.where(first, row[:, :LANES], row[:, LANES:])
            for g in range(2):
                to = g * LANES + h * size
                vec_s[t : t + 1, to : to + size] = row[:, g * size : (g + 1) * size]
    vec_s[3:4, :] = joined(0)
    vec_s[4:5, :] = joined(1)
    vec_s[5:6, :] = joined(4) + joined(5)
    for h in range(2):
        for n in range(2):
            to = h * units // 2 + n * 512
            bfc_s[0:1, to : to + 512] = jnp.where(first, line(h, 9 + n), line(h, 11 + n))
    gain_one, shift_one = vec_s[3:4, :], vec_s[4:5, :]
    gain_two, shift_two = joined(2), joined(3)
    bfc_s[1:2, :width] = gain_two
    mover.out(vec_s, vectors)

    def normal(rows):
        v = x_s[rows, :].astype(f32)
        center = v - jnp.mean(v, axis=-1, keepdims=True)
        spread = jnp.mean(center * center, axis=-1, keepdims=True)
        return center * lax.rsqrt(spread + epsilon)

    def arrive(c):
        rows = block(c, ROWS)
        h = (normal(rows) * gain_two + shift_two).astype(bf16)
        h_s[rows, :] = h
        ht_s[:, rows] = h.T

    load_x.wait()
    arrive(at.c)
    load_cot.wait()
    for t in range(2):
        pos = at.c * ROWS + lax.broadcasted_iota(jnp.int32, (ROWS, width), 0)
        cot_s[t] = jnp.where(pos < info_ref[t], cot_s[t].astype(f32), 0.0).astype(bf16)
    dy_s[block(at.c, ROWS), :] = cot_s[at.s]
    pass_x("fc0")
    send_x("fc1")
    pass_x("fc1")
    send_x("qkv")
    pass_y("fc0")

    def span(b):
        return slice(b * ROWS, (b + 1) * ROWS)

    chunk = 512

    def forward(c, half):
        rows = block(c, ROWS)
        steps = units // chunk // 2

        def one(q, carry):
            cols = block(q, chunk)
            up = dot_nn(h_s[rows, :], wf_s[:, cols]) + bfc_s[0:1, cols]
            part = 0.5 + 0.5 * lax.erf(up * (1.0 / math.sqrt(2.0)))
            act_s[rows, cols] = (up * part).astype(bf16)
            slope = part + up * (jnp.exp(-0.5 * up * up) * (1.0 / math.sqrt(2.0 * math.pi)))
            dup_s[rows, cols] = slope.astype(bf16)
            return carry

        lax.fori_loop(half * steps, (half + 1) * steps, one, 0, unroll=steps)

    arrived("fc0")
    forward(at.c, 0)
    pass_y("fc1")
    pass_x("qkv")
    send_x("out")
    x_far.wait_recv()
    mine = x_s.at[block(far_c, ROWS)]
    x_last = mover.to(mine, mine, *at.pair_to)
    grad_far = mover.to(cot_s.at[1 - at.s], dy_s.at[block(at.c, ROWS)], *at.far_to)
    arrive(far_c)
    x_near.wait_recv()
    arrive(pair_c)
    arrived("fc1")
    pass_x("out")
    send_x("proj")
    forward(at.c, 1)
    for c in (far_c, pair_c):
        forward(c, 0)
        forward(c, 1)
    x_last.wait_recv()
    grad_near = mover.to(cot_s.at[at.s], dy_s.at[block(at.c, ROWS)], *at.pair_to)
    arrive(last_c)
    pass_y("qkv")
    pass_y("out")
    forward(last_c, 0)
    forward(last_c, 1)
    mover.out(x_s, seq_in)
    arrived("qkv")
    arrived("out")
    mover.out(wq_s, w_qkv)
    mover.out(wo_s, w_out)

    load_rope.wait()

    def table(n, rows):
        piece = rope_s[n, rows, :]
        return jnp.concatenate([piece] * (inner // 128), axis=1)

    def turned(v, rows):
        left = pltpu.roll(v, inner - ROT // 2, 1)
        right = pltpu.roll(v, ROT // 2, 1)
        return v * table(0, rows) + left * table(1, rows) + right * table(2, rows)

    for r in range(blocks):
        rows = span(r)
        h = (normal(rows) * gain_one + shift_one).astype(bf16)
        q = turned(dot_nn(h, wq_s[:, :inner]) + vec_s[0:1, :inner], rows).astype(bf16)
        q_s[rows, :] = (q.astype(f32) * 0.125).astype(bf16)
        k = dot_nn(h, wq_s[:, inner : 2 * inner]) + vec_s[1:2, :inner]
        k_s[rows, :] = turned(k, rows).astype(bf16)
        v = dot_nn(h, wq_s[:, 2 * inner :]) + vec_s[2:3, :inner]
        vt_s[:, rows] = v.astype(bf16).T
    pass_x("proj")
    grad_far.wait_recv()
    mine = dy_s.at[block(far_c, ROWS)]
    grad_last = mover.to(mine, mine, *at.pair_to)
    key_pos = lax.broadcasted_iota(jnp.int32, (total, 128), 0)
    kb_s[...] = jnp.where(key_pos < length, 0.0, masked_score)
    lane = lax.broadcasted_iota(jnp.int32, (ROWS, LANES), 1)
    causal = lax.broadcasted_iota(jnp.int32, (ROWS, ROWS), 0) <= lax.broadcasted_iota(
        jnp.int32, (ROWS, ROWS), 1
    )

    def one_head(g, i, head, carry):
        feats = pl.ds(pl.multiple_of(head * head_size, head_size), head_size)
        from_v = pl.ds(pl.multiple_of(g * LANES + head * head_size, head_size), head_size)
        cols = slice(g * LANES, (g + 1) * LANES)
        mine = (lane // head_size) == head
        qm = jnp.where(mine, q_s[span(i), cols], jnp.zeros((ROWS, LANES), bf16))
        scores = []
        top = None
        for b in range(i + 1):
            sc = dot_nt(k_s[span(b), cols], qm)
            kb = kb_s[span(b), :]
            sc = sc + jnp.concatenate([kb, kb], axis=1)
            if b == i:
                sc = jnp.where(causal, sc, masked_score)
            best = jnp.max(sc, axis=0, keepdims=True)
            top = best if top is None else jnp.maximum(top, best)
            scores.append(sc)
        row_sum = None
        o_t = None
        for b in range(i + 1):
            e = jnp.exp(scores[b] - top)
            add = jnp.sum(e, axis=0, keepdims=True)
            row_sum = add if row_sum is None else row_sum + add
            add = dot_nn(vt_s[from_v, span(b)], e.astype(bf16))
            o_t = add if o_t is None else o_t + add
        ot_s[feats, :] = o_t / row_sum
        return carry

    for i in range(blocks):
        for g in range(2):
            lax.fori_loop(0, LANES // head_size, functools.partial(one_head, g, i), 0, unroll=2)
            o = ot_s[...].T.astype(bf16)
            for h in range(2):
                to = h * LANES + g * size
                o_s[span(i), to : to + size] = o[:, h * size : (h + 1) * size]
        if i == 1:
            pass_y("proj")
    arrived("proj")
    for i in range(blocks):
        both = dot_nn(act_s[span(i), :], wp_s[...]) + dot_nn(o_s[span(i), :], wo_s[...])
        home_s[i] = both.astype(bf16)
    nears = [
        mover.to(home_s.at[2 * t + 1 - at.j], got_s.at[t], *at.pair_to) for t in range(2)
    ]

    grad_near.wait_recv()
    grad_last.wait_recv()
    mover.out(dy_s, seq_grad)
    bfc_s[2:3, :] = jnp.zeros((1, units), f32)
    for r in range(8):
        grad = dot_nn(act_s[:, r * ROWS : (r + 1) * ROWS].T, dy_s[...]).astype(bf16)
        for k in range(2):
            gp_s[k, r % 2, r // 4, r // 2 % 2] = grad[k * ROWS // 2 : (k + 1) * ROWS // 2]
    to_core = [mover.to(gp_s.at[k, 1 - at.core], core_got.at[k], *at.core_to) for k in range(2)]
    to_x = []

    def step_core(k):
        to_core[k].wait_recv()
        own, got = gp_s.at[k, at.core], core_got.at[k]
        own[1 - at.f] = own[1 - at.f] + got[1 - at.f]
        if k == 0:
            to_x.append(mover.to(own.at[1 - at.f], x_got, *at.x_to))
        own[at.f] = own[at.f] + got[at.f]

    def step_x():
        to_x[0].wait_recv()
        own = gp_s.at[0, at.core, at.f]
        own[...] = own[...] + x_got[...]
        mover.out(own, gp.at[0, 0])

    gain_sum = jnp.zeros((1, width), f32)
    shift_sum = jnp.zeros((1, width), f32)
    dy_sum = jnp.zeros((1, width), f32)
    for i in range(blocks):
        rows = span(i)

        def one(q, carry):
            cols = block(q, chunk)
            act_grad = dot_nt(dy_s[rows, :], wp_s[cols, :])
            up_grad = (dup_s[rows, cols].astype(f32) * act_grad).astype(bf16)
            dup_s[rows, cols] = up_grad
            bfc_s[2:3, cols] += jnp.sum(up_grad.astype(f32), axis=0, keepdims=True)
            return carry

        lax.fori_loop(0, units // chunk, one, 0, unroll=4)
        dh = dot_nt(dup_s[rows, :], wf_s[...])
        pull_s[rows, :] = (dh * gain_two).astype(bf16)
        gain_sum = gain_sum + jnp.sum(dh * normal(rows), axis=0, keepdims=True)
        shift_sum = shift_sum + jnp.sum(dh, axis=0, keepdims=True)
        dy_sum = dy_sum + jnp.sum(dy_s[rows, :].astype(f32), axis=0, keepdims=True)
        if i == 0:
            step_core(0)
        if i == 1:
            step_core(1)
            mover.out(gp_s.at[1, at.core], gp.at[1])
    mover.out(pull_s, pull)
    part_s[2:3, :] = gain_sum
    part_s[3:4, :] = shift_sum
    part_s[4:5, :] = dy_sum * 0.5
    none = jnp.zeros((2, width), f32)
    sums = jnp.concatenate([none, bfc_s[2:3, :width], bfc_s[2:3, width:], none, none], axis=0)
    part_s[8:16, :] = jnp.where(first, sums, jnp.concatenate([sums[4:], sums[:4]], axis=0))
    mover.out(part_s, part)
    rows_each = width // 8
    for k in range(2):
        for r in range(8):
            cols = slice(k * units // 2, (k + 1) * units // 2)
            grad = dot_nn(ht_s[r * rows_each : (r + 1) * rows_each, :], dup_s[:, cols])
            gf_s[k, r % 2, r // 4, r // 2 % 2] = grad.astype(bf16)
        mover.out(gf_s.at[k], gf.at[k])
        if k == 0:
            step_x()

    for t in range(2):
        nears[t].wait_recv()
        mine = home_s.at[2 * t + at.j]
        mine[...] = (mine[...].astype(f32) + got_s[t].astype(f32)).astype(bf16)
        mover.out(mine, home.at[t])
    mover.finish()


def front(info, x, cot, fc, proj, qkv, out, rope, vectors):
    seqs, rows, width = x.shape
    total = 4 * rows
    units = proj.shape[0]
    inner = out.shape[0]
    cell = (rows // 2, width)
    hbm = pl.BlockSpec(memory_space=pl.ANY)
    shape = lambda *dims: jax.ShapeDtypeStruct(dims, bf16)
    buf = lambda *dims: pltpu.VMEM(dims, bf16)
    wide = lambda *dims: pltpu.VMEM(dims, f32)
    return pl.pallas_call(
        front_kernel,
        in_specs=[pl.BlockSpec(memory_space=pltpu.SMEM)]
        + [hbm] * 7
        + [pl.BlockSpec(memory_space=pltpu.VMEM)] * 8,
        out_specs=[hbm] * 10,
        out_shape=[
            shape(total, width),
            shape(total, width),
            shape(width, 3 * inner),
            shape(inner, width),
            shape(total, width),
            shape(2, rows, width),
            shape(2, 2, 2, *cell),
            shape(2, 2, 2, 2, *cell),
            jax.ShapeDtypeStruct((16, width), f32),
            jax.ShapeDtypeStruct((8, width), f32),
        ],
        scratch_shapes=[
            buf(total, width),
            buf(total, width),
            buf(2, rows, width),
            wide(16, width // 2),
            wide(2, 16, width // 2),
            buf(width, units),
            buf(units, width),
            buf(width, 3 * inner),
            buf(inner, width),
            buf(total, width),
            buf(width, total),
            buf(total, units),
            buf(total, units),
            wide(*rope.shape),
            buf(total, inner),
            buf(total, inner),
            buf(inner, total),
            buf(total, inner),
            wide(LANES, ROWS),
            wide(total, 128),
            buf(4, rows, width),
            buf(2, rows, width),
            buf(total, width),
            buf(2, 2, 2, 2, *cell),
            buf(2, 2, 2, 2, *cell),
            buf(2, 2, 2, *cell),
            buf(2, *cell),
            wide(8, width),
            wide(8, units),
            wide(16, width),
            pltpu.SemaphoreType.DMA((48,)),
            pltpu.SemaphoreType.DMA((48,)),
            pltpu.SemaphoreType.DMA((48,)),
        ],
        compiler_params=pltpu.CompilerParams(
            collective_id=0, has_side_effects=True, vmem_limit_bytes=62 * 2**20
        ),
        name="front",
    )(info, x, cot, fc, proj, qkv, out, rope, *vectors)


def branch_kernel(
    length_ref,
    x_ref,
    dy_ref,
    wqkv_ref,
    wo_ref,
    bias_ref,
    rope_ref,
    out_ref,
    ffn_pull_ref,
    gp_ref,
    gf_ref,
    small_ref,
    summed,
    branch,
    pull,
    small,
    x_s,
    dy_s,
    h_s,
    ht_s,
    wqkv_s,
    wo_s,
    rope_s,
    q_s,
    k_s,
    v_s,
    do_s,
    kt_s,
    vt_s,
    dot_s,
    ot_s,
    dqt_s,
    dk_s,
    dv_s,
    dp_s,
    kb_s,
    begun_s,
    own_s,
    mine_s,
    core_s,
    x_got,
    y_got,
    far_got,
    home_s,
    home_got,
    out_s,
    small_s,
    small_got,
    send,
    recv,
    local,
):
    at = Spot()
    mover = Mover(send, recv, local)
    total, width = x_s.shape
    blocks = total // ROWS
    inner = wo_s.shape[0]
    head_size = 64
    length = jnp.where(at.s == 0, length_ref[0], length_ref[1])

    load_x = mover.here(x_ref, x_s)
    load_w = mover.here(wqkv_ref, wqkv_s)
    load_rope = mover.here(rope_ref, rope_s)
    load_dy = mover.here(dy_ref, dy_s)
    half = LANES // 2
    load_wo = [
        mover.here(
            wo_ref.at[pl.ds(h * LANES + g * half, half)],
            wo_s.at[pl.ds(g * LANES + h * half, half)],
        )
        for g in range(2)
        for h in range(2)
    ]
    load_small = mover.here(small_ref, small_s.at[0])
    load_out = mover.here(out_ref, out_s)
    at.greet()

    links = ("c", "x", "y", "z", "p", "ya", "yy", "c1", "c2")

    def own_of(n):
        return own_s.at[n - 1] if n < 4 else mine_s.at[n - 4, at.core]

    def cell(n, y):
        return begun_s.at[y] if n < 1 else own_of(n).at[at.f, y]

    def link(n, name):
        mine, other = summed.at[n, at.y, at.core], summed.at[n, 1 - at.y, at.core]
        if name == "c":
            src = (gf_ref.at[n - 2] if n < 4 else mine_s.at[n - 4]).at[1 - at.core]
            ends = (src, core_s.at[n - 2], at.core_to)
        elif name == "x":
            ends = (own_of(n).at[1 - at.f], x_got.at[n - 1], at.x_to)
        elif name == "y":
            ends = (cell(n, 1 - at.y), y_got.at[n], at.y_to)
        elif name == "z":
            ends = (cell(n, at.y), far_got.at[n], at.far_to)
        elif name == "p":
            ends = (y_got.at[n], summed.at[n, at.y, at.core, at.j], at.pair_to)
        elif name == "ya":
            ends = (y_got.at[n], summed.at[n, at.y, at.core, at.j], at.y_to)
        elif name == "yy":
            part = summed.at[n, at.y, at.core, 1 - at.j]
            ends = (part, part, at.y_to)
        elif name == "c1":
            ends = (mine, mine, at.core_to)
        else:
            ends = (other, other, at.core_to)
        return mover.remote(ends[0], ends[1], n * len(links) + links.index(name), ends[2])

    def load(n):
        if n == 0:
            return mover.stay(gp_ref.at[0, 0], begun_s, 24)
        src = gp_ref.at[1] if n == 1 else gf_ref.at[n - 2, at.core]
        return mover.stay(src, own_s.at[n - 1], 24 + n)

    def keep(n):
        return mover.stay(y_got.at[n], summed.at[n, at.y, at.core, at.j], 28 + n)

    def step_start(n):
        if n < 4:
            load(n).start()
        link(n, "c").start()

    def step_core(n):
        if n < 4:
            load(n).wait()
        link(n, "c").wait_recv()
        own, got = own_of(n), core_s.at[n - 2]
        own[1 - at.f] = own[1 - at.f] + got[1 - at.f]
        link(n, "x").start()
        own[at.f] = own[at.f] + got[at.f]

    def step_x(n):
        link(n, "x").wait_recv()
        own, got = own_of(n), x_got.at[n - 1]
        own[at.f, 1 - at.y] = own[at.f, 1 - at.y] + got[1 - at.y]
        link(n, "y").start()
        own[at.f, at.y] = own[at.f, at.y] + got[at.y]

    def step_y(n):
        link(n, "y").wait_recv()
        mine = cell(n, at.y)
        mine[...] = mine[...] + y_got[n]
        link(n, "z").start()

    def step_far(n):
        link(n, "z").wait_recv()
        y_got[n] = cell(n, at.y)[...] + far_got[n]
        link(n, "p").start()
        link(n, "ya").start()
        keep(n).start()

    def step_pair(n):
        link(n, "p").wait_recv()
        keep(n).wait()
        link(n, "yy").start()
        link(n, "c1").start()

    def step_yy(n):
        link(n, "ya").wait_recv()
        link(n, "yy").wait_recv()
        link(n, "c2").start()

    base = 6 * len(links)

    def near(t):
        return mover.remote(home_s.at[2 * t + 1 - at.j], home_got.at[t], base + t, at.pair_to)

    def last(t):
        mine, dst = home_s.at[2 * t + at.j], pull.at[at.s]
        return mover.remote(mine, dst, base + 2, at.far_to), mover.stay(mine, dst, 34)

    def out_home():
        far = mover.remote(out_s.at[1 - at.s], branch.at[at.s], base + 3, at.far_to)
        return far, mover.stay(out_s.at[at.s], branch.at[at.s], 35)

    def out_start(_):
        load_out.wait()
        for copy in out_home():
            copy.start()

    def home_near(t):
        near(t).start()

    def home_sum(t):
        near(t).wait_recv()
        mine = home_s.at[2 * t + at.j]
        mine[...] = (mine[...].astype(f32) + home_got[t].astype(f32)).astype(bf16)
        far, stay = last(t)
        pl.when(at.s == t)(stay.start)
        pl.when(at.s != t)(far.start)

    trips = (at.core_to, at.x_to, at.y_to, at.far_to, at.pair_to)

    def small_trip(n):
        return mover.remote(small_s.at[n], small_got.at[n], base + 4 + n, trips[n])

    def small_step(n):
        if n > 0:
            small_trip(n - 1).wait_recv()
            small_s[n] = small_s[n - 1] + small_got[n - 1]
        if n < 5:
            small_trip(n).start()
        else:
            mover.out(small_s.at[5], small)

    def end():
        for n in range(6):
            link(n, "c1").wait_recv()
            link(n, "c2").wait_recv()
            for name in links[max(2 - n, 0) :]:
                link(n, name).wait_send()
        for far, stay in (last(0), out_home()):
            far.wait()
            stay.wait()
        for t in range(2):
            near(t).wait_send()
        for n in range(5):
            small_trip(n).wait_send()

    acts = dict(
        start=step_start,
        core=step_core,
        x=step_x,
        y=step_y,
        far=step_far,
        pair=step_pair,
        yy=step_yy,
        near=home_near,
        sum=home_sum,
        oh=out_start,
        small=small_step,
    )

    def turn(*place):
        for word in PLAN.get(",".join(str(v) for v in place), ()):
            name, n = word.split(":")
            acts[name](int(n))

    for n in range(2):
        load(n).start()
    for n in range(2, 4):
        step_start(n)
    load(0).wait()
    link(0, "y").start()
    load(1).wait()
    link(1, "x").start()

    def normal(rows):
        v = x_s[rows, :].astype(f32)
        center = v - jnp.mean(v, axis=-1, keepdims=True)
        spread = jnp.mean(center * center, axis=-1, keepdims=True)
        return center * lax.rsqrt(spread + epsilon)

    def table(n, rows):
        part = rope_s[n, rows, :]
        return jnp.concatenate([part, part], axis=1)

    def turned(v, rows, sign):
        left = pltpu.roll(v, LANES - ROT // 2, 1)
        right = pltpu.roll(v, ROT // 2, 1)
        moved = left * table(1, rows) + right * table(2, rows)
        return v * table(0, rows) + moved if sign > 0 else v * table(0, rows) - moved

    key_pos = lax.broadcasted_iota(jnp.int32, (total, 128), 0)
    kb_s[...] = jnp.where(key_pos < length, 0.0, masked_score)
    lane = lax.broadcasted_iota(jnp.int32, (ROWS, LANES), 1)
    causal = lax.broadcasted_iota(jnp.int32, (ROWS, ROWS), 0) <= lax.broadcasted_iota(
        jnp.int32, (ROWS, ROWS), 1
    )
    gain, offset = bias_ref[3:4, :], bias_ref[4:5, :]

    def span(b):
        return slice(b * ROWS, (b + 1) * ROWS)

    def project(g):
        cols = lambda t: slice(t * inner + g * LANES, t * inner + (g + 1) * LANES)
        bias = lambda t: bias_ref[t : t + 1, g * LANES : (g + 1) * LANES]
        for r in range(blocks):
            rows = span(r)
            if g == 0:
                hr = (normal(rows) * gain + offset).astype(bf16)
                h_s[rows, :] = hr
                ht_s[:, rows] = hr.T
                if r == 0:
                    load_w.wait()
                    load_rope.wait()
                    load_dy.wait()
                    for copy in load_wo:
                        copy.wait()
            else:
                hr = h_s[rows, :]
            q = turned(dot_nn(hr, wqkv_s[:, cols(0)]) + bias(0), rows, 1).astype(bf16)
            q_s[rows, :] = (q.astype(f32) * 0.125).astype(bf16)
            k = turned(dot_nn(hr, wqkv_s[:, cols(1)]) + bias(1), rows, 1).astype(bf16)
            k_s[rows, :] = k
            kt_s[:, rows] = k.T
            v = (dot_nn(hr, wqkv_s[:, cols(2)]) + bias(2)).astype(bf16)
            v_s[rows, :] = v
            vt_s[:, rows] = v.T
            do = dot_nt(dy_s[rows, :], wo_s[g * LANES : (g + 1) * LANES, :]).astype(bf16)
            do_s[rows, :] = do
            dot_s[:, rows] = do.T
            turn("p%d" % g, r)
        dk_s[...] = jnp.zeros_like(dk_s)
        dv_s[...] = jnp.zeros_like(dv_s)

    def one_head(g, i, head, carry):
        feats = pl.ds(pl.multiple_of(head * head_size, head_size), head_size)
        mine = (lane // head_size) == head
        zero = jnp.zeros((ROWS, LANES), bf16)
        rows = span(i)
        qm = jnp.where(mine, q_s[rows, :], zero)
        dom = jnp.where(mine, do_s[rows, :], zero)
        scores = []
        top = None
        for b in range(i + 1):
            sc = dot_nt(k_s[span(b), :], qm)
            kb = kb_s[span(b), :]
            sc = sc + jnp.concatenate([kb, kb], axis=1)
            if b == i:
                sc = jnp.where(causal, sc, masked_score)
            best = jnp.max(sc, axis=0, keepdims=True)
            top = best if top is None else jnp.maximum(top, best)
            scores.append(sc)
        row_sum = None
        for b in range(i + 1):
            scores[b] = jnp.exp(scores[b] - top)
            part = jnp.sum(scores[b], axis=0, keepdims=True)
            row_sum = part if row_sum is None else row_sum + part
        inverse = 1.0 / row_sum
        o_t = None
        for b in range(i + 1):
            scores[b] = scores[b] * inverse
            low = scores[b].astype(bf16)
            dv_s[span(b), :] += dot_nn(low, dom)
            part = dot_nn(vt_s[feats, span(b)], low)
            o_t = part if o_t is None else o_t + part
        ot_s[feats, rows] = o_t
        delta = jnp.sum(dot_s[feats, rows].astype(f32) * o_t, axis=0, keepdims=True)
        dq_t = None
        for b in range(i + 1):
            dp = dot_nt(v_s[span(b), :], dom)
            ds = (scores[b] * (dp - delta)).astype(bf16)
            dk_s[span(b), :] += dot_nn(ds, qm)
            part = dot_nn(kt_s[feats, span(b)], ds)
            dq_t = part if dq_t is None else dq_t + part
        dqt_s[feats, rows] = dq_t * 0.125
        for h in range(LANES // head_size):
            if "%d,%d,%d" % (g, i, h) in PLAN:
                pl.when(head == h)(functools.partial(turn, g, i, h))
        return carry

    def finish_block(g, i, sums):
        rows = span(i)
        cols = slice(g * LANES, (g + 1) * LANES)
        dq = turned(dqt_s[:, rows].T, rows, -1).astype(bf16)
        dk = turned(dk_s[rows, :], rows, -1).astype(bf16)
        dv = dv_s[rows, :].astype(bf16)
        for t, grad in enumerate((dq, dk, dv)):
            sums[t] = sums[t] + jnp.sum(grad.astype(f32), axis=0, keepdims=True)
            dp_s[t, rows, cols] = grad

    def finish_rows(i, gain_sum, shift_sum):
        rows = span(i)
        dh = dot_nt(dp_s[0, rows, :], wqkv_s[:, :inner])
        dh = dh + dot_nt(dp_s[1, rows, :], wqkv_s[:, inner : 2 * inner])
        dh = dh + dot_nt(dp_s[2, rows, :], wqkv_s[:, 2 * inner :])
        home_s[i] = (dh * gain + home_s[i].astype(f32)).astype(bf16)
        gain_sum = gain_sum + jnp.sum(dh * normal(rows), axis=0, keepdims=True)
        return gain_sum, shift_sum + jnp.sum(dh, axis=0, keepdims=True)

    def weight_grads(g):
        cols = slice(g * LANES, (g + 1) * LANES)
        size = width // 8
        for t in range(3):
            for r in range(8):
                grad = dot_nn(ht_s[r * size : (r + 1) * size, :], dp_s[t, :, cols])
                mine_s[g, r % 2, r // 4, r // 2 % 2, :, t * LANES : (t + 1) * LANES] = grad.astype(bf16)
        grad = dot_nn(ot_s[...].astype(bf16), dy_s[...]).astype(bf16)
        size = LANES // 8
        for r in range(8):
            for b in range(4):
                mine_s[
                    g, r % 2, r // 4, r // 2 % 2, b * size : (b + 1) * size, 3 * LANES :
                ] = grad[r * size : (r + 1) * size, b * LANES : (b + 1) * LANES]

    load_x.wait()
    loads_home = [
        mover.here(ffn_pull_ref.at[block(b, ROWS)], home_s.at[b]) for b in range(blocks)
    ]
    load_small.wait()
    gain_sum = jnp.zeros((1, width), f32)
    shift_sum = jnp.zeros((1, width), f32)
    for g in range(2):
        project(g)
        sums = [jnp.zeros((1, LANES), f32) for _ in range(3)]
        for i in reversed(range(blocks)):
            lax.fori_loop(0, LANES // head_size, functools.partial(one_head, g, i), 0)
            finish_block(g, i, sums)
            if g == 1:
                if i == blocks - 1:
                    for copy in loads_home:
                        copy.wait()
                gain_sum, shift_sum = finish_rows(i, gain_sum, shift_sum)
            turn(g, i)
        weight_grads(g)
        row = lax.broadcasted_iota(jnp.int32, (8, LANES), 0)
        for t in range(3):
            start = t % 2 * inner + g * LANES
            cols = slice(start, start + LANES)
            here = row == 4 * at.j + t // 2
            small_s[0, 8:16, cols] = jnp.where(here, sums[t], small_s[0, 8:16, cols])
        if g == 0:
            turn("grads")
    small_s[0, 0:1, :] = gain_sum
    small_s[0, 1:2, :] = shift_sum
    turn("tail")
    end()
    mover.finish()


PLAN = {
    "p0,3": ("y:0",),
    "0,3,1": ("core:2",),
    "0,3,2": ("x:1",),
    "0,2,2": ("y:1",),
    "0,2": ("far:0", "core:3",),
    "0,1,1": ("x:2",),
    "grads": ("y:2",),
    "p1,0": ("far:1",),
    "p1,2": ("x:3",),
    "1,3,3": ("far:2", "pair:0", "y:3",),
    "1,2,3": ("start:4",),
    "1,2": ("near:1",),
    "1,1,1": ("core:4",),
    "1,1,2": ("pair:1",),
    "1,0,0": ("oh:0",),
    "1,0,1": ("x:4",),
    "1,0": ("yy:1",),
    "tail": ("far:3", "small:0", "start:5", "pair:2", "y:4", "small:1", "near:0", "core:5", "x:5", "y:5", "pair:3", "small:2", "far:4", "small:3", "sum:0", "yy:0", "yy:3", "far:5", "pair:4", "yy:2", "pair:5", "sum:1", "small:4", "yy:4", "yy:5", "small:5",),
}


def branch_and_sums(length, x, dy, w_qkv, w_out, bias, rope, out, ffn_pull, gp, gf, small):
    total, width = x.shape
    inner = w_out.shape[0]
    cell = (ROWS // 2, width)
    hbm = pl.BlockSpec(memory_space=pl.ANY)
    vmem = pl.BlockSpec(memory_space=pltpu.VMEM)
    home = jax.ShapeDtypeStruct((2, ROWS, width), bf16)
    buf = lambda dims, kind=bf16: pltpu.VMEM(tuple(dims), kind)
    return pl.pallas_call(
        branch_kernel,
        in_specs=[pl.BlockSpec(memory_space=pltpu.SMEM)] + [hbm] * 4 + [vmem] + [hbm] * 6,
        out_specs=[hbm] * 4,
        out_shape=[
            jax.ShapeDtypeStruct((6, 2, 2, 2) + cell, bf16),
            home,
            home,
            jax.ShapeDtypeStruct(small.shape, f32),
        ],
        scratch_shapes=[
            buf((total, width)),
            buf((total, width)),
            buf((total, width)),
            buf((width, total)),
            buf((width, 3 * inner)),
            buf((inner, width)),
            buf((3, total, 128), f32),
            buf((total, LANES)),
            buf((total, LANES)),
            buf((total, LANES)),
            buf((total, LANES)),
            buf((LANES, total)),
            buf((LANES, total)),
            buf((LANES, total)),
            buf((LANES, total), f32),
            buf((LANES, total), f32),
            buf((total, LANES), f32),
            buf((total, LANES), f32),
            buf((3, total, inner)),
            buf((total, 128), f32),
            buf((2,) + cell),
            buf((3, 2, 2) + cell),
            buf((2, 2, 2, 2) + cell),
            buf((4, 2, 2) + cell),
            buf((5, 2) + cell),
            buf((6,) + cell),
            buf((6,) + cell),
            buf((total // ROWS, ROWS, width)),
            buf((2, ROWS, width)),
            buf((2, ROWS, width)),
            buf((6,) + small.shape, f32),
            buf((5,) + small.shape, f32),
            pltpu.SemaphoreType.DMA((80,)),
            pltpu.SemaphoreType.DMA((80,)),
            pltpu.SemaphoreType.DMA((40,)),
        ],
        compiler_params=pltpu.CompilerParams(
            collective_id=1, has_side_effects=True, vmem_limit_bytes=62 * 2**20
        ),
        name="branch",
    )(length, x, dy, w_qkv, w_out, bias, rope, out, ffn_pull, gp, gf, small)


def last_kernel(
    lengths_ref,
    summed_ref,
    x_ref,
    cot_ref,
    branch_ref,
    pull_ref,
    vectors_ref,
    sums_ref,
    residual_out,
    residual_grad,
    d_proj,
    d_fc,
    d_qkv,
    d_out,
    d_gain_one,
    d_shift_one,
    d_gain_two,
    d_shift_two,
    d_bias_out,
    d_bias_proj,
    d_bqkv,
    d_bfc,
):
    size, width = summed_ref.shape[4:]
    y, core = pl.program_id(0), pl.program_id(1)
    for k in range(2):
        for p in range(2):
            d_proj[p, 0, 0, k] = summed_ref[k, 0, 0, p].astype(f32)
            to = (2 * k + p) * width
            d_fc[:, to : to + width] = summed_ref[2 + k, 0, 0, p].astype(f32)

    rows = x_ref.shape[1]
    features = x_ref[0].astype(f32)
    residual_out[0] = (features + branch_ref[0].astype(f32) + vectors_ref[5:6, :]).astype(bf16)
    hat, inverse = normalize(features)
    pulled = pull_ref[0].astype(f32)
    pulled = inverse * (
        pulled
        - jnp.mean(pulled, axis=-1, keepdims=True)
        - hat * jnp.mean(pulled * hat, axis=-1, keepdims=True)
    )
    start = (lax.axis_index("ctx") * 2 + core) * rows
    valid = start + lax.broadcasted_iota(jnp.int32, (rows, width), 0) < lengths_ref[y]
    own = jnp.where(valid, cot_ref[0].astype(f32), 0.0)
    residual_grad[0] = (own + pulled).astype(bf16)

    for g in range(2):
        for p in range(2):
            for t in range(3):
                for h in range(2):
                    cols = slice((t * 2 + h) * 128, (t * 2 + h + 1) * 128)
                    to = t * 8 + h * 4 + p * 2 + g
                    got = summed_ref[4 + g, 0, 0, p, :, cols]
                    d_qkv[:, to * 128 : (to + 1) * 128] = got.astype(f32)
            for b in range(4):
                got = summed_ref[4 + g, 0, 0, p, b * size // 4 : (b + 1) * size // 4, 3 * LANES :]
                d_out[p, g, 0, 0, :, b * LANES : (b + 1) * LANES] = got.astype(f32)

    @pl.when(y * 2 + core == 0)
    def _():
        first = lax.axis_index("fsdp") == 0
        half = width // 2
        gains = (d_gain_one, d_shift_one, d_gain_two, d_shift_two, d_bias_out)
        for r, ref in (*enumerate(gains), (4, d_bias_proj)):
            line = sums_ref[r : r + 1, :]
            ref[...] = jnp.where(first, line[:, :half], line[:, half:]).reshape(half)
        pieces = []
        for t in range(3):
            for h in range(2):
                for p in range(2):
                    for g in range(2):
                        at = t % 2 * half + (g * 2 + h) * 128
                        pieces.append(sums_ref[8 + 4 * p + t // 2 : 9 + 4 * p + t // 2, at : at + 128])
        line = jnp.concatenate(pieces, axis=1)
        count = 3 * half
        d_bqkv[...] = jnp.where(first, line[:, :count], line[:, count:]).reshape(count)
        line = jnp.concatenate(
            [jnp.where(first, sums_ref[r : r + 1, :], sums_ref[r + 1 : r + 2, :]) for r in (10, 14)],
            axis=1,
        )
        d_bfc[...] = line.reshape(2 * width)


def last_pass(lengths, summed, x, cot, branch, pull, vectors, sums, proj_shape, fc_shape, qkv_shape, out_shape):
    size, width = summed.shape[4:]
    rows = x.shape[1] // 2
    shape = lambda *dims: jax.ShapeDtypeStruct(dims, f32)
    token = pl.BlockSpec((1, rows, width), lambda y, c: (y, c, 0))
    line = lambda count: pl.BlockSpec((count,), lambda y, c: (0,))
    table = lambda count: pl.BlockSpec((count, width), lambda y, c: (0, 0))
    counts = [width // 2] * 6 + [3 * width // 2, 2 * width]
    residual_out, residual_grad, d_proj, d_fc, d_qkv, d_out, *vectors_out = pl.pallas_call(
        last_kernel,
        grid=(2, 2),
        in_specs=[
            pl.BlockSpec(memory_space=pltpu.SMEM),
            pl.BlockSpec((6, 1, 1, 2, size, width), lambda y, c: (0, y, c, 0, 0, 0)),
            token,
            token,
            token,
            token,
            table(8),
            table(16),
        ],
        out_specs=[
            token,
            token,
            pl.BlockSpec((2, 1, 1, 2, size, width), lambda y, c: (0, y, c, 0, 0, 0)),
            pl.BlockSpec((size, 4 * width), lambda y, c: (y * 2 + c, 0)),
            pl.BlockSpec((size, qkv_shape[1]), lambda y, c: (y * 2 + c, 0)),
            pl.BlockSpec((2, 2, 1, 1, size // 4, width), lambda y, c: (0, 0, y, c, 0, 0)),
        ]
        + [line(count) for count in counts],
        out_shape=[
            jax.ShapeDtypeStruct(x.shape, bf16),
            jax.ShapeDtypeStruct(x.shape, bf16),
            shape(2, 2, 2, 2, size, width),
            shape(*fc_shape),
            shape(*qkv_shape),
            shape(2, 2, 2, 2, size // 4, width),
        ]
        + [shape(count) for count in counts],
        compiler_params=pltpu.CompilerParams(vmem_limit_bytes=62 * 2**20),
        name="last",
    )(lengths, summed, x, cot, branch, pull, vectors, sums)
    grads = (d_proj.reshape(proj_shape), d_fc, d_qkv, d_out.reshape(out_shape))
    return residual_out, residual_grad, grads, vectors_out


def normalize(features):
    center = features - jnp.mean(features, axis=-1, keepdims=True)
    spread = jnp.mean(center * center, axis=-1, keepdims=True)
    inverse = lax.rsqrt(spread + epsilon)
    return center * inverse, inverse


def rope_tables(total, head_size):
    half = ROT // 2
    inverse = (rope_base ** (-(2.0 * np.arange(half)) / ROT)).astype(np.float32)
    angles = np.arange(total, dtype=np.float32)[:, None] * inverse[None, :]
    cosine, sine = np.cos(angles), np.sin(angles)
    rest = np.zeros((total, head_size - ROT), np.float32)
    none = np.zeros((total, half), np.float32)
    same = np.concatenate([cosine, cosine, rest + 1.0], axis=1)
    ahead = np.concatenate([-sine, none, rest], axis=1)
    behind = np.concatenate([none, sine, rest], axis=1)
    return jnp.asarray(np.tile(np.stack([same, ahead, behind]), (1, 1, 128 // head_size)), f32)


def finish(residual_in, cotangent, lengths, start, branch, pulled, bias):
    features = residual_in.astype(f32)
    residual_out = (features + branch + bias).astype(bf16)
    own_hat, own_inverse = normalize(features)
    pulled = own_inverse * (
        pulled
        - jnp.mean(pulled, axis=-1, keepdims=True)
        - own_hat * jnp.mean(pulled * own_hat, axis=-1, keepdims=True)
    )
    own_pos = start + jnp.arange(residual_in.shape[1], dtype=jnp.int32)
    valid = (own_pos[None, :] < lengths[:, None])[..., None]
    residual_grad = (jnp.where(valid, cotangent.astype(f32), 0.0) + pulled).astype(bf16)
    return residual_out, residual_grad


def fast_block(residual_in, lengths, cotangent, weights, small, rope):
    weight_fc, weight_proj, weight_qkv, weight_out = weights
    seq_in, seq_grad, w_qkv, w_out, pull, home, gp, gf, part, vectors = front(
        lengths, residual_in, cotangent, *weights, rope, small
    )
    summed, branch, pulled, sums = branch_and_sums(
        lengths, seq_in, seq_grad, w_qkv, w_out, vectors, rope, home, pull, gp, gf, part
    )
    residual_out, residual_grad, grads, vectors_out = last_pass(
        lengths,
        summed,
        residual_in,
        cotangent,
        branch,
        pulled,
        vectors,
        sums,
        weight_proj.shape,
        weight_fc.shape,
        weight_qkv.shape,
        weight_out.shape,
    )
    d_proj, d_fc, d_qkv, d_out = grads
    d_gain_one, d_shift_one, d_gain_two, d_shift_two, d_bout, d_bproj, d_bqkv, d_bfc = vectors_out
    return (
        residual_out,
        residual_grad,
        d_gain_one,
        d_shift_one,
        d_qkv,
        d_bqkv,
        d_out,
        d_bout,
        d_gain_two,
        d_shift_two,
        d_fc,
        d_bfc,
        d_proj,
        d_bproj,
    )


def per_device(
    residual_in,
    lengths,
    gain_attn,
    shift_attn,
    weight_qkv,
    bias_qkv,
    weight_out,
    bias_out,
    gain_ffn,
    shift_ffn,
    weight_fc,
    bias_fc,
    weight_proj,
    bias_proj,
    cotangent,
):
    seqs, block_rows, width = residual_in.shape
    n_ctx, n_fsdp = lax.axis_size("ctx"), lax.axis_size("fsdp")
    parts = n_ctx // seqs
    total = n_ctx * block_rows
    units = weight_fc.shape[1]
    head_size = width // HEADS
    c, f, dp = lax.axis_index("ctx"), lax.axis_index("fsdp"), lax.axis_index("dp")
    s, j = c // parts, c % parts
    place = dict(c=c, f=f, dp=dp, s=s, j=j, y=dp // 2, core=dp % 2)
    spread_heads = HEADS % (n_fsdp * parts) == 0
    n_h = n_fsdp if spread_heads else 1
    inner = width // parts

    rows_here = weight_qkv.shape[0]
    own_heads = lambda v: pick(v.reshape(3, n_h, parts, -1), j, 2)
    fast = (seqs, n_ctx, n_fsdp, lax.axis_size("dp")) == (2, 4, 2, 4)
    small_local = jnp.concatenate(
        [gain_attn, shift_attn, gain_ffn, shift_ffn, bias_out, bias_proj, bias_qkv, bias_fc]
    )
    part_width = width // n_fsdp
    length = pick(lengths, s)
    rope = rope_tables(total, head_size)
    own_part = lambda v, size=part_width: lax.dynamic_slice_in_dim(v, f * size, size)
    if fast:
        return fast_block(
            residual_in,
            lengths,
            cotangent,
            (weight_fc, weight_proj, weight_qkv, weight_out),
            (gain_attn, shift_attn, gain_ffn, shift_ffn, bias_out, bias_proj, bias_qkv, bias_fc),
            rope,
        )
    small = lax.all_gather(small_local, "fsdp", axis=0)
    vec = lambda at, size: small[:, at : at + size].reshape(-1).astype(f32)
    gain_one, shift_one, gain_two, shift_two, b_out, b_proj = (
        vec(i * part_width, part_width) for i in range(6)
    )
    b_qkv = vec(6 * part_width, 3 * part_width)
    b_fc = vec(9 * part_width, units // n_fsdp)

    fc_local = pick(weight_fc.reshape(rows_here, n_fsdp, parts, -1), j, 2).reshape(rows_here, -1)
    proj_local = pick(weight_proj.reshape(parts, -1, width), j)
    qkv_local = pick(weight_qkv.reshape(rows_here, 3, n_h, parts, -1), j, 3).reshape(rows_here, -1)
    seq_in = gather_sequence(residual_in, place, parts)
    w_fc = gather_rows(fc_local, place).reshape(width, -1)
    w_proj = gather_rows(proj_local, place).reshape(-1, width)
    seq_grad = gather_sequence(cotangent, place, parts)
    w_qkv = gather_rows(qkv_local, place).reshape(width, -1)
    if spread_heads:
        w_out = gather_rows(pick(weight_out.reshape(parts, -1, width), j), place).reshape(-1, width)
    else:
        w_out = lax.all_gather(weight_out, "fsdp", axis=0, tiled=True)
        w_out = pick(w_out.reshape(parts, -1, width), j)
    b_qkv_j = own_heads(b_qkv).reshape(3, 1, inner)
    b_fc_j = pick(b_fc.reshape(n_fsdp, parts, -1), j, 1).reshape(1, -1)
    b_fc_j = jnp.broadcast_to(b_fc_j, (8, b_fc_j.shape[1]))

    positions = jnp.arange(total, dtype=jnp.int32)
    seq_grad = jnp.where((positions < length)[:, None], seq_grad, jnp.zeros((), bf16))
    xhat, _ = normalize(seq_in.astype(f32))
    hidden_one = (xhat * gain_one + shift_one).astype(bf16)
    hidden_two = (xhat * gain_two + shift_two).astype(bf16)

    ffn_out, ffn_dh, g_fc, g_proj, g_bfc = ffn_branch(
        hidden_two, seq_grad, w_fc, w_proj, b_fc_j
    )
    ffn_sums = (jnp.sum(ffn_dh * xhat, axis=0), jnp.sum(ffn_dh, axis=0))
    own_grad = jnp.sum(seq_grad.astype(f32), axis=0) / parts
    attn_out, attn_dh, g_qkv, g_out, g_bqkv = attention_branch(
        length[None],
        hidden_one,
        seq_grad,
        w_qkv,
        w_out,
        jnp.broadcast_to(b_qkv_j, (3, 8, inner)),
        jnp.tile(rope, (1, 1, LANES // 128)),
    )
    g_bqkv_all = jnp.zeros((3, n_h, parts, inner // n_h), f32)
    g_bqkv_all = lax.dynamic_update_index_in_dim(
        g_bqkv_all, g_bqkv[:, 0].reshape(3, n_h, -1), j, 2
    )
    g_bfc_all = jnp.zeros((n_fsdp, parts, units // (n_fsdp * parts)), f32)
    g_bfc_all = lax.dynamic_update_index_in_dim(g_bfc_all, g_bfc[0].reshape(n_fsdp, -1), j, 1)
    rows_of = (
        jnp.sum(attn_dh * xhat, axis=0),
        jnp.sum(attn_dh, axis=0),
        *ffn_sums,
        own_grad,
        g_bqkv_all.reshape(-1),
        g_bfc_all.reshape(-1),
    )
    flat = sum_everywhere(jnp.concatenate(rows_of).reshape(-1, 128)).reshape(-1)
    small_grads = []
    at = 0
    for entry in rows_of:
        size = entry.shape[0]
        small_grads.append(own_part(flat[at : at + size], size // n_fsdp))
        at += size
    d_gain_one, d_shift_one, d_gain_two, d_shift_two, d_bias, d_bqkv, d_bfc = small_grads
    branch_part = (attn_out + ffn_out).astype(bf16)
    pull_part = (attn_dh * gain_one + ffn_dh * gain_two).astype(bf16)
    d_proj = reduce_rows(g_proj.reshape(n_fsdp, -1, width), place, parts)
    d_fc = reduce_rows(g_fc.reshape(n_fsdp, rows_here, -1), place, parts)
    q_rows = jnp.swapaxes(g_qkv.reshape(3, n_fsdp, rows_here, inner), 0, 1)
    q_rows = jnp.swapaxes(q_rows, 1, 2).reshape(n_fsdp, rows_here, 3 * inner)
    d_qkv = reduce_rows(q_rows, place, parts)
    d_proj = jnp.swapaxes(d_proj, 0, 1).reshape(weight_proj.shape)
    d_fc = d_fc.reshape(rows_here, parts, n_fsdp, -1)
    d_fc = jnp.swapaxes(d_fc, 1, 2).reshape(weight_fc.shape)
    d_qkv = d_qkv.reshape(rows_here, parts, 3, n_h, -1)
    d_qkv = jnp.transpose(d_qkv, (0, 2, 3, 1, 4)).reshape(weight_qkv.shape)
    if spread_heads:
        d_out = reduce_rows(g_out.reshape(n_fsdp, -1, width), place, parts)
        d_out = jnp.swapaxes(d_out, 0, 1).reshape(weight_out.shape)
    else:
        full = jnp.zeros((parts, inner, width), bf16)
        full = lax.dynamic_update_index_in_dim(full, g_out, j, 0).reshape(width, width)
        d_out = lax.psum_scatter(full, "fsdp", scatter_dimension=0, tiled=True)
        d_out = lax.psum(d_out, ("dp", "ctx")).astype(f32)
    branch = return_blocks(branch_part, place, parts, seqs)
    pulled = return_blocks(pull_part, place, parts, seqs)

    residual_out, residual_grad = finish(
        residual_in, cotangent, lengths, c * block_rows, branch, pulled, b_out + b_proj
    )
    return (
        residual_out,
        residual_grad,
        d_gain_one,
        d_shift_one,
        d_qkv,
        d_bqkv,
        d_out,
        d_bias,
        d_gain_two,
        d_shift_two,
        d_fc,
        d_bfc,
        d_proj,
        d_bias,
    )


def solution(mesh):
    tokens = P(("dp", "fsdp"), "ctx", None)
    vector, matrix = P("fsdp"), P("fsdp", None)
    return jax.shard_map(
        per_device,
        mesh=mesh,
        in_specs=(
            tokens,
            P(("dp", "fsdp")),
            vector,
            vector,
            matrix,
            vector,
            matrix,
            vector,
            vector,
            vector,
            matrix,
            vector,
            matrix,
            vector,
            tokens,
        ),
        out_specs=(
            tokens,
            tokens,
            vector,
            vector,
            matrix,
            vector,
            matrix,
            vector,
            vector,
            vector,
            matrix,
            vector,
            matrix,
            vector,
        ),
        check_vma=False,
    )
```

```python
import functools
import math

import jax
import jax.numpy as jnp
import numpy as np
from jax import lax
from jax.experimental import pallas as pl
from jax.experimental.pallas import tpu as pltpu
from jax.sharding import PartitionSpec as P

HEADS = 16
ROT = 16
LANES = 256
ROWS = 256

epsilon = 1e-05
rope_base = 10000.0
masked_score = -1e30

f32 = jnp.float32
bf16 = jnp.bfloat16


def dot_nn(a, b):
    return lax.dot_general(a, b, (((1,), (0,)), ((), ())), preferred_element_type=f32)


def dot_nt(a, b):
    return lax.dot_general(a, b, (((1,), (1,)), ((), ())), preferred_element_type=f32)


def attn_kernel(
    length_ref,
    h_ref,
    dy_ref,
    wq_ref,
    wk_ref,
    wv_ref,
    wo_ref,
    b_ref,
    rope_ref,
    out_ref,
    dh_ref,
    gqkv_ref,
    gout_ref,
    gb_ref,
    ht_s,
    q_s,
    k_s,
    v_s,
    do_s,
    kt_s,
    vt_s,
    dot_s,
    ot_s,
    dqt_s,
    dk_s,
    dv_s,
    p_s,
    kb_s,
):
    group = pl.program_id(0)
    total, width = h_ref.shape
    blocks = total // ROWS
    head_size = 64
    heads_here = LANES // head_size
    length = length_ref[0]

    @pl.when(group == 0)
    def _():
        for r in range(blocks):
            ht_s[:, r * ROWS : (r + 1) * ROWS] = h_ref[r * ROWS : (r + 1) * ROWS, :].T
        key_pos = lax.broadcasted_iota(jnp.int32, (total, 128), 0)
        kb_s[...] = jnp.where(key_pos < length, 0.0, masked_score)

    def turn(v, rows):
        left = pltpu.roll(v, LANES - ROT // 2, 1)
        right = pltpu.roll(v, ROT // 2, 1)
        return v * rope_ref[0, rows, :] + left * rope_ref[1, rows, :] + right * rope_ref[2, rows, :]

    def turn_back(v, rows):
        left = pltpu.roll(v, LANES - ROT // 2, 1)
        right = pltpu.roll(v, ROT // 2, 1)
        return v * rope_ref[0, rows, :] - left * rope_ref[1, rows, :] - right * rope_ref[2, rows, :]

    for r in range(blocks):
        rows = slice(r * ROWS, (r + 1) * ROWS)
        hr = h_ref[rows, :]
        q = turn(dot_nn(hr, wq_ref[...]) + b_ref[0, 0:1, :], rows).astype(bf16)
        q_s[rows, :] = (q.astype(f32) * 0.125).astype(bf16)
        k = turn(dot_nn(hr, wk_ref[...]) + b_ref[1, 0:1, :], rows).astype(bf16)
        k_s[rows, :] = k
        kt_s[:, rows] = k.T
        v = (dot_nn(hr, wv_ref[...]) + b_ref[2, 0:1, :]).astype(bf16)
        v_s[rows, :] = v
        vt_s[:, rows] = v.T
        do = dot_nt(dy_ref[rows, :], wo_ref[...]).astype(bf16)
        do_s[rows, :] = do
        dot_s[:, rows] = do.T

    dk_s[...] = jnp.zeros_like(dk_s)
    dv_s[...] = jnp.zeros_like(dv_s)
    lane = lax.broadcasted_iota(jnp.int32, (ROWS, LANES), 1)
    causal = lax.broadcasted_iota(jnp.int32, (ROWS, ROWS), 0) <= lax.broadcasted_iota(
        jnp.int32, (ROWS, ROWS), 1
    )

    def one_head(head, carry):
        feats = pl.ds(pl.multiple_of(head * head_size, head_size), head_size)
        mine = (lane // head_size) == head
        zero = jnp.zeros((ROWS, LANES), bf16)
        for i in range(blocks):
            rows = slice(i * ROWS, (i + 1) * ROWS)
            qm = jnp.where(mine, q_s[rows, :], zero)
            dom = jnp.where(mine, do_s[rows, :], zero)
            scores = []
            top = None
            for b in range(i + 1):
                keys = slice(b * ROWS, (b + 1) * ROWS)
                sc = dot_nt(k_s[keys, :], qm)
                kb = kb_s[keys, :]
                sc = sc + jnp.concatenate([kb, kb], axis=1)
                if b == i:
                    sc = jnp.where(causal, sc, masked_score)
                best = jnp.max(sc, axis=0, keepdims=True)
                top = best if top is None else jnp.maximum(top, best)
                scores.append(sc)
            row_sum = None
            for b in range(i + 1):
                scores[b] = jnp.exp(scores[b] - top)
                part = jnp.sum(scores[b], axis=0, keepdims=True)
                row_sum = part if row_sum is None else row_sum + part
            inverse = 1.0 / row_sum
            o_t = None
            for b in range(i + 1):
                keys = slice(b * ROWS, (b + 1) * ROWS)
                scores[b] = scores[b] * inverse
                low = scores[b].astype(bf16)
                dv_s[keys, :] += dot_nn(low, dom)
                part = dot_nn(vt_s[feats, keys], low)
                o_t = part if o_t is None else o_t + part
            ot_s[feats, rows] = o_t
            delta = jnp.sum(dot_s[feats, rows].astype(f32) * o_t, axis=0, keepdims=True)
            dq_t = None
            for b in range(i + 1):
                keys = slice(b * ROWS, (b + 1) * ROWS)
                dp = dot_nt(v_s[keys, :], dom)
                ds = (scores[b] * (dp - delta)).astype(bf16)
                dk_s[keys, :] += dot_nn(ds, qm)
                part = dot_nn(kt_s[feats, keys], ds)
                dq_t = part if dq_t is None else dq_t + part
            dqt_s[feats, rows] = dq_t * 0.125
        return carry

    lax.fori_loop(0, heads_here, one_head, 0)

    sums = [jnp.zeros((1, LANES), f32) for _ in range(3)]
    for r in range(blocks):
        rows = slice(r * ROWS, (r + 1) * ROWS)
        dq = turn_back(dqt_s[:, rows].T, rows).astype(bf16)
        dk = turn_back(dk_s[rows, :], rows).astype(bf16)
        dv = dv_s[rows, :].astype(bf16)
        for at, grad in enumerate((dq, dk, dv)):
            sums[at] = sums[at] + jnp.sum(grad.astype(f32), axis=0, keepdims=True)
            p_s[at, rows, :] = grad
        o = ot_s[:, rows].T.astype(bf16)
        out_part = dot_nn(o, wo_ref[...])
        dh_part = (
            dot_nt(dq, wq_ref[...]) + dot_nt(dk, wk_ref[...]) + dot_nt(dv, wv_ref[...])
        )

        @pl.when(group == 0)
        def _():
            out_ref[rows, :] = out_part
            dh_ref[rows, :] = dh_part

        @pl.when(group > 0)
        def _():
            out_ref[rows, :] += out_part
            dh_ref[rows, :] += dh_part

    for at in range(3):
        gb_ref[at] = jnp.broadcast_to(sums[at], (8, LANES))
        for r in range(width // ROWS):
            rows = slice(r * ROWS, (r + 1) * ROWS)
            gqkv_ref[at, rows, :] = dot_nn(ht_s[rows, :], p_s[at]).astype(bf16)
    gout_ref[...] = dot_nn(ot_s[...].astype(bf16), dy_ref[...]).astype(bf16)


def attention_branch(length, hidden, out_grad, w_qkv, w_out, b_qkv, rope):
    total, width = hidden.shape
    inner = w_out.shape[0]
    groups = inner // LANES
    whole = lambda g: (0, 0)
    flops = 2 * total * width * inner * 12 + 2 * groups * 4 * total * total * LANES * 4
    return pl.pallas_call(
        attn_kernel,
        grid=(groups,),
        in_specs=[
            pl.BlockSpec(memory_space=pltpu.SMEM),
            pl.BlockSpec((total, width), whole),
            pl.BlockSpec((total, width), whole),
            pl.BlockSpec((width, LANES), lambda g: (0, g)),
            pl.BlockSpec((width, LANES), lambda g: (0, groups + g)),
            pl.BlockSpec((width, LANES), lambda g: (0, 2 * groups + g)),
            pl.BlockSpec((LANES, width), lambda g: (g, 0)),
            pl.BlockSpec((3, 8, LANES), lambda g: (0, 0, g)),
            pl.BlockSpec((3, total, LANES), lambda g: (0, 0, 0)),
        ],
        out_specs=[
            pl.BlockSpec((total, width), whole),
            pl.BlockSpec((total, width), whole),
            pl.BlockSpec((3, width, LANES), lambda g: (0, 0, g)),
            pl.BlockSpec((LANES, width), lambda g: (g, 0)),
            pl.BlockSpec((3, 8, LANES), lambda g: (0, 0, g)),
        ],
        out_shape=[
            jax.ShapeDtypeStruct((total, width), f32),
            jax.ShapeDtypeStruct((total, width), f32),
            jax.ShapeDtypeStruct((3, width, inner), bf16),
            jax.ShapeDtypeStruct((inner, width), bf16),
            jax.ShapeDtypeStruct((3, 8, inner), f32),
        ],
        scratch_shapes=[
            pltpu.VMEM((width, total), bf16),
            pltpu.VMEM((total, LANES), bf16),
            pltpu.VMEM((total, LANES), bf16),
            pltpu.VMEM((total, LANES), bf16),
            pltpu.VMEM((total, LANES), bf16),
            pltpu.VMEM((LANES, total), bf16),
            pltpu.VMEM((LANES, total), bf16),
            pltpu.VMEM((LANES, total), bf16),
            pltpu.VMEM((LANES, total), f32),
            pltpu.VMEM((LANES, total), f32),
            pltpu.VMEM((total, LANES), f32),
            pltpu.VMEM((total, LANES), f32),
            pltpu.VMEM((3, total, LANES), bf16),
            pltpu.VMEM((total, 128), f32),
        ],
        compiler_params=pltpu.CompilerParams(vmem_limit_bytes=60 * 2**20),
        cost_estimate=pl.CostEstimate(
            flops=flops, bytes_accessed=24 * 2**20, transcendentals=8 * total * total
        ),
        name="attention",
    )(length, hidden, out_grad, w_qkv, w_qkv, w_qkv, w_out, b_qkv, rope)


def ffn_kernel(
    h_ref,
    dy_ref,
    wf_ref,
    wp_ref,
    b_ref,
    out_ref,
    dh_ref,
    gf_ref,
    gp_ref,
    gb_ref,
    ht_s,
    act_s,
    dup_s,
):
    step = pl.program_id(0)
    total, width = h_ref.shape
    blocks = total // ROWS
    chunk = wf_ref.shape[1]

    @pl.when(step == 0)
    def _():
        for r in range(blocks):
            ht_s[:, r * ROWS : (r + 1) * ROWS] = h_ref[r * ROWS : (r + 1) * ROWS, :].T

    def one(r, total_grad):
        rows = pl.ds(pl.multiple_of(r * ROWS, ROWS), ROWS)
        up = dot_nn(h_ref[rows, :], wf_ref[...]) + b_ref[0:1, :]
        half = 0.5 + 0.5 * lax.erf(up * (1.0 / math.sqrt(2.0)))
        act = (up * half).astype(bf16)
        slope = half + up * (jnp.exp(-0.5 * up * up) * (1.0 / math.sqrt(2.0 * math.pi)))
        act_grad = dot_nt(dy_ref[rows, :], wp_ref[...])
        up_grad = (slope * act_grad).astype(bf16)
        act_s[rows, :] = act
        dup_s[rows, :] = up_grad
        out_part = dot_nn(act, wp_ref[...])
        dh_part = dot_nt(up_grad, wf_ref[...])

        @pl.when(step == 0)
        def _():
            out_ref[rows, :] = out_part
            dh_ref[rows, :] = dh_part

        @pl.when(step > 0)
        def _():
            out_ref[rows, :] += out_part
            dh_ref[rows, :] += dh_part

        return total_grad + jnp.sum(up_grad.astype(f32), axis=0, keepdims=True)

    sums = lax.fori_loop(0, blocks, one, jnp.zeros((1, chunk), f32))
    gb_ref[...] = jnp.broadcast_to(sums, (8, chunk))
    for r in range(8):
        size = width // 8
        rows = slice(r * size, (r + 1) * size)
        grad = dot_nn(ht_s[rows, :], dup_s[...]).astype(bf16)
        gf_ref[rows, :] = grad
    for r in range(chunk // ROWS):
        cols = slice(r * ROWS, (r + 1) * ROWS)
        grad = dot_nn(act_s[:, cols].T, dy_ref[...]).astype(bf16)
        gp_ref[cols, :] = grad


def ffn_branch(hidden, out_grad, w_fc, w_proj, b_fc):
    total, width = hidden.shape
    units = w_proj.shape[0]
    chunk = min(512, units)
    whole = lambda s: (0, 0)
    return pl.pallas_call(
        ffn_kernel,
        grid=(units // chunk,),
        in_specs=[
            pl.BlockSpec((total, width), whole),
            pl.BlockSpec((total, width), whole),
            pl.BlockSpec((width, chunk), lambda s: (0, s)),
            pl.BlockSpec((chunk, width), lambda s: (s, 0)),
            pl.BlockSpec((8, chunk), lambda s: (0, s)),
        ],
        out_specs=[
            pl.BlockSpec((total, width), whole),
            pl.BlockSpec((total, width), whole),
            pl.BlockSpec((width, chunk), lambda s: (0, s)),
            pl.BlockSpec((chunk, width), lambda s: (s, 0)),
            pl.BlockSpec((8, chunk), lambda s: (0, s)),
        ],
        out_shape=[
            jax.ShapeDtypeStruct((total, width), f32),
            jax.ShapeDtypeStruct((total, width), f32),
            jax.ShapeDtypeStruct((width, units), bf16),
            jax.ShapeDtypeStruct((units, width), bf16),
            jax.ShapeDtypeStruct((8, units), f32),
        ],
        scratch_shapes=[
            pltpu.VMEM((width, total), bf16),
            pltpu.VMEM((total, chunk), bf16),
            pltpu.VMEM((total, chunk), bf16),
        ],
        compiler_params=pltpu.CompilerParams(vmem_limit_bytes=60 * 2**20),
        cost_estimate=pl.CostEstimate(
            flops=2 * total * width * units * 6,
            bytes_accessed=28 * 2**20,
            transcendentals=2 * total * units,
        ),
        name="feed_forward",
    )(hidden, out_grad, w_fc, w_proj, b_fc)


def shift(block, axis, distance):
    count = lax.axis_size(axis)
    return lax.ppermute(block, axis, [(i, (i + distance) % count) for i in range(count)])


def swap_bit(block, axis, bit):
    return lax.ppermute(block, axis, [(i, i ^ bit) for i in range(lax.axis_size(axis))])


def shift_within(block, axis, size, distance):
    count = lax.axis_size(axis)
    return lax.ppermute(
        block,
        axis,
        [(i, i // size * size + (i % size + distance) % size) for i in range(count)],
    )


def pick(array, index, axis=0):
    return lax.dynamic_index_in_dim(array, index, axis, keepdims=False)


def order_two(flag, mine, other):
    first = flag == 0
    return jnp.stack([jnp.where(first, mine, other), jnp.where(first, other, mine)])


def gather_rows(local, place):
    dp, y, core, f = place["dp"], place["y"], place["core"], place["f"]
    count = lax.axis_size("fsdp")
    rows, cols = local.shape
    share = rows // lax.axis_size("dp")
    mine = lax.dynamic_slice_in_dim(local, dp * share, share, 0)
    got = jnp.stack([shift(mine, "fsdp", e) for e in range(1, count)])
    got = order_two(y, got, swap_bit(got, "dp", 2))
    got = order_two(core, got, swap_bit(got, "dp", 1))
    got = jnp.transpose(got, (2, 1, 0, 3, 4)).reshape(count - 1, rows, cols)
    if count == 2:
        return order_two(f, local, got[0])
    whole = jnp.zeros((count, rows, cols), local.dtype)
    whole = lax.dynamic_update_index_in_dim(whole, local, f, 0)
    for e in range(1, count):
        whole = lax.dynamic_update_index_in_dim(whole, got[e - 1], (f - e) % count, 0)
    return whole


def reduce_rows(partial, place, parts):
    dp, y, core, f, j = (place[k] for k in ("dp", "y", "core", "f", "j"))
    count, rows, cols = partial.shape
    share = rows // 4
    a = partial.reshape(count, 2, 2, share, cols)
    a = pick(a, core, 2) + swap_bit(pick(a, 1 - core, 2), "dp", 1)
    total = pick(a, f)
    for e in range(1, count):
        total = total + shift(pick(a, (f + e) % count), "fsdp", e)
    total = pick(total, y) + swap_bit(pick(total, 1 - y), "dp", 2)
    total = total + shift(total, "ctx", parts)
    if parts == 2:
        both = order_two(j, total, shift_within(total, "ctx", 2, 1))
    else:
        both = jnp.zeros((parts,) + total.shape, total.dtype)
        both = lax.dynamic_update_index_in_dim(both, total, j, 0)
        for e in range(1, parts):
            got = shift_within(total, "ctx", parts, e)
            both = lax.dynamic_update_index_in_dim(both, got, (j - e) % parts, 0)
    both = order_two(y, both, swap_bit(both, "dp", 2))
    both = order_two(core, both, swap_bit(both, "dp", 1))
    return jnp.transpose(both, (1, 0, 3, 2, 4)).reshape(rows, parts, cols).astype(f32)


def sum_everywhere(vector):
    for bit in (1, 2):
        vector = vector + swap_bit(vector, "dp", bit)
    for axis in ("fsdp", "ctx"):
        bit = 1
        while bit < lax.axis_size(axis):
            vector = vector + swap_bit(vector, axis, bit)
            bit *= 2
    return vector


def gather_sequence(blocks, place, parts):
    s, c = place["s"], place["c"]
    count = lax.axis_size("ctx")
    seqs, rows, width = blocks.shape
    pieces = [(c, pick(blocks, s))]
    for d in range(1, seqs):
        got = shift(pick(blocks, (s + d) % seqs), "ctx", d * parts)
        pieces.append(((c - d * parts) % count, got))
    arrived = []
    for d in range(seqs):
        arrived.append(pieces[d])
        for e in range(1, parts):
            source = s * parts + (place["j"] - e) % parts
            got = shift_within(pieces[d][1], "ctx", parts, e)
            arrived.append(((source - d * parts) % count, got))
    whole = jnp.zeros((count, rows, width), blocks.dtype)
    for at, piece in arrived:
        whole = lax.dynamic_update_index_in_dim(whole, piece, at, 0)
    return whole.reshape(count * rows, width)


def return_blocks(partial, place, parts, seqs):
    s, c, j = place["s"], place["c"], place["j"]
    count = lax.axis_size("ctx")
    rows = partial.shape[0] // count
    blocks = partial.reshape(seqs, parts, rows, -1)
    total = pick(blocks, j, 1).astype(f32)
    for e in range(1, parts):
        total = total + shift_within(pick(blocks, (j + e) % parts, 1), "ctx", parts, e).astype(f32)
    mine = [pick(total, s)]
    for d in range(1, seqs):
        mine.append(shift(pick(total, (s + d) % seqs).astype(bf16), "ctx", d * parts).astype(f32))
    if seqs == 2:
        return order_two(s, mine[0], mine[1])
    whole = jnp.zeros((seqs, rows, partial.shape[1]), f32)
    for d in range(seqs):
        whole = lax.dynamic_update_index_in_dim(whole, mine[d], (s - d) % seqs, 0)
    return whole


class Mover:
    def __init__(self, send, recv, local):
        self.send, self.recv, self.local = send, recv, local
        self.copies, self.left, self.started = [], [], 0

    def to(self, src, dst, axis, index):
        copy = self.remote(src, dst, len(self.copies), (axis, index))
        copy.start()
        self.copies.append(copy)
        return copy

    def here(self, src, dst):
        copy = pltpu.make_async_copy(src, dst, self.local.at[self.started])
        self.started += 1
        copy.start()
        return copy

    def out(self, src, dst):
        self.left.append(self.here(src, dst))

    def remote(self, src, dst, slot, to):
        return pltpu.make_async_remote_copy(
            src_ref=src,
            dst_ref=dst,
            send_sem=self.send.at[slot],
            recv_sem=self.recv.at[slot],
            device_id={to[0]: to[1]},
            device_id_type=pl.DeviceIdType.MESH,
        )

    def stay(self, src, dst, slot):
        return pltpu.make_async_copy(src, dst, self.local.at[slot])

    def finish(self):
        for copy in self.copies:
            copy.wait_send()
        for copy in self.left:
            copy.wait()


class Spot:
    def __init__(self):
        self.dp, self.c, self.f = (lax.axis_index(a) for a in ("dp", "ctx", "fsdp"))
        self.y, self.core = self.dp // 2, self.dp % 2
        self.s, self.j = self.c // 2, self.c % 2
        flip = lambda v: v + 1 - 2 * (v % 2)
        self.x_to = ("fsdp", 1 - self.f)
        self.y_to = ("dp", (1 - self.y) * 2 + self.core)
        self.core_to = ("dp", flip(self.dp))
        self.pair_to = ("ctx", flip(self.c))
        self.far_to = ("ctx", (1 - self.s) * 2 + self.j)

    def greet(self):
        barrier = pltpu.get_barrier_semaphore()
        partners = (self.x_to, self.y_to, self.core_to, self.pair_to, self.far_to)
        for axis, index in partners:
            pl.semaphore_signal(
                barrier, inc=1, device_id={axis: index}, device_id_type=pl.DeviceIdType.MESH
            )
        pl.semaphore_wait(barrier, len(partners))


def block(index, size):
    return pl.ds(pl.multiple_of(index * size, size), size)


def front_kernel(
    info_ref,
    x_ref,
    cot_ref,
    fc_ref,
    proj_ref,
    qkv_ref,
    out_ref,
    rope_ref,
    *rest,
):
    vector_refs, rest = rest[:8], rest[8:]
    (
        seq_in,
        seq_grad,
        w_qkv,
        w_out,
        pull,
        home,
        gp,
        gf,
        part,
        vectors,
        x_s,
        dy_s,
        cot_s,
        held_s,
        small_s,
        wf_s,
        wp_s,
        wq_s,
        wo_s,
        h_s,
        ht_s,
        act_s,
        dup_s,
        rope_s,
        q_s,
        k_s,
        vt_s,
        o_s,
        ot_s,
        kb_s,
        home_s,
        got_s,
        pull_s,
        gp_s,
        gf_s,
        core_got,
        x_got,
        vec_s,
        bfc_s,
        part_s,
        send,
        recv,
        local,
    ) = rest
    at = Spot()
    mover = Mover(send, recv, local)
    total, width = x_s.shape
    blocks = total // ROWS
    units = wp_s.shape[0]
    inner = wo_s.shape[0]
    head_size = 64
    length = jnp.where(at.s == 0, info_ref[0], info_ref[1])
    other = 1 - at.f
    far_c, pair_c = at.far_to[1], at.pair_to[1]
    last_c = (1 - at.s) * 2 + 1 - at.j

    load_x = mover.here(x_ref.at[at.s], x_s.at[block(at.c, ROWS)])
    load_cot = mover.here(cot_ref, cot_s)
    held_s[...] = jnp.zeros_like(held_s)
    row = 0
    for ref in vector_refs:
        size = small_s.shape[2]
        vector = ref[...].astype(f32).reshape(1, ref.shape[0])
        for start in range(0, ref.shape[0], size):
            held_s[row : row + 1, :] = vector[:, start : start + size]
            row += 1
    small_s[at.f] = held_s[...]
    load_rope = mover.here(rope_ref, rope_s)
    at.greet()

    small_copy = mover.to(held_s, small_s.at[at.f], *at.x_to)
    x_far = mover.to(x_ref.at[1 - at.s], x_s.at[block(at.c, ROWS)], *at.far_to)
    x_near = mover.to(x_ref.at[at.s], x_s.at[block(at.c, ROWS)], *at.pair_to)

    def fc_spans(k):
        size = units // 2
        return lambda r: [(fc_ref.at[r, block(2 * k + at.j, size)], pl.ds(0, size))]

    def qkv_spans(r):
        size = wq_s.shape[1] // 12
        return [
            (
                qkv_ref.at[r, block(t * 8 + h * 4 + at.j * 2 + g, size)],
                pl.ds((t * 4 + g * 2 + h) * size, size),
            )
            for t in range(3)
            for g in range(2)
            for h in range(2)
        ]

    def row_spans(ref, held):
        count = held.shape[0] // 2

        def spans(r):
            start = pl.multiple_of(at.j * count + r.start, r.size)
            return [(ref.at[pl.ds(start, r.size)], pl.ds(0, width))]

        return spans

    weights = dict(
        fc0=(wf_s.at[:, pl.ds(0, units // 2)], fc_spans(0)),
        fc1=(wf_s.at[:, pl.ds(units // 2, units // 2)], fc_spans(1)),
        qkv=(wq_s, qkv_spans),
        out=(wo_s, row_spans(out_ref, wo_s)),
        proj=(wp_s, row_spans(proj_ref, wp_s)),
    )
    got_x, got_y, got_core, stays = {}, {}, {}, {}

    def send_x(name):
        held, spans = weights[name]
        count = held.shape[0] // 2
        share = count // 4
        mine = pl.ds(pl.multiple_of(at.dp * share, share), share)
        there = pl.ds(pl.multiple_of(at.f * count + at.dp * share, share), share)
        got_x[name] = [mover.to(src, held.at[there, cols], *at.x_to) for src, cols in spans(mine)]

    def keep(name):
        held, spans = weights[name]
        count = held.shape[0] // 2
        there = block(at.f, count)
        stays[name] = [
            mover.here(src, held.at[there, cols]) for src, cols in spans(pl.ds(0, count))
        ]

    def quarter(name, dp):
        held = weights[name][0]
        count = held.shape[0] // 2
        share = count // 4
        return held.at[pl.ds(pl.multiple_of(other * count + dp * share, share), share)]

    def pass_x(name):
        for copy in got_x[name]:
            copy.wait_recv()
        mine = quarter(name, at.dp)
        got_y[name] = mover.to(mine, mine, *at.y_to)
        got_core[name] = [mover.to(mine, mine, *at.core_to)]

    def pass_y(name):
        got_y[name].wait_recv()
        mine = quarter(name, at.y_to[1])
        got_core[name].append(mover.to(mine, mine, *at.core_to))

    def arrived(name):
        for copy in got_core[name]:
            copy.wait_recv()
        for copy in stays[name]:
            copy.wait()

    send_x("fc0")
    for name in weights:
        keep(name)

    small_copy.wait_recv()

    def line(shard, r):
        return small_s[shard, r : r + 1, :]

    def joined(r):
        return jnp.concatenate([line(0, r), line(1, r)], axis=1)

    first = at.j == 0
    vec_s[...] = jnp.zeros_like(vec_s)
    part_s[...] = jnp.zeros_like(part_s)
    size = LANES // 2
    for t in range(3):
        for h in range(2):
            row = line((t * 2 + h) // 3, 6 + (t * 2 + h) % 3)
            row = jnp.where(first, row[:, :LANES], row[:, LANES:])
            for g in range(2):
                to = g * LANES + h * size
                vec_s[t : t + 1, to : to + size] = row[:, g * size : (g + 1) * size]
    vec_s[3:4, :] = joined(0)
    vec_s[4:5, :] = joined(1)
    vec_s[5:6, :] = joined(4) + joined(5)
    for h in range(2):
        for n in range(2):
            to = h * units // 2 + n * 512
            bfc_s[0:1, to : to + 512] = jnp.where(first, line(h, 9 + n), line(h, 11 + n))
    gain_one, shift_one = vec_s[3:4, :], vec_s[4:5, :]
    gain_two, shift_two = joined(2), joined(3)
    bfc_s[1:2, :width] = gain_two
    mover.out(vec_s, vectors)

    def normal(rows):
        v = x_s[rows, :].astype(f32)
        center = v - jnp.mean(v, axis=-1, keepdims=True)
        spread = jnp.mean(center * center, axis=-1, keepdims=True)
        return center * lax.rsqrt(spread + epsilon)

    def arrive(c):
        rows = block(c, ROWS)
        h = (normal(rows) * gain_two + shift_two).astype(bf16)
        h_s[rows, :] = h
        ht_s[:, rows] = h.T

    load_x.wait()
    arrive(at.c)
    load_cot.wait()
    for t in range(2):
        pos = at.c * ROWS + lax.broadcasted_iota(jnp.int32, (ROWS, width), 0)
        cot_s[t] = jnp.where(pos < info_ref[t], cot_s[t].astype(f32), 0.0).astype(bf16)
    dy_s[block(at.c, ROWS), :] = cot_s[at.s]
    pass_x("fc0")
    send_x("fc1")
    pass_x("fc1")
    send_x("qkv")
    pass_y("fc0")

    def span(b):
        return slice(b * ROWS, (b + 1) * ROWS)

    chunk = 512

    def forward(c, half):
        rows = block(c, ROWS)
        steps = units // chunk // 2

        def one(q, carry):
            cols = block(q, chunk)
            up = dot_nn(h_s[rows, :], wf_s[:, cols]) + bfc_s[0:1, cols]
            part = 0.5 + 0.5 * lax.erf(up * (1.0 / math.sqrt(2.0)))
            act_s[rows, cols] = (up * part).astype(bf16)
            slope = part + up * (jnp.exp(-0.5 * up * up) * (1.0 / math.sqrt(2.0 * math.pi)))
            dup_s[rows, cols] = slope.astype(bf16)
            return carry

        lax.fori_loop(half * steps, (half + 1) * steps, one, 0, unroll=steps)

    arrived("fc0")
    forward(at.c, 0)
    pass_y("fc1")
    pass_x("qkv")
    send_x("out")
    x_far.wait_recv()
    mine = x_s.at[block(far_c, ROWS)]
    x_last = mover.to(mine, mine, *at.pair_to)
    grad_far = mover.to(cot_s.at[1 - at.s], dy_s.at[block(at.c, ROWS)], *at.far_to)
    arrive(far_c)
    x_near.wait_recv()
    arrive(pair_c)
    arrived("fc1")
    pass_x("out")
    send_x("proj")
    forward(at.c, 1)
    forward(far_c, 0)
    forward(far_c, 1)
    grad_near = mover.to(cot_s.at[at.s], dy_s.at[block(at.c, ROWS)], *at.pair_to)
    forward(pair_c, 0)
    forward(pair_c, 1)
    x_last.wait_recv()
    arrive(last_c)
    pass_y("qkv")
    pass_y("out")
    forward(last_c, 0)
    forward(last_c, 1)
    mover.out(x_s, seq_in)
    arrived("qkv")
    arrived("out")
    mover.out(wq_s, w_qkv)
    mover.out(wo_s, w_out)

    load_rope.wait()

    def table(n, rows):
        piece = rope_s[n, rows, :]
        return jnp.concatenate([piece] * (inner // 128), axis=1)

    def turned(v, rows):
        left = pltpu.roll(v, inner - ROT // 2, 1)
        right = pltpu.roll(v, ROT // 2, 1)
        return v * table(0, rows) + left * table(1, rows) + right * table(2, rows)

    for r in range(blocks):
        rows = span(r)
        h = (normal(rows) * gain_one + shift_one).astype(bf16)
        q = turned(dot_nn(h, wq_s[:, :inner]) + vec_s[0:1, :inner], rows).astype(bf16)
        q_s[rows, :] = (q.astype(f32) * 0.125).astype(bf16)
        k = dot_nn(h, wq_s[:, inner : 2 * inner]) + vec_s[1:2, :inner]
        k_s[rows, :] = turned(k, rows).astype(bf16)
        v = dot_nn(h, wq_s[:, 2 * inner :]) + vec_s[2:3, :inner]
        vt_s[:, rows] = v.astype(bf16).T
    pass_x("proj")
    grad_far.wait_recv()
    mine = dy_s.at[block(far_c, ROWS)]
    grad_last = mover.to(mine, mine, *at.pair_to)
    key_pos = lax.broadcasted_iota(jnp.int32, (total, 128), 0)
    kb_s[...] = jnp.where(key_pos < length, 0.0, masked_score)
    lane = lax.broadcasted_iota(jnp.int32, (ROWS, LANES), 1)
    causal = lax.broadcasted_iota(jnp.int32, (ROWS, ROWS), 0) <= lax.broadcasted_iota(
        jnp.int32, (ROWS, ROWS), 1
    )

    def one_head(g, i, head, carry):
        feats = pl.ds(pl.multiple_of(head * head_size, head_size), head_size)
        from_v = pl.ds(pl.multiple_of(g * LANES + head * head_size, head_size), head_size)
        cols = slice(g * LANES, (g + 1) * LANES)
        mine = (lane // head_size) == head
        qm = jnp.where(mine, q_s[span(i), cols], jnp.zeros((ROWS, LANES), bf16))
        scores = []
        top = None
        for b in range(i + 1):
            sc = dot_nt(k_s[span(b), cols], qm)
            kb = kb_s[span(b), :]
            sc = sc + jnp.concatenate([kb, kb], axis=1)
            if b == i:
                sc = jnp.where(causal, sc, masked_score)
            best = jnp.max(sc, axis=0, keepdims=True)
            top = best if top is None else jnp.maximum(top, best)
            scores.append(sc)
        row_sum = None
        o_t = None
        for b in range(i + 1):
            e = jnp.exp(scores[b] - top)
            add = jnp.sum(e, axis=0, keepdims=True)
            row_sum = add if row_sum is None else row_sum + add
            add = dot_nn(vt_s[from_v, span(b)], e.astype(bf16))
            o_t = add if o_t is None else o_t + add
        ot_s[feats, :] = o_t / row_sum
        return carry

    for i in range(blocks):
        for g in range(2):
            lax.fori_loop(0, LANES // head_size, functools.partial(one_head, g, i), 0, unroll=2)
            o = ot_s[...].T.astype(bf16)
            for h in range(2):
                to = h * LANES + g * size
                o_s[span(i), to : to + size] = o[:, h * size : (h + 1) * size]
        if i == 1:
            pass_y("proj")
    arrived("proj")
    nears = []
    for i in range(blocks):
        both = dot_nn(act_s[span(i), :], wp_s[...]) + dot_nn(o_s[span(i), :], wo_s[...])
        home_s[i] = both.astype(bf16)
        if i % 2 == 1:
            t = i // 2
            nears.append(mover.to(home_s.at[2 * t + 1 - at.j], got_s.at[t], *at.pair_to))

    grad_near.wait_recv()
    grad_last.wait_recv()
    mover.out(dy_s, seq_grad)
    bfc_s[2:3, :] = jnp.zeros((1, units), f32)
    for r in range(8):
        grad = dot_nn(act_s[:, r * ROWS : (r + 1) * ROWS].T, dy_s[...]).astype(bf16)
        for k in range(2):
            gp_s[k, r % 2, r // 4, r // 2 % 2] = grad[k * ROWS // 2 : (k + 1) * ROWS // 2]
    to_core = [mover.to(gp_s.at[k, 1 - at.core], core_got.at[k], *at.core_to) for k in range(2)]
    to_x = []

    def step_core(k):
        to_core[k].wait_recv()
        own, got = gp_s.at[k, at.core], core_got.at[k]
        own[1 - at.f] = own[1 - at.f] + got[1 - at.f]
        if k == 0:
            to_x.append(mover.to(own.at[1 - at.f], x_got, *at.x_to))
        own[at.f] = own[at.f] + got[at.f]

    def step_x():
        to_x[0].wait_recv()
        own = gp_s.at[0, at.core, at.f]
        own[...] = own[...] + x_got[...]
        mover.out(own, gp.at[0, 0])

    gain_sum = jnp.zeros((1, width), f32)
    shift_sum = jnp.zeros((1, width), f32)
    dy_sum = jnp.zeros((1, width), f32)
    for i in range(blocks):
        rows = span(i)

        def one(q, carry):
            cols = block(q, chunk)
            act_grad = dot_nt(dy_s[rows, :], wp_s[cols, :])
            up_grad = (dup_s[rows, cols].astype(f32) * act_grad).astype(bf16)
            dup_s[rows, cols] = up_grad
            bfc_s[2:3, cols] += jnp.sum(up_grad.astype(f32), axis=0, keepdims=True)
            return carry

        lax.fori_loop(0, units // chunk, one, 0, unroll=4)
        dh = dot_nt(dup_s[rows, :], wf_s[...])
        pull_s[rows, :] = (dh * gain_two).astype(bf16)
        gain_sum = gain_sum + jnp.sum(dh * normal(rows), axis=0, keepdims=True)
        shift_sum = shift_sum + jnp.sum(dh, axis=0, keepdims=True)
        dy_sum = dy_sum + jnp.sum(dy_s[rows, :].astype(f32), axis=0, keepdims=True)
        if i == 0:
            step_core(0)
        if i == 1:
            step_core(1)
            mover.out(gp_s.at[1, at.core], gp.at[1])
    mover.out(pull_s, pull)
    part_s[2:3, :] = gain_sum
    part_s[3:4, :] = shift_sum
    part_s[4:5, :] = dy_sum * 0.5
    none = jnp.zeros((2, width), f32)
    sums = jnp.concatenate([none, bfc_s[2:3, :width], bfc_s[2:3, width:], none, none], axis=0)
    part_s[8:16, :] = jnp.where(first, sums, jnp.concatenate([sums[4:], sums[:4]], axis=0))
    mover.out(part_s, part)
    rows_each = width // 8
    for k in range(2):
        for r in range(8):
            cols = slice(k * units // 2, (k + 1) * units // 2)
            grad = dot_nn(ht_s[r * rows_each : (r + 1) * rows_each, :], dup_s[:, cols])
            gf_s[k, r % 2, r // 4, r // 2 % 2] = grad.astype(bf16)
        mover.out(gf_s.at[k], gf.at[k])
        if k == 0:
            step_x()

    for t in range(2):
        nears[t].wait_recv()
        mine = home_s.at[2 * t + at.j]
        mine[...] = (mine[...].astype(f32) + got_s[t].astype(f32)).astype(bf16)
        mover.out(mine, home.at[t])
    mover.finish()


def front(info, x, cot, fc, proj, qkv, out, rope, vectors):
    seqs, rows, width = x.shape
    total = 4 * rows
    units = proj.shape[0]
    inner = out.shape[0]
    cell = (rows // 2, width)
    hbm = pl.BlockSpec(memory_space=pl.ANY)
    shape = lambda *dims: jax.ShapeDtypeStruct(dims, bf16)
    buf = lambda *dims: pltpu.VMEM(dims, bf16)
    wide = lambda *dims: pltpu.VMEM(dims, f32)
    return pl.pallas_call(
        front_kernel,
        in_specs=[pl.BlockSpec(memory_space=pltpu.SMEM)]
        + [hbm] * 7
        + [pl.BlockSpec(memory_space=pltpu.VMEM)] * 8,
        out_specs=[hbm] * 10,
        out_shape=[
            shape(total, width),
            shape(total, width),
            shape(width, 3 * inner),
            shape(inner, width),
            shape(total, width),
            shape(2, rows, width),
            shape(2, 2, 2, *cell),
            shape(2, 2, 2, 2, *cell),
            jax.ShapeDtypeStruct((16, width), f32),
            jax.ShapeDtypeStruct((8, width), f32),
        ],
        scratch_shapes=[
            buf(total, width),
            buf(total, width),
            buf(2, rows, width),
            wide(16, width // 2),
            wide(2, 16, width // 2),
            buf(width, units),
            buf(units, width),
            buf(width, 3 * inner),
            buf(inner, width),
            buf(total, width),
            buf(width, total),
            buf(total, units),
            buf(total, units),
            wide(*rope.shape),
            buf(total, inner),
            buf(total, inner),
            buf(inner, total),
            buf(total, inner),
            wide(LANES, ROWS),
            wide(total, 128),
            buf(4, rows, width),
            buf(2, rows, width),
            buf(total, width),
            buf(2, 2, 2, 2, *cell),
            buf(2, 2, 2, 2, *cell),
            buf(2, 2, 2, *cell),
            buf(2, *cell),
            wide(8, width),
            wide(8, units),
            wide(16, width),
            pltpu.SemaphoreType.DMA((48,)),
            pltpu.SemaphoreType.DMA((48,)),
            pltpu.SemaphoreType.DMA((48,)),
        ],
        compiler_params=pltpu.CompilerParams(
            collective_id=0, has_side_effects=True, vmem_limit_bytes=62 * 2**20
        ),
        name="front",
    )(info, x, cot, fc, proj, qkv, out, rope, *vectors)


def branch_kernel(
    length_ref,
    x_ref,
    dy_ref,
    wqkv_ref,
    wo_ref,
    bias_ref,
    rope_ref,
    out_ref,
    ffn_pull_ref,
    gp_ref,
    gf_ref,
    small_ref,
    summed,
    branch,
    pull,
    small,
    x_s,
    dy_s,
    h_s,
    ht_s,
    wqkv_s,
    wo_s,
    rope_s,
    q_s,
    k_s,
    v_s,
    do_s,
    kt_s,
    vt_s,
    dot_s,
    ot_s,
    dqt_s,
    dk_s,
    dv_s,
    dp_s,
    kb_s,
    begun_s,
    own_s,
    mine_s,
    core_s,
    x_got,
    y_got,
    far_got,
    home_s,
    home_got,
    out_s,
    small_s,
    small_got,
    send,
    recv,
    local,
):
    at = Spot()
    mover = Mover(send, recv, local)
    total, width = x_s.shape
    blocks = total // ROWS
    inner = wo_s.shape[0]
    head_size = 64
    length = jnp.where(at.s == 0, length_ref[0], length_ref[1])

    load_x = mover.here(x_ref, x_s)
    load_w = mover.here(wqkv_ref, wqkv_s)
    load_rope = mover.here(rope_ref, rope_s)
    load_dy = mover.here(dy_ref, dy_s)
    half = LANES // 2
    load_wo = [
        mover.here(
            wo_ref.at[pl.ds(h * LANES + g * half, half)],
            wo_s.at[pl.ds(g * LANES + h * half, half)],
        )
        for g in range(2)
        for h in range(2)
    ]
    load_small = mover.here(small_ref, small_s.at[0])
    load_out = mover.here(out_ref, out_s)
    at.greet()

    links = ("c", "x", "y", "z", "p", "ya", "yy", "c1", "c2")

    def own_of(n):
        return own_s.at[n - 1] if n < 4 else mine_s.at[n - 4, at.core]

    def cell(n, y):
        return begun_s.at[y] if n < 1 else own_of(n).at[at.f, y]

    def link(n, name):
        mine, other = summed.at[n, at.y, at.core], summed.at[n, 1 - at.y, at.core]
        if name == "c":
            src = (gf_ref.at[n - 2] if n < 4 else mine_s.at[n - 4]).at[1 - at.core]
            ends = (src, core_s.at[n - 2], at.core_to)
        elif name == "x":
            ends = (own_of(n).at[1 - at.f], x_got.at[n - 1], at.x_to)
        elif name == "y":
            ends = (cell(n, 1 - at.y), y_got.at[n], at.y_to)
        elif name == "z":
            ends = (cell(n, at.y), far_got.at[n], at.far_to)
        elif name == "p":
            ends = (y_got.at[n], summed.at[n, at.y, at.core, at.j], at.pair_to)
        elif name == "ya":
            ends = (y_got.at[n], summed.at[n, at.y, at.core, at.j], at.y_to)
        elif name == "yy":
            part = summed.at[n, at.y, at.core, 1 - at.j]
            ends = (part, part, at.y_to)
        elif name == "c1":
            ends = (mine, mine, at.core_to)
        else:
            ends = (other, other, at.core_to)
        return mover.remote(ends[0], ends[1], n * len(links) + links.index(name), ends[2])

    def load(n):
        if n == 0:
            return mover.stay(gp_ref.at[0, 0], begun_s, 24)
        src = gp_ref.at[1] if n == 1 else gf_ref.at[n - 2, at.core]
        return mover.stay(src, own_s.at[n - 1], 24 + n)

    def keep(n):
        return mover.stay(y_got.at[n], summed.at[n, at.y, at.core, at.j], 28 + n)

    def step_start(n):
        if n < 4:
            load(n).start()
        link(n, "c").start()

    def step_core(n):
        if n < 4:
            load(n).wait()
        link(n, "c").wait_recv()
        own, got = own_of(n), core_s.at[n - 2]
        own[1 - at.f] = own[1 - at.f] + got[1 - at.f]
        link(n, "x").start()
        own[at.f] = own[at.f] + got[at.f]

    def step_x(n):
        link(n, "x").wait_recv()
        own, got = own_of(n), x_got.at[n - 1]
        own[at.f, 1 - at.y] = own[at.f, 1 - at.y] + got[1 - at.y]
        link(n, "y").start()
        own[at.f, at.y] = own[at.f, at.y] + got[at.y]

    def step_y(n):
        link(n, "y").wait_recv()
        mine = cell(n, at.y)
        mine[...] = mine[...] + y_got[n]
        link(n, "z").start()

    def step_far(n):
        link(n, "z").wait_recv()
        y_got[n] = cell(n, at.y)[...] + far_got[n]
        link(n, "p").start()
        link(n, "ya").start()
        keep(n).start()

    def step_pair(n):
        link(n, "p").wait_recv()
        keep(n).wait()
        link(n, "yy").start()
        link(n, "c1").start()

    def step_yy(n):
        link(n, "ya").wait_recv()
        link(n, "yy").wait_recv()
        link(n, "c2").start()

    base = 6 * len(links)

    def near(t):
        return mover.remote(home_s.at[2 * t + 1 - at.j], home_got.at[t], base + t, at.pair_to)

    def last(t):
        mine, dst = home_s.at[2 * t + at.j], pull.at[at.s]
        return mover.remote(mine, dst, base + 2, at.far_to), mover.stay(mine, dst, 34)

    def out_home():
        far = mover.remote(out_s.at[1 - at.s], branch.at[at.s], base + 3, at.far_to)
        return far, mover.stay(out_s.at[at.s], branch.at[at.s], 35)

    def out_start(_):
        load_out.wait()
        for copy in out_home():
            copy.start()

    def home_near(t):
        near(t).start()

    def home_sum(t):
        near(t).wait_recv()
        mine = home_s.at[2 * t + at.j]
        mine[...] = (mine[...].astype(f32) + home_got[t].astype(f32)).astype(bf16)
        far, stay = last(t)
        pl.when(at.s == t)(stay.start)
        pl.when(at.s != t)(far.start)

    trips = (at.core_to, at.x_to, at.y_to, at.far_to, at.pair_to)

    def small_trip(n):
        return mover.remote(small_s.at[n], small_got.at[n], base + 4 + n, trips[n])

    def small_step(n):
        if n > 0:
            small_trip(n - 1).wait_recv()
            small_s[n] = small_s[n - 1] + small_got[n - 1]
        if n < 5:
            small_trip(n).start()
        else:
            mover.out(small_s.at[5], small)

    def end():
        for n in range(6):
            link(n, "c1").wait_recv()
            link(n, "c2").wait_recv()
            for name in links[max(2 - n, 0) :]:
                link(n, name).wait_send()
        for far, stay in (last(0), out_home()):
            far.wait()
            stay.wait()
        for t in range(2):
            near(t).wait_send()
        for n in range(5):
            small_trip(n).wait_send()

    acts = dict(
        start=step_start,
        core=step_core,
        x=step_x,
        y=step_y,
        far=step_far,
        pair=step_pair,
        yy=step_yy,
        near=home_near,
        sum=home_sum,
        oh=out_start,
        small=small_step,
    )

    def turn(*place):
        for word in PLAN.get(",".join(str(v) for v in place), ()):
            name, n = word.split(":")
            acts[name](int(n))

    for n in range(2):
        load(n).start()
    for n in range(2, 4):
        step_start(n)
    load(0).wait()
    link(0, "y").start()
    load(1).wait()
    link(1, "x").start()

    def normal(rows):
        v = x_s[rows, :].astype(f32)
        center = v - jnp.mean(v, axis=-1, keepdims=True)
        spread = jnp.mean(center * center, axis=-1, keepdims=True)
        return center * lax.rsqrt(spread + epsilon)

    def table(n, rows):
        part = rope_s[n, rows, :]
        return jnp.concatenate([part, part], axis=1)

    def turned(v, rows, sign):
        left = pltpu.roll(v, LANES - ROT // 2, 1)
        right = pltpu.roll(v, ROT // 2, 1)
        moved = left * table(1, rows) + right * table(2, rows)
        return v * table(0, rows) + moved if sign > 0 else v * table(0, rows) - moved

    key_pos = lax.broadcasted_iota(jnp.int32, (total, 128), 0)
    kb_s[...] = jnp.where(key_pos < length, 0.0, masked_score)
    lane = lax.broadcasted_iota(jnp.int32, (ROWS, LANES), 1)
    causal = lax.broadcasted_iota(jnp.int32, (ROWS, ROWS), 0) <= lax.broadcasted_iota(
        jnp.int32, (ROWS, ROWS), 1
    )
    gain, offset = bias_ref[3:4, :], bias_ref[4:5, :]

    def span(b):
        return slice(b * ROWS, (b + 1) * ROWS)

    def project(g):
        cols = lambda t: slice(t * inner + g * LANES, t * inner + (g + 1) * LANES)
        bias = lambda t: bias_ref[t : t + 1, g * LANES : (g + 1) * LANES]
        for r in range(blocks):
            rows = span(r)
            if g == 0:
                hr = (normal(rows) * gain + offset).astype(bf16)
                h_s[rows, :] = hr
                ht_s[:, rows] = hr.T
                if r == 0:
                    load_w.wait()
                    load_rope.wait()
                    load_dy.wait()
                    for copy in load_wo:
                        copy.wait()
            else:
                hr = h_s[rows, :]
            q = turned(dot_nn(hr, wqkv_s[:, cols(0)]) + bias(0), rows, 1).astype(bf16)
            q_s[rows, :] = (q.astype(f32) * 0.125).astype(bf16)
            k = turned(dot_nn(hr, wqkv_s[:, cols(1)]) + bias(1), rows, 1).astype(bf16)
            k_s[rows, :] = k
            kt_s[:, rows] = k.T
            v = (dot_nn(hr, wqkv_s[:, cols(2)]) + bias(2)).astype(bf16)
            v_s[rows, :] = v
            vt_s[:, rows] = v.T
            do = dot_nt(dy_s[rows, :], wo_s[g * LANES : (g + 1) * LANES, :]).astype(bf16)
            do_s[rows, :] = do
            dot_s[:, rows] = do.T
            turn("p%d" % g, r)
        dk_s[...] = jnp.zeros_like(dk_s)
        dv_s[...] = jnp.zeros_like(dv_s)

    def one_head(g, i, head, carry):
        feats = pl.ds(pl.multiple_of(head * head_size, head_size), head_size)
        mine = (lane // head_size) == head
        zero = jnp.zeros((ROWS, LANES), bf16)
        rows = span(i)
        qm = jnp.where(mine, q_s[rows, :], zero)
        dom = jnp.where(mine, do_s[rows, :], zero)
        scores = []
        top = None
        for b in range(i + 1):
            sc = dot_nt(k_s[span(b), :], qm)
            kb = kb_s[span(b), :]
            sc = sc + jnp.concatenate([kb, kb], axis=1)
            if b == i:
                sc = jnp.where(causal, sc, masked_score)
            best = jnp.max(sc, axis=0, keepdims=True)
            top = best if top is None else jnp.maximum(top, best)
            scores.append(sc)
        row_sum = None
        for b in range(i + 1):
            scores[b] = jnp.exp(scores[b] - top)
            part = jnp.sum(scores[b], axis=0, keepdims=True)
            row_sum = part if row_sum is None else row_sum + part
        inverse = 1.0 / row_sum
        o_t = None
        for b in range(i + 1):
            scores[b] = scores[b] * inverse
            low = scores[b].astype(bf16)
            dv_s[span(b), :] += dot_nn(low, dom)
            part = dot_nn(vt_s[feats, span(b)], low)
            o_t = part if o_t is None else o_t + part
        ot_s[feats, rows] = o_t
        delta = jnp.sum(dot_s[feats, rows].astype(f32) * o_t, axis=0, keepdims=True)
        dq_t = None
        for b in range(i + 1):
            dp = dot_nt(v_s[span(b), :], dom)
            ds = (scores[b] * (dp - delta)).astype(bf16)
            dk_s[span(b), :] += dot_nn(ds, qm)
            part = dot_nn(kt_s[feats, span(b)], ds)
            dq_t = part if dq_t is None else dq_t + part
        dqt_s[feats, rows] = dq_t * 0.125
        for h in range(LANES // head_size):
            if "%d,%d,%d" % (g, i, h) in PLAN:
                pl.when(head == h)(functools.partial(turn, g, i, h))
        return carry

    def finish_block(g, i, sums):
        rows = span(i)
        cols = slice(g * LANES, (g + 1) * LANES)
        dq = turned(dqt_s[:, rows].T, rows, -1).astype(bf16)
        dk = turned(dk_s[rows, :], rows, -1).astype(bf16)
        dv = dv_s[rows, :].astype(bf16)
        for t, grad in enumerate((dq, dk, dv)):
            sums[t] = sums[t] + jnp.sum(grad.astype(f32), axis=0, keepdims=True)
            dp_s[t, rows, cols] = grad

    def finish_rows(i, gain_sum, shift_sum):
        rows = span(i)
        dh = dot_nt(dp_s[0, rows, :], wqkv_s[:, :inner])
        dh = dh + dot_nt(dp_s[1, rows, :], wqkv_s[:, inner : 2 * inner])
        dh = dh + dot_nt(dp_s[2, rows, :], wqkv_s[:, 2 * inner :])
        home_s[i] = (dh * gain + home_s[i].astype(f32)).astype(bf16)
        gain_sum = gain_sum + jnp.sum(dh * normal(rows), axis=0, keepdims=True)
        return gain_sum, shift_sum + jnp.sum(dh, axis=0, keepdims=True)

    def weight_grads(g):
        cols = slice(g * LANES, (g + 1) * LANES)
        size = width // 8
        for t in range(3):
            for r in range(8):
                grad = dot_nn(ht_s[r * size : (r + 1) * size, :], dp_s[t, :, cols])
                mine_s[g, r % 2, r // 4, r // 2 % 2, :, t * LANES : (t + 1) * LANES] = grad.astype(bf16)
        grad = dot_nn(ot_s[...].astype(bf16), dy_s[...]).astype(bf16)
        size = LANES // 8
        for r in range(8):
            for b in range(4):
                mine_s[
                    g, r % 2, r // 4, r // 2 % 2, b * size : (b + 1) * size, 3 * LANES :
                ] = grad[r * size : (r + 1) * size, b * LANES : (b + 1) * LANES]

    load_x.wait()
    loads_home = [
        mover.here(ffn_pull_ref.at[block(b, ROWS)], home_s.at[b]) for b in range(blocks)
    ]
    load_small.wait()
    gain_sum = jnp.zeros((1, width), f32)
    shift_sum = jnp.zeros((1, width), f32)
    for g in range(2):
        project(g)
        sums = [jnp.zeros((1, LANES), f32) for _ in range(3)]
        for i in reversed(range(blocks)):
            lax.fori_loop(0, LANES // head_size, functools.partial(one_head, g, i), 0)
            finish_block(g, i, sums)
            if g == 1:
                if i == blocks - 1:
                    for copy in loads_home:
                        copy.wait()
                gain_sum, shift_sum = finish_rows(i, gain_sum, shift_sum)
            turn(g, i)
        weight_grads(g)
        row = lax.broadcasted_iota(jnp.int32, (8, LANES), 0)
        for t in range(3):
            start = t % 2 * inner + g * LANES
            cols = slice(start, start + LANES)
            here = row == 4 * at.j + t // 2
            small_s[0, 8:16, cols] = jnp.where(here, sums[t], small_s[0, 8:16, cols])
        if g == 0:
            turn("grads")
    small_s[0, 0:1, :] = gain_sum
    small_s[0, 1:2, :] = shift_sum
    turn("tail")
    end()
    mover.finish()


PLAN = {
    "p0,3": ("y:0",),
    "0,3,1": ("core:2",),
    "0,3,2": ("x:1",),
    "0,2,2": ("y:1",),
    "0,2": ("far:0", "core:3",),
    "0,1,1": ("x:2",),
    "grads": ("y:2",),
    "p1,0": ("far:1",),
    "p1,2": ("x:3",),
    "1,3,3": ("far:2", "pair:0", "y:3",),
    "1,2,3": ("start:4",),
    "1,2": ("near:1",),
    "1,1,1": ("core:4",),
    "1,1,2": ("pair:1",),
    "1,0,0": ("oh:0",),
    "1,0,1": ("x:4",),
    "1,0": ("yy:1",),
    "tail": ("far:3", "small:0", "start:5", "pair:2", "y:4", "small:1", "near:0", "core:5", "x:5", "y:5", "pair:3", "small:2", "far:4", "small:3", "sum:0", "yy:0", "yy:3", "far:5", "pair:4", "yy:2", "pair:5", "sum:1", "small:4", "yy:4", "yy:5", "small:5",),
}


def branch_and_sums(length, x, dy, w_qkv, w_out, bias, rope, out, ffn_pull, gp, gf, small):
    total, width = x.shape
    inner = w_out.shape[0]
    cell = (ROWS // 2, width)
    hbm = pl.BlockSpec(memory_space=pl.ANY)
    vmem = pl.BlockSpec(memory_space=pltpu.VMEM)
    home = jax.ShapeDtypeStruct((2, ROWS, width), bf16)
    buf = lambda dims, kind=bf16: pltpu.VMEM(tuple(dims), kind)
    return pl.pallas_call(
        branch_kernel,
        in_specs=[pl.BlockSpec(memory_space=pltpu.SMEM)] + [hbm] * 4 + [vmem] + [hbm] * 6,
        out_specs=[hbm] * 4,
        out_shape=[
            jax.ShapeDtypeStruct((6, 2, 2, 2) + cell, bf16),
            home,
            home,
            jax.ShapeDtypeStruct(small.shape, f32),
        ],
        scratch_shapes=[
            buf((total, width)),
            buf((total, width)),
            buf((total, width)),
            buf((width, total)),
            buf((width, 3 * inner)),
            buf((inner, width)),
            buf((3, total, 128), f32),
            buf((total, LANES)),
            buf((total, LANES)),
            buf((total, LANES)),
            buf((total, LANES)),
            buf((LANES, total)),
            buf((LANES, total)),
            buf((LANES, total)),
            buf((LANES, total), f32),
            buf((LANES, total), f32),
            buf((total, LANES), f32),
            buf((total, LANES), f32),
            buf((3, total, inner)),
            buf((total, 128), f32),
            buf((2,) + cell),
            buf((3, 2, 2) + cell),
            buf((2, 2, 2, 2) + cell),
            buf((4, 2, 2) + cell),
            buf((5, 2) + cell),
            buf((6,) + cell),
            buf((6,) + cell),
            buf((total // ROWS, ROWS, width)),
            buf((2, ROWS, width)),
            buf((2, ROWS, width)),
            buf((6,) + small.shape, f32),
            buf((5,) + small.shape, f32),
            pltpu.SemaphoreType.DMA((80,)),
            pltpu.SemaphoreType.DMA((80,)),
            pltpu.SemaphoreType.DMA((40,)),
        ],
        compiler_params=pltpu.CompilerParams(
            collective_id=1, has_side_effects=True, vmem_limit_bytes=62 * 2**20
        ),
        name="branch",
    )(length, x, dy, w_qkv, w_out, bias, rope, out, ffn_pull, gp, gf, small)


def last_kernel(
    lengths_ref,
    summed_ref,
    x_ref,
    cot_ref,
    branch_ref,
    pull_ref,
    vectors_ref,
    sums_ref,
    residual_out,
    residual_grad,
    d_proj,
    d_fc,
    d_qkv,
    d_out,
    d_gain_one,
    d_shift_one,
    d_gain_two,
    d_shift_two,
    d_bias_out,
    d_bias_proj,
    d_bqkv,
    d_bfc,
):
    size, width = summed_ref.shape[4:]
    y, core = pl.program_id(0), pl.program_id(1)
    for k in range(2):
        for p in range(2):
            d_proj[p, 0, 0, k] = summed_ref[k, 0, 0, p].astype(f32)
            to = (2 * k + p) * width
            d_fc[:, to : to + width] = summed_ref[2 + k, 0, 0, p].astype(f32)

    rows = x_ref.shape[1]
    features = x_ref[0].astype(f32)
    residual_out[0] = (features + branch_ref[0].astype(f32) + vectors_ref[5:6, :]).astype(bf16)
    hat, inverse = normalize(features)
    pulled = pull_ref[0].astype(f32)
    pulled = inverse * (
        pulled
        - jnp.mean(pulled, axis=-1, keepdims=True)
        - hat * jnp.mean(pulled * hat, axis=-1, keepdims=True)
    )
    start = (lax.axis_index("ctx") * 2 + core) * rows
    valid = start + lax.broadcasted_iota(jnp.int32, (rows, width), 0) < lengths_ref[y]
    own = jnp.where(valid, cot_ref[0].astype(f32), 0.0)
    residual_grad[0] = (own + pulled).astype(bf16)

    for g in range(2):
        for p in range(2):
            for t in range(3):
                for h in range(2):
                    cols = slice((t * 2 + h) * 128, (t * 2 + h + 1) * 128)
                    to = t * 8 + h * 4 + p * 2 + g
                    got = summed_ref[4 + g, 0, 0, p, :, cols]
                    d_qkv[:, to * 128 : (to + 1) * 128] = got.astype(f32)
            for b in range(4):
                got = summed_ref[4 + g, 0, 0, p, b * size // 4 : (b + 1) * size // 4, 3 * LANES :]
                d_out[p, g, 0, 0, :, b * LANES : (b + 1) * LANES] = got.astype(f32)

    @pl.when(y * 2 + core == 0)
    def _():
        first = lax.axis_index("fsdp") == 0
        half = width // 2
        gains = (d_gain_one, d_shift_one, d_gain_two, d_shift_two, d_bias_out)
        for r, ref in (*enumerate(gains), (4, d_bias_proj)):
            line = sums_ref[r : r + 1, :]
            ref[...] = jnp.where(first, line[:, :half], line[:, half:]).reshape(half)
        pieces = []
        for t in range(3):
            for h in range(2):
                for p in range(2):
                    for g in range(2):
                        at = t % 2 * half + (g * 2 + h) * 128
                        pieces.append(sums_ref[8 + 4 * p + t // 2 : 9 + 4 * p + t // 2, at : at + 128])
        line = jnp.concatenate(pieces, axis=1)
        count = 3 * half
        d_bqkv[...] = jnp.where(first, line[:, :count], line[:, count:]).reshape(count)
        line = jnp.concatenate(
            [jnp.where(first, sums_ref[r : r + 1, :], sums_ref[r + 1 : r + 2, :]) for r in (10, 14)],
            axis=1,
        )
        d_bfc[...] = line.reshape(2 * width)


def last_pass(lengths, summed, x, cot, branch, pull, vectors, sums, proj_shape, fc_shape, qkv_shape, out_shape):
    size, width = summed.shape[4:]
    rows = x.shape[1] // 2
    shape = lambda *dims: jax.ShapeDtypeStruct(dims, f32)
    token = pl.BlockSpec((1, rows, width), lambda y, c: (y, c, 0))
    line = lambda count: pl.BlockSpec((count,), lambda y, c: (0,))
    table = lambda count: pl.BlockSpec((count, width), lambda y, c: (0, 0))
    counts = [width // 2] * 6 + [3 * width // 2, 2 * width]
    residual_out, residual_grad, d_proj, d_fc, d_qkv, d_out, *vectors_out = pl.pallas_call(
        last_kernel,
        grid=(2, 2),
        in_specs=[
            pl.BlockSpec(memory_space=pltpu.SMEM),
            pl.BlockSpec((6, 1, 1, 2, size, width), lambda y, c: (0, y, c, 0, 0, 0)),
            token,
            token,
            token,
            token,
            table(8),
            table(16),
        ],
        out_specs=[
            token,
            token,
            pl.BlockSpec((2, 1, 1, 2, size, width), lambda y, c: (0, y, c, 0, 0, 0)),
            pl.BlockSpec((size, 4 * width), lambda y, c: (y * 2 + c, 0)),
            pl.BlockSpec((size, qkv_shape[1]), lambda y, c: (y * 2 + c, 0)),
            pl.BlockSpec((2, 2, 1, 1, size // 4, width), lambda y, c: (0, 0, y, c, 0, 0)),
        ]
        + [line(count) for count in counts],
        out_shape=[
            jax.ShapeDtypeStruct(x.shape, bf16),
            jax.ShapeDtypeStruct(x.shape, bf16),
            shape(2, 2, 2, 2, size, width),
            shape(*fc_shape),
            shape(*qkv_shape),
            shape(2, 2, 2, 2, size // 4, width),
        ]
        + [shape(count) for count in counts],
        compiler_params=pltpu.CompilerParams(vmem_limit_bytes=62 * 2**20),
        name="last",
    )(lengths, summed, x, cot, branch, pull, vectors, sums)
    grads = (d_proj.reshape(proj_shape), d_fc, d_qkv, d_out.reshape(out_shape))
    return residual_out, residual_grad, grads, vectors_out


def normalize(features):
    center = features - jnp.mean(features, axis=-1, keepdims=True)
    spread = jnp.mean(center * center, axis=-1, keepdims=True)
    inverse = lax.rsqrt(spread + epsilon)
    return center * inverse, inverse


def rope_tables(total, head_size):
    half = ROT // 2
    inverse = (rope_base ** (-(2.0 * np.arange(half)) / ROT)).astype(np.float32)
    angles = np.arange(total, dtype=np.float32)[:, None] * inverse[None, :]
    cosine, sine = np.cos(angles), np.sin(angles)
    rest = np.zeros((total, head_size - ROT), np.float32)
    none = np.zeros((total, half), np.float32)
    same = np.concatenate([cosine, cosine, rest + 1.0], axis=1)
    ahead = np.concatenate([-sine, none, rest], axis=1)
    behind = np.concatenate([none, sine, rest], axis=1)
    return jnp.asarray(np.tile(np.stack([same, ahead, behind]), (1, 1, 128 // head_size)), f32)


def finish(residual_in, cotangent, lengths, start, branch, pulled, bias):
    features = residual_in.astype(f32)
    residual_out = (features + branch + bias).astype(bf16)
    own_hat, own_inverse = normalize(features)
    pulled = own_inverse * (
        pulled
        - jnp.mean(pulled, axis=-1, keepdims=True)
        - own_hat * jnp.mean(pulled * own_hat, axis=-1, keepdims=True)
    )
    own_pos = start + jnp.arange(residual_in.shape[1], dtype=jnp.int32)
    valid = (own_pos[None, :] < lengths[:, None])[..., None]
    residual_grad = (jnp.where(valid, cotangent.astype(f32), 0.0) + pulled).astype(bf16)
    return residual_out, residual_grad


def fast_block(residual_in, lengths, cotangent, weights, small, rope):
    weight_fc, weight_proj, weight_qkv, weight_out = weights
    seq_in, seq_grad, w_qkv, w_out, pull, home, gp, gf, part, vectors = front(
        lengths, residual_in, cotangent, *weights, rope, small
    )
    summed, branch, pulled, sums = branch_and_sums(
        lengths, seq_in, seq_grad, w_qkv, w_out, vectors, rope, home, pull, gp, gf, part
    )
    residual_out, residual_grad, grads, vectors_out = last_pass(
        lengths,
        summed,
        residual_in,
        cotangent,
        branch,
        pulled,
        vectors,
        sums,
        weight_proj.shape,
        weight_fc.shape,
        weight_qkv.shape,
        weight_out.shape,
    )
    d_proj, d_fc, d_qkv, d_out = grads
    d_gain_one, d_shift_one, d_gain_two, d_shift_two, d_bout, d_bproj, d_bqkv, d_bfc = vectors_out
    return (
        residual_out,
        residual_grad,
        d_gain_one,
        d_shift_one,
        d_qkv,
        d_bqkv,
        d_out,
        d_bout,
        d_gain_two,
        d_shift_two,
        d_fc,
        d_bfc,
        d_proj,
        d_bproj,
    )


def per_device(
    residual_in,
    lengths,
    gain_attn,
    shift_attn,
    weight_qkv,
    bias_qkv,
    weight_out,
    bias_out,
    gain_ffn,
    shift_ffn,
    weight_fc,
    bias_fc,
    weight_proj,
    bias_proj,
    cotangent,
):
    seqs, block_rows, width = residual_in.shape
    n_ctx, n_fsdp = lax.axis_size("ctx"), lax.axis_size("fsdp")
    parts = n_ctx // seqs
    total = n_ctx * block_rows
    units = weight_fc.shape[1]
    head_size = width // HEADS
    c, f, dp = lax.axis_index("ctx"), lax.axis_index("fsdp"), lax.axis_index("dp")
    s, j = c // parts, c % parts
    place = dict(c=c, f=f, dp=dp, s=s, j=j, y=dp // 2, core=dp % 2)
    spread_heads = HEADS % (n_fsdp * parts) == 0
    n_h = n_fsdp if spread_heads else 1
    inner = width // parts

    rows_here = weight_qkv.shape[0]
    own_heads = lambda v: pick(v.reshape(3, n_h, parts, -1), j, 2)
    fast = (seqs, n_ctx, n_fsdp, lax.axis_size("dp")) == (2, 4, 2, 4)
    small_local = jnp.concatenate(
        [gain_attn, shift_attn, gain_ffn, shift_ffn, bias_out, bias_proj, bias_qkv, bias_fc]
    )
    part_width = width // n_fsdp
    length = pick(lengths, s)
    rope = rope_tables(total, head_size)
    own_part = lambda v, size=part_width: lax.dynamic_slice_in_dim(v, f * size, size)
    if fast:
        return fast_block(
            residual_in,
            lengths,
            cotangent,
            (weight_fc, weight_proj, weight_qkv, weight_out),
            (gain_attn, shift_attn, gain_ffn, shift_ffn, bias_out, bias_proj, bias_qkv, bias_fc),
            rope,
        )
    small = lax.all_gather(small_local, "fsdp", axis=0)
    vec = lambda at, size: small[:, at : at + size].reshape(-1).astype(f32)
    gain_one, shift_one, gain_two, shift_two, b_out, b_proj = (
        vec(i * part_width, part_width) for i in range(6)
    )
    b_qkv = vec(6 * part_width, 3 * part_width)
    b_fc = vec(9 * part_width, units // n_fsdp)

    fc_local = pick(weight_fc.reshape(rows_here, n_fsdp, parts, -1), j, 2).reshape(rows_here, -1)
    proj_local = pick(weight_proj.reshape(parts, -1, width), j)
    qkv_local = pick(weight_qkv.reshape(rows_here, 3, n_h, parts, -1), j, 3).reshape(rows_here, -1)
    seq_in = gather_sequence(residual_in, place, parts)
    w_fc = gather_rows(fc_local, place).reshape(width, -1)
    w_proj = gather_rows(proj_local, place).reshape(-1, width)
    seq_grad = gather_sequence(cotangent, place, parts)
    w_qkv = gather_rows(qkv_local, place).reshape(width, -1)
    if spread_heads:
        w_out = gather_rows(pick(weight_out.reshape(parts, -1, width), j), place).reshape(-1, width)
    else:
        w_out = lax.all_gather(weight_out, "fsdp", axis=0, tiled=True)
        w_out = pick(w_out.reshape(parts, -1, width), j)
    b_qkv_j = own_heads(b_qkv).reshape(3, 1, inner)
    b_fc_j = pick(b_fc.reshape(n_fsdp, parts, -1), j, 1).reshape(1, -1)
    b_fc_j = jnp.broadcast_to(b_fc_j, (8, b_fc_j.shape[1]))

    positions = jnp.arange(total, dtype=jnp.int32)
    seq_grad = jnp.where((positions < length)[:, None], seq_grad, jnp.zeros((), bf16))
    xhat, _ = normalize(seq_in.astype(f32))
    hidden_one = (xhat * gain_one + shift_one).astype(bf16)
    hidden_two = (xhat * gain_two + shift_two).astype(bf16)

    ffn_out, ffn_dh, g_fc, g_proj, g_bfc = ffn_branch(
        hidden_two, seq_grad, w_fc, w_proj, b_fc_j
    )
    ffn_sums = (jnp.sum(ffn_dh * xhat, axis=0), jnp.sum(ffn_dh, axis=0))
    own_grad = jnp.sum(seq_grad.astype(f32), axis=0) / parts
    attn_out, attn_dh, g_qkv, g_out, g_bqkv = attention_branch(
        length[None],
        hidden_one,
        seq_grad,
        w_qkv,
        w_out,
        jnp.broadcast_to(b_qkv_j, (3, 8, inner)),
        jnp.tile(rope, (1, 1, LANES // 128)),
    )
    g_bqkv_all = jnp.zeros((3, n_h, parts, inner // n_h), f32)
    g_bqkv_all = lax.dynamic_update_index_in_dim(
        g_bqkv_all, g_bqkv[:, 0].reshape(3, n_h, -1), j, 2
    )
    g_bfc_all = jnp.zeros((n_fsdp, parts, units // (n_fsdp * parts)), f32)
    g_bfc_all = lax.dynamic_update_index_in_dim(g_bfc_all, g_bfc[0].reshape(n_fsdp, -1), j, 1)
    rows_of = (
        jnp.sum(attn_dh * xhat, axis=0),
        jnp.sum(attn_dh, axis=0),
        *ffn_sums,
        own_grad,
        g_bqkv_all.reshape(-1),
        g_bfc_all.reshape(-1),
    )
    flat = sum_everywhere(jnp.concatenate(rows_of).reshape(-1, 128)).reshape(-1)
    small_grads = []
    at = 0
    for entry in rows_of:
        size = entry.shape[0]
        small_grads.append(own_part(flat[at : at + size], size // n_fsdp))
        at += size
    d_gain_one, d_shift_one, d_gain_two, d_shift_two, d_bias, d_bqkv, d_bfc = small_grads
    branch_part = (attn_out + ffn_out).astype(bf16)
    pull_part = (attn_dh * gain_one + ffn_dh * gain_two).astype(bf16)
    d_proj = reduce_rows(g_proj.reshape(n_fsdp, -1, width), place, parts)
    d_fc = reduce_rows(g_fc.reshape(n_fsdp, rows_here, -1), place, parts)
    q_rows = jnp.swapaxes(g_qkv.reshape(3, n_fsdp, rows_here, inner), 0, 1)
    q_rows = jnp.swapaxes(q_rows, 1, 2).reshape(n_fsdp, rows_here, 3 * inner)
    d_qkv = reduce_rows(q_rows, place, parts)
    d_proj = jnp.swapaxes(d_proj, 0, 1).reshape(weight_proj.shape)
    d_fc = d_fc.reshape(rows_here, parts, n_fsdp, -1)
    d_fc = jnp.swapaxes(d_fc, 1, 2).reshape(weight_fc.shape)
    d_qkv = d_qkv.reshape(rows_here, parts, 3, n_h, -1)
    d_qkv = jnp.transpose(d_qkv, (0, 2, 3, 1, 4)).reshape(weight_qkv.shape)
    if spread_heads:
        d_out = reduce_rows(g_out.reshape(n_fsdp, -1, width), place, parts)
        d_out = jnp.swapaxes(d_out, 0, 1).reshape(weight_out.shape)
    else:
        full = jnp.zeros((parts, inner, width), bf16)
        full = lax.dynamic_update_index_in_dim(full, g_out, j, 0).reshape(width, width)
        d_out = lax.psum_scatter(full, "fsdp", scatter_dimension=0, tiled=True)
        d_out = lax.psum(d_out, ("dp", "ctx")).astype(f32)
    branch = return_blocks(branch_part, place, parts, seqs)
    pulled = return_blocks(pull_part, place, parts, seqs)

    residual_out, residual_grad = finish(
        residual_in, cotangent, lengths, c * block_rows, branch, pulled, b_out + b_proj
    )
    return (
        residual_out,
        residual_grad,
        d_gain_one,
        d_shift_one,
        d_qkv,
        d_bqkv,
        d_out,
        d_bias,
        d_gain_two,
        d_shift_two,
        d_fc,
        d_bfc,
        d_proj,
        d_bias,
    )


def solution(mesh):
    tokens = P(("dp", "fsdp"), "ctx", None)
    vector, matrix = P("fsdp"), P("fsdp", None)
    return jax.shard_map(
        per_device,
        mesh=mesh,
        in_specs=(
            tokens,
            P(("dp", "fsdp")),
            vector,
            vector,
            matrix,
            vector,
            matrix,
            vector,
            vector,
            vector,
            matrix,
            vector,
            matrix,
            vector,
            tokens,
        ),
        out_specs=(
            tokens,
            tokens,
            vector,
            vector,
            matrix,
            vector,
            matrix,
            vector,
            vector,
            vector,
            matrix,
            vector,
            matrix,
            vector,
        ),
        check_vma=False,
    )
```
